32 devices in a mesh: ctx: 8 (over y, x, core), fsdp: 4 (over z).
Axes of the slice: x: 2, y: 2, z: 4, core: 2. Of those that a mesh axis runs over, the one named last changes fastest.
Arguments:
- tokens: bfloat16 [4, 3072, 960], P('fsdp', 'ctx'), may hold values from -6 to 6
- attn_gain: bfloat16 [960], P('fsdp'), may hold values from 0.25 to 1.75
- query_weight: bfloat16 [960, 960], P('fsdp'), may hold values from -0.1875 to 0.1875
- key_weight: bfloat16 [960, 320], P('fsdp'), may hold values from -0.1875 to 0.1875
- value_weight: bfloat16 [960, 320], P('fsdp'), may hold values from -0.1875 to 0.1875
- out_weight: bfloat16 [960, 960], P('fsdp'), may hold values from -3.5 to 3.5
- mlp_gain: bfloat16 [960], P('fsdp'), may hold values from 0.25 to 1.75
- gate_weight: bfloat16 [960, 2560], P('fsdp'), may hold values from -0.1875 to 0.1875
- up_weight: bfloat16 [960, 2560], P('fsdp'), may hold values from -0.1875 to 0.1875
- down_weight: bfloat16 [2560, 960], P('fsdp'), may hold values from -0.125 to 0.125
- cotangent: bfloat16 [4, 3072, 960], P('fsdp', 'ctx'), may hold values from -6 to 6
- cont_lengths: int32 [4, 2], P('fsdp'), may hold values from 1 to 1024, 1536 in all within a row
- block_deal: int32 [16], replicated, may hold values from 0 to 15, as said below
Outputs:
- output: bfloat16 [4, 3072, 960], P('fsdp', 'ctx')
- tokens_grad: bfloat16 [4, 3072, 960], P('fsdp', 'ctx')
- attn_gain_grad: float32 [960], P('fsdp')
- query_grad: float32 [960, 960], P('fsdp')
- key_grad: float32 [960, 320], P('fsdp')
- value_grad: float32 [960, 320], P('fsdp')
- out_grad: float32 [960, 960], P('fsdp')
- mlp_gain_grad: float32 [960], P('fsdp')
- gate_grad: float32 [960, 2560], P('fsdp')
- up_grad: float32 [960, 2560], P('fsdp')
- down_grad: float32 [2560, 960], P('fsdp')
The draws below stay inside these ranges and needn't reach their ends.
Inputs may be any that keep to these rules, and one draw needn't show every extreme that they name: `block_deal`: stored blocks 2 c and 2 c + 1 hold natural blocks k and 15 - k, in either order, for some k; every block appears once. `cont_lengths`: each group's 2 lengths add up to 1536.
All inputs are finite; a program needn't handle non-finite values.
Results may differ from the reference program's by a relative error of at most 0.02.
Values may be sent and summed in bfloat16 or wider, within the bound.
A program may use at most 192 MiB of HBM per device.

```python
import math
import jax
import jax.numpy as jnp
import numpy as np
from jax import lax

D = 960
HEADS = 15
KVH = 5
HD = 64
FF = 2560
MOST = 1024
KVW = 320
GTOK = 3072
PROMPT = 1536
CONTS = 2
GROUPS = 4
BLOCKS = 16
BLOCK = 192


def draw_block_deal(key, part):
    key = jax.random.fold_in(key, 11)
    pair_key, flip_key = jax.random.split(key)
    pair_count = BLOCKS // 2
    order = jax.random.permutation(pair_key, pair_count).astype(jnp.int32)
    flips = jax.random.randint(flip_key, (pair_count,), 0, 2)
    leading = jnp.where(flips == 1, order, BLOCKS - 1 - order).astype(jnp.int32)
    trailing = (BLOCKS - 1 - leading).astype(jnp.int32)
    return jnp.stack([leading, trailing], axis=1).reshape(BLOCKS)


def levels(stream_key, dims, shards, low, top_value):
    level = 1.0
    for axis_at, parts in shards:
        draws = jax.random.uniform(jax.random.fold_in(jax.random.fold_in(stream_key, 6), axis_at), (parts,), jnp.float32, low / len(shards), top_value / len(shards))
        level = level * jnp.repeat(jnp.exp(draws), dims[axis_at] // parts).reshape((-1,) + (1,) * (len(dims) - 1 - axis_at))
    return level


def profile(number_of, total, reach, skew):
    portions = [(1 << 20) // math.isqrt(rank ** skew) + 1 for rank in range(2, number_of + 1)]
    surplus, holding = total - reach - (number_of - 1), [1] * (number_of - 1)
    while surplus > 0:
        movable = [i for i in range(number_of - 1) if holding[i] < reach]
        whole, budget = sum([portions[i] for i in movable]), surplus
        for i in movable:
            more = min(reach - holding[i], max(1, budget * portions[i] // whole), surplus)
            holding[i] = holding[i] + more
            surplus = surplus - more
    return np.array([reach] + holding)


def ragged_sizes(stream_key, number_of, total, bound, lean):
    if number_of == 2:
        one = jax.random.randint(stream_key, (), max(1, total - bound), min(bound, total - 1) + 1)
        return jnp.stack([one, total - one])
    sizes = jnp.asarray(profile(number_of, total, bound, lean), jnp.int32)
    twos = (number_of - 1) // 2
    donor, sink = sizes[1:1 + 2 * twos:2], sizes[2:2 + 2 * twos:2]
    room = jnp.minimum(donor - 1, bound - sink)
    shifted = jax.random.randint(jax.random.fold_in(stream_key, 1), (twos,), 0, 1 << 20) % (room + 1)
    sizes = sizes.at[1:1 + 2 * twos:2].set(donor - shifted).at[2:2 + 2 * twos:2].set(sink + shifted)
    return sizes[jax.random.permutation(jax.random.fold_in(stream_key, 2), number_of)]


def normal_values(stream_key, extent, deviation, bound, cuts=(), held_as=jnp.bfloat16):
    drawn = deviation * jax.random.normal(stream_key, extent, jnp.float32)
    if cuts:
        drawn = drawn * levels(stream_key, extent, cuts, -0.22, 0.18)
    return jnp.clip(drawn, -bound, bound).astype(held_as)


def setup_inputs(seed: int = 0) -> dict:
    arg_keys = jax.random.split(jax.random.key(seed), 14)
    return {
        "tokens": normal_values(arg_keys[0], (GROUPS, GTOK, D), 1.0, 6.0, ((0, 4), (1, 8))),
        "attn_gain": jnp.clip(1.0 + 0.15 * jax.random.normal(arg_keys[1], (D,), jnp.float32), 0.25, 1.75).astype(jnp.bfloat16),
        "query_weight": normal_values(arg_keys[2], (D, D), D ** -0.5, 0.1875, ((0, 4),)),
        "key_weight": normal_values(arg_keys[3], (D, KVW), D ** -0.5, 0.1875, ((0, 4),)),
        "value_weight": normal_values(arg_keys[4], (D, KVW), D ** -0.5, 0.1875, ((0, 4),)),
        "out_weight": normal_values(arg_keys[5], (D, D), (max(2, D // 256)) ** -0.5, 3.5, ((0, 4),)),
        "mlp_gain": jnp.clip(1.0 + 0.15 * jax.random.normal(arg_keys[6], (D,), jnp.float32), 0.25, 1.75).astype(jnp.bfloat16),
        "gate_weight": normal_values(arg_keys[7], (D, FF), D ** -0.5, 0.1875, ((0, 4),)),
        "up_weight": normal_values(arg_keys[8], (D, FF), D ** -0.5, 0.1875, ((0, 4),)),
        "down_weight": normal_values(arg_keys[9], (FF, D), FF ** -0.5, 0.125, ((0, 4),)),
        "cotangent": normal_values(arg_keys[10], (GROUPS, GTOK, D), 1.0, 6.0, ((0, 4), (1, 8))),
        "cont_lengths": jax.vmap(lambda own: ragged_sizes(own, CONTS, PROMPT, MOST, 1))(jax.random.split(arg_keys[11], GROUPS)).reshape((GROUPS, CONTS)).astype(jnp.int32),
        "block_deal": draw_block_deal(jax.random.fold_in(arg_keys[13], 71), 0),
    }


EPSILON = 1e-05
THETA = 100000.0
MASKED = -1e+30

@jax.custom_vjp
def low(v):
    return lax.optimization_barrier(v.astype(jnp.bfloat16)).astype(jnp.float32)

@jax.custom_vjp
def low_back(v):
    return v

def low_keep(v):
    return (low(v), None)

def low_pass(kept, grad):
    return (grad,)

def back_keep(v):
    return (v, None)

def back_low(kept, grad):
    return (low(grad),)
low.defvjp(low_keep, low_pass)
low_back.defvjp(back_keep, back_low)

def high_dot(left, right):
    return jnp.dot(left, right, precision=lax.Precision.HIGHEST, preferred_element_type=jnp.float32)

def token_info(row_ids, block_deal, lengths, block_size, prompt_size):
    block_count = block_deal.shape[0]
    picked = (row_ids // block_size)[:, None] == jnp.arange(block_count, dtype=jnp.int32)[None, :]
    natural = lax.optimization_barrier(jnp.sum(jnp.where(picked, block_deal[None, :], 0), axis=1)).astype(jnp.int32) * block_size + row_ids % block_size
    offset = (natural - prompt_size).astype(jnp.int32)
    ending = jnp.cumsum(lengths).astype(jnp.int32)
    starting = (ending - lengths).astype(jnp.int32)
    segment = lax.optimization_barrier(jnp.sum((offset[:, None] >= ending[None, :]).astype(jnp.int32), axis=1)).astype(jnp.int32)
    inside = segment[:, None] == jnp.arange(lengths.shape[0], dtype=jnp.int32)[None, :]
    beginning = lax.optimization_barrier(jnp.sum(jnp.where(inside, starting[None, :], 0), axis=1)).astype(jnp.int32)
    position = jnp.where(offset < 0, natural, prompt_size + offset - beginning).astype(jnp.int32)
    segment = jnp.where(offset < 0, -1, segment).astype(jnp.int32)
    return (natural, segment, position)

def rope_angles(position, head_size):
    half_size = head_size // 2
    frequency = THETA ** (-2.0 * jnp.arange(half_size, dtype=jnp.float32) / head_size)
    angle = position.astype(jnp.float32)[:, None] * frequency[None, :]
    return (jnp.cos(angle), jnp.sin(angle))

def rotate(values, cos_rows, sin_rows):
    row_count = values.shape[0]
    half_size = cos_rows.shape[1]
    split_up = values.reshape(row_count, -1, 2, half_size)
    leading = split_up[:, :, 0, :]
    trailing = split_up[:, :, 1, :]
    cos_part = cos_rows[:, None, :]
    sin_part = sin_rows[:, None, :]
    turned = jnp.stack([leading * cos_part - trailing * sin_part, trailing * cos_part + leading * sin_part], axis=2)
    return turned.reshape(row_count, -1)

def rms_scale(values):
    return values * lax.rsqrt(lax.optimization_barrier(jnp.mean(values * values, axis=1, keepdims=True)) + EPSILON)

def split_heads(matrix, count):
    return matrix.reshape(GTOK, count, HD).transpose(1, 0, 2)

def group_forward(inputs, attn_gain, query_weight, key_weight, value_weight, out_weight, mlp_gain, gate_weight, up_weight, down_weight, lengths, block_deal):
    row_ids = jnp.arange(GTOK, dtype=jnp.int32)
    natural, segment, position = token_info(row_ids, block_deal, lengths, BLOCK, PROMPT)
    allowed = (natural[None, :] <= natural[:, None]) & ((segment[None, :] < 0) | (segment[None, :] == segment[:, None]))
    cos_rows, sin_rows = rope_angles(position, HD)
    normed_one = low(rms_scale(inputs) * attn_gain)
    query = low(rotate(low_back(high_dot(normed_one, query_weight)), cos_rows, sin_rows))
    keys = low(rotate(low_back(high_dot(normed_one, key_weight)), cos_rows, sin_rows))
    value = low_back(low(high_dot(normed_one, value_weight)))
    share = HEADS // KVH

    def head_attend(pieces):
        query_head, key_head, value_head = pieces
        scores = low_back(high_dot(query_head, key_head.T) * 0.125)
        scores = jnp.where(allowed, scores, MASKED)
        biggest = lax.optimization_barrier(jnp.max(scores, axis=1, keepdims=True))
        weights = jnp.exp(scores - biggest)
        probs = weights / lax.optimization_barrier(jnp.sum(weights, axis=1, keepdims=True))
        return high_dot(low(probs), value_head)
    key_heads = jnp.repeat(split_heads(keys, KVH), share, axis=0)
    value_heads = jnp.repeat(split_heads(value, KVH), share, axis=0)
    per_head = lax.map(jax.checkpoint(head_attend), (split_heads(query, HEADS), key_heads, value_heads))
    attended = low_back(low(per_head.transpose(1, 0, 2).reshape(GTOK, D)))
    resid = inputs + low_back(high_dot(attended, out_weight))
    normed_two = low(rms_scale(resid) * mlp_gain)
    gate = low_back(high_dot(normed_two, gate_weight))
    upward = low_back(high_dot(normed_two, up_weight))
    product = low(jax.nn.silu(gate) * upward)
    return resid + high_dot(product, down_weight)

def reference(tokens, attn_gain, query_weight, key_weight, value_weight, out_weight, mlp_gain, gate_weight, up_weight, down_weight, cotangent, cont_lengths, block_deal):

    def forward(inputs, gain_one, w_query, w_key, w_value, w_out, gain_two, w_gate, w_up, w_down):

        def one_group(carry, pieces):
            group_inputs, group_lengths = pieces
            result = group_forward(group_inputs, gain_one, w_query, w_key, w_value, w_out, gain_two, w_gate, w_up, w_down, group_lengths, block_deal)
            return (carry, result)
        _, results = lax.scan(one_group, jnp.zeros((), jnp.float32), (inputs, cont_lengths))
        return results
    result, pullback = jax.vjp(forward, tokens.astype(jnp.float32), attn_gain.astype(jnp.float32), query_weight.astype(jnp.float32), key_weight.astype(jnp.float32), value_weight.astype(jnp.float32), out_weight.astype(jnp.float32), mlp_gain.astype(jnp.float32), gate_weight.astype(jnp.float32), up_weight.astype(jnp.float32), down_weight.astype(jnp.float32))
    grads = pullback(cotangent.astype(jnp.float32))
    return (result.astype(jnp.bfloat16), grads[0].astype(jnp.bfloat16), grads[1], grads[2], grads[3], grads[4], grads[5], grads[6], grads[7], grads[8], grads[9])
```

```python
import functools

import jax
import jax.numpy as jnp
from jax import lax
from jax.experimental import pallas as pl
from jax.experimental.pallas import tpu as pltpu
from jax.sharding import PartitionSpec as P

HD = 64
LANES = 128
EPSILON = 1e-05
THETA = 100000.0
MASKED = -1e30
LOG2E = 1.4426950408889634
VMEM_LIMIT = 63 * 1024 * 1024
F32 = jnp.float32
BF16 = jnp.bfloat16


def nt(left, right):
    return lax.dot_general(left, right, (((1,), (1,)), ((), ())), preferred_element_type=F32)


def nn(left, right):
    return lax.dot_general(left, right, (((1,), (0,)), ((), ())), preferred_element_type=F32)


def tn(left, right):
    return lax.dot_general(left, right, (((0,), (0,)), ((), ())), preferred_element_type=F32)


def rope_tile(tile, cos, sin):
    lane = lax.broadcasted_iota(jnp.int32, tile.shape, 1) % HD
    partner = jnp.where(
        lane < HD // 2,
        pltpu.roll(tile, LANES - HD // 2, 1),
        pltpu.roll(tile, HD // 2, 1),
    )
    return tile * cos + partner * sin


def head_of(tiles, index):
    start = (index % 2) * HD
    return tiles[index // 2][:, start : start + HD]


MESH = pl.DeviceIdType.MESH
ATTN, FF, DOWN = 0, 1, 2
CORE, FIRST, SECOND = -1, -2, -3


class Links:
    def __init__(self, core, fsdp, send, recv, plan):
        self.core = core
        self.fsdp = fsdp
        self.ctx = lax.axis_index("ctx")
        self.z = lax.axis_index("fsdp")
        self.chip = self.ctx // 2
        self.first = 1 if core == 0 else 2
        self.second = 3 - self.first
        self.send_sem, self.recv_sem = send, recv
        self.plan = plan
        self.open = []

    def target(self, hop):
        if hop == CORE:
            return (lax.bitwise_xor(self.ctx, 1), self.z)
        if hop == FIRST:
            return (lax.bitwise_xor(self.ctx, 2 * self.first), self.z)
        if hop == SECOND:
            return (lax.bitwise_xor(self.ctx, 2 * self.second), self.z)
        return (self.ctx, lax.bitwise_xor(self.z, hop))

    def copy(self, key, hop, src, dst):
        slot = self.plan.setdefault(key, len(self.plan))
        return pltpu.make_async_remote_copy(
            src_ref=src,
            dst_ref=dst,
            send_sem=self.send_sem.at[slot],
            recv_sem=self.recv_sem.at[slot],
            device_id=self.target(hop),
            device_id_type=MESH,
        )

    def send(self, key, hop, src, dst):
        copy = self.copy(key, hop, src, dst)
        copy.start()
        self.open.append((key, getattr(src, "ref", src), src.shape))

    def landed(self, key, dst):
        self.copy(key, CORE, dst, dst).wait_recv()

    def drain(self):
        for key, base, shape in self.open:
            at = (0,) * (len(base.shape) - len(shape)) + tuple(pl.ds(0, size) for size in shape)
            self.copy(key, CORE, base.at[at], base.at[at]).wait_send()


def greet(hops, fsdp):
    ctx, z = lax.axis_index("ctx"), lax.axis_index("fsdp")
    barrier = pltpu.get_barrier_semaphore()
    targets = [(lax.bitwise_xor(ctx, h), z) for h in (1, 2, 4)]
    if "z" in hops:
        targets += [(ctx, lax.bitwise_xor(z, d)) for d in range(1, fsdp)]
    for target in targets:
        pl.semaphore_signal(barrier, inc=1, device_id=target, device_id_type=MESH)
    pl.semaphore_wait(barrier, len(targets))


def by_core(program):
    for core in (0, 1):
        pl.when(lax.axis_index("ctx") % 2 == core)(functools.partial(program, core))


def sub(base, size, unit):
    return pl.ds(pl.multiple_of(base, unit), size)


def lanes(ref, tiles, rows=slice(None)):
    return jnp.concatenate([ref[t, rows, :] for t in tiles], axis=1)


def pack_tiles(parts):
    matrix = jnp.concatenate(parts, axis=1)
    short = -matrix.shape[1] % LANES
    if short:
        matrix = jnp.concatenate([matrix, jnp.zeros((matrix.shape[0], short), matrix.dtype)], axis=1)
    return [matrix[:, t * LANES : (t + 1) * LANES] for t in range(matrix.shape[1] // LANES)]


class Share:
    def __init__(self, name, core, shard):
        self.name, self.core = name, core
        self.shard = shard
        self.offset, self.rows = 0, shard
        if name == ATTN:
            half = -(-shard // 32) * 16
            self.offset, self.rows = (0, half) if core == 0 else (half, shard - half)

    def at(self, ref, zi, q):
        rows = sub(zi * self.shard + self.offset, self.rows, 16)
        if self.name == ATTN:
            return ref.at[pl.ds(q * (ref.shape[0] // 4), ref.shape[0] // 4), rows]
        if self.name == FF:
            return ref.at[self.core, pl.ds(q * (ref.shape[1] // 4), ref.shape[1] // 4), rows]
        return ref.at[2 * q + self.core, rows]

    def buffer(self, ref):
        return ref.at[:, pl.ds(0, self.rows)] if self.name == ATTN else ref


PACKAGES = (ATTN, FF, DOWN)


def both_cores(make):
    tables = [make(0), make(1)]

    def run(*names):
        for core in (0, 1):
            def program(core=core):
                for name in names:
                    tables[core][name]()

            pl.when(lax.axis_index("ctx") % 2 == core)(program)

    return run


def weight_stages(core, fsdp, plan, refs, send, recv):
    links = Links(core, fsdp, send, recv, plan)
    z, chip = links.z, links.chip
    near, far = lax.bitwise_xor(chip, links.first), lax.bitwise_xor(chip, links.second)
    corner = lax.bitwise_xor(chip, 3)
    shards = {ATTN: refs[ATTN].shape[1] // fsdp, FF: refs[FF].shape[2] // fsdp, DOWN: refs[DOWN].shape[1] // fsdp}
    mine = {k: Share(k, core, shards[k]) for k in PACKAGES}
    twin = {k: Share(k, 1 - core, shards[k]) for k in PACKAGES}
    stages = {}

    def over_z(k):
        here = mine[k].at(refs[k], z, chip)
        for d in range(1, fsdp):
            links.send((k, "z", d), d, here, here)

    def spread(k):
        for d in range(1, fsdp):
            piece = mine[k].at(refs[k], lax.bitwise_xor(z, d), chip)
            links.landed((k, "z", d), piece)
            links.send((k, FIRST, d), FIRST, piece, piece)
            links.send((k, SECOND, d), SECOND, piece, piece)
            links.send((k, CORE, d, 0), CORE, piece, piece)

    def forward(k):
        for d in range(1, fsdp):
            piece = mine[k].at(refs[k], lax.bitwise_xor(z, d), near)
            links.landed((k, FIRST, d), piece)
            links.send((k, "corner", d), SECOND, piece, piece)
            links.send((k, CORE, d, 1), CORE, piece, piece)

    def pass_on(k):
        for d in range(1, fsdp):
            for i, (what, q) in enumerate(((SECOND, far), ("corner", corner))):
                piece = mine[k].at(refs[k], lax.bitwise_xor(z, d), q)
                links.landed((k, what, d), piece)
                links.send((k, CORE, d, 2 + i), CORE, piece, piece)

    def finish(k):
        for d in range(1, fsdp):
            for i, q in ((0, chip), (1, far), (2, near), (3, corner)):
                links.landed((k, CORE, d, i), twin[k].at(refs[k], lax.bitwise_xor(z, d), q))

    for k in PACKAGES:
        for fn in (over_z, spread, forward, pass_on, finish):
            stages[fn.__name__, k] = functools.partial(fn, k)

    def gains_out():
        for d in range(1, fsdp):
            links.send(("gains", d), d, refs["gains"].at[z], refs["gains"].at[z])

    def gains_in():
        for d in range(1, fsdp):
            links.landed(("gains", d), refs["gains"].at[lax.bitwise_xor(z, d)])

    stages["gains_out"], stages["gains_in"], stages["drain"] = gains_out, gains_in, links.drain
    return stages


def kv_stages(core, plan, kv_all, send, recv):
    links = Links(core, 1, send, recv, plan)
    ctx = links.ctx
    near = lax.bitwise_xor(ctx, 2 * links.first)
    far = lax.bitwise_xor(ctx, 2 * links.second)
    corner = lax.bitwise_xor(ctx, 6)

    def start():
        for b in range(2):
            piece = kv_all.at[ctx, b]
            links.send(("kv first", b), FIRST, piece, piece)
            links.send(("kv second", b), SECOND, piece, piece)
            links.send(("kv core", 0, b), CORE, piece, piece)

    def forward():
        for b in range(2):
            piece = kv_all.at[near, b]
            links.landed(("kv first", b), piece)
            links.send(("kv corner", b), SECOND, piece, piece)
            links.send(("kv core", 1, b), CORE, piece, piece)

    def pass_on():
        for i, (what, owner) in enumerate((("kv second", far), ("kv corner", corner))):
            for b in range(2):
                piece = kv_all.at[owner, b]
                links.landed((what, b), piece)
                links.send(("kv core", 2 + i, b), CORE, piece, piece)

    def finish():
        for i, owner in ((0, ctx), (1, far), (2, near), (3, corner)):
            for b in range(2):
                links.landed(("kv core", i, b), kv_all.at[lax.bitwise_xor(owner, 1), b])

    return {"start": start, "forward": forward, "pass_on": pass_on, "finish": finish, "drain": links.drain}


def store_projection(sizes, raw_tiles, cos, sin, q_ref, kv_at):
    heads, kvh, block = sizes
    share = heads // kvh
    tiles = [rope_tile(raw_tiles[j], cos, sin).astype(BF16) for j in range((heads + kvh) // 2)]
    tiles += [raw_tiles[j].astype(BF16) for j in range((heads + kvh) // 2, len(raw_tiles))]

    def head(index):
        start = (index % 2) * HD
        return tiles[index // 2][:, start : start + HD]

    zero = jnp.zeros((block, HD), BF16)
    for h in range(heads):
        piece = head(h) * jnp.asarray(0.125, BF16)
        g, i = h // share, h % share
        for b in range(2):
            q_ref[g, b, i * block : (i + 1) * block, :] = jnp.concatenate(
                [piece[b * block : (b + 1) * block], zero], axis=1
            )
    for g in range(kvh):
        pair = jnp.concatenate([head(heads + g), head(heads + kvh + g)], axis=1)
        for b in range(2):
            kv_at(b, g)[...] = pair[b * block : (b + 1) * block]


def rms_inverse(x):
    return lax.rsqrt(jnp.mean(x * x, axis=1, keepdims=True) + EPSILON)


def attend_step(n, me, g, j, pick_ref, segq_ref, segk_ref, q_ref, kv_ref, top_ref, acc_ref):
    block = kv_ref.shape[3]
    rows = q_ref.shape[2]
    value_lane = lax.broadcasted_iota(jnp.int32, (block, LANES), 1) >= HD

    def scores(kind, tile, mask):
        s = nt(tile, q_ref[g, kind])
        return s if mask is None else jnp.where(mask, s, MASKED)

    def weigh(s, top, tile):
        p = jnp.exp2((s - top) * LOG2E).astype(BF16)
        return tn(jnp.where(value_lane, tile, jnp.asarray(1, BF16)), p)

    def own():
        lane_rows = lax.rem(lax.broadcasted_iota(jnp.int32, (block, rows), 1), block)
        tri = lax.broadcasted_iota(jnp.int32, (block, rows), 0) <= lane_rows
        own0, own1 = kv_ref[me, 0, g], kv_ref[me, 1, g]
        s0 = scores(0, own0, tri)
        top0 = jnp.max(s0, axis=0, keepdims=True)
        acc_ref[0] = weigh(s0, top0, own0)
        top_ref[0] = jnp.broadcast_to(top0, top_ref.shape[1:])
        s1 = scores(1, own1, tri & (segq_ref[0:1, :] == segk_ref[0]))
        s2 = scores(1, own0, None)
        top1 = jnp.maximum(jnp.max(s1, axis=0, keepdims=True), jnp.max(s2, axis=0, keepdims=True))
        acc_ref[1] = weigh(s1, top1, own1) + weigh(s2, top1, own0)
        top_ref[1] = jnp.broadcast_to(top1, top_ref.shape[1:])

    def other():
        at = lax.rem(me + j, n)
        kind = pick_ref[j]
        is_prompt = kind == 0
        tile0, tile1 = kv_ref[at, 0, g], kv_ref[at, kind, g]
        s1 = scores(1, tile0, None)
        s2 = scores(kind, tile1, (segq_ref[0:1, :] == segk_ref[j]) | is_prompt)
        old_p, old_c = top_ref[0, 0:1, :], top_ref[1, 0:1, :]
        high1 = jnp.max(s1, axis=0, keepdims=True)
        high2 = jnp.max(s2, axis=0, keepdims=True)
        top_p = jnp.where(is_prompt, jnp.maximum(old_p, high2), old_p)
        top_c = jnp.maximum(old_c, jnp.where(is_prompt, high1, jnp.maximum(high1, high2)))
        part1 = weigh(s1, top_c, tile0)
        part2 = weigh(s2, jnp.where(is_prompt, top_p, top_c), tile1)
        acc_ref[0] = acc_ref[0] * jnp.exp2((old_p - top_p) * LOG2E) + jnp.where(is_prompt, part2, 0.0)
        acc_ref[1] = (
            acc_ref[1] * jnp.exp2((old_c - top_c) * LOG2E) + part1 + jnp.where(is_prompt, 0.0, part2)
        )
        top_ref[0] = jnp.broadcast_to(top_p, top_ref.shape[1:])
        top_ref[1] = jnp.broadcast_to(top_c, top_ref.shape[1:])

    return own, other


def attend_close(g, top_ref, acc_ref, o_ref, lse_ref):
    for b in range(2):
        acc = acc_ref[b]
        total = acc[0:1, :]
        o_ref[g, b] = (acc / total).T
        lse_ref[g, b] = jnp.broadcast_to(top_ref[b, 0:1, :] * LOG2E + jnp.log2(total), lse_ref.shape[2:])


def attend_back_step(n, me, g, j, pick_ref, segq_ref, segk_ref, q_ref, kv_ref, do_ref, lse_ref, delta_ref, dqt_ref, dkv_ref):
    block = kv_ref.shape[3]
    rows = q_ref.shape[2]

    def pair(kind, tile, mask):
        q = q_ref[g, kind]
        do = do_ref[g, kind]
        p = jnp.exp2(nt(tile, q) * LOG2E - lse_ref[g, kind, 0:1, :])
        if mask is not None:
            p = jnp.where(mask, p, 0.0)
        ds = (p * (nt(tile, do) - delta_ref[g, kind, 0:1, :])).astype(BF16)
        return nn(ds, q) + nn(p.astype(BF16), do), tn(tile, ds)

    def own():
        lane_rows = lax.rem(lax.broadcasted_iota(jnp.int32, (block, rows), 1), block)
        tri = lax.broadcasted_iota(jnp.int32, (block, rows), 0) <= lane_rows
        own0, own1 = kv_ref[me, 0, g], kv_ref[me, 1, g]
        d0, q0 = pair(0, own0, tri)
        d1, q1 = pair(1, own1, tri & (segq_ref[0:1, :] == segk_ref[0]))
        d2, q2 = pair(1, own0, None)
        dkv_ref[me, 0, g] = (d0 + d2).astype(dkv_ref.dtype)
        dkv_ref[me, 1, g] = d1.astype(dkv_ref.dtype)
        dqt_ref[0] = q0
        dqt_ref[1] = q1 + q2

    def other():
        at = lax.rem(me + j, n)
        kind = pick_ref[j]
        is_prompt = kind == 0
        full, q_full = pair(1, kv_ref[at, 0, g], None)
        part, q_part = pair(kind, kv_ref[at, kind, g], (segq_ref[0:1, :] == segk_ref[j]) | is_prompt)
        dkv_ref[at, 0, g] = (full + jnp.where(is_prompt, part, 0.0)).astype(dkv_ref.dtype)
        dkv_ref[at, 1, g] = jnp.where(is_prompt, 0.0, part).astype(dkv_ref.dtype)
        dqt_ref[0] = dqt_ref[0] + jnp.where(is_prompt, q_part, 0.0)
        dqt_ref[1] = dqt_ref[1] + q_full + jnp.where(is_prompt, 0.0, q_part)

    return own, other


def row_deltas(g, do_ref, o_ref, row_ref):
    ones = jnp.ones((8, LANES), F32)
    for b in range(2):
        row_ref[b] = lax.dot_general(
            ones, do_ref[g, b].astype(F32) * o_ref[g, b], (((1,), (1,)), ((), ())),
            precision=lax.Precision.HIGHEST, preferred_element_type=F32,
        )


def gain_row(gains_ref, which, fsdp, shard):
    return jnp.concatenate([gains_ref[i, which : which + 1, :shard] for i in range(fsdp)], axis=1)


def project(sizes, fsdp, x_ref, gains_ref, attn_ref, cos_ref, sin_ref, n1_ref, q_ref, kv_at):
    heads, kvh, block = sizes
    x = x_ref[...].astype(F32)
    normed = (x * rms_inverse(x) * gain_row(gains_ref, 0, fsdp, x.shape[1] // fsdp)).astype(BF16)
    n1_ref[...] = normed
    count = -(-(heads + 2 * kvh) * HD // LANES)
    raw = []
    for t in range(0, count, 2):
        some = range(t, min(t + 2, count))
        wide = nn(normed, lanes(attn_ref, some))
        raw += [wide[:, i * LANES : (i + 1) * LANES] for i in range(len(some))]
    store_projection(sizes, raw, cos_ref[...], sin_ref[...], q_ref, kv_at)


def front_kernel(
    sizes, n, fsdp, plans, pick_ref, segq_ref, segk_ref, x_ref, gains_in, cos_ref, sin_ref,
    wq_ref, wk_ref, wv_ref, wo_ref, wg_ref, wu_ref, wd_ref,
    n1_ref, q_ref, kv_out, o_ref, lse_ref, gains_ref, attn_out, ff_out, down_out,
    attn, ff, down, kv_all, gains, top_ref, acc_ref, send, recv, kv_send, kv_recv, local,
):
    heads, kvh, block = sizes
    me, z = lax.axis_index("ctx"), lax.axis_index("fsdp")
    shard = wq_ref.shape[0]
    rows = sub(z * shard, shard, 16)
    half = (heads + 2 * kvh) * HD % LANES
    main = wo_ref.shape[1] - half
    wo = wo_ref[...]
    tiles = pack_tiles([wq_ref[...], wk_ref[...], wv_ref[...], wo[:, main:], wo[:, :main]])
    for t, tile in enumerate(tiles):
        attn[t, rows, :] = tile
    gains[z] = gains_in[...]
    greet("z", fsdp)
    refs = {ATTN: attn, FF: ff, DOWN: down, "gains": gains}
    run = both_cores(lambda core: weight_stages(core, fsdp, plans[0], refs, send, recv))
    run_kv = both_cores(lambda core: kv_stages(core, plans[1], kv_all, kv_send, kv_recv))
    run("gains_out", ("over_z", ATTN))
    for t in range(ff.shape[1]):
        ff[0, t, rows, :] = wg_ref[:, t * LANES : (t + 1) * LANES]
        ff[1, t, rows, :] = wu_ref[:, t * LANES : (t + 1) * LANES]
    down_rows = sub(z * wd_ref.shape[0], wd_ref.shape[0], 16)
    for t, tile in enumerate(pack_tiles([wd_ref[...]])):
        down[t, down_rows, :] = tile
    run(("spread", ATTN), ("over_z", FF), ("over_z", DOWN), ("forward", ATTN), ("pass_on", ATTN))
    run(("finish", ATTN), "gains_in")
    project(
        sizes, fsdp, x_ref, gains, attn, cos_ref, sin_ref, n1_ref, q_ref,
        lambda b, g: kv_all.at[me, b, g],
    )
    run_kv("start", "forward", "pass_on", "finish")
    gains_ref[...] = gains[...]
    outs = [pltpu.make_async_copy(attn, attn_out, local.at[0]), pltpu.make_async_copy(kv_all, kv_out, local.at[1])]
    for copy in outs:
        copy.start()
    schedule = {
        0: (("spread", FF),),
        6: (("forward", FF),),
        14: (("spread", DOWN),),
        20: (("pass_on", FF),),
        24: (("forward", DOWN),),
        34: (("pass_on", DOWN),),
    }

    @pl.loop(0, kvh * n)
    def _(step):
        g, j = step // n, step % n
        for at, names in schedule.items():
            pl.when(step == at)(functools.partial(run, *names))
        own, other = attend_step(n, me, g, j, pick_ref, segq_ref, segk_ref, q_ref, kv_all, top_ref, acc_ref)
        pl.when(j == 0)(own)
        pl.when(j > 0)(other)
        pl.when(j == n - 1)(lambda: attend_close(g, top_ref, acc_ref, o_ref, lse_ref))

    run(("finish", FF), ("finish", DOWN))
    outs += [pltpu.make_async_copy(ff, ff_out, local.at[2]), pltpu.make_async_copy(down, down_out, local.at[3])]
    for copy in outs[2:]:
        copy.start()
    run("drain")
    run_kv("drain")
    for copy in outs:
        copy.wait()


def head_columns(sizes, ref, low):
    heads, kvh, block = sizes
    share = heads // kvh
    return jnp.concatenate(
        [
            jnp.concatenate(
                [
                    ref[h // share, b, (h % share) * block : (h % share + 1) * block, low : low + HD]
                    for h in range(heads)
                ],
                axis=1,
            )
            for b in range(2)
        ],
        axis=0,
    )


def middle_kernel(
    sizes, fsdp, o_ref, x_ref, cot_ref, gains_ref, attn_ref, ff_ref, down_ref,
    result_ref, gr_ref, do_ref, delta_ref, gain_ref, out_grad_ref, ff_grad_ref, down_grad_ref,
    resid_ref, n2_ref, product_ref, gg_ref, gu_ref, attt_ref, turned_ref, gn_ref,
):
    heads, kvh, block = sizes
    share = heads // kvh
    width = x_ref.shape[1]
    rows = x_ref.shape[0]
    hidden = product_ref.shape[1]
    mixed = (heads + 2 * kvh) * HD // LANES
    half = (heads + 2 * kvh) * HD % LANES
    count = attn_ref.shape[0]
    down_tiles = down_ref.shape[0]
    gain = gain_row(gains_ref, 1, fsdp, width // fsdp)
    attended = head_columns(sizes, o_ref, HD).astype(BF16)
    attt_ref[...] = attended.T
    pieces = []
    for t in range(mixed, count, 2):
        pieces.append(nn(attended, lanes(attn_ref, range(t, min(t + 2, count)))))
    branch = jnp.concatenate(pieces, axis=1)
    branch = jnp.concatenate([branch[:, LANES:], branch[:, half:LANES]], axis=1)
    resid = x_ref[...].astype(F32) + branch
    resid_ref[...] = resid
    inverse = rms_inverse(resid)
    n2_ref[...] = (resid * inverse * gain).astype(BF16)
    cot = cot_ref[...]
    pad = down_tiles * LANES - width
    wide = 2 * LANES

    @pl.loop(0, hidden // wide)
    def _(j):
        at = pl.ds(pl.multiple_of(j * wide, wide), wide)
        n2 = n2_ref[...]
        gate = nn(n2, jnp.concatenate([ff_ref[0, 2 * j], ff_ref[0, 2 * j + 1]], axis=1))
        upward = nn(n2, jnp.concatenate([ff_ref[1, 2 * j], ff_ref[1, 2 * j + 1]], axis=1))
        cot_wide = jnp.concatenate([cot_ref[...], jnp.zeros((rows, pad), BF16)], axis=1)
        grad = nt(cot_wide, jnp.concatenate([down_ref[t, at, :] for t in range(down_tiles)], axis=1))
        sigma = 1.0 / (1.0 + jnp.exp(-gate))
        activated = gate * sigma
        product_ref[:, at] = (activated * upward).astype(BF16)
        gg_ref[:, at] = (grad * upward * (sigma + activated * (1.0 - sigma))).astype(BF16)
        gu_ref[:, at] = (grad * activated).astype(BF16)

    for t in range(0, down_tiles, 2):
        low, high = t * LANES, min((t + 2) * LANES, width)
        part = nn(product_ref[...], lanes(down_ref, (t, t + 1)))
        result_ref[:, low:high] = (resid_ref[:, low:high] + part[:, : high - low]).astype(BF16)

    for low in range(0, width, wide):
        size = min(wide, width - low)
        part = nt(gg_ref[...], lanes(ff_ref.at[0], range(hidden // LANES), slice(low, low + size)))
        part = part + nt(gu_ref[...], lanes(ff_ref.at[1], range(hidden // LANES), slice(low, low + size)))
        gn_ref[:, low : low + size] = part
    grad_normed = gn_ref[...]
    resid = resid_ref[...]
    inverse = rms_inverse(resid)
    scaled = resid * inverse
    weighted = grad_normed * gain
    gain_ref[0:1, :] = jnp.sum(grad_normed * scaled, axis=0, keepdims=True)
    grad_resid = cot.astype(F32) + inverse * (
        weighted - scaled * jnp.mean(weighted * scaled, axis=1, keepdims=True)
    )
    gr_ref[...] = grad_resid
    gb = grad_resid.astype(BF16)
    main = width - (LANES - half)
    lined = jnp.concatenate([jnp.zeros((rows, half), BF16), gb[:, main:], gb[:, :main]], axis=1)
    grad_att = []
    for low in range(0, width, wide):
        size = min(wide, width - low)
        grad_att.append(
            nt(lined, lanes(attn_ref, range(mixed, count), slice(low, low + size))).astype(BF16)
        )
    grad_att = jnp.concatenate(grad_att, axis=1)
    zero = jnp.zeros((block, HD), BF16)
    for h in range(heads):
        for b in range(2):
            do_ref[h // share, b, (h % share) * block : (h % share + 1) * block, :] = jnp.concatenate(
                [zero, grad_att[b * block : (b + 1) * block, h * HD : (h + 1) * HD]], axis=1
            )
    for g in range(kvh):
        row_deltas(g, do_ref, o_ref, delta_ref.at[g])
    for t in range(count - mixed):
        if t % 2 == 0:
            part = nn(attt_ref[...], lined[:, t * LANES : (t + 2) * LANES]).astype(BF16)
        out_grad_ref[t] = part[:, (t % 2) * LANES : (t % 2 + 1) * LANES]
    turned_ref[0:width, :] = n2_ref[...].T

    @pl.loop(0, hidden // wide)
    def _(j):
        at = pl.ds(pl.multiple_of(j * wide, wide), wide)
        for c, grad_ref in enumerate((gg_ref, gu_ref)):
            part = nn(turned_ref[0:width, :], grad_ref[:, at]).astype(BF16)
            ff_grad_ref[c, 2 * j] = part[:, :LANES]
            ff_grad_ref[c, 2 * j + 1] = part[:, LANES:]

    @pl.loop(0, hidden // wide)
    def _(j):
        at = pl.ds(pl.multiple_of(j * wide, wide), wide)
        flipped = product_ref[:, at].T
        cot_wide = jnp.concatenate([cot_ref[...], jnp.zeros((rows, pad), BF16)], axis=1)
        part = nn(flipped, cot_wide).astype(BF16)
        for t in range(down_tiles):
            down_grad_ref[t, at, :] = part[:, t * LANES : (t + 1) * LANES]


def add_rows(out, terms, rows):
    for lead in range(out.shape[0] if len(out.shape) == 3 else 1):
        views = [r.at[lead] if len(r.shape) == 3 else r for r in [out] + list(terms)]

        @pl.loop(0, rows // 16)
        def _(i):
            rs = pl.ds(pl.multiple_of(i * 16, 16), 16)
            total = views[1][rs, :].astype(F32)
            for term in views[2:]:
                total = total + term[rs, :].astype(F32)
            views[0][rs, :] = total.astype(out.dtype)


def grad_stages(core, fsdp, plan, sources, held, got, outs, gain_refs, send, recv, local):
    links = Links(core, fsdp, send, recv, plan)
    z, chip = links.z, links.chip
    near, far = lax.bitwise_xor(chip, links.first), lax.bitwise_xor(chip, links.second)
    corner = lax.bitwise_xor(chip, 3)
    shards = {k: sources[k].shape[-2] // fsdp for k in PACKAGES}
    mine = {k: Share(k, core, shards[k]) for k in PACKAGES}
    twin = {k: Share(k, 1 - core, shards[k]) for k in PACKAGES}
    stages = {}

    def hold(k, d, q):
        if k in held:
            return held[k].at[d, q]
        return mine[k].at(sources[k], lax.bitwise_xor(z, d), q)

    def load(k, d, q):
        slot = (PACKAGES.index(k) * fsdp + d) * 4 + q
        return pltpu.make_async_copy(
            mine[k].at(sources[k], lax.bitwise_xor(z, d), q), hold(k, d, q), local.at[slot]
        )

    def begin(k, d):
        zi = lax.bitwise_xor(z, d)
        for q in range(4):
            links.send((k, CORE, d, q), CORE, twin[k].at(sources[k], zi, q), twin[k].buffer(got[k][0].at[d, q]))
            if k in held:
                load(k, d, q).start()

    def stage1(k, d):
        share = mine[k]
        for q in range(4):
            links.landed((k, CORE, d, q), share.buffer(got[k][0].at[d, q]))
            if k in held:
                load(k, d, q).wait()
            add_rows(hold(k, d, q), (hold(k, d, q), got[k][0].at[d, q]), share.rows)
        for i, q in enumerate((near, corner)):
            links.send((k, FIRST, d, i), FIRST, hold(k, d, q), share.buffer(got[k][1].at[d, i]))

    def stage2(k, d):
        share = mine[k]
        for i in range(2):
            links.landed((k, FIRST, d, i), share.buffer(got[k][1].at[d, i]))
        add_rows(hold(k, d, far), (hold(k, d, far), got[k][1].at[d, 1]), share.rows)
        links.send((k, SECOND, d), SECOND, hold(k, d, far), share.buffer(got[k][2].at[d]))

    def stage3(k, d):
        share = mine[k]
        links.landed((k, SECOND, d), share.buffer(got[k][2].at[d]))
        add_rows(hold(k, d, chip), (hold(k, d, chip), got[k][1].at[d, 0], got[k][2].at[d]), share.rows)
        if d > 0:
            links.send((k, "z", d), d, hold(k, d, chip), share.buffer(got[k][3].at[d - 1]))

    def out_copy(k):
        slot = len(PACKAGES) * fsdp * 4 + PACKAGES.index(k)
        return pltpu.make_async_copy(hold(k, 0, chip), mine[k].at(outs[k], 0, chip), local.at[slot])

    def close(k):
        share = mine[k]
        for d in range(1, fsdp):
            links.landed((k, "z", d), share.buffer(got[k][3].at[d - 1]))
        final = hold(k, 0, chip)
        add_rows(final, [final] + [got[k][3].at[d - 1] for d in range(1, fsdp)], share.rows)
        for hop in (FIRST, SECOND):
            links.send((k, "out", hop), hop, final, share.at(outs[k], 0, chip))
        links.send((k, "out core", 0), CORE, final, share.at(outs[k], 0, chip))
        out_copy(k).start()

    def close2(k):
        share = mine[k]
        links.landed((k, "out", FIRST), share.at(outs[k], 0, near))
        piece = share.at(outs[k], 0, near)
        links.send((k, "out", "corner"), SECOND, piece, piece)
        links.send((k, "out core", 1), CORE, piece, piece)
        piece = share.at(outs[k], 0, far)
        links.landed((k, "out", SECOND), piece)
        links.send((k, "out core", 2), CORE, piece, piece)

    def close3(k):
        piece = mine[k].at(outs[k], 0, corner)
        links.landed((k, "out", "corner"), piece)
        links.send((k, "out core", 3), CORE, piece, piece)

    def close4(k):
        for i, q in ((0, chip), (1, far), (2, near), (3, corner)):
            links.landed((k, "out core", i), twin[k].at(outs[k], 0, q))
        out_copy(k).wait()

    for k in PACKAGES:
        for fn in (begin, stage1, stage2, stage3):
            for d in range(fsdp):
                stages[fn.__name__, k, d] = functools.partial(fn, k, d)
        for fn in (close, close2, close3, close4):
            stages[fn.__name__, k] = functools.partial(fn, k)

    gain_sum, gain_got, gain_z, gain_out = gain_refs

    def gain_step(i):
        if i > 0:
            links.landed(("gain", i - 1), gain_got.at[i - 1])
            gain_sum[i] = gain_sum[i - 1] + gain_got[i - 1]
        if i < 3:
            links.send(("gain", i), (CORE, FIRST, SECOND)[i], gain_sum.at[i], gain_got.at[i])
        else:
            for d in range(1, fsdp):
                links.send(("gain z", d), d, gain_sum.at[3, lax.bitwise_xor(z, d)], gain_z.at[d - 1])

    def gain_close():
        total = gain_sum[3, z]
        for d in range(1, fsdp):
            links.landed(("gain z", d), gain_z.at[d - 1])
            total = total + gain_z[d - 1]
        gain_out[...] = total

    for i in range(4):
        stages["gain", i] = functools.partial(gain_step, i)
    stages["gain close"] = gain_close
    stages["drain"] = links.drain
    return stages


def kv_grad_stages(core, plan, parts, kv_sum, got0, got1, got2, send, recv):
    links = Links(core, 1, send, recv, plan)
    chip = links.chip
    near, far = lax.bitwise_xor(chip, links.first), lax.bitwise_xor(chip, links.second)
    corner = lax.bitwise_xor(chip, 3)
    rows = parts.shape[3]

    def start():
        for b in range(2):
            for q in range(4):
                links.send(("kv core", b, q), CORE, parts.at[2 * q + 1 - core, b], got0.at[b, q])

    def stage1():
        for b in range(2):
            for q in range(4):
                links.landed(("kv core", b, q), got0.at[b, q])
                add_rows(got0.at[b, q], (parts.at[2 * q + core, b], got0.at[b, q]), rows)
            links.send(("kv first", b, 0), FIRST, got0.at[b, near], got1.at[b, 0])
            links.send(("kv first", b, 1), FIRST, got0.at[b, corner], got1.at[b, 1])

    def stage2():
        for b in range(2):
            links.landed(("kv first", b, 0), got1.at[b, 0])
            links.landed(("kv first", b, 1), got1.at[b, 1])
            add_rows(got0.at[b, far], (got0.at[b, far], got1.at[b, 1]), rows)
            links.send(("kv second", b), SECOND, got0.at[b, far], got2.at[b])

    def stage3():
        for b in range(2):
            links.landed(("kv second", b), got2.at[b])
            add_rows(kv_sum.at[b], (got0.at[b, chip], got1.at[b, 0], got2.at[b]), rows)

    return {"start": start, "stage1": stage1, "stage2": stage2, "stage3": stage3, "drain": links.drain}


def back_kernel(
    sizes, n, fsdp, plans, pick_ref, segq_ref, segk_ref, q_ref, kv_in, do_ref, delta_ref, lse_ref,
    x_ref, n1_ref, gr_ref, gains_ref, gain_two_ref, cos_ref, sin_ref, attn_ref, out_grad_ref, ff_grad, down_grad,
    tg_ref, gain_out, attn_out, ff_out, down_out,
    spill_ref, chunk_ref, dqt_ref, dq_ref, dkv_ref, kv_sum, kv_got0, kv_got1, kv_got2, gp_ref, gn_ref, attn_grad,
    ff_a, down_a, attn_0, ff_0, down_0, attn_1, ff_1, down_1, attn_2, ff_2, down_2, attn_3, ff_3, down_3,
    gain_sum, gain_got, gain_z, send, recv, kv_send, kv_recv, local, ahead_sem,
):
    heads, kvh, block = sizes
    share = heads // kvh
    me = lax.axis_index("ctx")
    width = x_ref.shape[1]
    rows = x_ref.shape[0]
    greet("z", fsdp)
    sources = {ATTN: attn_grad, FF: ff_grad, DOWN: down_grad}
    held = {FF: ff_a, DOWN: down_a}
    got = {ATTN: (attn_0, attn_1, attn_2, attn_3), FF: (ff_0, ff_1, ff_2, ff_3), DOWN: (down_0, down_1, down_2, down_3)}
    outs = {ATTN: attn_out, FF: ff_out, DOWN: down_out}
    run = both_cores(
        lambda core: grad_stages(
            core, fsdp, plans[0], sources, held, got, outs, (gain_sum, gain_got, gain_z, gain_out), send, recv, local
        )
    )
    run_kv = both_cores(
        lambda core: kv_grad_stages(core, plans[1], dkv_ref, kv_sum, kv_got0, kv_got1, kv_got2, kv_send, kv_recv)
    )
    order = [d for d in range(1, fsdp)] + [0]
    chunks = [(k, d) for k in (FF, DOWN) for d in order]
    steps = []
    for i in range(len(chunks) + 7):
        names = []
        if i + 1 < len(chunks):
            names.append(("begin",) + chunks[i + 1])
        if i < len(chunks):
            names.append(("stage1",) + chunks[i])
        if 1 <= i <= len(chunks):
            names.append(("stage2",) + chunks[i - 1])
        if 2 <= i <= len(chunks) + 1:
            names.append(("stage3",) + chunks[i - 2])
        for last, k in ((len(order) + 1, FF), (len(chunks) + 1, DOWN)):
            for extra, what in enumerate(("close", "close2", "close3", "close4")):
                if i == last + 1 + extra:
                    names.append((what, k))
        steps.append(names)
    run(("begin",) + chunks[0])
    width_tiles = -(-(heads + 2 * kvh) // 2)
    ahead = [
        pltpu.make_async_copy(out_grad_ref.at[0], spill_ref, ahead_sem.at[0]),
        pltpu.make_async_copy(
            out_grad_ref.at[pl.ds(1, attn_grad.shape[0] - width_tiles)],
            attn_grad.at[pl.ds(width_tiles, attn_grad.shape[0] - width_tiles)], ahead_sem.at[1],
        ),
    ]
    wide = 2 * LANES

    def weight_rows(i):
        size = min(wide, width - i * wide)
        return pltpu.make_async_copy(
            attn_ref.at[pl.ds(0, width_tiles), pl.ds(i * wide, size)],
            chunk_ref.at[i % 2, :, pl.ds(0, size)], ahead_sem.at[2 + i % 2],
        )

    for copy in ahead + [weight_rows(0), weight_rows(1)]:
        copy.start()
    total = kvh * n
    pace = 4

    @pl.loop(0, total)
    def _(step):
        g, j = step // n, step % n
        for i, names in enumerate(steps):
            if i * pace < total:
                pl.when(step == i * pace)(functools.partial(run, *names))
        own, other = attend_back_step(
            n, me, g, j, pick_ref, segq_ref, segk_ref, q_ref, kv_in, do_ref, lse_ref, delta_ref, dqt_ref, dkv_ref
        )
        pl.when(j == 0)(own)
        pl.when(j > 0)(other)

        @pl.when(j == n - 1)
        def _():
            dq_ref[g] = jnp.concatenate([(dqt_ref[b] * 0.125).T[:, :HD] for b in range(2)], axis=1)

    run_kv("start")
    rest = [names for i, names in enumerate(steps) if i * pace >= total]
    for i, names in enumerate(rest[:1]):
        run(*names)
    run_kv("stage1", "stage2", "stage3")
    cos, sin = cos_ref[...], -sin_ref[...]

    def head(index):
        if index < heads:
            return jnp.concatenate(
                [
                    dq_ref[index // share, (index % share) * block : (index % share + 1) * block, b * HD : (b + 1) * HD]
                    for b in range(2)
                ],
                axis=0,
            )
        g = index - heads
        low = 0 if g < kvh else HD
        return jnp.concatenate([kv_sum[b, g % kvh, :, low : low + HD] for b in range(2)], axis=0)

    count = heads + 2 * kvh
    tiles = -(-count // 2)
    for t in range(tiles):
        right = head(2 * t + 1) if 2 * t + 1 < count else jnp.zeros((rows, HD), F32)
        pair = jnp.concatenate([head(2 * t), right], axis=1)
        if 2 * t < heads + kvh:
            pair = rope_tile(pair, cos, sin)
        gp_ref[:, t * LANES : (t + 1) * LANES] = pair.astype(BF16)
    turned = n1_ref[...].T
    for copy in ahead:
        copy.wait()
    for t in range(0, tiles, 2):
        some = min(2, tiles - t)
        part = nn(turned, gp_ref[:, t * LANES : (t + some) * LANES]).astype(BF16)
        for i in range(some):
            tile = part[:, i * LANES : (i + 1) * LANES]
            attn_grad[t + i] = tile + spill_ref[...] if t + i == tiles - 1 else tile
    run(("begin", ATTN, order[0]))
    run(("begin", ATTN, order[1]), ("stage1", ATTN, order[0]))
    for i in range(-(-width // wide)):
        size = min(wide, width - i * wide)
        weight_rows(i).wait()
        rows_in = jnp.concatenate([chunk_ref[i % 2, t, 0:size, :] for t in range(tiles)], axis=1)
        gn_ref[:, i * wide : i * wide + size] = nt(gp_ref[...], rows_in)
        if (i + 2) * wide < width:
            weight_rows(i + 2).start()
    x = x_ref[...].astype(F32)
    inverse = rms_inverse(x)
    scaled = x * inverse
    grad_normed = gn_ref[...]
    weighted = grad_normed * gain_row(gains_ref, 0, fsdp, width // fsdp)
    gain_one = jnp.sum(grad_normed * scaled, axis=0, keepdims=True)
    gain_two = gain_two_ref[0:1, :]
    shard = width // fsdp
    tail = gain_sum.shape[3] - shard
    for i in range(fsdp):
        both = jnp.concatenate(
            [gain_one[:, i * shard : (i + 1) * shard], gain_two[:, i * shard : (i + 1) * shard]], axis=0
        )
        both = jnp.concatenate([both, jnp.zeros((2, tail), F32)], axis=1)
        gain_sum[0, i] = jnp.concatenate([both, jnp.zeros((6, gain_sum.shape[3]), F32)], axis=0)
    run(("gain", 0))
    tg_ref[...] = (
        gr_ref[...] + inverse * (weighted - scaled * jnp.mean(weighted * scaled, axis=1, keepdims=True))
    ).astype(BF16)
    chunk2 = [(ATTN, d) for d in order]
    for i in range(1, len(chunk2) + 2):
        names = []
        if i + 1 < len(chunk2):
            names.append(("begin",) + chunk2[i + 1])
        if i < len(chunk2):
            names.append(("stage1",) + chunk2[i])
        if i <= len(chunk2):
            names.append(("stage2",) + chunk2[i - 1])
        if i >= 2:
            names.append(("stage3",) + chunk2[i - 2])
        if i <= 3:
            names.append(("gain", i))
        if i < len(rest):
            names += rest[i]
        run(*names)
    for names in rest[len(chunk2) + 2 :]:
        run(*names)
    run(("close", ATTN))
    run(("close2", ATTN))
    run("gain close")
    run(("close3", ATTN))
    run(("close4", ATTN))
    run("drain")
    run_kv("drain")


def whole(shape, dtype):
    return jax.ShapeDtypeStruct(shape, dtype)


def params(ident=None):
    extra = {} if ident is None else {"collective_id": ident, "has_side_effects": True}
    return pltpu.CompilerParams(vmem_limit_bytes=VMEM_LIMIT, **extra)


SMEM = pl.BlockSpec(memory_space=pltpu.SMEM)
VMEM = pl.BlockSpec(memory_space=pltpu.VMEM)
ANY = pl.BlockSpec(memory_space=pl.ANY)


def layout(block_deal, lengths, block, total_rows, n, me, share):
    prompt_size = total_rows // 2
    deal = block_deal.reshape(n, 2)
    flip = deal[me, 0] > deal[me, 1]
    naturals = jnp.stack([jnp.min(deal, axis=1), jnp.max(deal, axis=1)], axis=1)
    natural = naturals[:, :, None] * block + jnp.arange(block, dtype=jnp.int32)
    offset = natural - prompt_size
    ending = jnp.cumsum(lengths)
    segment = jnp.sum((offset[..., None] >= ending).astype(jnp.int32), axis=-1)
    own_offset = offset[me].reshape(-1)
    inside = segment[me].reshape(-1)[:, None] == jnp.arange(lengths.shape[0], dtype=jnp.int32)
    beginning = jnp.sum(jnp.where(inside, ending - lengths, 0), axis=-1)
    position = jnp.where(own_offset < 0, natural[me].reshape(-1), prompt_size + own_offset - beginning)
    frequency = THETA ** (-2.0 * jnp.arange(HD // 2, dtype=F32) / HD)
    angle = position.astype(F32)[:, None] * frequency[None, :]
    cos, sin = jnp.cos(angle), jnp.sin(angle)
    around = (me + jnp.arange(n, dtype=jnp.int32)) % n
    first = naturals[:, 0]
    pick = (first[around] >= first[me]).astype(jnp.int32)
    return (
        flip,
        jnp.concatenate([cos, cos, cos, cos], axis=1),
        jnp.concatenate([-sin, sin, -sin, sin], axis=1),
        pick,
        jnp.tile(segment[me, 1], share)[None, :],
        segment[around, 1][:, :, None],
    )


def cube_body(
    tokens, attn_gain, query_weight, key_weight, value_weight, out_weight, mlp_gain, gate_weight,
    up_weight, down_weight, cotangent, cont_lengths, block_deal,
):
    n, fsdp = lax.axis_size("ctx"), lax.axis_size("fsdp")
    me = lax.axis_index("ctx")
    row_count, width = tokens.shape[1:]
    kv_width = key_weight.shape[1]
    shard, hidden = gate_weight.shape
    down_shard = down_weight.shape[0]
    block = row_count // 2
    heads, kvh = width // HD, kv_width // HD
    share = heads // kvh
    stack = share * block
    sizes = (heads, kvh, block)
    flip, cos, sin, pick, segq, segk = layout(
        block_deal, cont_lengths[0], block, row_count * n, n, me, share
    )

    def ordered(rows):
        halves = rows.reshape(2, block, rows.shape[-1])
        return jnp.where(flip, halves[::-1], halves).reshape(rows.shape)

    x = ordered(tokens[0])
    cot = ordered(cotangent[0])
    pad = -shard % LANES
    gains_in = jnp.pad(jnp.stack([attn_gain, mlp_gain]).astype(F32), ((0, 6), (0, pad)))
    gain_shape = (fsdp,) + gains_in.shape
    attn_tiles = (2 * width + 2 * kv_width) // LANES
    ff_tiles = hidden // LANES
    down_tiles = -(-width // LANES)
    heads_shape = (kvh, 2, stack, LANES)
    row_shape = (kvh, 2, 8, stack)
    kv_shape = (n, 2, kvh, block, LANES)
    dma = pltpu.SemaphoreType.DMA
    normed_one, q, kv_all, o, lse, gains, w_attn, w_ff, w_down = pl.pallas_call(
        functools.partial(front_kernel, sizes, n, fsdp, ({}, {})),
        out_shape=(
            whole((row_count, width), BF16),
            whole(heads_shape, BF16),
            whole(kv_shape, BF16),
            whole(heads_shape, F32),
            whole(row_shape, F32),
            whole(gain_shape, F32),
            whole((attn_tiles, fsdp * shard, LANES), BF16),
            whole((2, ff_tiles, fsdp * shard, LANES), BF16),
            whole((down_tiles, fsdp * down_shard, LANES), BF16),
        ),
        in_specs=[SMEM] + [VMEM] * 13,
        out_specs=(VMEM, VMEM, ANY, VMEM, VMEM, VMEM, ANY, ANY, ANY),
        scratch_shapes=[
            pltpu.VMEM((attn_tiles, fsdp * shard, LANES), BF16),
            pltpu.VMEM((2, ff_tiles, fsdp * shard, LANES), BF16),
            pltpu.VMEM((down_tiles, fsdp * down_shard, LANES), BF16),
            pltpu.VMEM(kv_shape, BF16),
            pltpu.VMEM(gain_shape, F32),
            pltpu.VMEM((2, 8, stack), F32),
            pltpu.VMEM((2, LANES, stack), F32),
            dma((75,)), dma((75,)), dma((14,)), dma((14,)), dma((4,)),
        ],
        compiler_params=params(0),
        name="front",
    )(
        pick, segq, segk, x, gains_in, cos, sin,
        query_weight, key_weight, value_weight, out_weight, gate_weight, up_weight, down_weight,
    )

    mixed = (width + 2 * kv_width) // LANES
    result, grad_resid, grad_heads, deltas, gain_two, out_grad, ff_grad, down_grad = pl.pallas_call(
        functools.partial(middle_kernel, sizes, fsdp),
        out_shape=(
            whole((row_count, width), BF16),
            whole((row_count, width), F32),
            whole(heads_shape, BF16),
            whole(row_shape, F32),
            whole((8, width), F32),
            whole((attn_tiles - mixed, width, LANES), BF16),
            whole((2, ff_tiles, width, LANES), BF16),
            whole((down_tiles, hidden, LANES), BF16),
        ),
        in_specs=[VMEM] * 7,
        out_specs=(VMEM,) * 8,
        scratch_shapes=[
            pltpu.VMEM((row_count, width), F32),
            pltpu.VMEM((row_count, width), BF16),
            pltpu.VMEM((row_count, hidden), BF16),
            pltpu.VMEM((row_count, hidden), BF16),
            pltpu.VMEM((row_count, hidden), BF16),
            pltpu.VMEM((width, row_count), BF16),
            pltpu.VMEM((width, row_count), BF16),
            pltpu.VMEM((row_count, width), F32),
        ],
        compiler_params=params(),
        name="middle",
    )(o, x, cot, gains, w_attn, w_ff, w_down)

    attn_rows = -(-shard // 32) * 16
    shapes = ((attn_tiles // 4, attn_rows, LANES), (ff_tiles // 4, shard, LANES), (down_shard, LANES))
    buffers = [pltpu.VMEM((fsdp, 4) + shape, BF16) for shape in shapes[1:]]
    for lead in ((fsdp, 4), (fsdp, 2), (fsdp,), (fsdp - 1,)):
        buffers += [pltpu.VMEM(lead + shape, BF16) for shape in shapes]
    qkv_tiles = -(-(width + 2 * kv_width) // LANES)
    piece = (kvh, block, LANES)
    tokens_grad, gain_grads, attn_w, ff_w, down_w = pl.pallas_call(
        functools.partial(back_kernel, sizes, n, fsdp, ({}, {})),
        out_shape=(
            whole((row_count, width), BF16),
            whole(gains_in.shape, F32),
            whole((attn_tiles, shard, LANES), BF16),
            whole((2, ff_tiles, shard, LANES), BF16),
            whole((down_tiles, down_shard, LANES), BF16),
        ),
        in_specs=[SMEM] + [VMEM] * 14 + [ANY] * 4,
        out_specs=(VMEM, VMEM, ANY, ANY, ANY),
        scratch_shapes=[
            pltpu.VMEM((width, LANES), BF16),
            pltpu.VMEM((2, qkv_tiles, 2 * LANES, LANES), BF16),
            pltpu.VMEM((2, LANES, stack), F32),
            pltpu.VMEM((kvh, stack, LANES), F32),
            pltpu.VMEM(kv_shape, BF16),
            pltpu.VMEM((2,) + piece, F32),
            pltpu.VMEM((2, 4) + piece, BF16),
            pltpu.VMEM((2, 2) + piece, BF16),
            pltpu.VMEM((2,) + piece, BF16),
            pltpu.VMEM((row_count, qkv_tiles * LANES), BF16),
            pltpu.VMEM((row_count, width), F32),
            pltpu.VMEM((attn_tiles, width, LANES), BF16),
        ]
        + buffers
        + [
            pltpu.VMEM((4,) + gain_shape, F32),
            pltpu.VMEM((3,) + gain_shape, F32),
            pltpu.VMEM((fsdp - 1,) + gains_in.shape, F32),
            dma((120,)), dma((120,)), dma((14,)), dma((14,)), dma((51,)), dma((4,)),
        ],
        compiler_params=params(1),
        name="back",
    )(
        pick, segq, segk, q, kv_all, grad_heads, deltas, lse, x, normed_one, grad_resid, gains, gain_two,
        cos, sin, w_attn, out_grad, ff_grad, down_grad,
    )

    def lined(tiles):
        return tiles.astype(F32).transpose(1, 0, 2).reshape(tiles.shape[1], tiles.shape[0] * LANES)

    flat = lined(attn_w)
    qkv = width + 2 * kv_width
    spill = qkv_tiles * LANES
    return (
        ordered(result)[None],
        ordered(tokens_grad)[None],
        gain_grads[0, :shard],
        flat[:, :width],
        flat[:, width : width + kv_width],
        flat[:, width + kv_width : qkv],
        jnp.concatenate([flat[:, spill:], flat[:, qkv:spill]], axis=1),
        gain_grads[1, :shard],
        lined(ff_w[0]),
        lined(ff_w[1]),
        lined(down_w)[:, :width],
    )


def head_of(tiles, index):
    start = (index % 2) * HD
    return tiles[index // 2][:, start : start + HD]


def project_kernel(sizes, x_ref, gain_ref, w_ref, cos_ref, sin_ref, n1_ref, q_ref, kv_ref):
    heads, kvh, block = sizes
    share = heads // kvh
    x = x_ref[...].astype(F32)
    inverse = lax.rsqrt(jnp.mean(x * x, axis=1, keepdims=True) + EPSILON)
    normed = (x * inverse * gain_ref[...]).astype(BF16)
    n1_ref[...] = normed
    width = (heads + 2 * kvh) * HD
    raw = nn(normed, w_ref[:, :width])
    cos = cos_ref[...]
    sin = sin_ref[...]
    tiles = []
    for j in range((heads + kvh) * HD // LANES):
        tiles.append(rope_tile(raw[:, j * LANES : (j + 1) * LANES], cos, sin).astype(BF16))
    zero = jnp.zeros((block, HD), BF16)
    for h in range(heads):
        piece = head_of(tiles, h) * jnp.asarray(0.125, BF16)
        g, i = h // share, h % share
        for b in range(2):
            q_ref[g, b, i * block : (i + 1) * block, :] = jnp.concatenate(
                [piece[b * block : (b + 1) * block], zero], axis=1
            )
    for g in range(kvh):
        start = (heads + kvh + g) * HD
        value = raw[:, start : start + HD].astype(BF16)
        pair = jnp.concatenate([head_of(tiles, heads + g), value], axis=1)
        for b in range(2):
            kv_ref[b, :, g * LANES : (g + 1) * LANES] = pair[b * block : (b + 1) * block]


def attend_kernel(
    n, me_ref, pick_ref, segq_ref, segk_ref, q_ref, kv_ref, o_ref, lse_ref, s1_ref, p1_ref, s2_ref, p2_ref
):
    me = me_ref[0]
    block = kv_ref.shape[2]
    rows = q_ref.shape[2]
    keys = n * block
    qc = q_ref[0, 1]
    prompt = kv_ref[:, 0].reshape(keys, LANES)
    s1_ref[...] = nt(qc, prompt)
    own = []
    for b in range(2):
        s2_ref[b] = nt(q_ref[0, b], kv_ref[me, b])
    for j in range(1, n):
        at = lax.rem(me + j, n)
        kind = pick_ref[j]
        s2_ref[j + 1] = nt(q_ref[0, kind], kv_ref[at, kind])
    step = 16
    kinds = [pick_ref[j] == 0 for j in range(n)]

    def fold(s):
        return jnp.maximum(
            s[:, :LANES],
            jnp.concatenate(
                [s[:, LANES:], jnp.full((step, 2 * LANES - block), MASKED, F32)], axis=1
            ),
        )

    def chunk(at, carry):
        r = pl.multiple_of(at * step, step)
        rs = pl.ds(r, step)
        in_block = lax.rem(r, block)
        tri = lax.broadcasted_iota(jnp.int32, (step, block), 1) <= (
            in_block + lax.broadcasted_iota(jnp.int32, (step, block), 0)
        )
        segq = segq_ref[rs, :]
        s1 = s1_ref[rs, :]
        top_c = s1[:, :LANES]
        for t in range(1, keys // LANES):
            top_c = jnp.maximum(top_c, s1[:, t * LANES : (t + 1) * LANES])
        dp = jnp.where(tri, s2_ref[0, rs, :], MASKED)
        dc = jnp.where(tri & (segq == segk_ref[0]), s2_ref[1, rs, :], MASKED)
        top_c = jnp.maximum(top_c, fold(dc))
        top_p = fold(dp)
        others = []
        for j in range(1, n):
            s = jnp.where((segq == segk_ref[j]) | kinds[j], s2_ref[j + 1, rs, :], MASKED)
            others.append(s)
            f = fold(s)
            top_p = jnp.maximum(top_p, jnp.where(kinds[j], f, MASKED))
            top_c = jnp.maximum(top_c, jnp.where(kinds[j], MASKED, f))
        m_p = jnp.max(top_p, axis=1, keepdims=True)
        m_c = jnp.max(top_c, axis=1, keepdims=True)
        p1_ref[rs, :] = jnp.exp2((s1 - m_c) * LOG2E).astype(BF16)
        p2_ref[0, rs, :] = jnp.exp2((dp - m_p) * LOG2E).astype(BF16)
        p2_ref[1, rs, :] = jnp.exp2((dc - m_c) * LOG2E).astype(BF16)
        for j in range(1, n):
            m = jnp.where(kinds[j], m_p, m_c)
            p2_ref[j + 1, rs, :] = jnp.exp2((others[j - 1] - m) * LOG2E).astype(BF16)
        lse_ref[0, 0, rs, :] = jnp.broadcast_to(m_p * LOG2E, (step, LANES))
        lse_ref[0, 1, rs, :] = jnp.broadcast_to(m_c * LOG2E, (step, LANES))
        return carry

    lax.fori_loop(0, rows // step, chunk, 0)

    def with_ones(tile):
        return jnp.concatenate([tile, jnp.ones(tile.shape, BF16)], axis=1)

    acc = [nn(p2_ref[b], with_ones(kv_ref[me, b])) for b in range(2)]
    acc[1] = acc[1] + nn(p1_ref[...], with_ones(prompt))
    for j in range(1, n):
        at = lax.rem(me + j, n)
        part = nn(p2_ref[j + 1], with_ones(kv_ref[at, pick_ref[j]]))
        acc[0] = acc[0] + jnp.where(kinds[j], part, 0.0)
        acc[1] = acc[1] + jnp.where(kinds[j], 0.0, part)
    for b in range(2):
        total = acc[b][:, LANES:]
        o_ref[0, b] = acc[b][:, :LANES] / total
        lse_ref[0, b] = lse_ref[0, b] + jnp.log2(total)


def attend_back_kernel(
    n, me_ref, pick_ref, segq_ref, segk_ref, q_ref, kv_ref, do_ref, o_ref, lse_ref, dq_ref, dkv_ref, row_ref, dqt_ref
):
    me = me_ref[0]
    block = kv_ref.shape[2]
    rows = q_ref.shape[2]
    first = (lax.broadcasted_iota(jnp.int32, (8, LANES), 1) == 0).astype(F32)
    ones = jnp.ones((8, LANES), F32)

    def to_row(lhs, matrix):
        return lax.dot_general(
            lhs, matrix, (((1,), (1,)), ((), ())), precision=lax.Precision.HIGHEST,
            preferred_element_type=F32,
        )

    for b in range(2):
        row_ref[b] = to_row(first, lse_ref[0, b])
        row_ref[2 + b] = to_row(ones, do_ref[0, b].astype(F32) * o_ref[0, b])
    lane_rows = lax.rem(lax.broadcasted_iota(jnp.int32, (block, rows), 1), block)
    tri = lax.broadcasted_iota(jnp.int32, (block, rows), 0) <= lane_rows

    def pair(kind, tile, mask):
        q = q_ref[0, kind]
        do = do_ref[0, kind]
        p = jnp.exp2(nt(tile, q) * LOG2E - row_ref[kind, 0:1, :])
        if mask is not None:
            p = jnp.where(mask, p, 0.0)
        ds = (p * (nt(tile, do) - row_ref[2 + kind, 0:1, :])).astype(BF16)
        return nn(ds, q) + nn(p.astype(BF16), do), tn(tile, ds)

    segq = segq_ref[0:1, :]
    same_own = segq == segk_ref[0]
    own0, own1 = kv_ref[me, 0], kv_ref[me, 1]
    d0, q0 = pair(0, own0, tri)
    d1, q1 = pair(1, own1, tri & same_own)
    d2, q2 = pair(1, own0, None)
    dkv_ref[me, 0] = (d0 + d2).astype(dkv_ref.dtype)
    dkv_ref[me, 1] = d1.astype(dkv_ref.dtype)
    dqt_ref[0] = q0
    dqt_ref[1] = q1 + q2

    def other(j, carry):
        at = lax.rem(me + j, n)
        kind = pick_ref[j]
        is_prompt = kind == 0
        full, q_full = pair(1, kv_ref[at, 0], None)
        mask = (segq == segk_ref[j]) | is_prompt
        part, q_part = pair(kind, kv_ref[at, kind], mask)
        dkv_ref[at, 0] = (full + jnp.where(is_prompt, part, 0.0)).astype(dkv_ref.dtype)
        dkv_ref[at, 1] = jnp.where(is_prompt, 0.0, part).astype(dkv_ref.dtype)
        dqt_ref[0] = dqt_ref[0] + jnp.where(is_prompt, q_part, 0.0)
        dqt_ref[1] = dqt_ref[1] + q_full + jnp.where(is_prompt, 0.0, q_part)
        return carry

    lax.fori_loop(1, n, other, 0)
    for b in range(2):
        dq_ref[0, b] = (dqt_ref[b] * 0.125).T


def mid_kernel(sizes, o_ref, x_ref, wo_ref, gain_ref, att_ref, resid_ref, n2_ref):
    heads, kvh, block = sizes
    share = heads // kvh
    for b in range(2):
        columns = []
        for h in range(heads):
            g, i = h // share, h % share
            columns.append(o_ref[g, b, i * block : (i + 1) * block, HD:])
        attended = jnp.concatenate(columns, axis=1).astype(BF16)
        rs = slice(b * block, (b + 1) * block)
        att_ref[rs, :] = attended
        resid = x_ref[rs, :].astype(F32) + nn(attended, wo_ref[...])
        resid_ref[rs, :] = resid
        inverse = lax.rsqrt(jnp.mean(resid * resid, axis=1, keepdims=True) + EPSILON)
        n2_ref[rs, :] = (resid * inverse * gain_ref[...]).astype(BF16)


def branch_kernel(sizes, gb_ref, wo_ref, do_ref):
    heads, kvh, block = sizes
    share = heads // kvh
    grad = nt(gb_ref[...], wo_ref[...]).astype(BF16)
    zero = jnp.zeros((block, HD), BF16)
    for h in range(heads):
        g, i = h // share, h % share
        for b in range(2):
            do_ref[g, b, i * block : (i + 1) * block, :] = jnp.concatenate(
                [zero, grad[b * block : (b + 1) * block, h * HD : (h + 1) * HD]], axis=1
            )


def unrope_kernel(sizes, dq_ref, dkv_ref, cos_ref, sin_ref, out_ref):
    heads, kvh, block = sizes
    share = heads // kvh
    for b in range(2):
        rs = slice(b * block, (b + 1) * block)
        cos, sin = cos_ref[rs, :], -sin_ref[rs, :]
        columns = [
            dq_ref[h // share, b, (h % share) * block : (h % share + 1) * block, :HD]
            for h in range(heads)
        ]
        columns += [dkv_ref[b, :, g * LANES : g * LANES + HD].astype(F32) for g in range(kvh)]
        tiles = []
        for j in range((heads + kvh) // 2):
            pair = jnp.concatenate(columns[2 * j : 2 * j + 2], axis=1)
            tiles.append(rope_tile(pair, cos, sin).astype(BF16))
        values = [dkv_ref[b, :, g * LANES + HD : (g + 1) * LANES].astype(BF16) for g in range(kvh)]
        out_ref[rs, :] = jnp.concatenate(tiles + values, axis=1)


def local_call(kernel, out_shape, name, **extra):
    return pl.pallas_call(
        kernel,
        out_shape=out_shape,
        compiler_params=pltpu.CompilerParams(vmem_limit_bytes=VMEM_LIMIT),
        name=name,
        **extra,
    )


def gather_rows(array, axis):
    return lax.all_gather(array, axis, axis=0, tiled=True)


def norm_back(grad_normed, scaled, inverse, gain):
    weighted = grad_normed * gain
    return inverse * (weighted - scaled * jnp.mean(weighted * scaled, axis=1, keepdims=True))


def general_body(
    tokens, attn_gain, query_weight, key_weight, value_weight, out_weight, mlp_gain, gate_weight,
    up_weight, down_weight, cotangent, cont_lengths, block_deal,
):
    n = lax.axis_size("ctx")
    me = lax.axis_index("ctx")
    row_count, width = tokens.shape[1:]
    kv_width = key_weight.shape[1]
    hidden = gate_weight.shape[1]
    block = row_count // 2
    total_rows = row_count * n
    prompt_size = total_rows // 2
    heads, kvh = width // HD, kv_width // HD
    share = heads // kvh
    stack = share * block
    sizes = (heads, kvh, block)

    deal = block_deal.reshape(n, 2)
    flip = deal[me, 0] > deal[me, 1]

    def ordered(rows):
        halves = rows.reshape(2, block, rows.shape[-1])
        return jnp.where(flip, halves[::-1], halves).reshape(rows.shape)

    x = ordered(tokens[0])
    cot = ordered(cotangent[0])
    naturals = jnp.sort(deal, axis=1)
    natural = naturals[:, :, None] * block + jnp.arange(block, dtype=jnp.int32)
    offset = natural - prompt_size
    lengths = cont_lengths[0]
    ending = jnp.cumsum(lengths)
    segment = jnp.sum((offset[..., None] >= ending).astype(jnp.int32), axis=-1)
    inside = segment[..., None] == jnp.arange(lengths.shape[0], dtype=jnp.int32)
    beginning = jnp.sum(jnp.where(inside, ending - lengths, 0), axis=-1)
    position = jnp.where(offset < 0, natural, prompt_size + offset - beginning)
    own_position = position[me].reshape(row_count)
    frequency = THETA ** (-2.0 * jnp.arange(HD // 2, dtype=F32) / HD)
    angle = own_position.astype(F32)[:, None] * frequency[None, :]
    cos, sin = jnp.cos(angle), jnp.sin(angle)
    cos = jnp.concatenate([cos, cos, cos, cos], axis=1)
    sin = jnp.concatenate([-sin, sin, -sin, sin], axis=1)
    around = (me + jnp.arange(n, dtype=jnp.int32)) % n
    first_natural = naturals[:, 0]
    pick = (first_natural[around] >= first_natural[me]).astype(jnp.int32)
    segk = segment[around, 1]
    segq = jnp.tile(segment[me, 1], share)
    me_arr = me.reshape(1).astype(jnp.int32)

    attn_rows = jnp.concatenate([query_weight, key_weight, value_weight, out_weight], axis=1)
    w_attn = gather_rows(attn_rows, "fsdp")
    qkv_width = width + 2 * kv_width
    w_qkv = w_attn[:, :qkv_width]
    w_out = w_attn[:, qkv_width:]
    gain_one = gather_rows(attn_gain, "fsdp").astype(F32)
    gain_two = gather_rows(mlp_gain, "fsdp").astype(F32)
    w_gate = gather_rows(gate_weight, "fsdp")
    w_up = gather_rows(up_weight, "fsdp")
    w_down = gather_rows(down_weight, "fsdp")

    normed_one, q, kv = local_call(
        functools.partial(project_kernel, sizes),
        (
            whole((row_count, width), BF16),
            whole((kvh, 2, stack, LANES), BF16),
            whole((2, block, kvh * LANES), BF16),
        ),
        "project",
    )(x, gain_one[None], w_attn, cos, sin)
    kv_all = lax.all_gather(kv, "ctx", axis=0)

    smem = pl.BlockSpec(memory_space=pltpu.SMEM)
    per_group = pl.BlockSpec((1, 2, stack, LANES), lambda g: (g, 0, 0, 0))
    kv_spec = pl.BlockSpec((n, 2, block, LANES), lambda g: (0, 0, 0, g))

    def full(array):
        rank = array.ndim
        return pl.BlockSpec(array.shape, lambda g: (0,) * rank)

    segq_col, segk_row = segq[:, None], segk[:, None, :]
    attended_heads, lse = local_call(
        functools.partial(attend_kernel, n),
        (whole((kvh, 2, stack, LANES), F32), whole((kvh, 2, stack, LANES), F32)),
        "attend",
        grid=(kvh,),
        in_specs=[smem, smem, full(segq_col), full(segk_row), per_group, kv_spec],
        out_specs=(per_group, per_group),
        scratch_shapes=[
            pltpu.VMEM((stack, n * block), F32),
            pltpu.VMEM((stack, n * block), BF16),
            pltpu.VMEM((n + 1, stack, block), F32),
            pltpu.VMEM((n + 1, stack, block), BF16),
        ],
    )(me_arr, pick, segq_col, segk_row, q, kv_all)

    attended, resid, normed_two = local_call(
        functools.partial(mid_kernel, sizes),
        (
            whole((row_count, width), BF16),
            whole((row_count, width), F32),
            whole((row_count, width), BF16),
        ),
        "mid",
    )(attended_heads, x, w_out, gain_two[None])

    inverse_two = lax.rsqrt(jnp.mean(resid * resid, axis=1, keepdims=True) + EPSILON)
    scaled_two = resid * inverse_two
    gate = nn(normed_two, w_gate)
    upward = nn(normed_two, w_up)
    sigma = jax.nn.sigmoid(gate)
    activated = gate * sigma
    product = (activated * upward).astype(BF16)
    result = resid + nn(product, w_down)
    grad_prod = nt(cot, w_down)
    grad_gate = (grad_prod * upward * sigma * (1.0 + gate * (1.0 - sigma))).astype(BF16)
    grad_up = (grad_prod * activated).astype(BF16)
    grad_normed_two = nt(grad_gate, w_gate) + nt(grad_up, w_up)
    gain_two_part = jnp.sum(grad_normed_two * scaled_two, axis=0)
    grad_resid = cot.astype(F32) + norm_back(grad_normed_two, scaled_two, inverse_two, gain_two)
    grad_branch = grad_resid.astype(BF16)

    grad_heads = local_call(
        functools.partial(branch_kernel, sizes), whole((kvh, 2, stack, LANES), BF16), "branch"
    )(grad_branch, w_out)

    segq_row, segk_col = segq[None, :], segk[:, :, None]
    grad_query, grad_kv = local_call(
        functools.partial(attend_back_kernel, n),
        (whole((kvh, 2, stack, LANES), F32), whole((n, 2, block, kvh * LANES), F32)),
        "attend_back",
        grid=(kvh,),
        in_specs=[smem, smem, full(segq_row), full(segk_col)]
        + [per_group, kv_spec, per_group, per_group, per_group],
        out_specs=(per_group, kv_spec),
        scratch_shapes=[
            pltpu.VMEM((4, 8, stack), F32),
            pltpu.VMEM((2, LANES, stack), F32),
        ],
    )(me_arr, pick, segq_row, segk_col, q, kv_all, grad_heads, attended_heads, lse)

    kv_sum = lax.psum_scatter(grad_kv, "ctx", scatter_dimension=0, tiled=False)
    grad_projected = local_call(
        functools.partial(unrope_kernel, sizes), whole((row_count, qkv_width), BF16), "unrope"
    )(grad_query, kv_sum, cos, sin)

    x_float = x.astype(F32)
    inverse_one = lax.rsqrt(jnp.mean(x_float * x_float, axis=1, keepdims=True) + EPSILON)
    scaled_one = x_float * inverse_one
    grad_normed_one = nt(grad_projected, w_qkv)
    gain_one_part = jnp.sum(grad_normed_one * scaled_one, axis=0)
    tokens_grad = (
        grad_resid + norm_back(grad_normed_one, scaled_one, inverse_one, gain_one)
    ).astype(BF16)

    def spread(partial):
        rows = lax.psum_scatter(partial.astype(BF16), "fsdp", scatter_dimension=0, tiled=True)
        return lax.psum(rows, "ctx").astype(F32)

    grad_gate_w = spread(tn(normed_two, grad_gate))
    grad_up_w = spread(tn(normed_two, grad_up))
    grad_down_w = spread(tn(product, cot))
    grad_out_w = spread(tn(attended, grad_branch))
    grad_qkv_w = spread(tn(normed_one, grad_projected))
    gains = spread(jnp.stack([gain_one_part, gain_two_part], axis=1))
    return (
        ordered(result.astype(BF16))[None],
        ordered(tokens_grad)[None],
        gains[:, 0],
        grad_qkv_w[:, :width],
        grad_qkv_w[:, width : width + kv_width],
        grad_qkv_w[:, width + kv_width :],
        grad_out_w,
        gains[:, 1],
        grad_gate_w,
        grad_up_w,
        grad_down_w,
    )


def solution(mesh):
    rows, matrix, vector = P("fsdp", "ctx", None), P("fsdp", None), P("fsdp")
    cube = dict(mesh.shape) == {"ctx": 8, "fsdp": 4}
    return jax.shard_map(
        cube_body if cube else general_body,
        mesh=mesh,
        in_specs=(rows, vector, matrix, matrix, matrix, matrix, vector, matrix, matrix, matrix)
        + (rows, matrix, P()),
        out_specs=(rows, rows, vector, matrix, matrix, matrix, matrix, vector, matrix, matrix, matrix),
        check_vma=False,
    )
```

```python
import functools

import jax
import jax.numpy as jnp
from jax import lax
from jax.experimental import pallas as pl
from jax.experimental.pallas import tpu as pltpu
from jax.sharding import PartitionSpec as P

HD = 64
LANES = 128
EPSILON = 1e-05
THETA = 100000.0
MASKED = -1e30
LOG2E = 1.4426950408889634
VMEM_LIMIT = 63 * 1024 * 1024
F32 = jnp.float32
BF16 = jnp.bfloat16


def nt(left, right):
    return lax.dot_general(left, right, (((1,), (1,)), ((), ())), preferred_element_type=F32)


def nn(left, right):
    return lax.dot_general(left, right, (((1,), (0,)), ((), ())), preferred_element_type=F32)


def tn(left, right):
    return lax.dot_general(left, right, (((0,), (0,)), ((), ())), preferred_element_type=F32)


def rope_tile(tile, cos, sin):
    lane = lax.broadcasted_iota(jnp.int32, tile.shape, 1) % HD
    partner = jnp.where(
        lane < HD // 2,
        pltpu.roll(tile, LANES - HD // 2, 1),
        pltpu.roll(tile, HD // 2, 1),
    )
    return tile * cos + partner * sin


def head_of(tiles, index):
    start = (index % 2) * HD
    return tiles[index // 2][:, start : start + HD]


MESH = pl.DeviceIdType.MESH
ATTN, FF, DOWN = 0, 1, 2
CORE, FIRST, SECOND = -1, -2, -3


class Links:
    def __init__(self, core, fsdp, send, recv, plan):
        self.core = core
        self.fsdp = fsdp
        self.ctx = lax.axis_index("ctx")
        self.z = lax.axis_index("fsdp")
        self.chip = self.ctx // 2
        self.first = 1 if core == 0 else 2
        self.second = 3 - self.first
        self.send_sem, self.recv_sem = send, recv
        self.plan = plan
        self.open = []

    def target(self, hop):
        if hop == CORE:
            return (lax.bitwise_xor(self.ctx, 1), self.z)
        if hop == FIRST:
            return (lax.bitwise_xor(self.ctx, 2 * self.first), self.z)
        if hop == SECOND:
            return (lax.bitwise_xor(self.ctx, 2 * self.second), self.z)
        return (self.ctx, lax.bitwise_xor(self.z, hop))

    def copy(self, key, hop, src, dst):
        slot = self.plan.setdefault(key, len(self.plan))
        return pltpu.make_async_remote_copy(
            src_ref=src,
            dst_ref=dst,
            send_sem=self.send_sem.at[slot],
            recv_sem=self.recv_sem.at[slot],
            device_id=self.target(hop),
            device_id_type=MESH,
        )

    def send(self, key, hop, src, dst):
        copy = self.copy(key, hop, src, dst)
        copy.start()
        self.open.append((key, getattr(src, "ref", src), src.shape))

    def landed(self, key, dst):
        self.copy(key, CORE, dst, dst).wait_recv()

    def drain(self):
        for key, base, shape in self.open:
            at = (0,) * (len(base.shape) - len(shape)) + tuple(pl.ds(0, size) for size in shape)
            self.copy(key, CORE, base.at[at], base.at[at]).wait_send()


def greet(hops, fsdp):
    ctx, z = lax.axis_index("ctx"), lax.axis_index("fsdp")
    barrier = pltpu.get_barrier_semaphore()
    targets = [(lax.bitwise_xor(ctx, h), z) for h in (1, 2, 4)]
    if "z" in hops:
        targets += [(ctx, lax.bitwise_xor(z, d)) for d in range(1, fsdp)]
    for target in targets:
        pl.semaphore_signal(barrier, inc=1, device_id=target, device_id_type=MESH)
    pl.semaphore_wait(barrier, len(targets))


def by_core(program):
    for core in (0, 1):
        pl.when(lax.axis_index("ctx") % 2 == core)(functools.partial(program, core))


def sub(base, size, unit):
    return pl.ds(pl.multiple_of(base, unit), size)


def lanes(ref, tiles, rows=slice(None)):
    return jnp.concatenate([ref[t, rows, :] for t in tiles], axis=1)


def pack_tiles(parts):
    matrix = jnp.concatenate(parts, axis=1)
    short = -matrix.shape[1] % LANES
    if short:
        matrix = jnp.concatenate([matrix, jnp.zeros((matrix.shape[0], short), matrix.dtype)], axis=1)
    return [matrix[:, t * LANES : (t + 1) * LANES] for t in range(matrix.shape[1] // LANES)]


class Share:
    def __init__(self, name, core, shard):
        self.name, self.core = name, core
        self.shard = shard
        self.offset, self.rows = 0, shard
        if name == ATTN:
            half = -(-shard // 32) * 16
            self.offset, self.rows = (0, half) if core == 0 else (half, shard - half)

    def at(self, ref, zi, q):
        rows = sub(zi * self.shard + self.offset, self.rows, 16)
        if self.name == ATTN:
            return ref.at[pl.ds(q * (ref.shape[0] // 4), ref.shape[0] // 4), rows]
        if self.name == FF:
            return ref.at[self.core, pl.ds(q * (ref.shape[1] // 4), ref.shape[1] // 4), rows]
        return ref.at[2 * q + self.core, rows]

    def buffer(self, ref):
        return ref.at[:, pl.ds(0, self.rows)] if self.name == ATTN else ref


PACKAGES = (ATTN, FF, DOWN)
FINISH = 0


def both_cores(make):
    tables = [make(0), make(1)]

    def run(*names):
        for core in (0, 1):
            def program(core=core):
                for name in names:
                    tables[core][name]()

            pl.when(lax.axis_index("ctx") % 2 == core)(program)

    return run


def weight_stages(core, fsdp, plan, refs, send, recv):
    links = Links(core, fsdp, send, recv, plan)
    z, chip = links.z, links.chip
    near, far = lax.bitwise_xor(chip, links.first), lax.bitwise_xor(chip, links.second)
    corner = lax.bitwise_xor(chip, 3)
    shards = {ATTN: refs[ATTN].shape[1] // fsdp, FF: refs[FF].shape[2] // fsdp, DOWN: refs[DOWN].shape[1] // fsdp}
    mine = {k: Share(k, core, shards[k]) for k in PACKAGES}
    twin = {k: Share(k, 1 - core, shards[k]) for k in PACKAGES}
    stages = {}

    def over_z(k):
        here = mine[k].at(refs[k], z, chip)
        for d in range(1, fsdp):
            links.send((k, "z", d), d, here, here)

    def spread(k):
        for d in range(1, fsdp):
            piece = mine[k].at(refs[k], lax.bitwise_xor(z, d), chip)
            links.landed((k, "z", d), piece)
            links.send((k, FIRST, d), FIRST, piece, piece)
            links.send((k, SECOND, d), SECOND, piece, piece)
            links.send((k, CORE, d, 0), CORE, piece, piece)

    def forward(k):
        for d in range(1, fsdp):
            piece = mine[k].at(refs[k], lax.bitwise_xor(z, d), near)
            links.landed((k, FIRST, d), piece)
            links.send((k, "corner", d), SECOND, piece, piece)
            links.send((k, CORE, d, 1), CORE, piece, piece)

    def pass_some(k, i, what, q):
        for d in range(1, fsdp):
            piece = mine[k].at(refs[k], lax.bitwise_xor(z, d), q)
            links.landed((k, what, d), piece)
            links.send((k, CORE, d, i), CORE, piece, piece)

    def pass_far(k):
        pass_some(k, 2, SECOND, far)

    def pass_corner(k):
        pass_some(k, 3, "corner", corner)

    def finish_some(k, i, q):
        for d in range(1, fsdp):
            links.landed((k, CORE, d, i), twin[k].at(refs[k], lax.bitwise_xor(z, d), q))

    def finish(k):
        for i in range(4):
            stages[FINISH, k, i]()

    for k in PACKAGES:
        for i, q in ((0, chip), (1, far), (2, near), (3, corner)):
            stages[FINISH, k, i] = functools.partial(finish_some, k, i, q)
    for k in PACKAGES:
        for fn in (over_z, spread, forward, pass_far, pass_corner, finish):
            stages[fn.__name__, k] = functools.partial(fn, k)

    def gains_out():
        for d in range(1, fsdp):
            links.send(("gains", d), d, refs["gains"].at[z], refs["gains"].at[z])

    def gains_in():
        for d in range(1, fsdp):
            links.landed(("gains", d), refs["gains"].at[lax.bitwise_xor(z, d)])

    stages["gains_out"], stages["gains_in"], stages["drain"] = gains_out, gains_in, links.drain
    return stages


def kv_stages(core, plan, kv_all, send, recv):
    links = Links(core, 1, send, recv, plan)
    ctx = links.ctx
    near = lax.bitwise_xor(ctx, 2 * links.first)
    far = lax.bitwise_xor(ctx, 2 * links.second)
    corner = lax.bitwise_xor(ctx, 6)

    def start():
        for b in range(2):
            piece = kv_all.at[ctx, b]
            links.send(("kv first", b), FIRST, piece, piece)
            links.send(("kv second", b), SECOND, piece, piece)
            links.send(("kv core", 0, b), CORE, piece, piece)

    def forward():
        for b in range(2):
            piece = kv_all.at[near, b]
            links.landed(("kv first", b), piece)
            links.send(("kv corner", b), SECOND, piece, piece)
            links.send(("kv core", 1, b), CORE, piece, piece)

    def pass_on():
        for i, (what, owner) in enumerate((("kv second", far), ("kv corner", corner))):
            for b in range(2):
                piece = kv_all.at[owner, b]
                links.landed((what, b), piece)
                links.send(("kv core", 2 + i, b), CORE, piece, piece)

    def finish():
        for i, owner in ((0, ctx), (1, far), (2, near), (3, corner)):
            for b in range(2):
                links.landed(("kv core", i, b), kv_all.at[lax.bitwise_xor(owner, 1), b])

    return {"start": start, "forward": forward, "pass_on": pass_on, "finish": finish, "drain": links.drain}


def store_projection(sizes, raw_tiles, cos, sin, q_ref, kv_at):
    heads, kvh, block = sizes
    share = heads // kvh
    tiles = [rope_tile(raw_tiles[j], cos, sin).astype(BF16) for j in range((heads + kvh) // 2)]
    tiles += [raw_tiles[j].astype(BF16) for j in range((heads + kvh) // 2, len(raw_tiles))]

    def head(index):
        start = (index % 2) * HD
        return tiles[index // 2][:, start : start + HD]

    zero = jnp.zeros((block, HD), BF16)
    for h in range(heads):
        piece = head(h) * jnp.asarray(0.125, BF16)
        g, i = h // share, h % share
        for b in range(2):
            q_ref[g, b, i * block : (i + 1) * block, :] = jnp.concatenate(
                [piece[b * block : (b + 1) * block], zero], axis=1
            )
    for g in range(kvh):
        pair = jnp.concatenate([head(heads + g), head(heads + kvh + g)], axis=1)
        for b in range(2):
            kv_at(b, g)[...] = pair[b * block : (b + 1) * block]


def rms_inverse(x):
    return lax.rsqrt(jnp.mean(x * x, axis=1, keepdims=True) + EPSILON)


def natural_blocks(deal_ref, c):
    one, two = deal_ref[2 * c], deal_ref[2 * c + 1]
    return jnp.minimum(one, two), jnp.maximum(one, two)


def segment_start(lengths_ref, offset):
    start = jnp.zeros_like(offset)
    ending = 0
    for c in range(lengths_ref.shape[1]):
        ending = ending + lengths_ref[0, c]
        start = jnp.where(offset >= ending, ending, start)
    return start


def ordered(flip, rows):
    half = rows.shape[0] // 2
    return jnp.where(flip, jnp.concatenate([rows[half:], rows[:half]], axis=0), rows)


def first_keys(n, deal_ref, lengths_ref, block, rows):
    _, last = natural_blocks(deal_ref, lax.axis_index("ctx"))
    offset = (last - n) * block + lax.rem(lax.broadcasted_iota(jnp.int32, (8, rows), 1), block)
    return segment_start(lengths_ref, offset)


def attend_masks(n, deal_ref, start_ref, block, rows):
    key = lax.broadcasted_iota(jnp.int32, (block, rows), 0)

    def own(b):
        allowed = key <= lax.rem(lax.broadcasted_iota(jnp.int32, (block, rows), 1), block)
        if b == 0:
            return allowed
        _, last = natural_blocks(deal_ref, lax.axis_index("ctx"))
        return allowed & (key >= start_ref[0:1, :] - (last - n) * block)

    def other(at):
        mine, _ = natural_blocks(deal_ref, lax.axis_index("ctx"))
        first, last = natural_blocks(deal_ref, at)
        kind = jnp.where(first >= mine, 1, 0)
        bound = jnp.where(kind == 0, -1, start_ref[0:1, :] - (last - n) * block)
        return kind, key >= bound

    return own, other


def attend_step(n, me, g, j, deal_ref, start_ref, q_ref, kv_ref, top_ref, acc_ref):
    block = kv_ref.shape[3]
    rows = q_ref.shape[2]
    value_lane = lax.broadcasted_iota(jnp.int32, (block, LANES), 1) >= HD
    own_mask, other_mask = attend_masks(n, deal_ref, start_ref, block, rows)

    def scores(kind, tile, mask):
        s = nt(tile, q_ref[g, kind])
        return s if mask is None else jnp.where(mask, s, MASKED)

    def weigh(s, top, tile):
        p = jnp.exp2((s - top) * LOG2E).astype(BF16)
        return tn(jnp.where(value_lane, tile, jnp.asarray(1, BF16)), p)

    def own():
        own0, own1 = kv_ref[me, 0, g], kv_ref[me, 1, g]
        s0 = scores(0, own0, own_mask(0))
        top0 = jnp.max(s0, axis=0, keepdims=True)
        acc_ref[0] = weigh(s0, top0, own0)
        top_ref[0] = jnp.broadcast_to(top0, top_ref.shape[1:])
        s1 = scores(1, own1, own_mask(1))
        s2 = scores(1, own0, None)
        top1 = jnp.maximum(jnp.max(s1, axis=0, keepdims=True), jnp.max(s2, axis=0, keepdims=True))
        acc_ref[1] = weigh(s1, top1, own1) + weigh(s2, top1, own0)
        top_ref[1] = jnp.broadcast_to(top1, top_ref.shape[1:])

    def other():
        at = lax.rem(me + j, n)
        kind, mask = other_mask(at)
        is_prompt = kind == 0
        tile0, tile1 = kv_ref[at, 0, g], kv_ref[at, kind, g]
        s1 = scores(1, tile0, None)
        s2 = scores(kind, tile1, mask)
        old_p, old_c = top_ref[0, 0:1, :], top_ref[1, 0:1, :]
        high1 = jnp.max(s1, axis=0, keepdims=True)
        high2 = jnp.max(s2, axis=0, keepdims=True)
        top_p = jnp.where(is_prompt, jnp.maximum(old_p, high2), old_p)
        top_c = jnp.maximum(old_c, jnp.where(is_prompt, high1, jnp.maximum(high1, high2)))
        part1 = weigh(s1, top_c, tile0)
        part2 = weigh(s2, jnp.where(is_prompt, top_p, top_c), tile1)
        acc_ref[0] = acc_ref[0] * jnp.exp2((old_p - top_p) * LOG2E) + jnp.where(is_prompt, part2, 0.0)
        acc_ref[1] = (
            acc_ref[1] * jnp.exp2((old_c - top_c) * LOG2E) + part1 + jnp.where(is_prompt, 0.0, part2)
        )
        top_ref[0] = jnp.broadcast_to(top_p, top_ref.shape[1:])
        top_ref[1] = jnp.broadcast_to(top_c, top_ref.shape[1:])

    return own, other


def attend_close(g, top_ref, acc_ref, o_ref, lse_ref):
    for b in range(2):
        acc = acc_ref[b]
        total = acc[0:1, :]
        o_ref[g, b] = (acc / total).T
        lse_ref[g, b] = jnp.broadcast_to(top_ref[b, 0:1, :] * LOG2E + jnp.log2(total), lse_ref.shape[2:])


def attend_back_step(n, me, g, j, deal_ref, start_ref, q_ref, kv_ref, do_ref, lse_ref, delta_ref, dqt_ref, dkv_ref):
    block = kv_ref.shape[3]
    rows = q_ref.shape[2]
    own_mask, other_mask = attend_masks(n, deal_ref, start_ref, block, rows)

    def pair(kind, tile, mask):
        q = q_ref[g, kind]
        do = do_ref[g, kind]
        p = jnp.exp2(nt(tile, q) * LOG2E - lse_ref[g, kind, 0:1, :])
        if mask is not None:
            p = jnp.where(mask, p, 0.0)
        ds = (p * (nt(tile, do) - delta_ref[g, kind, 0:1, :])).astype(BF16)
        return nn(ds, q) + nn(p.astype(BF16), do), tn(tile, ds)

    def own():
        own0, own1 = kv_ref[me, 0, g], kv_ref[me, 1, g]
        d0, q0 = pair(0, own0, own_mask(0))
        d1, q1 = pair(1, own1, own_mask(1))
        d2, q2 = pair(1, own0, None)
        dkv_ref[me, g, 0] = (d0 + d2).astype(dkv_ref.dtype)
        dkv_ref[me, g, 1] = d1.astype(dkv_ref.dtype)
        dqt_ref[0] = q0
        dqt_ref[1] = q1 + q2

    def other():
        at = lax.rem(me + j, n)
        kind, mask = other_mask(at)
        is_prompt = kind == 0
        full, q_full = pair(1, kv_ref[at, 0, g], None)
        part, q_part = pair(kind, kv_ref[at, kind, g], mask)
        dkv_ref[at, g, 0] = (full + jnp.where(is_prompt, part, 0.0)).astype(dkv_ref.dtype)
        dkv_ref[at, g, 1] = jnp.where(is_prompt, 0.0, part).astype(dkv_ref.dtype)
        dqt_ref[0] = dqt_ref[0] + jnp.where(is_prompt, q_part, 0.0)
        dqt_ref[1] = dqt_ref[1] + q_full + jnp.where(is_prompt, 0.0, q_part)

    return own, other


def row_deltas(g, do_ref, o_ref, row_ref):
    ones = jnp.ones((8, LANES), F32)
    for b in range(2):
        row_ref[b] = lax.dot_general(
            ones, do_ref[g, b].astype(F32) * o_ref[g, b], (((1,), (1,)), ((), ())),
            precision=lax.Precision.HIGHEST, preferred_element_type=F32,
        )


def gain_row(gains_ref, which, fsdp, shard):
    return jnp.concatenate([gains_ref[i, which : which + 1, :shard] for i in range(fsdp)], axis=1)


def project(sizes, fsdp, x_ref, gains_ref, attn_ref, cos_ref, sin_ref, n1_ref, q_ref, kv_at):
    heads, kvh, block = sizes
    x = x_ref[...].astype(F32)
    normed = (x * rms_inverse(x) * gain_row(gains_ref, 0, fsdp, x.shape[1] // fsdp)).astype(BF16)
    n1_ref[...] = normed
    count = -(-(heads + 2 * kvh) * HD // LANES)
    raw = []
    for t in range(0, count, 2):
        some = range(t, min(t + 2, count))
        wide = nn(normed, lanes(attn_ref, some))
        raw += [wide[:, i * LANES : (i + 1) * LANES] for i in range(len(some))]
    store_projection(sizes, raw, cos_ref[...], sin_ref[...], q_ref, kv_at)


def front_kernel(
    sizes, n, fsdp, plans, deal_ref, lengths_ref, xt_ref, gains_in, turns_ref,
    wq_ref, wkt_ref, wvt_ref, wo_ref, wg_ref, wu_ref, wdt_ref, cott_ref,
    x_ref, cos_ref, sin_ref, n1_ref, q_ref, kv_out, lse_ref, gains_ref, attn_out,
    result_ref, gr_ref, do_ref, delta_ref, gain_ref, out_grad, ff_grad, down_grad,
    attn, ff, down, kv_all, o_ref, gains, start_ref, top_ref, acc_ref, cot_ref,
    resid_ref, n2_ref, product_ref, gg_ref, gu_ref, turned_ref, gn_ref, out_stage, ff_stage, down_stage,
    send, recv, kv_send, kv_recv, local, out_sem,
):
    heads, kvh, block = sizes
    me, z = lax.axis_index("ctx"), lax.axis_index("fsdp")
    shard = wq_ref.shape[0]
    rows = sub(z * shard, shard, 16)
    half = (heads + 2 * kvh) * HD % LANES
    main = wo_ref.shape[1] - half
    wo = wo_ref[...]
    tiles = pack_tiles([wq_ref[...], wkt_ref[...].T, wvt_ref[...].T, wo[:, main:], wo[:, :main]])
    for t, tile in enumerate(tiles):
        attn[t, rows, :] = tile
    gains[z] = gains_in[...]
    greet("z", fsdp)
    refs = {ATTN: attn, FF: ff, DOWN: down, "gains": gains}
    run = both_cores(lambda core: weight_stages(core, fsdp, plans[0], refs, send, recv))
    run_kv = both_cores(lambda core: kv_stages(core, plans[1], kv_all, kv_send, kv_recv))
    run("gains_out", ("over_z", ATTN))
    for t in range(ff.shape[1]):
        ff[0, t, rows, :] = wg_ref[:, t * LANES : (t + 1) * LANES]
        ff[1, t, rows, :] = wu_ref[:, t * LANES : (t + 1) * LANES]
    down_shard = wdt_ref.shape[1]
    down_rows = sub(z * down_shard, down_shard, 16)
    for t, tile in enumerate(pack_tiles([wdt_ref[...].T])):
        down[t, down_rows, :] = tile
    first, last = natural_blocks(deal_ref, me)
    flip = deal_ref[2 * me] > deal_ref[2 * me + 1]
    x_ref[...] = ordered(flip, xt_ref[...].T)
    cot_ref[...] = ordered(flip, cott_ref[...].T)
    row = lax.broadcasted_iota(jnp.int32, cos_ref.shape, 0)
    natural = jnp.where(row < block, first * block + row, (last - 1) * block + row)
    offset = natural - n * block
    position = jnp.where(offset < 0, natural, natural - segment_start(lengths_ref, offset))
    angle = position.astype(F32) * turns_ref[0:1, :]
    lane = lax.broadcasted_iota(jnp.int32, cos_ref.shape, 1)
    cos_ref[...] = jnp.cos(angle)
    sine = jnp.sin(angle)
    sin_ref[...] = jnp.where(lax.rem(lane, HD) < HD // 2, -sine, sine)
    start_ref[...] = first_keys(n, deal_ref, lengths_ref, block, start_ref.shape[1])
    run(("spread", ATTN), ("over_z", DOWN), ("over_z", FF), ("forward", ATTN))
    run(("pass_far", ATTN), ("pass_corner", ATTN))
    run(("finish", ATTN), "gains_in")
    project(
        sizes, fsdp, x_ref, gains, attn, cos_ref, sin_ref, n1_ref, q_ref,
        lambda b, g: kv_all.at[me, b, g],
    )
    run_kv("start", "forward")
    run(("spread", DOWN))
    run_kv("pass_on", "finish")
    gains_ref[...] = gains[...]
    outs = [pltpu.make_async_copy(attn, attn_out, local.at[0]), pltpu.make_async_copy(kv_all, kv_out, local.at[1])]
    for copy in outs:
        copy.start()
    schedule = {
        4: (("forward", DOWN),),
        10: (("spread", FF),),
        16: (("pass_far", DOWN), ("pass_corner", DOWN)),
        24: (("forward", FF),),
        30: (("finish", DOWN),),
        38: (("pass_far", FF),),
    }

    @pl.loop(0, kvh * n)
    def _(step):
        g, j = step // n, step % n
        for at, names in schedule.items():
            pl.when(step == at)(functools.partial(run, *names))
        own, other = attend_step(n, me, g, j, deal_ref, start_ref, q_ref, kv_all, top_ref, acc_ref)
        pl.when(j == 0)(own)
        pl.when(j > 0)(other)
        pl.when(j == n - 1)(lambda: attend_close(g, top_ref, acc_ref, o_ref, lse_ref))

    def quarter_ready(i):
        pl.when(i == 0)(lambda: run((FINISH, FF, 0)))
        pl.when(i == 1)(lambda: run((FINISH, FF, 1), (FINISH, FF, 2)))
        pl.when(i == 3)(lambda: run(("pass_corner", FF), (FINISH, FF, 3)))
        return lax.bitwise_xor(me // 2, i)

    feed_forward(
        sizes, fsdp, quarter_ready, lambda: None, x_ref, cot_ref, gains, attn, ff, down, o_ref,
        result_ref, gr_ref, do_ref, delta_ref, gain_ref, out_grad, ff_grad, down_grad,
        resid_ref, n2_ref, product_ref, gg_ref, gu_ref, turned_ref, gn_ref, out_stage, ff_stage, down_stage, out_sem,
    )
    run("drain")
    run_kv("drain")
    for copy in outs:
        copy.wait()


def head_columns(sizes, ref, low):
    heads, kvh, block = sizes
    share = heads // kvh
    return jnp.concatenate(
        [
            jnp.concatenate(
                [
                    ref[h // share, b, (h % share) * block : (h % share + 1) * block, low : low + HD]
                    for h in range(heads)
                ],
                axis=1,
            )
            for b in range(2)
        ],
        axis=0,
    )


def feed_forward(
    sizes, fsdp, quarter_ready, all_ready, x_ref, cot_ref, gains_ref, attn_ref, ff_ref, down_ref, o_ref,
    result_ref, gr_ref, do_ref, delta_ref, gain_ref, out_grad, ff_grad, down_grad,
    resid_ref, n2_ref, product_ref, gg_ref, gu_ref, turned_ref, gn_ref, out_stage, ff_stage, down_stage, sem,
):
    heads, kvh, block = sizes
    share = heads // kvh
    rows, width = x_ref.shape
    hidden = product_ref.shape[1]
    mixed = (heads + 2 * kvh) * HD // LANES
    half = (heads + 2 * kvh) * HD % LANES
    count = attn_ref.shape[0]
    down_tiles = down_ref.shape[0]
    gain = gain_row(gains_ref, 1, fsdp, width // fsdp)
    attended = head_columns(sizes, o_ref, HD).astype(BF16)
    pieces = []
    for t in range(mixed, count, 2):
        pieces.append(nn(attended, lanes(attn_ref, range(t, min(t + 2, count)))))
    branch = jnp.concatenate(pieces, axis=1)
    branch = jnp.concatenate([branch[:, LANES:], branch[:, half:LANES]], axis=1)
    resid = x_ref[...].astype(F32) + branch
    resid_ref[...] = resid
    n2_ref[...] = (resid * rms_inverse(resid) * gain).astype(BF16)
    pad = down_tiles * LANES - width
    wide = 2 * LANES
    per = ff_ref.shape[1] // 4

    @pl.loop(0, 4)
    def _(i):
        q = quarter_ready(i)
        cot_wide = jnp.concatenate([cot_ref[...], jnp.zeros((rows, pad), BF16)], axis=1)
        for low in range(0, per, 2):
            size = min(2, per - low)
            first = q * per + low
            at = pl.ds(pl.multiple_of(first * LANES, LANES), size * LANES)
            n2 = n2_ref[...]
            gate = nn(n2, jnp.concatenate([ff_ref[0, first + t] for t in range(size)], axis=1))
            upward = nn(n2, jnp.concatenate([ff_ref[1, first + t] for t in range(size)], axis=1))
            grad = nt(cot_wide, jnp.concatenate([down_ref[t, at, :] for t in range(down_tiles)], axis=1))
            sigma = 1.0 / (1.0 + jnp.exp(-gate))
            activated = gate * sigma
            product_ref[:, at] = (activated * upward).astype(BF16)
            gg_ref[:, at] = (grad * upward * (sigma + activated * (1.0 - sigma))).astype(BF16)
            gu_ref[:, at] = (grad * activated).astype(BF16)

    all_ready()
    for low in range(0, width, wide):
        size = min(wide, width - low)
        part = nt(gg_ref[...], lanes(ff_ref.at[0], range(hidden // LANES), slice(low, low + size)))
        part = part + nt(gu_ref[...], lanes(ff_ref.at[1], range(hidden // LANES), slice(low, low + size)))
        gn_ref[:, low : low + size] = part
    turned_ref[...] = n2_ref[...].T

    def ff_out(j):
        return pltpu.make_async_copy(ff_stage.at[j % 2], ff_grad.at[:, pl.ds(2 * j, 2)], sem.at[j % 2])

    def down_out(j):
        at = pl.ds(pl.multiple_of(j * wide, wide), wide)
        return pltpu.make_async_copy(down_stage.at[j % 2], down_grad.at[:, at], sem.at[2 + j % 2])

    @pl.loop(0, hidden // wide)
    def _(j):
        at = pl.ds(pl.multiple_of(j * wide, wide), wide)
        slot = lax.rem(j, 2)

        @pl.when(j >= 2)
        def _():
            ff_out(j - 2).wait()
            down_out(j - 2).wait()

        for c, grad_ref in enumerate((gg_ref, gu_ref)):
            part = nn(turned_ref[...], grad_ref[:, at]).astype(BF16)
            ff_stage[slot, c, 0] = part[:, :LANES]
            ff_stage[slot, c, 1] = part[:, LANES:]
        flipped = product_ref[:, at].T
        cot_wide = jnp.concatenate([cot_ref[...], jnp.zeros((rows, pad), BF16)], axis=1)
        part = nn(flipped, cot_wide).astype(BF16)
        for t in range(down_tiles):
            down_stage[slot, t] = part[:, t * LANES : (t + 1) * LANES]
        ff_out(j).start()
        down_out(j).start()

    grad_normed = gn_ref[...]
    resid = resid_ref[...]
    inverse = rms_inverse(resid)
    scaled = resid * inverse
    weighted = grad_normed * gain
    gain_ref[0:1, :] = jnp.sum(grad_normed * scaled, axis=0, keepdims=True)
    grad_resid = cot_ref[...].astype(F32) + inverse * (
        weighted - scaled * jnp.mean(weighted * scaled, axis=1, keepdims=True)
    )
    gr_ref[...] = grad_resid
    gb = grad_resid.astype(BF16)
    main = width - (LANES - half)
    lined = jnp.concatenate([jnp.zeros((rows, half), BF16), gb[:, main:], gb[:, :main]], axis=1)
    turned_ref[...] = head_columns(sizes, o_ref, HD).astype(BF16).T
    for t in range(0, count - mixed, 2):
        part = nn(turned_ref[...], lined[:, t * LANES : (t + 2) * LANES]).astype(BF16)
        out_stage[t] = part[:, :LANES]
        out_stage[t + 1] = part[:, LANES:]
    out_copy = pltpu.make_async_copy(out_stage, out_grad, sem.at[4])
    out_copy.start()
    grad_att = []
    for low in range(0, width, wide):
        size = min(wide, width - low)
        grad_att.append(
            nt(lined, lanes(attn_ref, range(mixed, count), slice(low, low + size))).astype(BF16)
        )
    grad_att = jnp.concatenate(grad_att, axis=1)
    zero = jnp.zeros((block, HD), BF16)
    for h in range(heads):
        for b in range(2):
            do_ref[h // share, b, (h % share) * block : (h % share + 1) * block, :] = jnp.concatenate(
                [zero, grad_att[b * block : (b + 1) * block, h * HD : (h + 1) * HD]], axis=1
            )
    for g in range(kvh):
        row_deltas(g, do_ref, o_ref, delta_ref.at[g])
    for t in range(0, down_tiles, 2):
        low, high = t * LANES, min((t + 2) * LANES, width)
        part = nn(product_ref[...], lanes(down_ref, (t, t + 1)))
        result_ref[:, low:high] = (resid_ref[:, low:high] + part[:, : high - low]).astype(BF16)
    last = hidden // wide
    for j in (last - 2, last - 1):
        ff_out(j).wait()
        down_out(j).wait()
    out_copy.wait()


def add_rows(out, terms, rows):
    def add(views):
        total = views[1][0:rows, :].astype(F32)
        for term in views[2:]:
            total = total + term[0:rows, :].astype(F32)
        views[0][0:rows, :] = total.astype(out.dtype)

    refs = [out] + list(terms)
    if len(out.shape) == 2:
        add(refs)
    else:

        @pl.loop(0, out.shape[0])
        def _(lead):
            add([r.at[lead] for r in refs])


def grad_stages(core, fsdp, plan, sources, held, got, outs, gain_refs, send, recv, local):
    links = Links(core, fsdp, send, recv, plan)
    z, chip = links.z, links.chip
    near, far = lax.bitwise_xor(chip, links.first), lax.bitwise_xor(chip, links.second)
    corner = lax.bitwise_xor(chip, 3)
    shards = {k: sources[k].shape[-2] // fsdp for k in PACKAGES}
    mine = {k: Share(k, core, shards[k]) for k in PACKAGES}
    twin = {k: Share(k, 1 - core, shards[k]) for k in PACKAGES}
    stages = {}

    def hold(k, d, q):
        if k in held:
            return held[k].at[d, q]
        return mine[k].at(sources[k], lax.bitwise_xor(z, d), q)

    def load(k, d, q):
        slot = (PACKAGES.index(k) * fsdp + d) * 4 + q
        return pltpu.make_async_copy(
            mine[k].at(sources[k], lax.bitwise_xor(z, d), q), hold(k, d, q), local.at[slot]
        )

    def begin(k, d):
        zi = lax.bitwise_xor(z, d)
        for q in range(4):
            links.send((k, CORE, d, q), CORE, twin[k].at(sources[k], zi, q), twin[k].buffer(got[k][0].at[d, q]))
            if k in held:
                load(k, d, q).start()

    def stage1(k, d):
        share = mine[k]
        for q in range(4):
            links.landed((k, CORE, d, q), share.buffer(got[k][0].at[d, q]))
            if k in held:
                load(k, d, q).wait()
            add_rows(hold(k, d, q), (hold(k, d, q), got[k][0].at[d, q]), share.rows)
        for i, q in enumerate((near, corner)):
            links.send((k, FIRST, d, i), FIRST, hold(k, d, q), share.buffer(got[k][1].at[d, i]))

    def stage2(k, d):
        share = mine[k]
        for i in range(2):
            links.landed((k, FIRST, d, i), share.buffer(got[k][1].at[d, i]))
        add_rows(hold(k, d, far), (hold(k, d, far), got[k][1].at[d, 1]), share.rows)
        links.send((k, SECOND, d), SECOND, hold(k, d, far), share.buffer(got[k][2].at[d]))

    def stage3(k, d):
        share = mine[k]
        links.landed((k, SECOND, d), share.buffer(got[k][2].at[d]))
        add_rows(hold(k, d, chip), (hold(k, d, chip), got[k][1].at[d, 0], got[k][2].at[d]), share.rows)
        if d > 0:
            links.send((k, "z", d), d, hold(k, d, chip), share.buffer(got[k][3].at[d - 1]))

    def out_copy(k):
        slot = len(PACKAGES) * fsdp * 4 + PACKAGES.index(k)
        return pltpu.make_async_copy(hold(k, 0, chip), mine[k].at(outs[k], 0, chip), local.at[slot])

    def close(k):
        share = mine[k]
        for d in range(1, fsdp):
            links.landed((k, "z", d), share.buffer(got[k][3].at[d - 1]))
        final = hold(k, 0, chip)
        add_rows(final, [final] + [got[k][3].at[d - 1] for d in range(1, fsdp)], share.rows)
        for hop in (FIRST, SECOND):
            links.send((k, "out", hop), hop, final, share.at(outs[k], 0, chip))
        links.send((k, "out core", 0), CORE, final, share.at(outs[k], 0, chip))
        out_copy(k).start()

    def close2(k):
        share = mine[k]
        links.landed((k, "out", FIRST), share.at(outs[k], 0, near))
        piece = share.at(outs[k], 0, near)
        links.send((k, "out", "corner"), SECOND, piece, piece)
        links.send((k, "out core", 1), CORE, piece, piece)
        piece = share.at(outs[k], 0, far)
        links.landed((k, "out", SECOND), piece)
        links.send((k, "out core", 2), CORE, piece, piece)

    def close3(k):
        piece = mine[k].at(outs[k], 0, corner)
        links.landed((k, "out", "corner"), piece)
        links.send((k, "out core", 3), CORE, piece, piece)

    def close4(k):
        for i, q in ((0, chip), (1, far), (2, near), (3, corner)):
            links.landed((k, "out core", i), twin[k].at(outs[k], 0, q))
        out_copy(k).wait()

    for k in PACKAGES:
        for fn in (begin, stage1, stage2, stage3):
            for d in range(fsdp):
                stages[fn.__name__, k, d] = functools.partial(fn, k, d)
        for fn in (close, close2, close3, close4):
            stages[fn.__name__, k] = functools.partial(fn, k)

    gain_sum, gain_got, gain_z, gain_out = gain_refs

    def gain_step(i):
        if i > 0:
            links.landed(("gain", i - 1), gain_got.at[i - 1])
            gain_sum[i] = gain_sum[i - 1] + gain_got[i - 1]
        if i < 3:
            links.send(("gain", i), (CORE, FIRST, SECOND)[i], gain_sum.at[i], gain_got.at[i])
        else:
            for d in range(1, fsdp):
                links.send(("gain z", d), d, gain_sum.at[3, lax.bitwise_xor(z, d)], gain_z.at[d - 1])

    def gain_close():
        total = gain_sum[3, z]
        for d in range(1, fsdp):
            links.landed(("gain z", d), gain_z.at[d - 1])
            total = total + gain_z[d - 1]
        gain_out[...] = total

    for i in range(4):
        stages["gain", i] = functools.partial(gain_step, i)
    stages["gain close"] = gain_close
    stages["drain"] = links.drain
    return stages


def kv_grad_stages(core, plan, parts, kv_sum, got0, got1, got2, send, recv):
    links = Links(core, 1, send, recv, plan)
    chip = links.chip
    near, far = lax.bitwise_xor(chip, links.first), lax.bitwise_xor(chip, links.second)
    corner = lax.bitwise_xor(chip, 3)
    rows = parts.shape[3]
    stages = {}

    def start(g):
        for q in range(4):
            links.send((0, g, q), CORE, parts.at[2 * q + 1 - core, g], got0.at[g, q])

    def stage1(g):
        for q in range(4):
            links.landed((0, g, q), got0.at[g, q])
            add_rows(got0.at[g, q], (parts.at[2 * q + core, g], got0.at[g, q]), rows)
        for i, q in enumerate((near, corner)):
            links.send((1, g, i), FIRST, got0.at[g, q], got1.at[g, i])

    def stage2(g):
        for i in range(2):
            links.landed((1, g, i), got1.at[g, i])
        add_rows(got0.at[g, far], (got0.at[g, far], got1.at[g, 1]), rows)
        links.send((2, g), SECOND, got0.at[g, far], got2.at[g])

    def stage3(g):
        links.landed((2, g), got2.at[g])
        add_rows(kv_sum.at[g], (got0.at[g, chip], got1.at[g, 0], got2.at[g]), rows)

    for g in range(parts.shape[1]):
        for i, fn in enumerate((start, stage1, stage2, stage3)):
            stages[i, g] = functools.partial(fn, g)
    stages["drain"] = links.drain
    return stages


def back_kernel(
    sizes, n, fsdp, plans, deal_ref, lengths_ref, q_ref, kv_in, do_ref, delta_ref, lse_ref,
    x_ref, n1_ref, gr_ref, gains_ref, gain_two_ref, cos_ref, sin_ref, attn_ref, out_grad_ref, ff_grad, down_grad,
    tg_ref, gain_out, attn_out, ff_out, down_out,
    start_ref, spill_ref, chunk_ref, dqt_ref, dq_ref, dkv_ref, kv_sum, kv_got0, kv_got1, kv_got2, gp_ref, gn_ref, turned_ref, attn_grad,
    ff_a, down_a, attn_0, ff_0, down_0, attn_1, ff_1, down_1, attn_2, ff_2, down_2, attn_3, ff_3, down_3,
    gain_sum, gain_got, gain_z, send, recv, kv_send, kv_recv, local, ahead_sem,
):
    heads, kvh, block = sizes
    share = heads // kvh
    me = lax.axis_index("ctx")
    width = x_ref.shape[1]
    rows = x_ref.shape[0]
    greet("z", fsdp)
    sources = {ATTN: attn_grad, FF: ff_grad, DOWN: down_grad}
    held = {FF: ff_a, DOWN: down_a}
    got = {ATTN: (attn_0, attn_1, attn_2, attn_3), FF: (ff_0, ff_1, ff_2, ff_3), DOWN: (down_0, down_1, down_2, down_3)}
    outs = {ATTN: attn_out, FF: ff_out, DOWN: down_out}
    run = both_cores(
        lambda core: grad_stages(
            core, fsdp, plans[0], sources, held, got, outs, (gain_sum, gain_got, gain_z, gain_out), send, recv, local
        )
    )
    run_kv = both_cores(
        lambda core: kv_grad_stages(core, plans[1], dkv_ref, kv_sum, kv_got0, kv_got1, kv_got2, kv_send, kv_recv)
    )
    start_ref[...] = first_keys(n, deal_ref, lengths_ref, block, start_ref.shape[1])
    order = [d for d in range(1, fsdp)] + [0]
    chunks = [(k, d) for k in (FF, DOWN) for d in order]
    steps = []
    for i in range(len(chunks) + 7):
        names = []
        if i + 1 < len(chunks):
            names.append(("begin",) + chunks[i + 1])
        if i < len(chunks):
            names.append(("stage1",) + chunks[i])
        if 1 <= i <= len(chunks):
            names.append(("stage2",) + chunks[i - 1])
        if 2 <= i <= len(chunks) + 1:
            names.append(("stage3",) + chunks[i - 2])
        for last, k in ((len(order) + 1, FF), (len(chunks) + 1, DOWN)):
            for extra, what in enumerate(("close", "close2", "close3", "close4")):
                if i == last + 1 + extra:
                    names.append((what, k))
        steps.append(names)
    run(("begin",) + chunks[0])
    width_tiles = -(-(heads + 2 * kvh) // 2)
    ahead = [
        pltpu.make_async_copy(out_grad_ref.at[0], spill_ref, ahead_sem.at[0]),
        pltpu.make_async_copy(
            out_grad_ref.at[pl.ds(1, attn_grad.shape[0] - width_tiles)],
            attn_grad.at[pl.ds(width_tiles, attn_grad.shape[0] - width_tiles)], ahead_sem.at[1],
        ),
    ]
    wide = 2 * LANES

    def weight_rows(i):
        size = min(wide, width - i * wide)
        return pltpu.make_async_copy(
            attn_ref.at[pl.ds(0, width_tiles), pl.ds(i * wide, size)],
            chunk_ref.at[i % 2, :, pl.ds(0, size)], ahead_sem.at[2 + i % 2],
        )

    for copy in ahead + [weight_rows(0), weight_rows(1)]:
        copy.start()
    total = kvh * n
    pace = 12
    kv_due = sorted((8 * (i + 1) + (0, 3, 11, 19)[stage], stage, i) for i in range(kvh) for stage in range(4))

    @pl.loop(0, total)
    def _(step):
        g, j = step // n, step % n
        for i, names in enumerate(steps):
            if i * pace < total:
                pl.when(step == i * pace)(functools.partial(run, *names))
        for due, stage, i in kv_due:
            if due < total:
                pl.when(step == due)(functools.partial(run_kv, (stage, i)))
        own, other = attend_back_step(
            n, me, g, j, deal_ref, start_ref, q_ref, kv_in, do_ref, lse_ref, delta_ref, dqt_ref, dkv_ref
        )
        pl.when(j == 0)(own)
        pl.when(j > 0)(other)

        @pl.when(j == n - 1)
        def _():
            dq_ref[g] = jnp.concatenate([(dqt_ref[b] * 0.125).T[:, :HD] for b in range(2)], axis=1)

    cos, sin = cos_ref[...], -sin_ref[...]

    def head(index):
        if index < heads:
            return jnp.concatenate(
                [
                    dq_ref[index // share, (index % share) * block : (index % share + 1) * block, b * HD : (b + 1) * HD]
                    for b in range(2)
                ],
                axis=0,
            )
        g = index - heads
        low = 0 if g < kvh else HD
        return jnp.concatenate([kv_sum[g % kvh, b, :, low : low + HD] for b in range(2)], axis=0)

    count = heads + 2 * kvh
    tiles = -(-count // 2)
    turned_ref[...] = n1_ref[...].T

    def some_tiles(low, high):
        for t in range(low, high):
            right = head(2 * t + 1) if 2 * t + 1 < count else jnp.zeros((rows, HD), F32)
            pair = jnp.concatenate([head(2 * t), right], axis=1)
            if 2 * t < heads + kvh:
                pair = rope_tile(pair, cos, sin)
            gp_ref[:, t * LANES : (t + 1) * LANES] = pair.astype(BF16)
        for t in range(low, high, 2):
            some = min(2, high - t)
            part = nn(turned_ref[...], gp_ref[:, t * LANES : (t + some) * LANES]).astype(BF16)
            for i in range(some):
                tile = part[:, i * LANES : (i + 1) * LANES]
                attn_grad[t + i] = tile + spill_ref[...] if t + i == tiles - 1 else tile

    rest = [names for i, names in enumerate(steps) if i * pace >= total]
    late = [(stage, i) for due, stage, i in kv_due if due >= total]
    run_kv(late[0])
    some_tiles(0, heads // 2)
    for copy in ahead:
        copy.wait()
    run_kv(*[key for key in late[1:] if key[0] < 2 or key[1] < kvh - 1])
    run(*rest[0])
    run_kv(*[key for key in late[1:] if key[0] >= 2 and key[1] == kvh - 1])
    some_tiles(heads // 2, tiles)
    run(("begin", ATTN, order[0]), ("begin", ATTN, order[1]), ("stage1", ATTN, order[0]), *rest[1])
    for i in range(-(-width // wide)):
        size = min(wide, width - i * wide)
        weight_rows(i).wait()
        rows_in = jnp.concatenate([chunk_ref[i % 2, t, 0:size, :] for t in range(tiles)], axis=1)
        gn_ref[:, i * wide : i * wide + size] = nt(gp_ref[...], rows_in)
        if (i + 2) * wide < width:
            weight_rows(i + 2).start()
    x = x_ref[...].astype(F32)
    inverse = rms_inverse(x)
    scaled = x * inverse
    grad_normed = gn_ref[...]
    weighted = grad_normed * gain_row(gains_ref, 0, fsdp, width // fsdp)
    gain_one = jnp.sum(grad_normed * scaled, axis=0, keepdims=True)
    gain_two = gain_two_ref[0:1, :]
    shard = width // fsdp
    tail = gain_sum.shape[3] - shard
    for i in range(fsdp):
        both = jnp.concatenate(
            [gain_one[:, i * shard : (i + 1) * shard], gain_two[:, i * shard : (i + 1) * shard]], axis=0
        )
        both = jnp.concatenate([both, jnp.zeros((2, tail), F32)], axis=1)
        gain_sum[0, i] = jnp.concatenate([both, jnp.zeros((6, gain_sum.shape[3]), F32)], axis=0)
    run(("gain", 0))
    tg_ref[...] = (
        gr_ref[...] + inverse * (weighted - scaled * jnp.mean(weighted * scaled, axis=1, keepdims=True))
    ).astype(BF16)
    chunk2 = [(ATTN, d) for d in order]
    for i in range(1, len(chunk2) + 2):
        names = []
        if i + 1 < len(chunk2):
            names.append(("begin",) + chunk2[i + 1])
        if i < len(chunk2):
            names.append(("stage1",) + chunk2[i])
        if i <= len(chunk2):
            names.append(("stage2",) + chunk2[i - 1])
        if i >= 2:
            names.append(("stage3",) + chunk2[i - 2])
        if i <= 3:
            names.append(("gain", i))
        if i + 1 < len(rest):
            names += rest[i + 1]
        run(*names)
    for i, what in enumerate(("close", "close2", "close3", "close4")):
        names = rest[len(chunk2) + 3 + i] if len(chunk2) + 3 + i < len(rest) else []
        run((what, ATTN), *names)
    for names in rest[len(chunk2) + 7 :]:
        run(*names)
    run("gain close", "drain")
    run_kv("drain")


def whole(shape, dtype):
    return jax.ShapeDtypeStruct(shape, dtype)


def params(ident=None):
    extra = {} if ident is None else {"collective_id": ident, "has_side_effects": True}
    return pltpu.CompilerParams(vmem_limit_bytes=VMEM_LIMIT, **extra)


SMEM = pl.BlockSpec(memory_space=pltpu.SMEM)
VMEM = pl.BlockSpec(memory_space=pltpu.VMEM)
ANY = pl.BlockSpec(memory_space=pl.ANY)


def finish_kernel(
    heads, deal_ref, result_ref, tokens_ref, attn_ref, ff_ref, down_ref,
    out_ref, tg_ref, q_ref, kt_ref, vt_ref, o_ref, gate_ref, up_ref, dt_ref,
):
    me = lax.axis_index("ctx")
    flip = deal_ref[2 * me] > deal_ref[2 * me + 1]
    out_ref[...] = ordered(flip, result_ref[...]).T
    tg_ref[...] = ordered(flip, tokens_ref[...]).T
    width, kv_width = q_ref.shape[1], kt_ref.shape[0]
    half = width % LANES
    full = width // LANES

    def tile(t):
        return attn_ref[t].astype(F32)

    for t in range(full):
        q_ref[:, t * LANES : (t + 1) * LANES] = tile(t)
    q_ref[:, full * LANES :] = tile(full)[:, :half]
    kt_ref[0 : LANES - half, :] = tile(full).T[half:, :]
    at = LANES - half
    for t in range(full + 1, (width + kv_width) // LANES):
        kt_ref[at : at + LANES, :] = tile(t).T
        at += LANES
    first = (width + kv_width) // LANES
    spill = (width + 2 * kv_width) // LANES
    for i in range(spill - first):
        vt_ref[i * LANES : (i + 1) * LANES, :] = tile(first + i).T
    vt_ref[(spill - first) * LANES :, :] = tile(spill).T[: kv_width % LANES, :]
    for i in range(full):
        o_ref[:, i * LANES : (i + 1) * LANES] = tile(spill + 1 + i)
    o_ref[:, full * LANES :] = tile(spill)[:, LANES - half :]
    for t in range(ff_ref.shape[1]):
        gate_ref[:, t * LANES : (t + 1) * LANES] = ff_ref[0, t].astype(F32)
        up_ref[:, t * LANES : (t + 1) * LANES] = ff_ref[1, t].astype(F32)
    for t in range(down_ref.shape[0]):
        high = min((t + 1) * LANES, dt_ref.shape[0])
        dt_ref[t * LANES : high, :] = down_ref[t].astype(F32).T[: high - t * LANES, :]


def cube_body(
    tokens, attn_gain, query_weight, key_weight, value_weight, out_weight, mlp_gain, gate_weight,
    up_weight, down_weight, cotangent, cont_lengths, block_deal,
):
    n, fsdp = lax.axis_size("ctx"), lax.axis_size("fsdp")
    me = lax.axis_index("ctx")
    row_count, width = tokens.shape[1:]
    kv_width = key_weight.shape[1]
    shard, hidden = gate_weight.shape
    down_shard = down_weight.shape[0]
    block = row_count // 2
    heads, kvh = width // HD, kv_width // HD
    share = heads // kvh
    stack = share * block
    sizes = (heads, kvh, block)
    half_turns = THETA ** (-2.0 * jnp.arange(HD // 2, dtype=F32) / HD)
    turns = jnp.tile(half_turns, (8, LANES // (HD // 2)))
    pad = -shard % LANES
    gains_in = jnp.pad(jnp.stack([attn_gain, mlp_gain]).astype(F32), ((0, 6), (0, pad)))
    gain_shape = (fsdp,) + gains_in.shape
    attn_tiles = (2 * width + 2 * kv_width) // LANES
    ff_tiles = hidden // LANES
    down_tiles = -(-width // LANES)
    heads_shape = (kvh, 2, stack, LANES)
    row_shape = (kvh, 2, 8, stack)
    kv_shape = (n, 2, kvh, block, LANES)
    dma = pltpu.SemaphoreType.DMA
    mixed = (width + 2 * kv_width) // LANES
    wide = 2 * LANES
    (
        x, cos, sin, normed_one, q, kv_all, lse, gains, w_attn,
        result, grad_resid, grad_heads, deltas, gain_two, out_grad, ff_grad, down_grad,
    ) = pl.pallas_call(
        functools.partial(front_kernel, sizes, n, fsdp, ({}, {})),
        out_shape=(
            whole((row_count, width), BF16),
            whole((row_count, LANES), F32),
            whole((row_count, LANES), F32),
            whole((row_count, width), BF16),
            whole(heads_shape, BF16),
            whole(kv_shape, BF16),
            whole(row_shape, F32),
            whole(gain_shape, F32),
            whole((attn_tiles, fsdp * shard, LANES), BF16),
            whole((row_count, width), BF16),
            whole((row_count, width), F32),
            whole(heads_shape, BF16),
            whole(row_shape, F32),
            whole((8, width), F32),
            whole((attn_tiles - mixed, width, LANES), BF16),
            whole((2, ff_tiles, width, LANES), BF16),
            whole((down_tiles, hidden, LANES), BF16),
        ),
        in_specs=[SMEM] * 2 + [VMEM] * 11,
        out_specs=(VMEM,) * 5 + (ANY, VMEM, VMEM, ANY) + (VMEM,) * 5 + (ANY,) * 3,
        scratch_shapes=[
            pltpu.VMEM((attn_tiles, fsdp * shard, LANES), BF16),
            pltpu.VMEM((2, ff_tiles, fsdp * shard, LANES), BF16),
            pltpu.VMEM((down_tiles, fsdp * down_shard, LANES), BF16),
            pltpu.VMEM(kv_shape, BF16),
            pltpu.VMEM(heads_shape, F32),
            pltpu.VMEM(gain_shape, F32),
            pltpu.VMEM((8, stack), jnp.int32),
            pltpu.VMEM((2, 8, stack), F32),
            pltpu.VMEM((2, LANES, stack), F32),
            pltpu.VMEM((row_count, width), BF16),
            pltpu.VMEM((row_count, width), F32),
            pltpu.VMEM((row_count, width), BF16),
            pltpu.VMEM((row_count, hidden), BF16),
            pltpu.VMEM((row_count, hidden), BF16),
            pltpu.VMEM((row_count, hidden), BF16),
            pltpu.VMEM((width, row_count), BF16),
            pltpu.VMEM((row_count, width), F32),
            pltpu.VMEM((attn_tiles - mixed, width, LANES), BF16),
            pltpu.VMEM((2, 2, 2, width, LANES), BF16),
            pltpu.VMEM((2, down_tiles, wide, LANES), BF16),
            dma((75,)), dma((75,)), dma((14,)), dma((14,)), dma((2,)), dma((5,)),
        ],
        compiler_params=params(0),
        name="front",
    )(
        block_deal, cont_lengths, tokens[0].T, gains_in, turns,
        query_weight, key_weight.T, value_weight.T, out_weight, gate_weight, up_weight, down_weight.T,
        cotangent[0].T,
    )

    attn_rows = -(-shard // 32) * 16
    shapes = ((attn_tiles // 4, attn_rows, LANES), (ff_tiles // 4, shard, LANES), (down_shard, LANES))
    buffers = [pltpu.VMEM((fsdp, 4) + shape, BF16) for shape in shapes[1:]]
    for lead in ((fsdp, 4), (fsdp, 2), (fsdp,), (fsdp - 1,)):
        buffers += [pltpu.VMEM(lead + shape, BF16) for shape in shapes]
    qkv_tiles = -(-(width + 2 * kv_width) // LANES)
    piece = (2, block, LANES)
    tokens_grad, gain_grads, attn_w, ff_w, down_w = pl.pallas_call(
        functools.partial(back_kernel, sizes, n, fsdp, ({}, {})),
        out_shape=(
            whole((row_count, width), BF16),
            whole(gains_in.shape, F32),
            whole((attn_tiles, shard, LANES), BF16),
            whole((2, ff_tiles, shard, LANES), BF16),
            whole((down_tiles, down_shard, LANES), BF16),
        ),
        in_specs=[SMEM] * 2 + [VMEM] * 12 + [ANY] * 4,
        out_specs=(VMEM, VMEM, ANY, ANY, ANY),
        scratch_shapes=[
            pltpu.VMEM((8, stack), jnp.int32),
            pltpu.VMEM((width, LANES), BF16),
            pltpu.VMEM((2, qkv_tiles, 2 * LANES, LANES), BF16),
            pltpu.VMEM((2, LANES, stack), F32),
            pltpu.VMEM((kvh, stack, LANES), F32),
            pltpu.VMEM((n, kvh) + piece, BF16),
            pltpu.VMEM((kvh,) + piece, F32),
            pltpu.VMEM((kvh, 4) + piece, BF16),
            pltpu.VMEM((kvh, 2) + piece, BF16),
            pltpu.VMEM((kvh,) + piece, BF16),
            pltpu.VMEM((row_count, qkv_tiles * LANES), BF16),
            pltpu.VMEM((row_count, width), F32),
            pltpu.VMEM((width, row_count), BF16),
            pltpu.VMEM((attn_tiles, width, LANES), BF16),
        ]
        + buffers
        + [
            pltpu.VMEM((4,) + gain_shape, F32),
            pltpu.VMEM((3,) + gain_shape, F32),
            pltpu.VMEM((fsdp - 1,) + gains_in.shape, F32),
            dma((120,)), dma((120,)), dma((7 * kvh,)), dma((7 * kvh,)), dma((51,)), dma((4,)),
        ],
        compiler_params=params(1),
        name="back",
    )(
        block_deal, cont_lengths, q, kv_all, grad_heads, deltas, lse, x, normed_one, grad_resid, gains, gain_two,
        cos, sin, w_attn, out_grad, ff_grad, down_grad,
    )

    out_t, tg_t, q_w, k_t, v_t, o_w, gate_w, up_w, d_t = pl.pallas_call(
        functools.partial(finish_kernel, heads),
        out_shape=(
            whole((width, row_count), BF16),
            whole((width, row_count), BF16),
            whole((shard, width), F32),
            whole((kv_width, shard), F32),
            whole((kv_width, shard), F32),
            whole((shard, width), F32),
            whole((shard, hidden), F32),
            whole((shard, hidden), F32),
            whole((width, down_shard), F32),
        ),
        in_specs=[SMEM] + [VMEM] * 5,
        out_specs=(VMEM,) * 9,
        compiler_params=params(),
        name="finish",
    )(block_deal, result, tokens_grad, attn_w, ff_w, down_w)
    return (
        out_t.T[None],
        tg_t.T[None],
        gain_grads[0, :shard],
        q_w,
        k_t.T,
        v_t.T,
        o_w,
        gain_grads[1, :shard],
        gate_w,
        up_w,
        d_t.T,
    )


def head_of(tiles, index):
    start = (index % 2) * HD
    return tiles[index // 2][:, start : start + HD]


def project_kernel(sizes, x_ref, gain_ref, w_ref, cos_ref, sin_ref, n1_ref, q_ref, kv_ref):
    heads, kvh, block = sizes
    share = heads // kvh
    x = x_ref[...].astype(F32)
    inverse = lax.rsqrt(jnp.mean(x * x, axis=1, keepdims=True) + EPSILON)
    normed = (x * inverse * gain_ref[...]).astype(BF16)
    n1_ref[...] = normed
    width = (heads + 2 * kvh) * HD
    raw = nn(normed, w_ref[:, :width])
    cos = cos_ref[...]
    sin = sin_ref[...]
    tiles = []
    for j in range((heads + kvh) * HD // LANES):
        tiles.append(rope_tile(raw[:, j * LANES : (j + 1) * LANES], cos, sin).astype(BF16))
    zero = jnp.zeros((block, HD), BF16)
    for h in range(heads):
        piece = head_of(tiles, h) * jnp.asarray(0.125, BF16)
        g, i = h // share, h % share
        for b in range(2):
            q_ref[g, b, i * block : (i + 1) * block, :] = jnp.concatenate(
                [piece[b * block : (b + 1) * block], zero], axis=1
            )
    for g in range(kvh):
        start = (heads + kvh + g) * HD
        value = raw[:, start : start + HD].astype(BF16)
        pair = jnp.concatenate([head_of(tiles, heads + g), value], axis=1)
        for b in range(2):
            kv_ref[b, :, g * LANES : (g + 1) * LANES] = pair[b * block : (b + 1) * block]


def attend_kernel(
    n, me_ref, pick_ref, segq_ref, segk_ref, q_ref, kv_ref, o_ref, lse_ref, s1_ref, p1_ref, s2_ref, p2_ref
):
    me = me_ref[0]
    block = kv_ref.shape[2]
    rows = q_ref.shape[2]
    keys = n * block
    qc = q_ref[0, 1]
    prompt = kv_ref[:, 0].reshape(keys, LANES)
    s1_ref[...] = nt(qc, prompt)
    own = []
    for b in range(2):
        s2_ref[b] = nt(q_ref[0, b], kv_ref[me, b])
    for j in range(1, n):
        at = lax.rem(me + j, n)
        kind = pick_ref[j]
        s2_ref[j + 1] = nt(q_ref[0, kind], kv_ref[at, kind])
    step = 16
    kinds = [pick_ref[j] == 0 for j in range(n)]

    def fold(s):
        return jnp.maximum(
            s[:, :LANES],
            jnp.concatenate(
                [s[:, LANES:], jnp.full((step, 2 * LANES - block), MASKED, F32)], axis=1
            ),
        )

    def chunk(at, carry):
        r = pl.multiple_of(at * step, step)
        rs = pl.ds(r, step)
        in_block = lax.rem(r, block)
        tri = lax.broadcasted_iota(jnp.int32, (step, block), 1) <= (
            in_block + lax.broadcasted_iota(jnp.int32, (step, block), 0)
        )
        segq = segq_ref[rs, :]
        s1 = s1_ref[rs, :]
        top_c = s1[:, :LANES]
        for t in range(1, keys // LANES):
            top_c = jnp.maximum(top_c, s1[:, t * LANES : (t + 1) * LANES])
        dp = jnp.where(tri, s2_ref[0, rs, :], MASKED)
        dc = jnp.where(tri & (segq == segk_ref[0]), s2_ref[1, rs, :], MASKED)
        top_c = jnp.maximum(top_c, fold(dc))
        top_p = fold(dp)
        others = []
        for j in range(1, n):
            s = jnp.where((segq == segk_ref[j]) | kinds[j], s2_ref[j + 1, rs, :], MASKED)
            others.append(s)
            f = fold(s)
            top_p = jnp.maximum(top_p, jnp.where(kinds[j], f, MASKED))
            top_c = jnp.maximum(top_c, jnp.where(kinds[j], MASKED, f))
        m_p = jnp.max(top_p, axis=1, keepdims=True)
        m_c = jnp.max(top_c, axis=1, keepdims=True)
        p1_ref[rs, :] = jnp.exp2((s1 - m_c) * LOG2E).astype(BF16)
        p2_ref[0, rs, :] = jnp.exp2((dp - m_p) * LOG2E).astype(BF16)
        p2_ref[1, rs, :] = jnp.exp2((dc - m_c) * LOG2E).astype(BF16)
        for j in range(1, n):
            m = jnp.where(kinds[j], m_p, m_c)
            p2_ref[j + 1, rs, :] = jnp.exp2((others[j - 1] - m) * LOG2E).astype(BF16)
        lse_ref[0, 0, rs, :] = jnp.broadcast_to(m_p * LOG2E, (step, LANES))
        lse_ref[0, 1, rs, :] = jnp.broadcast_to(m_c * LOG2E, (step, LANES))
        return carry

    lax.fori_loop(0, rows // step, chunk, 0)

    def with_ones(tile):
        return jnp.concatenate([tile, jnp.ones(tile.shape, BF16)], axis=1)

    acc = [nn(p2_ref[b], with_ones(kv_ref[me, b])) for b in range(2)]
    acc[1] = acc[1] + nn(p1_ref[...], with_ones(prompt))
    for j in range(1, n):
        at = lax.rem(me + j, n)
        part = nn(p2_ref[j + 1], with_ones(kv_ref[at, pick_ref[j]]))
        acc[0] = acc[0] + jnp.where(kinds[j], part, 0.0)
        acc[1] = acc[1] + jnp.where(kinds[j], 0.0, part)
    for b in range(2):
        total = acc[b][:, LANES:]
        o_ref[0, b] = acc[b][:, :LANES] / total
        lse_ref[0, b] = lse_ref[0, b] + jnp.log2(total)


def attend_back_kernel(
    n, me_ref, pick_ref, segq_ref, segk_ref, q_ref, kv_ref, do_ref, o_ref, lse_ref, dq_ref, dkv_ref, row_ref, dqt_ref
):
    me = me_ref[0]
    block = kv_ref.shape[2]
    rows = q_ref.shape[2]
    first = (lax.broadcasted_iota(jnp.int32, (8, LANES), 1) == 0).astype(F32)
    ones = jnp.ones((8, LANES), F32)

    def to_row(lhs, matrix):
        return lax.dot_general(
            lhs, matrix, (((1,), (1,)), ((), ())), precision=lax.Precision.HIGHEST,
            preferred_element_type=F32,
        )

    for b in range(2):
        row_ref[b] = to_row(first, lse_ref[0, b])
        row_ref[2 + b] = to_row(ones, do_ref[0, b].astype(F32) * o_ref[0, b])
    lane_rows = lax.rem(lax.broadcasted_iota(jnp.int32, (block, rows), 1), block)
    tri = lax.broadcasted_iota(jnp.int32, (block, rows), 0) <= lane_rows

    def pair(kind, tile, mask):
        q = q_ref[0, kind]
        do = do_ref[0, kind]
        p = jnp.exp2(nt(tile, q) * LOG2E - row_ref[kind, 0:1, :])
        if mask is not None:
            p = jnp.where(mask, p, 0.0)
        ds = (p * (nt(tile, do) - row_ref[2 + kind, 0:1, :])).astype(BF16)
        return nn(ds, q) + nn(p.astype(BF16), do), tn(tile, ds)

    segq = segq_ref[0:1, :]
    same_own = segq == segk_ref[0]
    own0, own1 = kv_ref[me, 0], kv_ref[me, 1]
    d0, q0 = pair(0, own0, tri)
    d1, q1 = pair(1, own1, tri & same_own)
    d2, q2 = pair(1, own0, None)
    dkv_ref[me, 0] = (d0 + d2).astype(dkv_ref.dtype)
    dkv_ref[me, 1] = d1.astype(dkv_ref.dtype)
    dqt_ref[0] = q0
    dqt_ref[1] = q1 + q2

    def other(j, carry):
        at = lax.rem(me + j, n)
        kind = pick_ref[j]
        is_prompt = kind == 0
        full, q_full = pair(1, kv_ref[at, 0], None)
        mask = (segq == segk_ref[j]) | is_prompt
        part, q_part = pair(kind, kv_ref[at, kind], mask)
        dkv_ref[at, 0] = (full + jnp.where(is_prompt, part, 0.0)).astype(dkv_ref.dtype)
        dkv_ref[at, 1] = jnp.where(is_prompt, 0.0, part).astype(dkv_ref.dtype)
        dqt_ref[0] = dqt_ref[0] + jnp.where(is_prompt, q_part, 0.0)
        dqt_ref[1] = dqt_ref[1] + q_full + jnp.where(is_prompt, 0.0, q_part)
        return carry

    lax.fori_loop(1, n, other, 0)
    for b in range(2):
        dq_ref[0, b] = (dqt_ref[b] * 0.125).T


def mid_kernel(sizes, o_ref, x_ref, wo_ref, gain_ref, att_ref, resid_ref, n2_ref):
    heads, kvh, block = sizes
    share = heads // kvh
    for b in range(2):
        columns = []
        for h in range(heads):
            g, i = h // share, h % share
            columns.append(o_ref[g, b, i * block : (i + 1) * block, HD:])
        attended = jnp.concatenate(columns, axis=1).astype(BF16)
        rs = slice(b * block, (b + 1) * block)
        att_ref[rs, :] = attended
        resid = x_ref[rs, :].astype(F32) + nn(attended, wo_ref[...])
        resid_ref[rs, :] = resid
        inverse = lax.rsqrt(jnp.mean(resid * resid, axis=1, keepdims=True) + EPSILON)
        n2_ref[rs, :] = (resid * inverse * gain_ref[...]).astype(BF16)


def branch_kernel(sizes, gb_ref, wo_ref, do_ref):
    heads, kvh, block = sizes
    share = heads // kvh
    grad = nt(gb_ref[...], wo_ref[...]).astype(BF16)
    zero = jnp.zeros((block, HD), BF16)
    for h in range(heads):
        g, i = h // share, h % share
        for b in range(2):
            do_ref[g, b, i * block : (i + 1) * block, :] = jnp.concatenate(
                [zero, grad[b * block : (b + 1) * block, h * HD : (h + 1) * HD]], axis=1
            )


def unrope_kernel(sizes, dq_ref, dkv_ref, cos_ref, sin_ref, out_ref):
    heads, kvh, block = sizes
    share = heads // kvh
    for b in range(2):
        rs = slice(b * block, (b + 1) * block)
        cos, sin = cos_ref[rs, :], -sin_ref[rs, :]
        columns = [
            dq_ref[h // share, b, (h % share) * block : (h % share + 1) * block, :HD]
            for h in range(heads)
        ]
        columns += [dkv_ref[b, :, g * LANES : g * LANES + HD].astype(F32) for g in range(kvh)]
        tiles = []
        for j in range((heads + kvh) // 2):
            pair = jnp.concatenate(columns[2 * j : 2 * j + 2], axis=1)
            tiles.append(rope_tile(pair, cos, sin).astype(BF16))
        values = [dkv_ref[b, :, g * LANES + HD : (g + 1) * LANES].astype(BF16) for g in range(kvh)]
        out_ref[rs, :] = jnp.concatenate(tiles + values, axis=1)


def local_call(kernel, out_shape, name, **extra):
    return pl.pallas_call(
        kernel,
        out_shape=out_shape,
        compiler_params=pltpu.CompilerParams(vmem_limit_bytes=VMEM_LIMIT),
        name=name,
        **extra,
    )


def gather_rows(array, axis):
    return lax.all_gather(array, axis, axis=0, tiled=True)


def norm_back(grad_normed, scaled, inverse, gain):
    weighted = grad_normed * gain
    return inverse * (weighted - scaled * jnp.mean(weighted * scaled, axis=1, keepdims=True))


def general_body(
    tokens, attn_gain, query_weight, key_weight, value_weight, out_weight, mlp_gain, gate_weight,
    up_weight, down_weight, cotangent, cont_lengths, block_deal,
):
    n = lax.axis_size("ctx")
    me = lax.axis_index("ctx")
    row_count, width = tokens.shape[1:]
    kv_width = key_weight.shape[1]
    hidden = gate_weight.shape[1]
    block = row_count // 2
    total_rows = row_count * n
    prompt_size = total_rows // 2
    heads, kvh = width // HD, kv_width // HD
    share = heads // kvh
    stack = share * block
    sizes = (heads, kvh, block)

    deal = block_deal.reshape(n, 2)
    flip = deal[me, 0] > deal[me, 1]

    def ordered(rows):
        halves = rows.reshape(2, block, rows.shape[-1])
        return jnp.where(flip, halves[::-1], halves).reshape(rows.shape)

    x = ordered(tokens[0])
    cot = ordered(cotangent[0])
    naturals = jnp.sort(deal, axis=1)
    natural = naturals[:, :, None] * block + jnp.arange(block, dtype=jnp.int32)
    offset = natural - prompt_size
    lengths = cont_lengths[0]
    ending = jnp.cumsum(lengths)
    segment = jnp.sum((offset[..., None] >= ending).astype(jnp.int32), axis=-1)
    inside = segment[..., None] == jnp.arange(lengths.shape[0], dtype=jnp.int32)
    beginning = jnp.sum(jnp.where(inside, ending - lengths, 0), axis=-1)
    position = jnp.where(offset < 0, natural, prompt_size + offset - beginning)
    own_position = position[me].reshape(row_count)
    frequency = THETA ** (-2.0 * jnp.arange(HD // 2, dtype=F32) / HD)
    angle = own_position.astype(F32)[:, None] * frequency[None, :]
    cos, sin = jnp.cos(angle), jnp.sin(angle)
    cos = jnp.concatenate([cos, cos, cos, cos], axis=1)
    sin = jnp.concatenate([-sin, sin, -sin, sin], axis=1)
    around = (me + jnp.arange(n, dtype=jnp.int32)) % n
    first_natural = naturals[:, 0]
    pick = (first_natural[around] >= first_natural[me]).astype(jnp.int32)
    segk = segment[around, 1]
    segq = jnp.tile(segment[me, 1], share)
    me_arr = me.reshape(1).astype(jnp.int32)

    attn_rows = jnp.concatenate([query_weight, key_weight, value_weight, out_weight], axis=1)
    w_attn = gather_rows(attn_rows, "fsdp")
    qkv_width = width + 2 * kv_width
    w_qkv = w_attn[:, :qkv_width]
    w_out = w_attn[:, qkv_width:]
    gain_one = gather_rows(attn_gain, "fsdp").astype(F32)
    gain_two = gather_rows(mlp_gain, "fsdp").astype(F32)
    w_gate = gather_rows(gate_weight, "fsdp")
    w_up = gather_rows(up_weight, "fsdp")
    w_down = gather_rows(down_weight, "fsdp")

    normed_one, q, kv = local_call(
        functools.partial(project_kernel, sizes),
        (
            whole((row_count, width), BF16),
            whole((kvh, 2, stack, LANES), BF16),
            whole((2, block, kvh * LANES), BF16),
        ),
        "project",
    )(x, gain_one[None], w_attn, cos, sin)
    kv_all = lax.all_gather(kv, "ctx", axis=0)

    smem = pl.BlockSpec(memory_space=pltpu.SMEM)
    per_group = pl.BlockSpec((1, 2, stack, LANES), lambda g: (g, 0, 0, 0))
    kv_spec = pl.BlockSpec((n, 2, block, LANES), lambda g: (0, 0, 0, g))

    def full(array):
        rank = array.ndim
        return pl.BlockSpec(array.shape, lambda g: (0,) * rank)

    segq_col, segk_row = segq[:, None], segk[:, None, :]
    attended_heads, lse = local_call(
        functools.partial(attend_kernel, n),
        (whole((kvh, 2, stack, LANES), F32), whole((kvh, 2, stack, LANES), F32)),
        "attend",
        grid=(kvh,),
        in_specs=[smem, smem, full(segq_col), full(segk_row), per_group, kv_spec],
        out_specs=(per_group, per_group),
        scratch_shapes=[
            pltpu.VMEM((stack, n * block), F32),
            pltpu.VMEM((stack, n * block), BF16),
            pltpu.VMEM((n + 1, stack, block), F32),
            pltpu.VMEM((n + 1, stack, block), BF16),
        ],
    )(me_arr, pick, segq_col, segk_row, q, kv_all)

    attended, resid, normed_two = local_call(
        functools.partial(mid_kernel, sizes),
        (
            whole((row_count, width), BF16),
            whole((row_count, width), F32),
            whole((row_count, width), BF16),
        ),
        "mid",
    )(attended_heads, x, w_out, gain_two[None])

    inverse_two = lax.rsqrt(jnp.mean(resid * resid, axis=1, keepdims=True) + EPSILON)
    scaled_two = resid * inverse_two
    gate = nn(normed_two, w_gate)
    upward = nn(normed_two, w_up)
    sigma = jax.nn.sigmoid(gate)
    activated = gate * sigma
    product = (activated * upward).astype(BF16)
    result = resid + nn(product, w_down)
    grad_prod = nt(cot, w_down)
    grad_gate = (grad_prod * upward * sigma * (1.0 + gate * (1.0 - sigma))).astype(BF16)
    grad_up = (grad_prod * activated).astype(BF16)
    grad_normed_two = nt(grad_gate, w_gate) + nt(grad_up, w_up)
    gain_two_part = jnp.sum(grad_normed_two * scaled_two, axis=0)
    grad_resid = cot.astype(F32) + norm_back(grad_normed_two, scaled_two, inverse_two, gain_two)
    grad_branch = grad_resid.astype(BF16)

    grad_heads = local_call(
        functools.partial(branch_kernel, sizes), whole((kvh, 2, stack, LANES), BF16), "branch"
    )(grad_branch, w_out)

    segq_row, segk_col = segq[None, :], segk[:, :, None]
    grad_query, grad_kv = local_call(
        functools.partial(attend_back_kernel, n),
        (whole((kvh, 2, stack, LANES), F32), whole((n, 2, block, kvh * LANES), F32)),
        "attend_back",
        grid=(kvh,),
        in_specs=[smem, smem, full(segq_row), full(segk_col)]
        + [per_group, kv_spec, per_group, per_group, per_group],
        out_specs=(per_group, kv_spec),
        scratch_shapes=[
            pltpu.VMEM((4, 8, stack), F32),
            pltpu.VMEM((2, LANES, stack), F32),
        ],
    )(me_arr, pick, segq_row, segk_col, q, kv_all, grad_heads, attended_heads, lse)

    kv_sum = lax.psum_scatter(grad_kv, "ctx", scatter_dimension=0, tiled=False)
    grad_projected = local_call(
        functools.partial(unrope_kernel, sizes), whole((row_count, qkv_width), BF16), "unrope"
    )(grad_query, kv_sum, cos, sin)

    x_float = x.astype(F32)
    inverse_one = lax.rsqrt(jnp.mean(x_float * x_float, axis=1, keepdims=True) + EPSILON)
    scaled_one = x_float * inverse_one
    grad_normed_one = nt(grad_projected, w_qkv)
    gain_one_part = jnp.sum(grad_normed_one * scaled_one, axis=0)
    tokens_grad = (
        grad_resid + norm_back(grad_normed_one, scaled_one, inverse_one, gain_one)
    ).astype(BF16)

    def spread(partial):
        rows = lax.psum_scatter(partial.astype(BF16), "fsdp", scatter_dimension=0, tiled=True)
        return lax.psum(rows, "ctx").astype(F32)

    grad_gate_w = spread(tn(normed_two, grad_gate))
    grad_up_w = spread(tn(normed_two, grad_up))
    grad_down_w = spread(tn(product, cot))
    grad_out_w = spread(tn(attended, grad_branch))
    grad_qkv_w = spread(tn(normed_one, grad_projected))
    gains = spread(jnp.stack([gain_one_part, gain_two_part], axis=1))
    return (
        ordered(result.astype(BF16))[None],
        ordered(tokens_grad)[None],
        gains[:, 0],
        grad_qkv_w[:, :width],
        grad_qkv_w[:, width : width + kv_width],
        grad_qkv_w[:, width + kv_width :],
        grad_out_w,
        gains[:, 1],
        grad_gate_w,
        grad_up_w,
        grad_down_w,
    )


def solution(mesh):
    rows, matrix, vector = P("fsdp", "ctx", None), P("fsdp", None), P("fsdp")
    cube = dict(mesh.shape) == {"ctx": 8, "fsdp": 4}
    return jax.shard_map(
        cube_body if cube else general_body,
        mesh=mesh,
        in_specs=(rows, vector, matrix, matrix, matrix, matrix, vector, matrix, matrix, matrix)
        + (rows, matrix, P()),
        out_specs=(rows, rows, vector, matrix, matrix, matrix, matrix, vector, matrix, matrix, matrix),
        check_vma=False,
    )
```

```python
import functools

import jax
import jax.numpy as jnp
from jax import lax
from jax.experimental import pallas as pl
from jax.experimental.pallas import tpu as pltpu
from jax.sharding import PartitionSpec as P

HD = 64
LANES = 128
EPSILON = 1e-05
THETA = 100000.0
MASKED = -1e30
LOG2E = 1.4426950408889634
VMEM_LIMIT = 63 * 1024 * 1024
F32 = jnp.float32
BF16 = jnp.bfloat16


def nt(left, right):
    return lax.dot_general(left, right, (((1,), (1,)), ((), ())), preferred_element_type=F32)


def nn(left, right):
    return lax.dot_general(left, right, (((1,), (0,)), ((), ())), preferred_element_type=F32)


def tn(left, right):
    return lax.dot_general(left, right, (((0,), (0,)), ((), ())), preferred_element_type=F32)


def rope_tile(tile, cos, sin):
    lane = lax.broadcasted_iota(jnp.int32, tile.shape, 1) % HD
    partner = jnp.where(
        lane < HD // 2,
        pltpu.roll(tile, LANES - HD // 2, 1),
        pltpu.roll(tile, HD // 2, 1),
    )
    return tile * cos + partner * sin


def head_of(tiles, index):
    start = (index % 2) * HD
    return tiles[index // 2][:, start : start + HD]


MESH = pl.DeviceIdType.MESH
ATTN, FF, DOWN = 0, 1, 2
CORE, FIRST, SECOND = -1, -2, -3


class Links:
    def __init__(self, core, fsdp, send, recv, plan):
        self.core = core
        self.fsdp = fsdp
        self.ctx = lax.axis_index("ctx")
        self.z = lax.axis_index("fsdp")
        self.chip = self.ctx // 2
        self.first = 1 if core == 0 else 2
        self.second = 3 - self.first
        self.send_sem, self.recv_sem = send, recv
        self.plan = plan
        self.open = []

    def target(self, hop):
        if hop == CORE:
            return (lax.bitwise_xor(self.ctx, 1), self.z)
        if hop == FIRST:
            return (lax.bitwise_xor(self.ctx, 2 * self.first), self.z)
        if hop == SECOND:
            return (lax.bitwise_xor(self.ctx, 2 * self.second), self.z)
        return (self.ctx, lax.bitwise_xor(self.z, hop))

    def copy(self, key, hop, src, dst):
        slot = self.plan.setdefault(key, len(self.plan))
        return pltpu.make_async_remote_copy(
            src_ref=src,
            dst_ref=dst,
            send_sem=self.send_sem.at[slot],
            recv_sem=self.recv_sem.at[slot],
            device_id=self.target(hop),
            device_id_type=MESH,
        )

    def send(self, key, hop, src, dst):
        copy = self.copy(key, hop, src, dst)
        copy.start()
        self.open.append((key, getattr(src, "ref", src), src.shape))

    def landed(self, key, dst):
        self.copy(key, CORE, dst, dst).wait_recv()

    def drain(self):
        for key, base, shape in self.open:
            at = (0,) * (len(base.shape) - len(shape)) + tuple(pl.ds(0, size) for size in shape)
            self.copy(key, CORE, base.at[at], base.at[at]).wait_send()


def greet(hops, fsdp):
    ctx, z = lax.axis_index("ctx"), lax.axis_index("fsdp")
    barrier = pltpu.get_barrier_semaphore()
    targets = [(lax.bitwise_xor(ctx, h), z) for h in (1, 2, 4)]
    if "z" in hops:
        targets += [(ctx, lax.bitwise_xor(z, d)) for d in range(1, fsdp)]
    for target in targets:
        pl.semaphore_signal(barrier, inc=1, device_id=target, device_id_type=MESH)
    pl.semaphore_wait(barrier, len(targets))


def by_core(program):
    for core in (0, 1):
        pl.when(lax.axis_index("ctx") % 2 == core)(functools.partial(program, core))


def sub(base, size, unit):
    return pl.ds(pl.multiple_of(base, unit), size)


def lanes(ref, tiles, rows=slice(None)):
    return jnp.concatenate([ref[t, rows, :] for t in tiles], axis=1)


def flat_lanes(ref, tiles, shard):
    stacked = [
        jnp.concatenate([ref[zi, t * shard : (t + 1) * shard, :] for zi in range(ref.shape[0])], axis=0)
        for t in tiles
    ]
    return jnp.concatenate(stacked, axis=1)


def pack_tiles(parts):
    matrix = jnp.concatenate(parts, axis=1)
    short = -matrix.shape[1] % LANES
    if short:
        matrix = jnp.concatenate([matrix, jnp.zeros((matrix.shape[0], short), matrix.dtype)], axis=1)
    return [matrix[:, t * LANES : (t + 1) * LANES] for t in range(matrix.shape[1] // LANES)]


class Share:
    def __init__(self, name, core, shard):
        self.name, self.core = name, core
        self.shard = shard
        self.offset, self.rows = 0, shard
        if name == ATTN:
            half = -(-shard // 32) * 16
            self.offset, self.rows = (0, half) if core == 0 else (half, shard - half)

    def at(self, ref, zi, q):
        rows = sub(zi * self.shard + self.offset, self.rows, 16)
        if self.name == ATTN:
            return ref.at[pl.ds(q * (ref.shape[0] // 4), ref.shape[0] // 4), rows]
        if self.name == FF:
            return ref.at[self.core, pl.ds(q * (ref.shape[1] // 4), ref.shape[1] // 4), rows]
        return ref.at[2 * q + self.core, rows]

    def buffer(self, ref):
        return ref.at[:, pl.ds(0, self.rows)] if self.name == ATTN else ref


class Flat:
    def __init__(self, core):
        self.core = core

    def at(self, ref, zi, q):
        size = ref.shape[1] // 8
        return ref.at[zi, sub((2 * q + self.core) * size, size, 16)]


PACKAGES = (ATTN, FF, DOWN)
QKV, OUT = 3, 4
GATHERED = (QKV, OUT, FF, DOWN)
FINISH = 0


def both_cores(make):
    tables = [make(0), make(1)]

    def run(*names):
        for core in (0, 1):
            def program(core=core):
                for name in names:
                    tables[core][name]()

            pl.when(lax.axis_index("ctx") % 2 == core)(program)

    return run


def weight_stages(core, fsdp, plan, refs, send, recv):
    links = Links(core, fsdp, send, recv, plan)
    z, chip = links.z, links.chip
    near, far = lax.bitwise_xor(chip, links.first), lax.bitwise_xor(chip, links.second)
    corner = lax.bitwise_xor(chip, 3)
    shards = {FF: refs[FF].shape[2] // fsdp, DOWN: refs[DOWN].shape[1] // fsdp}

    def shares(core):
        cut = {k: Share(k, core, shards[k]) for k in shards}
        return {**cut, QKV: Flat(core), OUT: Flat(core)}

    mine, twin = shares(core), shares(1 - core)
    stages = {}

    def over_z(k):
        here = mine[k].at(refs[k], z, chip)
        for d in range(1, fsdp):
            links.send((k, "z", d), d, here, here)

    def spread(k):
        for d in range(1, fsdp):
            piece = mine[k].at(refs[k], lax.bitwise_xor(z, d), chip)
            links.landed((k, "z", d), piece)
            links.send((k, FIRST, d), FIRST, piece, piece)
            links.send((k, SECOND, d), SECOND, piece, piece)
            links.send((k, CORE, d, 0), CORE, piece, piece)

    def forward(k):
        for d in range(1, fsdp):
            piece = mine[k].at(refs[k], lax.bitwise_xor(z, d), near)
            links.landed((k, FIRST, d), piece)
            links.send((k, "corner", d), SECOND, piece, piece)
            links.send((k, CORE, d, 1), CORE, piece, piece)

    def pass_some(k, i, what, q):
        for d in range(1, fsdp):
            piece = mine[k].at(refs[k], lax.bitwise_xor(z, d), q)
            links.landed((k, what, d), piece)
            links.send((k, CORE, d, i), CORE, piece, piece)

    def pass_far(k):
        pass_some(k, 2, SECOND, far)

    def pass_corner(k):
        pass_some(k, 3, "corner", corner)

    def finish_some(k, i, q):
        for d in range(1, fsdp):
            links.landed((k, CORE, d, i), twin[k].at(refs[k], lax.bitwise_xor(z, d), q))

    def finish(k):
        for i in range(4):
            stages[FINISH, k, i]()

    for k in GATHERED:
        for i, q in ((0, chip), (1, far), (2, near), (3, corner)):
            stages[FINISH, k, i] = functools.partial(finish_some, k, i, q)
    for k in GATHERED:
        for fn in (over_z, spread, forward, pass_far, pass_corner, finish):
            stages[fn.__name__, k] = functools.partial(fn, k)

    def gains_out():
        for d in range(1, fsdp):
            links.send(("gains", d), d, refs["gains"].at[z], refs["gains"].at[z])

    def gains_in():
        for d in range(1, fsdp):
            links.landed(("gains", d), refs["gains"].at[lax.bitwise_xor(z, d)])

    stages["gains_out"], stages["gains_in"], stages["drain"] = gains_out, gains_in, links.drain
    return stages


def kv_stages(core, plan, kv_all, send, recv):
    links = Links(core, 1, send, recv, plan)
    ctx = links.ctx
    near = lax.bitwise_xor(ctx, 2 * links.first)
    far = lax.bitwise_xor(ctx, 2 * links.second)
    corner = lax.bitwise_xor(ctx, 6)

    def start():
        for b in range(2):
            piece = kv_all.at[ctx, b]
            links.send(("kv first", b), FIRST, piece, piece)
            links.send(("kv second", b), SECOND, piece, piece)
            links.send(("kv core", 0, b), CORE, piece, piece)

    def forward():
        for b in range(2):
            piece = kv_all.at[near, b]
            links.landed(("kv first", b), piece)
            links.send(("kv corner", b), SECOND, piece, piece)
            links.send(("kv core", 1, b), CORE, piece, piece)

    def pass_some(i, what, owner):
        for b in range(2):
            piece = kv_all.at[owner, b]
            links.landed((what, b), piece)
            links.send(("kv core", i, b), CORE, piece, piece)

    def finish(i, owner):
        for b in range(2):
            links.landed(("kv core", i, b), kv_all.at[lax.bitwise_xor(owner, 1), b])

    stages = {"start": start, "forward": forward, "drain": links.drain}
    stages["pass_far"] = functools.partial(pass_some, 2, "kv second", far)
    stages["pass_corner"] = functools.partial(pass_some, 3, "kv corner", corner)
    for i, owner in ((0, ctx), (1, far), (2, near), (3, corner)):
        stages[FINISH, i] = functools.partial(finish, i, owner)
    return stages


def store_projection(sizes, raw_tiles, cos, sin, q_ref, kv_at):
    heads, kvh, block = sizes
    share = heads // kvh
    tiles = [rope_tile(raw_tiles[j], cos, sin).astype(BF16) for j in range((heads + kvh) // 2)]
    tiles += [raw_tiles[j].astype(BF16) for j in range((heads + kvh) // 2, len(raw_tiles))]

    def head(index):
        start = (index % 2) * HD
        return tiles[index // 2][:, start : start + HD]

    zero = jnp.zeros((block, HD), BF16)
    for h in range(heads):
        piece = head(h) * jnp.asarray(0.125, BF16)
        g, i = h // share, h % share
        for b in range(2):
            q_ref[g, b, i * block : (i + 1) * block, :] = jnp.concatenate(
                [piece[b * block : (b + 1) * block], zero], axis=1
            )
    for g in range(kvh):
        pair = jnp.concatenate([head(heads + g), head(heads + kvh + g)], axis=1)
        for b in range(2):
            kv_at(b, g)[...] = pair[b * block : (b + 1) * block]


def rms_inverse(x):
    return lax.rsqrt(jnp.mean(x * x, axis=1, keepdims=True) + EPSILON)


def natural_blocks(deal_ref, c):
    one, two = deal_ref[2 * c], deal_ref[2 * c + 1]
    return jnp.minimum(one, two), jnp.maximum(one, two)


def segment_start(lengths_ref, offset):
    start = jnp.zeros_like(offset)
    ending = 0
    for c in range(lengths_ref.shape[1]):
        ending = ending + lengths_ref[0, c]
        start = jnp.where(offset >= ending, ending, start)
    return start


def ordered(flip, rows):
    half = rows.shape[0] // 2
    return jnp.where(flip, jnp.concatenate([rows[half:], rows[:half]], axis=0), rows)


def first_keys(n, deal_ref, lengths_ref, block, rows):
    _, last = natural_blocks(deal_ref, lax.axis_index("ctx"))
    offset = (last - n) * block + lax.rem(lax.broadcasted_iota(jnp.int32, (8, rows), 1), block)
    return segment_start(lengths_ref, offset)


def attend_masks(n, deal_ref, start_ref, block, rows):
    key = lax.broadcasted_iota(jnp.int32, (block, rows), 0)

    def own(b):
        allowed = key <= lax.rem(lax.broadcasted_iota(jnp.int32, (block, rows), 1), block)
        if b == 0:
            return allowed
        _, last = natural_blocks(deal_ref, lax.axis_index("ctx"))
        return allowed & (key >= start_ref[0:1, :] - (last - n) * block)

    def other(at):
        mine, _ = natural_blocks(deal_ref, lax.axis_index("ctx"))
        first, last = natural_blocks(deal_ref, at)
        kind = jnp.where(first >= mine, 1, 0)
        bound = jnp.where(kind == 0, -1, start_ref[0:1, :] - (last - n) * block)
        return kind, key >= bound

    return own, other


def attend_step(n, me, g, at, deal_ref, start_ref, q_ref, kv_ref, top_ref, acc_ref):
    block = kv_ref.shape[3]
    rows = q_ref.shape[2]
    value_lane = lax.broadcasted_iota(jnp.int32, (block, LANES), 1) >= HD
    own_mask, other_mask = attend_masks(n, deal_ref, start_ref, block, rows)

    def scores(kind, tile, mask):
        s = nt(tile, q_ref[g, kind])
        return s if mask is None else jnp.where(mask, s, MASKED)

    def weigh(s, top, tile):
        p = jnp.exp2((s - top) * LOG2E).astype(BF16)
        return tn(jnp.where(value_lane, tile, jnp.asarray(1, BF16)), p)

    def own():
        own0, own1 = kv_ref[me, 0, g], kv_ref[me, 1, g]
        s0 = scores(0, own0, own_mask(0))
        top0 = jnp.max(s0, axis=0, keepdims=True)
        acc_ref[g, 0] = weigh(s0, top0, own0)
        top_ref[g, 0] = jnp.broadcast_to(top0, top_ref.shape[2:])
        s1 = scores(1, own1, own_mask(1))
        s2 = scores(1, own0, None)
        top1 = jnp.maximum(jnp.max(s1, axis=0, keepdims=True), jnp.max(s2, axis=0, keepdims=True))
        acc_ref[g, 1] = weigh(s1, top1, own1) + weigh(s2, top1, own0)
        top_ref[g, 1] = jnp.broadcast_to(top1, top_ref.shape[2:])

    def other():
        kind, mask = other_mask(at)
        is_prompt = kind == 0
        tile0 = kv_ref[at, 0, g]
        tile1 = jnp.where(is_prompt, tile0, kv_ref[at, 1, g])
        s1 = scores(1, tile0, None)
        s2 = scores(kind, tile1, mask)
        old_p, old_c = top_ref[g, 0, 0:1, :], top_ref[g, 1, 0:1, :]
        high1 = jnp.max(s1, axis=0, keepdims=True)
        high2 = jnp.max(s2, axis=0, keepdims=True)
        top_p = jnp.where(is_prompt, jnp.maximum(old_p, high2), old_p)
        top_c = jnp.maximum(old_c, jnp.where(is_prompt, high1, jnp.maximum(high1, high2)))
        part1 = weigh(s1, top_c, tile0)
        part2 = weigh(s2, jnp.where(is_prompt, top_p, top_c), tile1)
        acc_ref[g, 0] = acc_ref[g, 0] * jnp.exp2((old_p - top_p) * LOG2E) + jnp.where(is_prompt, part2, 0.0)
        acc_ref[g, 1] = (
            acc_ref[g, 1] * jnp.exp2((old_c - top_c) * LOG2E) + part1 + jnp.where(is_prompt, 0.0, part2)
        )
        top_ref[g, 0] = jnp.broadcast_to(top_p, top_ref.shape[2:])
        top_ref[g, 1] = jnp.broadcast_to(top_c, top_ref.shape[2:])

    return own, other


def attend_close(g, top_ref, acc_ref, o_ref, lse_ref):
    for b in range(2):
        acc = acc_ref[g, b]
        total = acc[0:1, :]
        o_ref[g, b] = (acc / total).T
        lse_ref[g, b] = jnp.broadcast_to(top_ref[g, b, 0:1, :] * LOG2E + jnp.log2(total), lse_ref.shape[2:])


def attend_back_step(n, me, g, j, deal_ref, start_ref, q_ref, kv_ref, do_ref, lse_ref, delta_ref, dqt_ref, dkv_ref):
    block = kv_ref.shape[3]
    rows = q_ref.shape[2]
    own_mask, other_mask = attend_masks(n, deal_ref, start_ref, block, rows)

    def pair(kind, tile, mask):
        q = q_ref[g, kind]
        do = do_ref[g, kind]
        p = jnp.exp2(nt(tile, q) * LOG2E - lse_ref[g, kind, 0:1, :])
        if mask is not None:
            p = jnp.where(mask, p, 0.0)
        ds = (p * (nt(tile, do) - delta_ref[g, kind, 0:1, :])).astype(BF16)
        return nn(ds, q) + nn(p.astype(BF16), do), tn(tile, ds)

    def own():
        own0, own1 = kv_ref[me, 0, g], kv_ref[me, 1, g]
        d0, q0 = pair(0, own0, own_mask(0))
        d1, q1 = pair(1, own1, own_mask(1))
        d2, q2 = pair(1, own0, None)
        dkv_ref[me, g, 0] = (d0 + d2).astype(dkv_ref.dtype)
        dkv_ref[me, g, 1] = d1.astype(dkv_ref.dtype)
        dqt_ref[0] = q0
        dqt_ref[1] = q1 + q2

    def other():
        at = lax.rem(me + j, n)
        kind, mask = other_mask(at)
        is_prompt = kind == 0
        full, q_full = pair(1, kv_ref[at, 0, g], None)
        part, q_part = pair(kind, kv_ref[at, kind, g], mask)
        dkv_ref[at, g, 0] = (full + jnp.where(is_prompt, part, 0.0)).astype(dkv_ref.dtype)
        dkv_ref[at, g, 1] = jnp.where(is_prompt, 0.0, part).astype(dkv_ref.dtype)
        dqt_ref[0] = dqt_ref[0] + jnp.where(is_prompt, q_part, 0.0)
        dqt_ref[1] = dqt_ref[1] + q_full + jnp.where(is_prompt, 0.0, q_part)

    return own, other


def row_deltas(g, do_ref, o_ref, row_ref):
    ones = jnp.ones((8, LANES), F32)
    for b in range(2):
        row_ref[b] = lax.dot_general(
            ones, do_ref[g, b].astype(F32) * o_ref[g, b], (((1,), (1,)), ((), ())),
            precision=lax.Precision.HIGHEST, preferred_element_type=F32,
        )


def gain_row(gains_ref, which, fsdp, shard):
    return jnp.concatenate([gains_ref[i, which : which + 1, :shard] for i in range(fsdp)], axis=1)


def project(sizes, fsdp, x_ref, gains_ref, attn_ref, cos_ref, sin_ref, n1_ref, q_ref, kv_at):
    heads, kvh, block = sizes
    x = x_ref[...].astype(F32)
    normed = (x * rms_inverse(x) * gain_row(gains_ref, 0, fsdp, x.shape[1] // fsdp)).astype(BF16)
    n1_ref[...] = normed
    count = -(-(heads + 2 * kvh) * HD // LANES)
    shard = x.shape[1] // fsdp
    raw = []
    for t in range(0, count, 2):
        some = range(t, min(t + 2, count))
        wide = nn(normed, flat_lanes(attn_ref, some, shard))
        raw += [wide[:, i * LANES : (i + 1) * LANES] for i in range(len(some))]
    store_projection(sizes, raw, cos_ref[...], sin_ref[...], q_ref, kv_at)


def front_kernel(
    sizes, n, fsdp, plans, deal_ref, lengths_ref, xt_ref, gains_in, turns_ref,
    wq_ref, wkt_ref, wvt_ref, wo_ref, wg_ref, wu_ref, wdt_ref, cott_ref,
    x_ref, cos_ref, sin_ref, n1_ref, q_ref, kv_out, lse_ref, gains_ref, qkv_out,
    result_ref, gr_ref, do_ref, delta_ref, gain_ref, out_grad, ff_grad, down_grad,
    qkv, wout, ff, down, kv_all, o_ref, gains, start_ref, top_ref, acc_ref, cot_ref,
    resid_ref, n2_ref, product_ref, gg_ref, gu_ref, turned_ref, gn_ref, out_stage, ff_stage, down_stage,
    send, recv, kv_send, kv_recv, local, out_sem,
):
    heads, kvh, block = sizes
    me, z = lax.axis_index("ctx"), lax.axis_index("fsdp")
    shard = wq_ref.shape[0]
    rows = sub(z * shard, shard, 16)
    for ref, parts in ((qkv, [wq_ref[...], wkt_ref[...].T, wvt_ref[...].T]), (wout, [wo_ref[...]])):
        for t, tile in enumerate(pack_tiles(parts)):
            ref[z, t * shard : (t + 1) * shard, :] = tile
    used = -(-(heads + 2 * kvh) * HD // LANES) * shard
    qkv[z, used:, :] = jnp.zeros((qkv.shape[1] - used, LANES), BF16)
    gains[z] = gains_in[...]
    greet("z", fsdp)
    refs = {QKV: qkv, OUT: wout, FF: ff, DOWN: down, "gains": gains}
    run = both_cores(lambda core: weight_stages(core, fsdp, plans[0], refs, send, recv))
    run_kv = both_cores(lambda core: kv_stages(core, plans[1], kv_all, kv_send, kv_recv))
    run("gains_out", ("over_z", QKV))
    for t in range(ff.shape[1]):
        ff[0, t, rows, :] = wg_ref[:, t * LANES : (t + 1) * LANES]
        ff[1, t, rows, :] = wu_ref[:, t * LANES : (t + 1) * LANES]
    down_shard = wdt_ref.shape[1]
    down_rows = sub(z * down_shard, down_shard, 16)
    for t, tile in enumerate(pack_tiles([wdt_ref[...].T])):
        down[t, down_rows, :] = tile
    first, last = natural_blocks(deal_ref, me)
    flip = deal_ref[2 * me] > deal_ref[2 * me + 1]
    x_ref[...] = ordered(flip, xt_ref[...].T)
    cot_ref[...] = ordered(flip, cott_ref[...].T)
    row = lax.broadcasted_iota(jnp.int32, cos_ref.shape, 0)
    natural = jnp.where(row < block, first * block + row, (last - 1) * block + row)
    offset = natural - n * block
    position = jnp.where(offset < 0, natural, natural - segment_start(lengths_ref, offset))
    angle = position.astype(F32) * turns_ref[0:1, :]
    lane = lax.broadcasted_iota(jnp.int32, cos_ref.shape, 1)
    cos_ref[...] = jnp.cos(angle)
    sine = jnp.sin(angle)
    sin_ref[...] = jnp.where(lax.rem(lane, HD) < HD // 2, -sine, sine)
    start_ref[...] = first_keys(n, deal_ref, lengths_ref, block, start_ref.shape[1])
    run(("spread", QKV), ("over_z", OUT), ("over_z", DOWN), ("over_z", FF), ("forward", QKV))
    run(("pass_far", QKV), ("pass_corner", QKV), ("finish", QKV), "gains_in")
    project(
        sizes, fsdp, x_ref, gains, qkv, cos_ref, sin_ref, n1_ref, q_ref,
        lambda b, g: kv_all.at[me, b, g],
    )
    run_kv("start")
    gains_ref[...] = gains[...]
    outs = [pltpu.make_async_copy(qkv, qkv_out, local.at[0]), pltpu.make_async_copy(kv_all, kv_out, local.at[1])]
    outs[0].start()
    kv_schedule = {
        kvh: ((FINISH, 0),),
        2 * kvh: ("forward", "pass_far"),
        4 * kvh: ((FINISH, 1), (FINISH, 2)),
        6 * kvh: ("pass_corner",),
        7 * kvh: ((FINISH, 3),),
    }
    schedule = {
        3: (("spread", OUT),),
        11: (("spread", DOWN),),
        14: (("forward", OUT),),
        18: (("forward", DOWN),),
        20: (("spread", FF),),
        24: (("pass_far", OUT), ("pass_corner", OUT)),
        28: (("pass_far", DOWN), ("pass_corner", DOWN)),
        32: (("forward", FF),),
        38: (("finish", OUT), ("finish", DOWN)),
    }

    @pl.loop(0, kvh * n)
    def _(step):
        j, g = step // kvh, step % kvh
        turn = jnp.where(j == 3, 4, jnp.where(j == 4, 3, j))
        for at, names in kv_schedule.items():
            pl.when(step == at)(functools.partial(run_kv, *names))
        for at, names in schedule.items():
            pl.when(step == at)(functools.partial(run, *names))
        own, other = attend_step(
            n, me, g, lax.bitwise_xor(me, turn), deal_ref, start_ref, q_ref, kv_all, top_ref, acc_ref
        )
        pl.when(j == 0)(own)
        pl.when(j > 0)(other)
        pl.when(j == n - 1)(lambda: attend_close(g, top_ref, acc_ref, o_ref, lse_ref))

    outs[1].start()
    run(("pass_far", FF))

    def quarter_ready(i):
        pl.when(i == 0)(lambda: run((FINISH, FF, 0)))
        pl.when(i == 1)(lambda: run((FINISH, FF, 1), (FINISH, FF, 2)))
        pl.when(i == 3)(lambda: run(("pass_corner", FF), (FINISH, FF, 3)))
        return lax.bitwise_xor(me // 2, i)

    feed_forward(
        sizes, fsdp, quarter_ready, x_ref, cot_ref, gains, wout, ff, down, o_ref,
        result_ref, gr_ref, do_ref, delta_ref, gain_ref, out_grad, ff_grad, down_grad,
        resid_ref, n2_ref, product_ref, gg_ref, gu_ref, turned_ref, gn_ref, out_stage, ff_stage, down_stage, out_sem,
    )
    run("drain")
    run_kv("drain")
    for copy in outs:
        copy.wait()


def head_columns(sizes, ref, low):
    heads, kvh, block = sizes
    share = heads // kvh
    return jnp.concatenate(
        [
            jnp.concatenate(
                [
                    ref[h // share, b, (h % share) * block : (h % share + 1) * block, low : low + HD]
                    for h in range(heads)
                ],
                axis=1,
            )
            for b in range(2)
        ],
        axis=0,
    )


def feed_forward(
    sizes, fsdp, quarter_ready, x_ref, cot_ref, gains_ref, wout_ref, ff_ref, down_ref, o_ref,
    result_ref, gr_ref, do_ref, delta_ref, gain_ref, out_grad, ff_grad, down_grad,
    resid_ref, n2_ref, product_ref, gg_ref, gu_ref, turned_ref, gn_ref, out_stage, ff_stage, down_stage, sem,
):
    heads, kvh, block = sizes
    share = heads // kvh
    rows, width = x_ref.shape
    shard = width // fsdp
    half = (heads + 2 * kvh) * HD % LANES
    out_tiles = -(-width // LANES)
    down_tiles = down_ref.shape[0]
    gain = gain_row(gains_ref, 1, fsdp, width // fsdp)
    attended = head_columns(sizes, o_ref, HD).astype(BF16)
    pieces = []
    for t in range(0, out_tiles, 2):
        pieces.append(nn(attended, flat_lanes(wout_ref, range(t, min(t + 2, out_tiles)), shard)))
    resid = x_ref[...].astype(F32) + jnp.concatenate(pieces, axis=1)[:, :width]
    resid_ref[...] = resid
    n2_ref[...] = (resid * rms_inverse(resid) * gain).astype(BF16)
    pad = down_tiles * LANES - width
    wide = 2 * LANES
    per = ff_ref.shape[1] // 4
    turned_ref[...] = n2_ref[...].T
    gn_ref[...] = jnp.zeros(gn_ref.shape, F32)
    gr_ref[...] = jnp.zeros(gr_ref.shape, F32)

    def moves(q):
        columns = sub(q * per * LANES, per * LANES, LANES)
        return (
            pltpu.make_async_copy(ff_stage, ff_grad.at[:, pl.ds(q * per, per)], sem.at[0]),
            pltpu.make_async_copy(down_stage, down_grad.at[:, columns], sem.at[1]),
        )

    @pl.loop(0, 4)
    def _(i):
        q = quarter_ready(i)
        cot_wide = jnp.concatenate([cot_ref[...], jnp.zeros((rows, pad), BF16)], axis=1)
        for low in range(0, per, 2):
            size = min(2, per - low)
            first = q * per + low
            at = sub(first * LANES, size * LANES, LANES)
            n2 = n2_ref[...]
            gate = nn(n2, jnp.concatenate([ff_ref[0, first + t] for t in range(size)], axis=1))
            upward = nn(n2, jnp.concatenate([ff_ref[1, first + t] for t in range(size)], axis=1))
            grad = nt(cot_wide, jnp.concatenate([down_ref[t, at, :] for t in range(down_tiles)], axis=1))
            sigma = 1.0 / (1.0 + jnp.exp(-gate))
            activated = gate * sigma
            here = slice(low * LANES, (low + size) * LANES)
            product_ref[:, here] = (activated * upward).astype(BF16)
            gg_ref[:, here] = (grad * upward * (sigma + activated * (1.0 - sigma))).astype(BF16)
            gu_ref[:, here] = (grad * activated).astype(BF16)
        for low in range(0, width, wide):
            size = min(wide, width - low)
            part = 0.0
            for c, grad_ref in enumerate((gg_ref, gu_ref)):
                weights = [ff_ref[c, q * per + t, low : low + size, :] for t in range(per)]
                part = part + nt(grad_ref[...], jnp.concatenate(weights, axis=1))
            gn_ref[:, low : low + size] = gn_ref[:, low : low + size] + part
        columns = sub(q * per * LANES, per * LANES, LANES)
        for t in range(0, down_tiles, 2):
            low, high = t * LANES, min((t + 2) * LANES, width)
            weights = jnp.concatenate([down_ref[t, columns, :], down_ref[t + 1, columns, :]], axis=1)
            part = nn(product_ref[...], weights)
            gr_ref[:, low:high] = gr_ref[:, low:high] + part[:, : high - low]

        @pl.when(i >= 1)
        def _():
            for copy in moves(q):
                copy.wait()

        for low in range(0, per, 2):
            size = min(2, per - low)
            here = slice(low * LANES, (low + size) * LANES)
            for c, grad_ref in enumerate((gg_ref, gu_ref)):
                part = nn(turned_ref[...], grad_ref[:, here]).astype(BF16)
                for t in range(size):
                    ff_stage[c, low + t] = part[:, t * LANES : (t + 1) * LANES]
            part = nn(product_ref[:, here].T, cot_wide).astype(BF16)
            for t in range(down_tiles):
                down_stage[t, here, :] = part[:, t * LANES : (t + 1) * LANES]
        for copy in moves(q):
            copy.start()

    result_ref[...] = (resid_ref[...] + gr_ref[...]).astype(BF16)
    grad_normed = gn_ref[...]
    resid = resid_ref[...]
    inverse = rms_inverse(resid)
    scaled = resid * inverse
    weighted = grad_normed * gain
    gain_ref[0:1, :] = jnp.sum(grad_normed * scaled, axis=0, keepdims=True)
    grad_resid = cot_ref[...].astype(F32) + inverse * (
        weighted - scaled * jnp.mean(weighted * scaled, axis=1, keepdims=True)
    )
    gr_ref[...] = grad_resid
    gb = grad_resid.astype(BF16)
    main = width - (LANES - half)
    lined = jnp.concatenate([jnp.zeros((rows, half), BF16), gb[:, main:], gb[:, :main]], axis=1)
    turned_ref[...] = head_columns(sizes, o_ref, HD).astype(BF16).T
    for t in range(0, out_tiles, 2):
        part = nn(turned_ref[...], lined[:, t * LANES : (t + 2) * LANES]).astype(BF16)
        out_stage[t] = part[:, :LANES]
        out_stage[t + 1] = part[:, LANES:]
    out_copy = pltpu.make_async_copy(out_stage, out_grad, sem.at[2])
    out_copy.start()
    gb_wide = jnp.concatenate([gb, jnp.zeros((rows, out_tiles * LANES - width), BF16)], axis=1)
    grad_att = []
    for zi in range(fsdp):
        weights = [wout_ref[zi, t * shard : (t + 1) * shard, :] for t in range(out_tiles)]
        grad_att.append(nt(gb_wide, jnp.concatenate(weights, axis=1)).astype(BF16))
    grad_att = jnp.concatenate(grad_att, axis=1)
    zero = jnp.zeros((block, HD), BF16)
    for h in range(heads):
        for b in range(2):
            do_ref[h // share, b, (h % share) * block : (h % share + 1) * block, :] = jnp.concatenate(
                [zero, grad_att[b * block : (b + 1) * block, h * HD : (h + 1) * HD]], axis=1
            )
    for g in range(kvh):
        row_deltas(g, do_ref, o_ref, delta_ref.at[g])
    for copy in moves(0):
        copy.wait()
    out_copy.wait()


def add_rows(out, terms, rows):
    def add(views):
        total = views[1][0:rows, :].astype(F32)
        for term in views[2:]:
            total = total + term[0:rows, :].astype(F32)
        views[0][0:rows, :] = total.astype(out.dtype)

    refs = [out] + list(terms)
    if len(out.shape) == 2:
        add(refs)
    else:

        @pl.loop(0, out.shape[0])
        def _(lead):
            add([r.at[lead] for r in refs])


def grad_stages(core, fsdp, plan, sources, held, got, outs, gain_refs, send, recv, local):
    links = Links(core, fsdp, send, recv, plan)
    z, chip = links.z, links.chip
    near, far = lax.bitwise_xor(chip, links.first), lax.bitwise_xor(chip, links.second)
    corner = lax.bitwise_xor(chip, 3)
    shards = {k: sources[k].shape[-2] // fsdp for k in PACKAGES}
    mine = {k: Share(k, core, shards[k]) for k in PACKAGES}
    twin = {k: Share(k, 1 - core, shards[k]) for k in PACKAGES}
    stages = {}

    def slot_of(d):
        return max(d - 1, 0)

    def hold(k, d, q):
        if k in held:
            return held[k].at[d, q]
        return mine[k].at(sources[k], lax.bitwise_xor(z, d), q)

    def load(k, d, q):
        slot = (PACKAGES.index(k) * fsdp + d) * 4 + q
        return pltpu.make_async_copy(
            mine[k].at(sources[k], lax.bitwise_xor(z, d), q), hold(k, d, q), local.at[slot]
        )

    def begin(k, d):
        zi = lax.bitwise_xor(z, d)
        for q in range(4):
            links.send((k, CORE, d, q), CORE, twin[k].at(sources[k], zi, q), twin[k].buffer(got[k][0].at[d, q]))
            if k in held:
                load(k, d, q).start()

    def stage1(k, d):
        share = mine[k]
        for q in range(4):
            links.landed((k, CORE, d, q), share.buffer(got[k][0].at[d, q]))
            if k in held:
                load(k, d, q).wait()
            terms = [hold(k, d, q), got[k][0].at[d, q]]
            if d == 0:
                links.landed((k, "direct", q), share.buffer(got[k][4].at[q]))
                terms.append(got[k][4].at[q])
            add_rows(hold(k, d, q), terms, share.rows)
            if d == 1:
                links.send((k, "direct", q), d, hold(k, d, q), share.buffer(got[k][4].at[q]))
        for i, q in enumerate((near, corner)):
            if d != 1:
                links.send((k, FIRST, d, i), FIRST, hold(k, d, q), share.buffer(got[k][1].at[slot_of(d), i]))

    def stage2(k, d):
        share, slot = mine[k], slot_of(d)
        if d == 1:
            return
        for i in range(2):
            links.landed((k, FIRST, d, i), share.buffer(got[k][1].at[slot, i]))
        add_rows(hold(k, d, far), (hold(k, d, far), got[k][1].at[slot, 1]), share.rows)
        links.send((k, SECOND, d), SECOND, hold(k, d, far), share.buffer(got[k][2].at[slot]))

    def stage3(k, d):
        share, slot = mine[k], slot_of(d)
        if d == 1:
            return
        links.landed((k, SECOND, d), share.buffer(got[k][2].at[slot]))
        add_rows(hold(k, d, chip), (hold(k, d, chip), got[k][1].at[slot, 0], got[k][2].at[slot]), share.rows)
        if d > 0:
            links.send((k, "z", d), d, hold(k, d, chip), share.buffer(got[k][3].at[d - 2]))

    def out_copy(k):
        slot = len(PACKAGES) * fsdp * 4 + PACKAGES.index(k)
        return pltpu.make_async_copy(hold(k, 0, chip), mine[k].at(outs[k], 0, chip), local.at[slot])

    def close(k):
        share = mine[k]
        for d in range(2, fsdp):
            links.landed((k, "z", d), share.buffer(got[k][3].at[d - 2]))
        final = hold(k, 0, chip)
        add_rows(final, [final] + [got[k][3].at[d - 2] for d in range(2, fsdp)], share.rows)
        for hop in (FIRST, SECOND):
            links.send((k, "out", hop), hop, final, share.at(outs[k], 0, chip))
        links.send((k, "out core", 0), CORE, final, share.at(outs[k], 0, chip))
        out_copy(k).start()

    def close2(k):
        share = mine[k]
        links.landed((k, "out", FIRST), share.at(outs[k], 0, near))
        piece = share.at(outs[k], 0, near)
        links.send((k, "out", "corner"), SECOND, piece, piece)
        links.send((k, "out core", 1), CORE, piece, piece)
        piece = share.at(outs[k], 0, far)
        links.landed((k, "out", SECOND), piece)
        links.send((k, "out core", 2), CORE, piece, piece)

    def close3(k):
        piece = mine[k].at(outs[k], 0, corner)
        links.landed((k, "out", "corner"), piece)
        links.send((k, "out core", 3), CORE, piece, piece)

    def close4(k):
        for i, q in ((0, chip), (1, far), (2, near), (3, corner)):
            links.landed((k, "out core", i), twin[k].at(outs[k], 0, q))
        out_copy(k).wait()

    for k in PACKAGES:
        for fn in (begin, stage1, stage2, stage3):
            for d in range(fsdp):
                stages[fn.__name__, k, d] = functools.partial(fn, k, d)
        for fn in (close, close2, close3, close4):
            stages[fn.__name__, k] = functools.partial(fn, k)

    gain_sum, gain_got, gain_z, gain_out = gain_refs

    def gain_step(i):
        if i > 0:
            links.landed(("gain", i - 1), gain_got.at[i - 1])
            gain_sum[i] = gain_sum[i - 1] + gain_got[i - 1]
        if i < 3:
            links.send(("gain", i), (CORE, FIRST, SECOND)[i], gain_sum.at[i], gain_got.at[i])
        else:
            for d in range(1, fsdp):
                links.send(("gain z", d), d, gain_sum.at[3, lax.bitwise_xor(z, d)], gain_z.at[d - 1])

    def gain_close():
        total = gain_sum[3, z]
        for d in range(1, fsdp):
            links.landed(("gain z", d), gain_z.at[d - 1])
            total = total + gain_z[d - 1]
        gain_out[...] = total

    for i in range(4):
        stages["gain", i] = functools.partial(gain_step, i)
    stages["gain close"] = gain_close
    stages["drain"] = links.drain
    return stages


def kv_grad_stages(core, plan, parts, kv_sum, got0, got1, got2, send, recv):
    links = Links(core, 1, send, recv, plan)
    chip = links.chip
    near, far = lax.bitwise_xor(chip, links.first), lax.bitwise_xor(chip, links.second)
    corner = lax.bitwise_xor(chip, 3)
    rows = parts.shape[3]
    stages = {}

    def start(g):
        for q in range(4):
            links.send((0, g, q), CORE, parts.at[2 * q + 1 - core, g], got0.at[g, q])

    def stage1(g):
        for q in range(4):
            links.landed((0, g, q), got0.at[g, q])
            add_rows(got0.at[g, q], (parts.at[2 * q + core, g], got0.at[g, q]), rows)
        for i, q in enumerate((near, corner)):
            links.send((1, g, i), FIRST, got0.at[g, q], got1.at[g, i])

    def stage2(g):
        for i in range(2):
            links.landed((1, g, i), got1.at[g, i])
        add_rows(got0.at[g, far], (got0.at[g, far], got1.at[g, 1]), rows)
        links.send((2, g), SECOND, got0.at[g, far], got2.at[g])

    def stage3(g):
        links.landed((2, g), got2.at[g])
        add_rows(kv_sum.at[g], (got0.at[g, chip], got1.at[g, 0], got2.at[g]), rows)

    for g in range(parts.shape[1]):
        for i, fn in enumerate((start, stage1, stage2, stage3)):
            stages[i, g] = functools.partial(fn, g)
    stages["drain"] = links.drain
    return stages


def back_kernel(
    sizes, n, fsdp, plans, deal_ref, lengths_ref, q_ref, kv_in, do_ref, delta_ref, lse_ref,
    x_ref, n1_ref, gr_ref, gains_ref, gain_two_ref, cos_ref, sin_ref, qkv_ref, out_grad_ref, ff_grad, down_grad,
    tg_ref, gain_out, attn_out, ff_out, down_out,
    start_ref, spill_ref, chunk_ref, dqt_ref, dq_ref, dkv_ref, kv_sum, kv_got0, kv_got1, kv_got2, gp_ref, gn_ref, turned_ref, attn_grad,
    ff_a, down_a, attn_0, ff_0, down_0, attn_1, ff_1, down_1, attn_2, ff_2, down_2, attn_3, ff_3, down_3, attn_4, ff_4, down_4,
    gain_sum, gain_got, gain_z, send, recv, kv_send, kv_recv, local, ahead_sem,
):
    heads, kvh, block = sizes
    share = heads // kvh
    me = lax.axis_index("ctx")
    width = x_ref.shape[1]
    rows = x_ref.shape[0]
    greet("z", fsdp)
    sources = {ATTN: attn_grad, FF: ff_grad, DOWN: down_grad}
    held = {FF: ff_a, DOWN: down_a}
    got = {
        ATTN: (attn_0, attn_1, attn_2, attn_3, attn_4),
        FF: (ff_0, ff_1, ff_2, ff_3, ff_4),
        DOWN: (down_0, down_1, down_2, down_3, down_4),
    }
    outs = {ATTN: attn_out, FF: ff_out, DOWN: down_out}
    run = both_cores(
        lambda core: grad_stages(
            core, fsdp, plans[0], sources, held, got, outs, (gain_sum, gain_got, gain_z, gain_out), send, recv, local
        )
    )
    run_kv = both_cores(
        lambda core: kv_grad_stages(core, plans[1], dkv_ref, kv_sum, kv_got0, kv_got1, kv_got2, kv_send, kv_recv)
    )
    start_ref[...] = first_keys(n, deal_ref, lengths_ref, block, start_ref.shape[1])
    order = [d for d in range(1, fsdp)] + [0]
    chunks = [(k, d) for k in (FF, DOWN) for d in order]
    steps = []
    for i in range(len(chunks) + 7):
        names = []
        if i + 1 < len(chunks):
            names.append(("begin",) + chunks[i + 1])
        if i < len(chunks):
            names.append(("stage1",) + chunks[i])
        if 1 <= i <= len(chunks):
            names.append(("stage2",) + chunks[i - 1])
        if 2 <= i <= len(chunks) + 1:
            names.append(("stage3",) + chunks[i - 2])
        for last, k in ((len(order) + 1, FF), (len(chunks) + 1, DOWN)):
            for extra, what in enumerate(("close", "close2", "close3", "close4")):
                if i == last + 1 + extra:
                    names.append((what, k))
        steps.append(names)
    run(("begin",) + chunks[0])
    width_tiles = -(-(heads + 2 * kvh) // 2)
    ahead = [
        pltpu.make_async_copy(out_grad_ref.at[0], spill_ref, ahead_sem.at[0]),
        pltpu.make_async_copy(
            out_grad_ref.at[pl.ds(1, attn_grad.shape[0] - width_tiles)],
            attn_grad.at[pl.ds(width_tiles, attn_grad.shape[0] - width_tiles)], ahead_sem.at[1],
        ),
    ]
    def weight_rows(i):
        size = chunk_ref.shape[1]
        return pltpu.make_async_copy(qkv_ref.at[i, pl.ds(0, size)], chunk_ref.at[i % 2], ahead_sem.at[2 + i % 2])

    for copy in ahead + [weight_rows(0), weight_rows(1)]:
        copy.start()
    total = kvh * n
    pace = 12
    kv_due = sorted((8 * (i + 1) + (0, 3, 11, 19)[stage], stage, i) for i in range(kvh) for stage in range(4))

    @pl.loop(0, total)
    def _(step):
        g, j = step // n, step % n
        for i, names in enumerate(steps):
            if i * pace < total:
                pl.when(step == i * pace)(functools.partial(run, *names))
        for due, stage, i in kv_due:
            if due < total:
                pl.when(step == due)(functools.partial(run_kv, (stage, i)))
        own, other = attend_back_step(
            n, me, g, j, deal_ref, start_ref, q_ref, kv_in, do_ref, lse_ref, delta_ref, dqt_ref, dkv_ref
        )
        pl.when(j == 0)(own)
        pl.when(j > 0)(other)

        @pl.when(j == n - 1)
        def _():
            dq_ref[g] = jnp.concatenate([(dqt_ref[b] * 0.125).T[:, :HD] for b in range(2)], axis=1)

    cos, sin = cos_ref[...], -sin_ref[...]

    def head(index):
        if index < heads:
            return jnp.concatenate(
                [
                    dq_ref[index // share, (index % share) * block : (index % share + 1) * block, b * HD : (b + 1) * HD]
                    for b in range(2)
                ],
                axis=0,
            )
        g = index - heads
        low = 0 if g < kvh else HD
        return jnp.concatenate([kv_sum[g % kvh, b, :, low : low + HD] for b in range(2)], axis=0)

    count = heads + 2 * kvh
    tiles = -(-count // 2)
    turned_ref[...] = n1_ref[...].T

    def some_tiles(low, high):
        for t in range(low, high):
            right = head(2 * t + 1) if 2 * t + 1 < count else jnp.zeros((rows, HD), F32)
            pair = jnp.concatenate([head(2 * t), right], axis=1)
            if 2 * t < heads + kvh:
                pair = rope_tile(pair, cos, sin)
            gp_ref[:, t * LANES : (t + 1) * LANES] = pair.astype(BF16)
        for t in range(low, high, 2):
            some = min(2, high - t)
            part = nn(turned_ref[...], gp_ref[:, t * LANES : (t + some) * LANES]).astype(BF16)
            for i in range(some):
                tile = part[:, i * LANES : (i + 1) * LANES]
                attn_grad[t + i] = tile + spill_ref[...] if t + i == tiles - 1 else tile

    rest = [names for i, names in enumerate(steps) if i * pace >= total]
    late = [(stage, i) for due, stage, i in kv_due if due >= total]
    run_kv(late[0])
    some_tiles(0, heads // 2)
    for copy in ahead:
        copy.wait()
    run_kv(*[key for key in late[1:] if key[0] < 2 or key[1] < kvh - 1])
    run(*rest[0])
    run_kv(*[key for key in late[1:] if key[0] >= 2 and key[1] == kvh - 1])
    some_tiles(heads // 2, tiles)
    run(("begin", ATTN, order[0]), ("begin", ATTN, order[1]), ("stage1", ATTN, order[0]), *rest[1])
    shard = width // fsdp
    pieces = []
    for i in range(fsdp):
        weight_rows(i).wait()
        rows_in = jnp.concatenate([chunk_ref[i % 2, t * shard : (t + 1) * shard, :] for t in range(tiles)], axis=1)
        pieces.append(nt(gp_ref[...], rows_in))
        if i + 2 < fsdp:
            weight_rows(i + 2).start()
    gn_ref[...] = jnp.concatenate(pieces, axis=1)
    x = x_ref[...].astype(F32)
    inverse = rms_inverse(x)
    scaled = x * inverse
    grad_normed = gn_ref[...]
    weighted = grad_normed * gain_row(gains_ref, 0, fsdp, width // fsdp)
    gain_one = jnp.sum(grad_normed * scaled, axis=0, keepdims=True)
    gain_two = gain_two_ref[0:1, :]
    tail = gain_sum.shape[3] - shard
    for i in range(fsdp):
        both = jnp.concatenate(
            [gain_one[:, i * shard : (i + 1) * shard], gain_two[:, i * shard : (i + 1) * shard]], axis=0
        )
        both = jnp.concatenate([both, jnp.zeros((2, tail), F32)], axis=1)
        gain_sum[0, i] = jnp.concatenate([both, jnp.zeros((6, gain_sum.shape[3]), F32)], axis=0)
    run(("gain", 0))
    tg_ref[...] = (
        gr_ref[...] + inverse * (weighted - scaled * jnp.mean(weighted * scaled, axis=1, keepdims=True))
    ).astype(BF16)
    chunk2 = [(ATTN, d) for d in order]
    for i in range(1, len(chunk2) + 2):
        names = []
        if i + 1 < len(chunk2):
            names.append(("begin",) + chunk2[i + 1])
        if i < len(chunk2):
            names.append(("stage1",) + chunk2[i])
        if i <= len(chunk2):
            names.append(("stage2",) + chunk2[i - 1])
        if i >= 2:
            names.append(("stage3",) + chunk2[i - 2])
        if i <= 3:
            names.append(("gain", i))
        if i + 1 < len(rest):
            names += rest[i + 1]
        run(*names)
    for i, what in enumerate(("close", "close2", "close3", "close4")):
        names = rest[len(chunk2) + 3 + i] if len(chunk2) + 3 + i < len(rest) else []
        run((what, ATTN), *names)
    for names in rest[len(chunk2) + 7 :]:
        run(*names)
    run("gain close", "drain")
    run_kv("drain")


def whole(shape, dtype):
    return jax.ShapeDtypeStruct(shape, dtype)


def params(ident=None):
    extra = {} if ident is None else {"collective_id": ident, "has_side_effects": True}
    return pltpu.CompilerParams(vmem_limit_bytes=VMEM_LIMIT, **extra)


SMEM = pl.BlockSpec(memory_space=pltpu.SMEM)
VMEM = pl.BlockSpec(memory_space=pltpu.VMEM)
ANY = pl.BlockSpec(memory_space=pl.ANY)


def finish_kernel(
    heads, deal_ref, result_ref, tokens_ref, attn_ref, ff_ref, down_ref,
    out_ref, tg_ref, q_ref, kt_ref, vt_ref, o_ref, gate_ref, up_ref, dt_ref,
):
    me = lax.axis_index("ctx")
    flip = deal_ref[2 * me] > deal_ref[2 * me + 1]
    out_ref[...] = ordered(flip, result_ref[...]).T
    tg_ref[...] = ordered(flip, tokens_ref[...]).T
    width, kv_width = q_ref.shape[1], kt_ref.shape[0]
    half = width % LANES
    full = width // LANES

    def tile(t):
        return attn_ref[t].astype(F32)

    for t in range(full):
        q_ref[:, t * LANES : (t + 1) * LANES] = tile(t)
    q_ref[:, full * LANES :] = tile(full)[:, :half]
    kt_ref[0 : LANES - half, :] = tile(full).T[half:, :]
    at = LANES - half
    for t in range(full + 1, (width + kv_width) // LANES):
        kt_ref[at : at + LANES, :] = tile(t).T
        at += LANES
    first = (width + kv_width) // LANES
    spill = (width + 2 * kv_width) // LANES
    for i in range(spill - first):
        vt_ref[i * LANES : (i + 1) * LANES, :] = tile(first + i).T
    vt_ref[(spill - first) * LANES :, :] = tile(spill).T[: kv_width % LANES, :]
    for i in range(full):
        o_ref[:, i * LANES : (i + 1) * LANES] = tile(spill + 1 + i)
    o_ref[:, full * LANES :] = tile(spill)[:, LANES - half :]
    for t in range(ff_ref.shape[1]):
        gate_ref[:, t * LANES : (t + 1) * LANES] = ff_ref[0, t].astype(F32)
        up_ref[:, t * LANES : (t + 1) * LANES] = ff_ref[1, t].astype(F32)
    for t in range(down_ref.shape[0]):
        high = min((t + 1) * LANES, dt_ref.shape[0])
        dt_ref[t * LANES : high, :] = down_ref[t].astype(F32).T[: high - t * LANES, :]


def cube_body(
    tokens, attn_gain, query_weight, key_weight, value_weight, out_weight, mlp_gain, gate_weight,
    up_weight, down_weight, cotangent, cont_lengths, block_deal,
):
    n, fsdp = lax.axis_size("ctx"), lax.axis_size("fsdp")
    me = lax.axis_index("ctx")
    row_count, width = tokens.shape[1:]
    kv_width = key_weight.shape[1]
    shard, hidden = gate_weight.shape
    down_shard = down_weight.shape[0]
    block = row_count // 2
    heads, kvh = width // HD, kv_width // HD
    share = heads // kvh
    stack = share * block
    sizes = (heads, kvh, block)
    half_turns = THETA ** (-2.0 * jnp.arange(HD // 2, dtype=F32) / HD)
    turns = jnp.tile(half_turns, (8, LANES // (HD // 2)))
    pad = -shard % LANES
    gains_in = jnp.pad(jnp.stack([attn_gain, mlp_gain]).astype(F32), ((0, 6), (0, pad)))
    gain_shape = (fsdp,) + gains_in.shape
    attn_tiles = (2 * width + 2 * kv_width) // LANES
    ff_tiles = hidden // LANES
    down_tiles = -(-width // LANES)
    heads_shape = (kvh, 2, stack, LANES)
    row_shape = (kvh, 2, 8, stack)
    kv_shape = (n, 2, kvh, block, LANES)
    dma = pltpu.SemaphoreType.DMA
    mixed = (width + 2 * kv_width) // LANES
    qkv_tiles = -(-(width + 2 * kv_width) // LANES)
    qkv_shape = (fsdp, -(-qkv_tiles * shard // LANES) * LANES, LANES)
    (
        x, cos, sin, normed_one, q, kv_all, lse, gains, w_qkv,
        result, grad_resid, grad_heads, deltas, gain_two, out_grad, ff_grad, down_grad,
    ) = pl.pallas_call(
        functools.partial(front_kernel, sizes, n, fsdp, ({}, {})),
        out_shape=(
            whole((row_count, width), BF16),
            whole((row_count, LANES), F32),
            whole((row_count, LANES), F32),
            whole((row_count, width), BF16),
            whole(heads_shape, BF16),
            whole(kv_shape, BF16),
            whole(row_shape, F32),
            whole(gain_shape, F32),
            whole(qkv_shape, BF16),
            whole((row_count, width), BF16),
            whole((row_count, width), F32),
            whole(heads_shape, BF16),
            whole(row_shape, F32),
            whole((8, width), F32),
            whole((attn_tiles - mixed, width, LANES), BF16),
            whole((2, ff_tiles, width, LANES), BF16),
            whole((down_tiles, hidden, LANES), BF16),
        ),
        in_specs=[SMEM] * 2 + [VMEM] * 11,
        out_specs=(VMEM,) * 5 + (ANY, VMEM, VMEM, ANY) + (VMEM,) * 5 + (ANY,) * 3,
        scratch_shapes=[
            pltpu.VMEM(qkv_shape, BF16),
            pltpu.VMEM((fsdp, down_tiles * shard, LANES), BF16),
            pltpu.VMEM((2, ff_tiles, fsdp * shard, LANES), BF16),
            pltpu.VMEM((down_tiles, fsdp * down_shard, LANES), BF16),
            pltpu.VMEM(kv_shape, BF16),
            pltpu.VMEM(heads_shape, F32),
            pltpu.VMEM(gain_shape, F32),
            pltpu.VMEM((8, stack), jnp.int32),
            pltpu.VMEM((kvh, 2, 8, stack), F32),
            pltpu.VMEM((kvh, 2, LANES, stack), F32),
            pltpu.VMEM((row_count, width), BF16),
            pltpu.VMEM((row_count, width), F32),
            pltpu.VMEM((row_count, width), BF16),
            pltpu.VMEM((row_count, hidden // 4), BF16),
            pltpu.VMEM((row_count, hidden // 4), BF16),
            pltpu.VMEM((row_count, hidden // 4), BF16),
            pltpu.VMEM((width, row_count), BF16),
            pltpu.VMEM((row_count, width), F32),
            pltpu.VMEM((attn_tiles - mixed, width, LANES), BF16),
            pltpu.VMEM((2, ff_tiles // 4, width, LANES), BF16),
            pltpu.VMEM((down_tiles, hidden // 4, LANES), BF16),
            dma((99,)), dma((99,)), dma((14,)), dma((14,)), dma((2,)), dma((3,)),
        ],
        compiler_params=params(0),
        name="front",
    )(
        block_deal, cont_lengths, tokens[0].T, gains_in, turns,
        query_weight, key_weight.T, value_weight.T, out_weight, gate_weight, up_weight, down_weight.T,
        cotangent[0].T,
    )

    attn_rows = -(-shard // 32) * 16
    shapes = ((attn_tiles // 4, attn_rows, LANES), (ff_tiles // 4, shard, LANES), (down_shard, LANES))
    buffers = [pltpu.VMEM((fsdp, 4) + shape, BF16) for shape in shapes[1:]]
    for lead in ((fsdp, 4), (fsdp - 1, 2), (fsdp - 1,), (fsdp - 2,), (4,)):
        buffers += [pltpu.VMEM(lead + shape, BF16) for shape in shapes]
    piece = (2, block, LANES)
    tokens_grad, gain_grads, attn_w, ff_w, down_w = pl.pallas_call(
        functools.partial(back_kernel, sizes, n, fsdp, ({}, {})),
        out_shape=(
            whole((row_count, width), BF16),
            whole(gains_in.shape, F32),
            whole((attn_tiles, shard, LANES), BF16),
            whole((2, ff_tiles, shard, LANES), BF16),
            whole((down_tiles, down_shard, LANES), BF16),
        ),
        in_specs=[SMEM] * 2 + [VMEM] * 12 + [ANY] * 4,
        out_specs=(VMEM, VMEM, ANY, ANY, ANY),
        scratch_shapes=[
            pltpu.VMEM((8, stack), jnp.int32),
            pltpu.VMEM((width, LANES), BF16),
            pltpu.VMEM((2, qkv_tiles * shard, LANES), BF16),
            pltpu.VMEM((2, LANES, stack), F32),
            pltpu.VMEM((kvh, stack, LANES), F32),
            pltpu.VMEM((n, kvh) + piece, BF16),
            pltpu.VMEM((kvh,) + piece, F32),
            pltpu.VMEM((kvh, 4) + piece, BF16),
            pltpu.VMEM((kvh, 2) + piece, BF16),
            pltpu.VMEM((kvh,) + piece, BF16),
            pltpu.VMEM((row_count, qkv_tiles * LANES), BF16),
            pltpu.VMEM((row_count, width), F32),
            pltpu.VMEM((width, row_count), BF16),
            pltpu.VMEM((attn_tiles, width, LANES), BF16),
        ]
        + buffers
        + [
            pltpu.VMEM((4,) + gain_shape, F32),
            pltpu.VMEM((3,) + gain_shape, F32),
            pltpu.VMEM((fsdp - 1,) + gains_in.shape, F32),
            dma((123,)), dma((123,)), dma((7 * kvh,)), dma((7 * kvh,)), dma((51,)), dma((4,)),
        ],
        compiler_params=params(1),
        name="back",
    )(
        block_deal, cont_lengths, q, kv_all, grad_heads, deltas, lse, x, normed_one, grad_resid, gains, gain_two,
        cos, sin, w_qkv, out_grad, ff_grad, down_grad,
    )

    out_t, tg_t, q_w, k_t, v_t, o_w, gate_w, up_w, d_t = pl.pallas_call(
        functools.partial(finish_kernel, heads),
        out_shape=(
            whole((width, row_count), BF16),
            whole((width, row_count), BF16),
            whole((shard, width), F32),
            whole((kv_width, shard), F32),
            whole((kv_width, shard), F32),
            whole((shard, width), F32),
            whole((shard, hidden), F32),
            whole((shard, hidden), F32),
            whole((width, down_shard), F32),
        ),
        in_specs=[SMEM] + [VMEM] * 5,
        out_specs=(VMEM,) * 9,
        compiler_params=params(),
        name="finish",
    )(block_deal, result, tokens_grad, attn_w, ff_w, down_w)
    return (
        out_t.T[None],
        tg_t.T[None],
        gain_grads[0, :shard],
        q_w,
        k_t.T,
        v_t.T,
        o_w,
        gain_grads[1, :shard],
        gate_w,
        up_w,
        d_t.T,
    )


def head_of(tiles, index):
    start = (index % 2) * HD
    return tiles[index // 2][:, start : start + HD]


def project_kernel(sizes, x_ref, gain_ref, w_ref, cos_ref, sin_ref, n1_ref, q_ref, kv_ref):
    heads, kvh, block = sizes
    share = heads // kvh
    x = x_ref[...].astype(F32)
    inverse = lax.rsqrt(jnp.mean(x * x, axis=1, keepdims=True) + EPSILON)
    normed = (x * inverse * gain_ref[...]).astype(BF16)
    n1_ref[...] = normed
    width = (heads + 2 * kvh) * HD
    raw = nn(normed, w_ref[:, :width])
    cos = cos_ref[...]
    sin = sin_ref[...]
    tiles = []
    for j in range((heads + kvh) * HD // LANES):
        tiles.append(rope_tile(raw[:, j * LANES : (j + 1) * LANES], cos, sin).astype(BF16))
    zero = jnp.zeros((block, HD), BF16)
    for h in range(heads):
        piece = head_of(tiles, h) * jnp.asarray(0.125, BF16)
        g, i = h // share, h % share
        for b in range(2):
            q_ref[g, b, i * block : (i + 1) * block, :] = jnp.concatenate(
                [piece[b * block : (b + 1) * block], zero], axis=1
            )
    for g in range(kvh):
        start = (heads + kvh + g) * HD
        value = raw[:, start : start + HD].astype(BF16)
        pair = jnp.concatenate([head_of(tiles, heads + g), value], axis=1)
        for b in range(2):
            kv_ref[b, :, g * LANES : (g + 1) * LANES] = pair[b * block : (b + 1) * block]


def attend_kernel(
    n, me_ref, pick_ref, segq_ref, segk_ref, q_ref, kv_ref, o_ref, lse_ref, s1_ref, p1_ref, s2_ref, p2_ref
):
    me = me_ref[0]
    block = kv_ref.shape[2]
    rows = q_ref.shape[2]
    keys = n * block
    qc = q_ref[0, 1]
    prompt = kv_ref[:, 0].reshape(keys, LANES)
    s1_ref[...] = nt(qc, prompt)
    own = []
    for b in range(2):
        s2_ref[b] = nt(q_ref[0, b], kv_ref[me, b])
    for j in range(1, n):
        at = lax.rem(me + j, n)
        kind = pick_ref[j]
        s2_ref[j + 1] = nt(q_ref[0, kind], kv_ref[at, kind])
    step = 16
    kinds = [pick_ref[j] == 0 for j in range(n)]

    def fold(s):
        return jnp.maximum(
            s[:, :LANES],
            jnp.concatenate(
                [s[:, LANES:], jnp.full((step, 2 * LANES - block), MASKED, F32)], axis=1
            ),
        )

    def chunk(at, carry):
        r = pl.multiple_of(at * step, step)
        rs = pl.ds(r, step)
        in_block = lax.rem(r, block)
        tri = lax.broadcasted_iota(jnp.int32, (step, block), 1) <= (
            in_block + lax.broadcasted_iota(jnp.int32, (step, block), 0)
        )
        segq = segq_ref[rs, :]
        s1 = s1_ref[rs, :]
        top_c = s1[:, :LANES]
        for t in range(1, keys // LANES):
            top_c = jnp.maximum(top_c, s1[:, t * LANES : (t + 1) * LANES])
        dp = jnp.where(tri, s2_ref[0, rs, :], MASKED)
        dc = jnp.where(tri & (segq == segk_ref[0]), s2_ref[1, rs, :], MASKED)
        top_c = jnp.maximum(top_c, fold(dc))
        top_p = fold(dp)
        others = []
        for j in range(1, n):
            s = jnp.where((segq == segk_ref[j]) | kinds[j], s2_ref[j + 1, rs, :], MASKED)
            others.append(s)
            f = fold(s)
            top_p = jnp.maximum(top_p, jnp.where(kinds[j], f, MASKED))
            top_c = jnp.maximum(top_c, jnp.where(kinds[j], MASKED, f))
        m_p = jnp.max(top_p, axis=1, keepdims=True)
        m_c = jnp.max(top_c, axis=1, keepdims=True)
        p1_ref[rs, :] = jnp.exp2((s1 - m_c) * LOG2E).astype(BF16)
        p2_ref[0, rs, :] = jnp.exp2((dp - m_p) * LOG2E).astype(BF16)
        p2_ref[1, rs, :] = jnp.exp2((dc - m_c) * LOG2E).astype(BF16)
        for j in range(1, n):
            m = jnp.where(kinds[j], m_p, m_c)
            p2_ref[j + 1, rs, :] = jnp.exp2((others[j - 1] - m) * LOG2E).astype(BF16)
        lse_ref[0, 0, rs, :] = jnp.broadcast_to(m_p * LOG2E, (step, LANES))
        lse_ref[0, 1, rs, :] = jnp.broadcast_to(m_c * LOG2E, (step, LANES))
        return carry

    lax.fori_loop(0, rows // step, chunk, 0)

    def with_ones(tile):
        return jnp.concatenate([tile, jnp.ones(tile.shape, BF16)], axis=1)

    acc = [nn(p2_ref[b], with_ones(kv_ref[me, b])) for b in range(2)]
    acc[1] = acc[1] + nn(p1_ref[...], with_ones(prompt))
    for j in range(1, n):
        at = lax.rem(me + j, n)
        part = nn(p2_ref[j + 1], with_ones(kv_ref[at, pick_ref[j]]))
        acc[0] = acc[0] + jnp.where(kinds[j], part, 0.0)
        acc[1] = acc[1] + jnp.where(kinds[j], 0.0, part)
    for b in range(2):
        total = acc[b][:, LANES:]
        o_ref[0, b] = acc[b][:, :LANES] / total
        lse_ref[0, b] = lse_ref[0, b] + jnp.log2(total)


def attend_back_kernel(
    n, me_ref, pick_ref, segq_ref, segk_ref, q_ref, kv_ref, do_ref, o_ref, lse_ref, dq_ref, dkv_ref, row_ref, dqt_ref
):
    me = me_ref[0]
    block = kv_ref.shape[2]
    rows = q_ref.shape[2]
    first = (lax.broadcasted_iota(jnp.int32, (8, LANES), 1) == 0).astype(F32)
    ones = jnp.ones((8, LANES), F32)

    def to_row(lhs, matrix):
        return lax.dot_general(
            lhs, matrix, (((1,), (1,)), ((), ())), precision=lax.Precision.HIGHEST,
            preferred_element_type=F32,
        )

    for b in range(2):
        row_ref[b] = to_row(first, lse_ref[0, b])
        row_ref[2 + b] = to_row(ones, do_ref[0, b].astype(F32) * o_ref[0, b])
    lane_rows = lax.rem(lax.broadcasted_iota(jnp.int32, (block, rows), 1), block)
    tri = lax.broadcasted_iota(jnp.int32, (block, rows), 0) <= lane_rows

    def pair(kind, tile, mask):
        q = q_ref[0, kind]
        do = do_ref[0, kind]
        p = jnp.exp2(nt(tile, q) * LOG2E - row_ref[kind, 0:1, :])
        if mask is not None:
            p = jnp.where(mask, p, 0.0)
        ds = (p * (nt(tile, do) - row_ref[2 + kind, 0:1, :])).astype(BF16)
        return nn(ds, q) + nn(p.astype(BF16), do), tn(tile, ds)

    segq = segq_ref[0:1, :]
    same_own = segq == segk_ref[0]
    own0, own1 = kv_ref[me, 0], kv_ref[me, 1]
    d0, q0 = pair(0, own0, tri)
    d1, q1 = pair(1, own1, tri & same_own)
    d2, q2 = pair(1, own0, None)
    dkv_ref[me, 0] = (d0 + d2).astype(dkv_ref.dtype)
    dkv_ref[me, 1] = d1.astype(dkv_ref.dtype)
    dqt_ref[0] = q0
    dqt_ref[1] = q1 + q2

    def other(j, carry):
        at = lax.rem(me + j, n)
        kind = pick_ref[j]
        is_prompt = kind == 0
        full, q_full = pair(1, kv_ref[at, 0], None)
        mask = (segq == segk_ref[j]) | is_prompt
        part, q_part = pair(kind, kv_ref[at, kind], mask)
        dkv_ref[at, 0] = (full + jnp.where(is_prompt, part, 0.0)).astype(dkv_ref.dtype)
        dkv_ref[at, 1] = jnp.where(is_prompt, 0.0, part).astype(dkv_ref.dtype)
        dqt_ref[0] = dqt_ref[0] + jnp.where(is_prompt, q_part, 0.0)
        dqt_ref[1] = dqt_ref[1] + q_full + jnp.where(is_prompt, 0.0, q_part)
        return carry

    lax.fori_loop(1, n, other, 0)
    for b in range(2):
        dq_ref[0, b] = (dqt_ref[b] * 0.125).T


def mid_kernel(sizes, o_ref, x_ref, wo_ref, gain_ref, att_ref, resid_ref, n2_ref):
    heads, kvh, block = sizes
    share = heads // kvh
    for b in range(2):
        columns = []
        for h in range(heads):
            g, i = h // share, h % share
            columns.append(o_ref[g, b, i * block : (i + 1) * block, HD:])
        attended = jnp.concatenate(columns, axis=1).astype(BF16)
        rs = slice(b * block, (b + 1) * block)
        att_ref[rs, :] = attended
        resid = x_ref[rs, :].astype(F32) + nn(attended, wo_ref[...])
        resid_ref[rs, :] = resid
        inverse = lax.rsqrt(jnp.mean(resid * resid, axis=1, keepdims=True) + EPSILON)
        n2_ref[rs, :] = (resid * inverse * gain_ref[...]).astype(BF16)


def branch_kernel(sizes, gb_ref, wo_ref, do_ref):
    heads, kvh, block = sizes
    share = heads // kvh
    grad = nt(gb_ref[...], wo_ref[...]).astype(BF16)
    zero = jnp.zeros((block, HD), BF16)
    for h in range(heads):
        g, i = h // share, h % share
        for b in range(2):
            do_ref[g, b, i * block : (i + 1) * block, :] = jnp.concatenate(
                [zero, grad[b * block : (b + 1) * block, h * HD : (h + 1) * HD]], axis=1
            )


def unrope_kernel(sizes, dq_ref, dkv_ref, cos_ref, sin_ref, out_ref):
    heads, kvh, block = sizes
    share = heads // kvh
    for b in range(2):
        rs = slice(b * block, (b + 1) * block)
        cos, sin = cos_ref[rs, :], -sin_ref[rs, :]
        columns = [
            dq_ref[h // share, b, (h % share) * block : (h % share + 1) * block, :HD]
            for h in range(heads)
        ]
        columns += [dkv_ref[b, :, g * LANES : g * LANES + HD].astype(F32) for g in range(kvh)]
        tiles = []
        for j in range((heads + kvh) // 2):
            pair = jnp.concatenate(columns[2 * j : 2 * j + 2], axis=1)
            tiles.append(rope_tile(pair, cos, sin).astype(BF16))
        values = [dkv_ref[b, :, g * LANES + HD : (g + 1) * LANES].astype(BF16) for g in range(kvh)]
        out_ref[rs, :] = jnp.concatenate(tiles + values, axis=1)


def local_call(kernel, out_shape, name, **extra):
    return pl.pallas_call(
        kernel,
        out_shape=out_shape,
        compiler_params=pltpu.CompilerParams(vmem_limit_bytes=VMEM_LIMIT),
        name=name,
        **extra,
    )


def gather_rows(array, axis):
    return lax.all_gather(array, axis, axis=0, tiled=True)


def norm_back(grad_normed, scaled, inverse, gain):
    weighted = grad_normed * gain
    return inverse * (weighted - scaled * jnp.mean(weighted * scaled, axis=1, keepdims=True))


def general_body(
    tokens, attn_gain, query_weight, key_weight, value_weight, out_weight, mlp_gain, gate_weight,
    up_weight, down_weight, cotangent, cont_lengths, block_deal,
):
    n = lax.axis_size("ctx")
    me = lax.axis_index("ctx")
    row_count, width = tokens.shape[1:]
    kv_width = key_weight.shape[1]
    hidden = gate_weight.shape[1]
    block = row_count // 2
    total_rows = row_count * n
    prompt_size = total_rows // 2
    heads, kvh = width // HD, kv_width // HD
    share = heads // kvh
    stack = share * block
    sizes = (heads, kvh, block)

    deal = block_deal.reshape(n, 2)
    flip = deal[me, 0] > deal[me, 1]

    def ordered(rows):
        halves = rows.reshape(2, block, rows.shape[-1])
        return jnp.where(flip, halves[::-1], halves).reshape(rows.shape)

    x = ordered(tokens[0])
    cot = ordered(cotangent[0])
    naturals = jnp.sort(deal, axis=1)
    natural = naturals[:, :, None] * block + jnp.arange(block, dtype=jnp.int32)
    offset = natural - prompt_size
    lengths = cont_lengths[0]
    ending = jnp.cumsum(lengths)
    segment = jnp.sum((offset[..., None] >= ending).astype(jnp.int32), axis=-1)
    inside = segment[..., None] == jnp.arange(lengths.shape[0], dtype=jnp.int32)
    beginning = jnp.sum(jnp.where(inside, ending - lengths, 0), axis=-1)
    position = jnp.where(offset < 0, natural, prompt_size + offset - beginning)
    own_position = position[me].reshape(row_count)
    frequency = THETA ** (-2.0 * jnp.arange(HD // 2, dtype=F32) / HD)
    angle = own_position.astype(F32)[:, None] * frequency[None, :]
    cos, sin = jnp.cos(angle), jnp.sin(angle)
    cos = jnp.concatenate([cos, cos, cos, cos], axis=1)
    sin = jnp.concatenate([-sin, sin, -sin, sin], axis=1)
    around = (me + jnp.arange(n, dtype=jnp.int32)) % n
    first_natural = naturals[:, 0]
    pick = (first_natural[around] >= first_natural[me]).astype(jnp.int32)
    segk = segment[around, 1]
    segq = jnp.tile(segment[me, 1], share)
    me_arr = me.reshape(1).astype(jnp.int32)

    attn_rows = jnp.concatenate([query_weight, key_weight, value_weight, out_weight], axis=1)
    w_attn = gather_rows(attn_rows, "fsdp")
    qkv_width = width + 2 * kv_width
    w_qkv = w_attn[:, :qkv_width]
    w_out = w_attn[:, qkv_width:]
    gain_one = gather_rows(attn_gain, "fsdp").astype(F32)
    gain_two = gather_rows(mlp_gain, "fsdp").astype(F32)
    w_gate = gather_rows(gate_weight, "fsdp")
    w_up = gather_rows(up_weight, "fsdp")
    w_down = gather_rows(down_weight, "fsdp")

    normed_one, q, kv = local_call(
        functools.partial(project_kernel, sizes),
        (
            whole((row_count, width), BF16),
            whole((kvh, 2, stack, LANES), BF16),
            whole((2, block, kvh * LANES), BF16),
        ),
        "project",
    )(x, gain_one[None], w_attn, cos, sin)
    kv_all = lax.all_gather(kv, "ctx", axis=0)

    smem = pl.BlockSpec(memory_space=pltpu.SMEM)
    per_group = pl.BlockSpec((1, 2, stack, LANES), lambda g: (g, 0, 0, 0))
    kv_spec = pl.BlockSpec((n, 2, block, LANES), lambda g: (0, 0, 0, g))

    def full(array):
        rank = array.ndim
        return pl.BlockSpec(array.shape, lambda g: (0,) * rank)

    segq_col, segk_row = segq[:, None], segk[:, None, :]
    attended_heads, lse = local_call(
        functools.partial(attend_kernel, n),
        (whole((kvh, 2, stack, LANES), F32), whole((kvh, 2, stack, LANES), F32)),
        "attend",
        grid=(kvh,),
        in_specs=[smem, smem, full(segq_col), full(segk_row), per_group, kv_spec],
        out_specs=(per_group, per_group),
        scratch_shapes=[
            pltpu.VMEM((stack, n * block), F32),
            pltpu.VMEM((stack, n * block), BF16),
            pltpu.VMEM((n + 1, stack, block), F32),
            pltpu.VMEM((n + 1, stack, block), BF16),
        ],
    )(me_arr, pick, segq_col, segk_row, q, kv_all)

    attended, resid, normed_two = local_call(
        functools.partial(mid_kernel, sizes),
        (
            whole((row_count, width), BF16),
            whole((row_count, width), F32),
            whole((row_count, width), BF16),
        ),
        "mid",
    )(attended_heads, x, w_out, gain_two[None])

    inverse_two = lax.rsqrt(jnp.mean(resid * resid, axis=1, keepdims=True) + EPSILON)
    scaled_two = resid * inverse_two
    gate = nn(normed_two, w_gate)
    upward = nn(normed_two, w_up)
    sigma = jax.nn.sigmoid(gate)
    activated = gate * sigma
    product = (activated * upward).astype(BF16)
    result = resid + nn(product, w_down)
    grad_prod = nt(cot, w_down)
    grad_gate = (grad_prod * upward * sigma * (1.0 + gate * (1.0 - sigma))).astype(BF16)
    grad_up = (grad_prod * activated).astype(BF16)
    grad_normed_two = nt(grad_gate, w_gate) + nt(grad_up, w_up)
    gain_two_part = jnp.sum(grad_normed_two * scaled_two, axis=0)
    grad_resid = cot.astype(F32) + norm_back(grad_normed_two, scaled_two, inverse_two, gain_two)
    grad_branch = grad_resid.astype(BF16)

    grad_heads = local_call(
        functools.partial(branch_kernel, sizes), whole((kvh, 2, stack, LANES), BF16), "branch"
    )(grad_branch, w_out)

    segq_row, segk_col = segq[None, :], segk[:, :, None]
    grad_query, grad_kv = local_call(
        functools.partial(attend_back_kernel, n),
        (whole((kvh, 2, stack, LANES), F32), whole((n, 2, block, kvh * LANES), F32)),
        "attend_back",
        grid=(kvh,),
        in_specs=[smem, smem, full(segq_row), full(segk_col)]
        + [per_group, kv_spec, per_group, per_group, per_group],
        out_specs=(per_group, kv_spec),
        scratch_shapes=[
            pltpu.VMEM((4, 8, stack), F32),
            pltpu.VMEM((2, LANES, stack), F32),
        ],
    )(me_arr, pick, segq_row, segk_col, q, kv_all, grad_heads, attended_heads, lse)

    kv_sum = lax.psum_scatter(grad_kv, "ctx", scatter_dimension=0, tiled=False)
    grad_projected = local_call(
        functools.partial(unrope_kernel, sizes), whole((row_count, qkv_width), BF16), "unrope"
    )(grad_query, kv_sum, cos, sin)

    x_float = x.astype(F32)
    inverse_one = lax.rsqrt(jnp.mean(x_float * x_float, axis=1, keepdims=True) + EPSILON)
    scaled_one = x_float * inverse_one
    grad_normed_one = nt(grad_projected, w_qkv)
    gain_one_part = jnp.sum(grad_normed_one * scaled_one, axis=0)
    tokens_grad = (
        grad_resid + norm_back(grad_normed_one, scaled_one, inverse_one, gain_one)
    ).astype(BF16)

    def spread(partial):
        rows = lax.psum_scatter(partial.astype(BF16), "fsdp", scatter_dimension=0, tiled=True)
        return lax.psum(rows, "ctx").astype(F32)

    grad_gate_w = spread(tn(normed_two, grad_gate))
    grad_up_w = spread(tn(normed_two, grad_up))
    grad_down_w = spread(tn(product, cot))
    grad_out_w = spread(tn(attended, grad_branch))
    grad_qkv_w = spread(tn(normed_one, grad_projected))
    gains = spread(jnp.stack([gain_one_part, gain_two_part], axis=1))
    return (
        ordered(result.astype(BF16))[None],
        ordered(tokens_grad)[None],
        gains[:, 0],
        grad_qkv_w[:, :width],
        grad_qkv_w[:, width : width + kv_width],
        grad_qkv_w[:, width + kv_width :],
        grad_out_w,
        gains[:, 1],
        grad_gate_w,
        grad_up_w,
        grad_down_w,
    )


def solution(mesh):
    rows, matrix, vector = P("fsdp", "ctx", None), P("fsdp", None), P("fsdp")
    cube = dict(mesh.shape) == {"ctx": 8, "fsdp": 4}
    return jax.shard_map(
        cube_body if cube else general_body,
        mesh=mesh,
        in_specs=(rows, vector, matrix, matrix, matrix, matrix, vector, matrix, matrix, matrix)
        + (rows, matrix, P()),
        out_specs=(rows, rows, vector, matrix, matrix, matrix, matrix, vector, matrix, matrix, matrix),
        check_vma=False,
    )
```

```python
import functools

import jax
import jax.numpy as jnp
from jax import lax
from jax.experimental import pallas as pl
from jax.experimental.pallas import tpu as pltpu
from jax.sharding import PartitionSpec as P

HD = 64
LANES = 128
EPSILON = 1e-05
THETA = 100000.0
MASKED = -1e30
LOG2E = 1.4426950408889634
VMEM_LIMIT = 63 * 1024 * 1024
F32 = jnp.float32
BF16 = jnp.bfloat16


def nt(left, right):
    return lax.dot_general(left, right, (((1,), (1,)), ((), ())), preferred_element_type=F32)


def nn(left, right):
    return lax.dot_general(left, right, (((1,), (0,)), ((), ())), preferred_element_type=F32)


def tn(left, right):
    return lax.dot_general(left, right, (((0,), (0,)), ((), ())), preferred_element_type=F32)


def rope_tile(tile, cos, sin):
    lane = lax.broadcasted_iota(jnp.int32, tile.shape, 1) % HD
    partner = jnp.where(
        lane < HD // 2,
        pltpu.roll(tile, LANES - HD // 2, 1),
        pltpu.roll(tile, HD // 2, 1),
    )
    return tile * cos + partner * sin


def head_of(tiles, index):
    start = (index % 2) * HD
    return tiles[index // 2][:, start : start + HD]


MESH = pl.DeviceIdType.MESH
ATTN, FF, DOWN = 0, 1, 2
CORE, FIRST, SECOND = -1, -2, -3


class Links:
    def __init__(self, core, fsdp, send, recv, plan):
        self.core = core
        self.fsdp = fsdp
        self.ctx = lax.axis_index("ctx")
        self.z = lax.axis_index("fsdp")
        self.chip = self.ctx // 2
        self.first = 1 if core == 0 else 2
        self.second = 3 - self.first
        self.send_sem, self.recv_sem = send, recv
        self.plan = plan
        self.open = []

    def target(self, hop):
        if hop == CORE:
            return (lax.bitwise_xor(self.ctx, 1), self.z)
        if hop == FIRST:
            return (lax.bitwise_xor(self.ctx, 2 * self.first), self.z)
        if hop == SECOND:
            return (lax.bitwise_xor(self.ctx, 2 * self.second), self.z)
        return (self.ctx, lax.bitwise_xor(self.z, hop))

    def copy(self, key, hop, src, dst):
        slot = self.plan.setdefault(key, len(self.plan))
        return pltpu.make_async_remote_copy(
            src_ref=src,
            dst_ref=dst,
            send_sem=self.send_sem.at[slot],
            recv_sem=self.recv_sem.at[slot],
            device_id=self.target(hop),
            device_id_type=MESH,
        )

    def send(self, key, hop, src, dst):
        copy = self.copy(key, hop, src, dst)
        copy.start()
        self.open.append((key, getattr(src, "ref", src), src.shape))

    def landed(self, key, dst):
        self.copy(key, CORE, dst, dst).wait_recv()

    def drain(self):
        for key, base, shape in self.open:
            at = (0,) * (len(base.shape) - len(shape)) + tuple(pl.ds(0, size) for size in shape)
            self.copy(key, CORE, base.at[at], base.at[at]).wait_send()


def greet(hops, fsdp):
    ctx, z = lax.axis_index("ctx"), lax.axis_index("fsdp")
    barrier = pltpu.get_barrier_semaphore()
    targets = [(lax.bitwise_xor(ctx, h), z) for h in (1, 2, 4)]
    if "z" in hops:
        targets += [(ctx, lax.bitwise_xor(z, d)) for d in range(1, fsdp)]
    for target in targets:
        pl.semaphore_signal(barrier, inc=1, device_id=target, device_id_type=MESH)
    pl.semaphore_wait(barrier, len(targets))


def by_core(program):
    for core in (0, 1):
        pl.when(lax.axis_index("ctx") % 2 == core)(functools.partial(program, core))


def sub(base, size, unit):
    return pl.ds(pl.multiple_of(base, unit), size)


def lanes(ref, tiles, rows=slice(None)):
    return jnp.concatenate([ref[t, rows, :] for t in tiles], axis=1)


def flat_lanes(ref, tiles, shard):
    stacked = [
        jnp.concatenate([ref[zi, t * shard : (t + 1) * shard, :] for zi in range(ref.shape[0])], axis=0)
        for t in tiles
    ]
    return jnp.concatenate(stacked, axis=1)


def pack_tiles(parts):
    matrix = jnp.concatenate(parts, axis=1)
    short = -matrix.shape[1] % LANES
    if short:
        matrix = jnp.concatenate([matrix, jnp.zeros((matrix.shape[0], short), matrix.dtype)], axis=1)
    return [matrix[:, t * LANES : (t + 1) * LANES] for t in range(matrix.shape[1] // LANES)]


class Share:
    def __init__(self, name, core, shard):
        self.name, self.core = name, core
        self.shard = shard
        self.offset, self.rows = 0, shard
        if name == ATTN:
            half = -(-shard // 32) * 16
            self.offset, self.rows = (0, half) if core == 0 else (half, shard - half)

    def at(self, ref, zi, q):
        rows = sub(zi * self.shard + self.offset, self.rows, 16)
        if self.name == ATTN:
            return ref.at[pl.ds(q * (ref.shape[0] // 4), ref.shape[0] // 4), rows]
        if self.name == FF:
            return ref.at[self.core, pl.ds(q * (ref.shape[1] // 4), ref.shape[1] // 4), rows]
        return ref.at[2 * q + self.core, rows]

    def buffer(self, ref):
        return ref.at[:, pl.ds(0, self.rows)] if self.name == ATTN else ref


class Flat:
    def __init__(self, core):
        self.core = core

    def at(self, ref, zi, q):
        size = ref.shape[1] // 8
        return ref.at[zi, sub((2 * q + self.core) * size, size, 16)]


PACKAGES = (ATTN, FF, DOWN)
QKV, OUT = 3, 4
GATHERED = (QKV, OUT, FF, DOWN)
FINISH = 0


def both_cores(make):
    tables = [make(0), make(1)]

    def run(*names):
        for core in (0, 1):
            def program(core=core):
                for name in names:
                    tables[core][name]()

            pl.when(lax.axis_index("ctx") % 2 == core)(program)

    return run


def weight_stages(core, fsdp, plan, refs, send, recv):
    links = Links(core, fsdp, send, recv, plan)
    z, chip = links.z, links.chip
    near, far = lax.bitwise_xor(chip, links.first), lax.bitwise_xor(chip, links.second)
    corner = lax.bitwise_xor(chip, 3)
    shards = {FF: refs[FF].shape[2] // fsdp, DOWN: refs[DOWN].shape[1] // fsdp}

    def shares(core):
        cut = {k: Share(k, core, shards[k]) for k in shards}
        return {**cut, QKV: Flat(core), OUT: Flat(core)}

    mine, twin = shares(core), shares(1 - core)
    stages = {}

    def over_z(k):
        here = mine[k].at(refs[k], z, chip)
        for d in range(1, fsdp):
            links.send((k, "z", d), d, here, here)

    def spread(k):
        for d in range(1, fsdp):
            piece = mine[k].at(refs[k], lax.bitwise_xor(z, d), chip)
            links.landed((k, "z", d), piece)
            links.send((k, FIRST, d), FIRST, piece, piece)
            links.send((k, SECOND, d), SECOND, piece, piece)
            links.send((k, CORE, d, 0), CORE, piece, piece)

    def forward(k):
        for d in range(1, fsdp):
            piece = mine[k].at(refs[k], lax.bitwise_xor(z, d), near)
            links.landed((k, FIRST, d), piece)
            links.send((k, "corner", d), SECOND, piece, piece)
            links.send((k, CORE, d, 1), CORE, piece, piece)

    def pass_some(k, i, what, q):
        for d in range(1, fsdp):
            piece = mine[k].at(refs[k], lax.bitwise_xor(z, d), q)
            links.landed((k, what, d), piece)
            links.send((k, CORE, d, i), CORE, piece, piece)

    def pass_far(k):
        pass_some(k, 2, SECOND, far)

    def pass_corner(k):
        pass_some(k, 3, "corner", corner)

    def finish_some(k, i, q):
        for d in range(1, fsdp):
            links.landed((k, CORE, d, i), twin[k].at(refs[k], lax.bitwise_xor(z, d), q))

    def finish(k):
        for i in range(4):
            stages[FINISH, k, i]()

    for k in GATHERED:
        for i, q in ((0, chip), (1, far), (2, near), (3, corner)):
            stages[FINISH, k, i] = functools.partial(finish_some, k, i, q)
    for k in GATHERED:
        for fn in (over_z, spread, forward, pass_far, pass_corner, finish):
            stages[fn.__name__, k] = functools.partial(fn, k)

    def gains_out():
        for d in range(1, fsdp):
            links.send(("gains", d), d, refs["gains"].at[z], refs["gains"].at[z])

    def gains_in():
        for d in range(1, fsdp):
            links.landed(("gains", d), refs["gains"].at[lax.bitwise_xor(z, d)])

    stages["gains_out"], stages["gains_in"], stages["drain"] = gains_out, gains_in, links.drain
    return stages


def kv_stages(core, plan, kv_all, send, recv):
    links = Links(core, 1, send, recv, plan)
    ctx = links.ctx
    near = lax.bitwise_xor(ctx, 2 * links.first)
    far = lax.bitwise_xor(ctx, 2 * links.second)
    corner = lax.bitwise_xor(ctx, 6)

    def start():
        for b in range(2):
            piece = kv_all.at[ctx, b]
            links.send(("kv first", b), FIRST, piece, piece)
            links.send(("kv second", b), SECOND, piece, piece)
            links.send(("kv core", 0, b), CORE, piece, piece)

    def forward():
        for b in range(2):
            piece = kv_all.at[near, b]
            links.landed(("kv first", b), piece)
            links.send(("kv corner", b), SECOND, piece, piece)
            links.send(("kv core", 1, b), CORE, piece, piece)

    def pass_some(i, what, owner):
        for b in range(2):
            piece = kv_all.at[owner, b]
            links.landed((what, b), piece)
            links.send(("kv core", i, b), CORE, piece, piece)

    def finish(i, owner):
        for b in range(2):
            links.landed(("kv core", i, b), kv_all.at[lax.bitwise_xor(owner, 1), b])

    stages = {"start": start, "forward": forward, "drain": links.drain}
    stages["pass_far"] = functools.partial(pass_some, 2, "kv second", far)
    stages["pass_corner"] = functools.partial(pass_some, 3, "kv corner", corner)
    for i, owner in ((0, ctx), (1, far), (2, near), (3, corner)):
        stages[FINISH, i] = functools.partial(finish, i, owner)
    return stages


def store_projection(sizes, raw_tiles, cos, sin, q_ref, kv_at):
    heads, kvh, block = sizes
    share = heads // kvh
    tiles = [rope_tile(raw_tiles[j], cos, sin).astype(BF16) for j in range((heads + kvh) // 2)]
    tiles += [raw_tiles[j].astype(BF16) for j in range((heads + kvh) // 2, len(raw_tiles))]

    def head(index):
        start = (index % 2) * HD
        return tiles[index // 2][:, start : start + HD]

    zero = jnp.zeros((block, HD), BF16)
    for h in range(heads):
        piece = head(h) * jnp.asarray(0.125, BF16)
        g, i = h // share, h % share
        for b in range(2):
            q_ref[g, b, i * block : (i + 1) * block, :] = jnp.concatenate(
                [piece[b * block : (b + 1) * block], zero], axis=1
            )
    for g in range(kvh):
        pair = jnp.concatenate([head(heads + g), head(heads + kvh + g)], axis=1)
        for b in range(2):
            kv_at(b, g)[...] = pair[b * block : (b + 1) * block]


def rms_inverse(x):
    return lax.rsqrt(jnp.mean(x * x, axis=1, keepdims=True) + EPSILON)


def natural_blocks(deal_ref, c):
    one, two = deal_ref[2 * c], deal_ref[2 * c + 1]
    return jnp.minimum(one, two), jnp.maximum(one, two)


def segment_start(lengths_ref, offset):
    start = jnp.zeros_like(offset)
    ending = 0
    for c in range(lengths_ref.shape[1]):
        ending = ending + lengths_ref[0, c]
        start = jnp.where(offset >= ending, ending, start)
    return start


def ordered(flip, rows):
    half = rows.shape[0] // 2
    return jnp.where(flip, jnp.concatenate([rows[half:], rows[:half]], axis=0), rows)


def first_keys(n, deal_ref, lengths_ref, block, rows):
    _, last = natural_blocks(deal_ref, lax.axis_index("ctx"))
    offset = (last - n) * block + lax.rem(lax.broadcasted_iota(jnp.int32, (8, rows), 1), block)
    return segment_start(lengths_ref, offset)


def attend_masks(n, deal_ref, start_ref, block, rows):
    key = lax.broadcasted_iota(jnp.int32, (block, rows), 0)

    def own(b):
        allowed = key <= lax.rem(lax.broadcasted_iota(jnp.int32, (block, rows), 1), block)
        if b == 0:
            return allowed
        _, last = natural_blocks(deal_ref, lax.axis_index("ctx"))
        return allowed & (key >= start_ref[0:1, :] - (last - n) * block)

    def other(at):
        mine, _ = natural_blocks(deal_ref, lax.axis_index("ctx"))
        first, last = natural_blocks(deal_ref, at)
        kind = jnp.where(first >= mine, 1, 0)
        bound = jnp.where(kind == 0, -1, start_ref[0:1, :] - (last - n) * block)
        return kind, key >= bound

    return own, other


def attend_step(n, me, g, at, deal_ref, start_ref, q_ref, kv_ref, top_ref, acc_ref):
    block = kv_ref.shape[3]
    rows = q_ref.shape[2]
    value_lane = lax.broadcasted_iota(jnp.int32, (block, LANES), 1) >= HD
    own_mask, other_mask = attend_masks(n, deal_ref, start_ref, block, rows)

    def scores(kind, tile, mask):
        s = nt(tile, q_ref[g, kind])
        return s if mask is None else jnp.where(mask, s, MASKED)

    def weigh(s, top, tile):
        p = jnp.exp2((s - top) * LOG2E).astype(BF16)
        return tn(jnp.where(value_lane, tile, jnp.asarray(1, BF16)), p)

    def own():
        own0, own1 = kv_ref[me, 0, g], kv_ref[me, 1, g]
        s0 = scores(0, own0, own_mask(0))
        top0 = jnp.max(s0, axis=0, keepdims=True)
        acc_ref[g, 0] = weigh(s0, top0, own0)
        top_ref[g, 0] = jnp.broadcast_to(top0, top_ref.shape[2:])
        s1 = scores(1, own1, own_mask(1))
        s2 = scores(1, own0, None)
        top1 = jnp.maximum(jnp.max(s1, axis=0, keepdims=True), jnp.max(s2, axis=0, keepdims=True))
        acc_ref[g, 1] = weigh(s1, top1, own1) + weigh(s2, top1, own0)
        top_ref[g, 1] = jnp.broadcast_to(top1, top_ref.shape[2:])

    def other():
        kind, mask = other_mask(at)
        is_prompt = kind == 0
        tile0 = kv_ref[at, 0, g]
        tile1 = jnp.where(is_prompt, tile0, kv_ref[at, 1, g])
        s1 = scores(1, tile0, None)
        s2 = scores(kind, tile1, mask)
        old_p, old_c = top_ref[g, 0, 0:1, :], top_ref[g, 1, 0:1, :]
        high1 = jnp.max(s1, axis=0, keepdims=True)
        high2 = jnp.max(s2, axis=0, keepdims=True)
        top_p = jnp.where(is_prompt, jnp.maximum(old_p, high2), old_p)
        top_c = jnp.maximum(old_c, jnp.where(is_prompt, high1, jnp.maximum(high1, high2)))
        part1 = weigh(s1, top_c, tile0)
        part2 = weigh(s2, jnp.where(is_prompt, top_p, top_c), tile1)
        acc_ref[g, 0] = acc_ref[g, 0] * jnp.exp2((old_p - top_p) * LOG2E) + jnp.where(is_prompt, part2, 0.0)
        acc_ref[g, 1] = (
            acc_ref[g, 1] * jnp.exp2((old_c - top_c) * LOG2E) + part1 + jnp.where(is_prompt, 0.0, part2)
        )
        top_ref[g, 0] = jnp.broadcast_to(top_p, top_ref.shape[2:])
        top_ref[g, 1] = jnp.broadcast_to(top_c, top_ref.shape[2:])

    return own, other


def attend_close(g, top_ref, acc_ref, o_ref, lse_ref):
    for b in range(2):
        acc = acc_ref[g, b]
        total = acc[0:1, :]
        o_ref[g, b] = (acc / total).T
        lse_ref[g, b] = jnp.broadcast_to(top_ref[g, b, 0:1, :] * LOG2E + jnp.log2(total), lse_ref.shape[2:])


def attend_back_step(n, me, g, j, deal_ref, start_ref, q_ref, kv_ref, do_ref, lse_ref, delta_ref, dqt_ref, dkv_ref):
    block = kv_ref.shape[3]
    rows = q_ref.shape[2]
    own_mask, other_mask = attend_masks(n, deal_ref, start_ref, block, rows)

    def pair(kind, tile, mask):
        q = q_ref[g, kind]
        do = do_ref[g, kind]
        p = jnp.exp2(nt(tile, q) * LOG2E - lse_ref[g, kind, 0:1, :])
        if mask is not None:
            p = jnp.where(mask, p, 0.0)
        ds = (p * (nt(tile, do) - delta_ref[g, kind, 0:1, :])).astype(BF16)
        return nn(ds, q) + nn(p.astype(BF16), do), tn(tile, ds)

    def own():
        own0, own1 = kv_ref[me, 0, g], kv_ref[me, 1, g]
        d0, q0 = pair(0, own0, own_mask(0))
        d1, q1 = pair(1, own1, own_mask(1))
        d2, q2 = pair(1, own0, None)
        dkv_ref[me, g, 0] = (d0 + d2).astype(dkv_ref.dtype)
        dkv_ref[me, g, 1] = d1.astype(dkv_ref.dtype)
        dqt_ref[0] = q0
        dqt_ref[1] = q1 + q2

    def other():
        at = lax.rem(me + j, n)
        kind, mask = other_mask(at)
        is_prompt = kind == 0
        full, q_full = pair(1, kv_ref[at, 0, g], None)
        part, q_part = pair(kind, kv_ref[at, kind, g], mask)
        dkv_ref[at, g, 0] = (full + jnp.where(is_prompt, part, 0.0)).astype(dkv_ref.dtype)
        dkv_ref[at, g, 1] = jnp.where(is_prompt, 0.0, part).astype(dkv_ref.dtype)
        dqt_ref[0] = dqt_ref[0] + jnp.where(is_prompt, q_part, 0.0)
        dqt_ref[1] = dqt_ref[1] + q_full + jnp.where(is_prompt, 0.0, q_part)

    return own, other


def row_deltas(g, do_ref, o_ref, row_ref):
    ones = jnp.ones((8, LANES), F32)
    for b in range(2):
        row_ref[b] = lax.dot_general(
            ones, do_ref[g, b].astype(F32) * o_ref[g, b], (((1,), (1,)), ((), ())),
            precision=lax.Precision.HIGHEST, preferred_element_type=F32,
        )


def gain_row(gains_ref, which, fsdp, shard):
    return jnp.concatenate([gains_ref[i, which : which + 1, :shard] for i in range(fsdp)], axis=1)


def project(sizes, fsdp, x_ref, gains_ref, attn_ref, cos_ref, sin_ref, n1_ref, q_ref, kv_at):
    heads, kvh, block = sizes
    x = x_ref[...].astype(F32)
    normed = (x * rms_inverse(x) * gain_row(gains_ref, 0, fsdp, x.shape[1] // fsdp)).astype(BF16)
    n1_ref[...] = normed
    count = -(-(heads + 2 * kvh) * HD // LANES)
    shard = x.shape[1] // fsdp
    raw = []
    for t in range(0, count, 2):
        some = range(t, min(t + 2, count))
        wide = nn(normed, flat_lanes(attn_ref, some, shard))
        raw += [wide[:, i * LANES : (i + 1) * LANES] for i in range(len(some))]
    store_projection(sizes, raw, cos_ref[...], sin_ref[...], q_ref, kv_at)


def front_kernel(
    sizes, n, fsdp, plans, deal_ref, lengths_ref, xt_ref, gains_in, turns_ref,
    wq_ref, wkt_ref, wvt_ref, wo_ref, wg_ref, wu_ref, wdt_ref, cott_ref,
    x_ref, cos_ref, sin_ref, n1_ref, q_ref, kv_out, lse_ref, gains_ref, qkv_out,
    result_ref, gr_ref, do_ref, delta_ref, gain_ref, out_grad, ff_grad, down_grad,
    qkv, wout, ff, down, kv_all, o_ref, gains, start_ref, top_ref, acc_ref, cot_ref,
    resid_ref, n2_ref, product_ref, gg_ref, gu_ref, turned_ref, gn_ref, out_stage, ff_stage, down_stage,
    send, recv, kv_send, kv_recv, local, out_sem,
):
    heads, kvh, block = sizes
    me, z = lax.axis_index("ctx"), lax.axis_index("fsdp")
    shard = wq_ref.shape[0]
    rows = sub(z * shard, shard, 16)
    for ref, parts in ((qkv, [wq_ref[...], wkt_ref[...].T, wvt_ref[...].T]), (wout, [wo_ref[...]])):
        for t, tile in enumerate(pack_tiles(parts)):
            ref[z, t * shard : (t + 1) * shard, :] = tile
    used = -(-(heads + 2 * kvh) * HD // LANES) * shard
    qkv[z, used:, :] = jnp.zeros((qkv.shape[1] - used, LANES), BF16)
    gains[z] = gains_in[...]
    greet("z", fsdp)
    refs = {QKV: qkv, OUT: wout, FF: ff, DOWN: down, "gains": gains}
    run = both_cores(lambda core: weight_stages(core, fsdp, plans[0], refs, send, recv))
    run_kv = both_cores(lambda core: kv_stages(core, plans[1], kv_all, kv_send, kv_recv))
    run("gains_out", ("over_z", QKV))
    for t in range(ff.shape[1]):
        ff[0, t, rows, :] = wg_ref[:, t * LANES : (t + 1) * LANES]
        ff[1, t, rows, :] = wu_ref[:, t * LANES : (t + 1) * LANES]
    down_shard = wdt_ref.shape[1]
    down_rows = sub(z * down_shard, down_shard, 16)
    for t, tile in enumerate(pack_tiles([wdt_ref[...].T])):
        down[t, down_rows, :] = tile
    first, last = natural_blocks(deal_ref, me)
    flip = deal_ref[2 * me] > deal_ref[2 * me + 1]
    x_ref[...] = ordered(flip, xt_ref[...].T)
    cot_ref[...] = ordered(flip, cott_ref[...].T)
    row = lax.broadcasted_iota(jnp.int32, cos_ref.shape, 0)
    natural = jnp.where(row < block, first * block + row, (last - 1) * block + row)
    offset = natural - n * block
    position = jnp.where(offset < 0, natural, natural - segment_start(lengths_ref, offset))
    angle = position.astype(F32) * turns_ref[0:1, :]
    lane = lax.broadcasted_iota(jnp.int32, cos_ref.shape, 1)
    cos_ref[...] = jnp.cos(angle)
    sine = jnp.sin(angle)
    sin_ref[...] = jnp.where(lax.rem(lane, HD) < HD // 2, -sine, sine)
    start_ref[...] = first_keys(n, deal_ref, lengths_ref, block, start_ref.shape[1])
    run(("spread", QKV), ("over_z", OUT), ("over_z", DOWN), ("over_z", FF), ("forward", QKV))
    run(("pass_far", QKV), ("pass_corner", QKV), ("finish", QKV), "gains_in")
    project(
        sizes, fsdp, x_ref, gains, qkv, cos_ref, sin_ref, n1_ref, q_ref,
        lambda b, g: kv_all.at[me, b, g],
    )
    run_kv("start")
    gains_ref[...] = gains[...]
    outs = [pltpu.make_async_copy(qkv, qkv_out, local.at[0]), pltpu.make_async_copy(kv_all, kv_out, local.at[1])]
    outs[0].start()
    kv_schedule = {
        kvh: ((FINISH, 0),),
        2 * kvh: ("forward", "pass_far"),
        4 * kvh: ((FINISH, 1), (FINISH, 2)),
        6 * kvh: ("pass_corner",),
        7 * kvh: ((FINISH, 3),),
    }
    schedule = {
        3: (("spread", OUT),),
        11: (("spread", DOWN),),
        14: (("forward", OUT),),
        18: (("forward", DOWN),),
        20: (("spread", FF),),
        24: (("pass_far", OUT), ("pass_corner", OUT)),
        28: (("pass_far", DOWN), ("pass_corner", DOWN)),
        32: (("forward", FF),),
        38: (("finish", OUT), ("finish", DOWN)),
    }

    @pl.loop(0, kvh * n)
    def _(step):
        j, g = step // kvh, step % kvh
        turn = jnp.where(j == 3, 4, jnp.where(j == 4, 3, j))
        for at, names in kv_schedule.items():
            pl.when(step == at)(functools.partial(run_kv, *names))
        for at, names in schedule.items():
            pl.when(step == at)(functools.partial(run, *names))
        own, other = attend_step(
            n, me, g, lax.bitwise_xor(me, turn), deal_ref, start_ref, q_ref, kv_all, top_ref, acc_ref
        )
        pl.when(j == 0)(own)
        pl.when(j > 0)(other)
        pl.when(j == n - 1)(lambda: attend_close(g, top_ref, acc_ref, o_ref, lse_ref))

    outs[1].start()
    run(("pass_far", FF))

    def quarter_ready(i):
        pl.when(i == 0)(lambda: run((FINISH, FF, 0)))
        pl.when(i == 1)(lambda: run((FINISH, FF, 1), (FINISH, FF, 2)))
        pl.when(i == 3)(lambda: run(("pass_corner", FF), (FINISH, FF, 3)))
        return lax.bitwise_xor(me // 2, i)

    feed_forward(
        sizes, fsdp, quarter_ready, x_ref, cot_ref, gains, wout, ff, down, o_ref,
        result_ref, gr_ref, do_ref, delta_ref, gain_ref, out_grad, ff_grad, down_grad,
        resid_ref, n2_ref, product_ref, gg_ref, gu_ref, turned_ref, gn_ref, out_stage, ff_stage, down_stage, out_sem,
    )
    run("drain")
    run_kv("drain")
    for copy in outs:
        copy.wait()


def head_columns(sizes, ref, low):
    heads, kvh, block = sizes
    share = heads // kvh
    return jnp.concatenate(
        [
            jnp.concatenate(
                [
                    ref[h // share, b, (h % share) * block : (h % share + 1) * block, low : low + HD]
                    for h in range(heads)
                ],
                axis=1,
            )
            for b in range(2)
        ],
        axis=0,
    )


def feed_forward(
    sizes, fsdp, quarter_ready, x_ref, cot_ref, gains_ref, wout_ref, ff_ref, down_ref, o_ref,
    result_ref, gr_ref, do_ref, delta_ref, gain_ref, out_grad, ff_grad, down_grad,
    resid_ref, n2_ref, product_ref, gg_ref, gu_ref, turned_ref, gn_ref, out_stage, ff_stage, down_stage, sem,
):
    heads, kvh, block = sizes
    share = heads // kvh
    rows, width = x_ref.shape
    shard = width // fsdp
    half = (heads + 2 * kvh) * HD % LANES
    out_tiles = -(-width // LANES)
    down_tiles = down_ref.shape[0]
    gain = gain_row(gains_ref, 1, fsdp, width // fsdp)
    attended = head_columns(sizes, o_ref, HD).astype(BF16)
    pieces = []
    for t in range(0, out_tiles, 2):
        pieces.append(nn(attended, flat_lanes(wout_ref, range(t, min(t + 2, out_tiles)), shard)))
    resid = x_ref[...].astype(F32) + jnp.concatenate(pieces, axis=1)[:, :width]
    resid_ref[...] = resid
    n2_ref[...] = (resid * rms_inverse(resid) * gain).astype(BF16)
    pad = down_tiles * LANES - width
    wide = 2 * LANES
    per = ff_ref.shape[1] // 4
    turned_ref[...] = n2_ref[...].T
    gn_ref[...] = jnp.zeros(gn_ref.shape, F32)
    gr_ref[...] = jnp.zeros(gr_ref.shape, F32)

    def moves(q):
        columns = sub(q * per * LANES, per * LANES, LANES)
        return (
            pltpu.make_async_copy(ff_stage, ff_grad.at[:, pl.ds(q * per, per)], sem.at[0]),
            pltpu.make_async_copy(down_stage, down_grad.at[:, columns], sem.at[1]),
        )

    @pl.loop(0, 4)
    def _(i):
        q = quarter_ready(i)
        cot_wide = jnp.concatenate([cot_ref[...], jnp.zeros((rows, pad), BF16)], axis=1)
        for low in range(0, per, 2):
            size = min(2, per - low)
            first = q * per + low
            at = sub(first * LANES, size * LANES, LANES)
            n2 = n2_ref[...]
            gate = nn(n2, jnp.concatenate([ff_ref[0, first + t] for t in range(size)], axis=1))
            upward = nn(n2, jnp.concatenate([ff_ref[1, first + t] for t in range(size)], axis=1))
            grad = nt(cot_wide, jnp.concatenate([down_ref[t, at, :] for t in range(down_tiles)], axis=1))
            sigma = 1.0 / (1.0 + jnp.exp(-gate))
            activated = gate * sigma
            here = slice(low * LANES, (low + size) * LANES)
            product_ref[:, here] = (activated * upward).astype(BF16)
            gg_ref[:, here] = (grad * upward * (sigma + activated * (1.0 - sigma))).astype(BF16)
            gu_ref[:, here] = (grad * activated).astype(BF16)
        for low in range(0, width, wide):
            size = min(wide, width - low)
            part = 0.0
            for c, grad_ref in enumerate((gg_ref, gu_ref)):
                weights = [ff_ref[c, q * per + t, low : low + size, :] for t in range(per)]
                part = part + nt(grad_ref[...], jnp.concatenate(weights, axis=1))
            gn_ref[:, low : low + size] = gn_ref[:, low : low + size] + part
        columns = sub(q * per * LANES, per * LANES, LANES)
        for t in range(0, down_tiles, 2):
            low, high = t * LANES, min((t + 2) * LANES, width)
            weights = jnp.concatenate([down_ref[t, columns, :], down_ref[t + 1, columns, :]], axis=1)
            part = nn(product_ref[...], weights)
            gr_ref[:, low:high] = gr_ref[:, low:high] + part[:, : high - low]

        @pl.when(i >= 1)
        def _():
            for copy in moves(q):
                copy.wait()

        for low in range(0, per, 2):
            size = min(2, per - low)
            here = slice(low * LANES, (low + size) * LANES)
            for c, grad_ref in enumerate((gg_ref, gu_ref)):
                part = nn(turned_ref[...], grad_ref[:, here]).astype(BF16)
                for t in range(size):
                    ff_stage[c, low + t] = part[:, t * LANES : (t + 1) * LANES]
            part = nn(product_ref[:, here].T, cot_wide).astype(BF16)
            for t in range(down_tiles):
                down_stage[t, here, :] = part[:, t * LANES : (t + 1) * LANES]
        for copy in moves(q):
            copy.start()

    result_ref[...] = (resid_ref[...] + gr_ref[...]).astype(BF16)
    grad_normed = gn_ref[...]
    resid = resid_ref[...]
    inverse = rms_inverse(resid)
    scaled = resid * inverse
    weighted = grad_normed * gain
    gain_ref[0:1, :] = jnp.sum(grad_normed * scaled, axis=0, keepdims=True)
    grad_resid = cot_ref[...].astype(F32) + inverse * (
        weighted - scaled * jnp.mean(weighted * scaled, axis=1, keepdims=True)
    )
    gr_ref[...] = grad_resid
    gb = grad_resid.astype(BF16)
    main = width - (LANES - half)
    lined = jnp.concatenate([jnp.zeros((rows, half), BF16), gb[:, main:], gb[:, :main]], axis=1)
    turned_ref[...] = head_columns(sizes, o_ref, HD).astype(BF16).T
    for t in range(0, out_tiles, 2):
        part = nn(turned_ref[...], lined[:, t * LANES : (t + 2) * LANES]).astype(BF16)
        out_stage[t] = part[:, :LANES]
        out_stage[t + 1] = part[:, LANES:]
    out_copy = pltpu.make_async_copy(out_stage, out_grad, sem.at[2])
    out_copy.start()
    gb_wide = jnp.concatenate([gb, jnp.zeros((rows, out_tiles * LANES - width), BF16)], axis=1)
    grad_att = []
    for zi in range(fsdp):
        weights = [wout_ref[zi, t * shard : (t + 1) * shard, :] for t in range(out_tiles)]
        grad_att.append(nt(gb_wide, jnp.concatenate(weights, axis=1)).astype(BF16))
    grad_att = jnp.concatenate(grad_att, axis=1)
    zero = jnp.zeros((block, HD), BF16)
    for h in range(heads):
        for b in range(2):
            do_ref[h // share, b, (h % share) * block : (h % share + 1) * block, :] = jnp.concatenate(
                [zero, grad_att[b * block : (b + 1) * block, h * HD : (h + 1) * HD]], axis=1
            )
    for g in range(kvh):
        row_deltas(g, do_ref, o_ref, delta_ref.at[g])
    for copy in moves(0):
        copy.wait()
    out_copy.wait()


def add_rows(out, terms, rows):
    def add(views):
        total = views[1][0:rows, :].astype(F32)
        for term in views[2:]:
            total = total + term[0:rows, :].astype(F32)
        views[0][0:rows, :] = total.astype(out.dtype)

    refs = [out] + list(terms)
    if len(out.shape) == 2:
        add(refs)
    else:

        @pl.loop(0, out.shape[0])
        def _(lead):
            add([r.at[lead] for r in refs])


def grad_stages(core, fsdp, plan, sources, held, got, outs, gain_refs, send, recv, local):
    links = Links(core, fsdp, send, recv, plan)
    z, chip = links.z, links.chip
    near, far = lax.bitwise_xor(chip, links.first), lax.bitwise_xor(chip, links.second)
    corner = lax.bitwise_xor(chip, 3)
    shards = {k: sources[k].shape[-2] // fsdp for k in PACKAGES}
    mine = {k: Share(k, core, shards[k]) for k in PACKAGES}
    twin = {k: Share(k, 1 - core, shards[k]) for k in PACKAGES}
    stages = {}

    def slot_of(d):
        return max(d - 1, 0)

    def hold(k, d, q):
        if k in held:
            return held[k].at[d, q]
        return mine[k].at(sources[k], lax.bitwise_xor(z, d), q)

    def load(k, d, q):
        slot = (PACKAGES.index(k) * fsdp + d) * 4 + q
        return pltpu.make_async_copy(
            mine[k].at(sources[k], lax.bitwise_xor(z, d), q), hold(k, d, q), local.at[slot]
        )

    def begin(k, d):
        zi = lax.bitwise_xor(z, d)
        for q in range(4):
            links.send((k, CORE, d, q), CORE, twin[k].at(sources[k], zi, q), twin[k].buffer(got[k][0].at[d, q]))
            if k in held:
                load(k, d, q).start()

    def stage1(k, d):
        share = mine[k]
        for q in range(4):
            links.landed((k, CORE, d, q), share.buffer(got[k][0].at[d, q]))
            if k in held:
                load(k, d, q).wait()
            terms = [hold(k, d, q), got[k][0].at[d, q]]
            if d == 0:
                links.landed((k, "direct", q), share.buffer(got[k][4].at[q]))
                terms.append(got[k][4].at[q])
            add_rows(hold(k, d, q), terms, share.rows)
            if d == 1:
                links.send((k, "direct", q), d, hold(k, d, q), share.buffer(got[k][4].at[q]))
        for i, q in enumerate((near, corner)):
            if d != 1:
                links.send((k, FIRST, d, i), FIRST, hold(k, d, q), share.buffer(got[k][1].at[slot_of(d), i]))

    def stage2(k, d):
        share, slot = mine[k], slot_of(d)
        if d == 1:
            return
        for i in range(2):
            links.landed((k, FIRST, d, i), share.buffer(got[k][1].at[slot, i]))
        add_rows(hold(k, d, far), (hold(k, d, far), got[k][1].at[slot, 1]), share.rows)
        links.send((k, SECOND, d), SECOND, hold(k, d, far), share.buffer(got[k][2].at[slot]))

    def stage3(k, d):
        share, slot = mine[k], slot_of(d)
        if d == 1:
            return
        links.landed((k, SECOND, d), share.buffer(got[k][2].at[slot]))
        add_rows(hold(k, d, chip), (hold(k, d, chip), got[k][1].at[slot, 0], got[k][2].at[slot]), share.rows)
        if d > 0:
            links.send((k, "z", d), d, hold(k, d, chip), share.buffer(got[k][3].at[d - 2]))

    def out_copy(k):
        slot = len(PACKAGES) * fsdp * 4 + PACKAGES.index(k)
        return pltpu.make_async_copy(hold(k, 0, chip), mine[k].at(outs[k], 0, chip), local.at[slot])

    def close(k):
        share = mine[k]
        for d in range(2, fsdp):
            links.landed((k, "z", d), share.buffer(got[k][3].at[d - 2]))
        final = hold(k, 0, chip)
        add_rows(final, [final] + [got[k][3].at[d - 2] for d in range(2, fsdp)], share.rows)
        for hop in (FIRST, SECOND):
            links.send((k, "out", hop), hop, final, share.at(outs[k], 0, chip))
        links.send((k, "out core", 0), CORE, final, share.at(outs[k], 0, chip))
        out_copy(k).start()

    def close2(k):
        share = mine[k]
        links.landed((k, "out", FIRST), share.at(outs[k], 0, near))
        piece = share.at(outs[k], 0, near)
        links.send((k, "out", "corner"), SECOND, piece, piece)
        links.send((k, "out core", 1), CORE, piece, piece)
        piece = share.at(outs[k], 0, far)
        links.landed((k, "out", SECOND), piece)
        links.send((k, "out core", 2), CORE, piece, piece)

    def close3(k):
        piece = mine[k].at(outs[k], 0, corner)
        links.landed((k, "out", "corner"), piece)
        links.send((k, "out core", 3), CORE, piece, piece)

    def close4(k):
        for i, q in ((0, chip), (1, far), (2, near), (3, corner)):
            links.landed((k, "out core", i), twin[k].at(outs[k], 0, q))
        out_copy(k).wait()

    for k in PACKAGES:
        for fn in (begin, stage1, stage2, stage3):
            for d in range(fsdp):
                stages[fn.__name__, k, d] = functools.partial(fn, k, d)
        for fn in (close, close2, close3, close4):
            stages[fn.__name__, k] = functools.partial(fn, k)

    gain_sum, gain_got, gain_z, gain_out = gain_refs

    def gain_step(i):
        if i > 0:
            links.landed(("gain", i - 1), gain_got.at[i - 1])
            gain_sum[i] = gain_sum[i - 1] + gain_got[i - 1]
        if i < 3:
            links.send(("gain", i), (CORE, FIRST, SECOND)[i], gain_sum.at[i], gain_got.at[i])
        else:
            for d in range(1, fsdp):
                links.send(("gain z", d), d, gain_sum.at[3, lax.bitwise_xor(z, d)], gain_z.at[d - 1])

    def gain_close():
        total = gain_sum[3, z]
        for d in range(1, fsdp):
            links.landed(("gain z", d), gain_z.at[d - 1])
            total = total + gain_z[d - 1]
        gain_out[...] = total

    for i in range(4):
        stages["gain", i] = functools.partial(gain_step, i)
    stages["gain close"] = gain_close
    stages["drain"] = links.drain
    return stages


def kv_grad_stages(core, plan, parts, kv_sum, got0, got1, got2, send, recv):
    links = Links(core, 1, send, recv, plan)
    chip = links.chip
    near, far = lax.bitwise_xor(chip, links.first), lax.bitwise_xor(chip, links.second)
    corner = lax.bitwise_xor(chip, 3)
    rows = parts.shape[3]
    stages = {}

    def start(g):
        for q in range(4):
            links.send((0, g, q), CORE, parts.at[2 * q + 1 - core, g], got0.at[g, q])

    def stage1(g):
        for q in range(4):
            links.landed((0, g, q), got0.at[g, q])
            add_rows(got0.at[g, q], (parts.at[2 * q + core, g], got0.at[g, q]), rows)
        for i, q in enumerate((near, corner)):
            links.send((1, g, i), FIRST, got0.at[g, q], got1.at[g, i])

    def stage2(g):
        for i in range(2):
            links.landed((1, g, i), got1.at[g, i])
        add_rows(got0.at[g, far], (got0.at[g, far], got1.at[g, 1]), rows)
        links.send((2, g), SECOND, got0.at[g, far], got2.at[g])

    def stage3(g):
        links.landed((2, g), got2.at[g])
        add_rows(kv_sum.at[g], (got0.at[g, chip], got1.at[g, 0], got2.at[g]), rows)

    for g in range(parts.shape[1]):
        for i, fn in enumerate((start, stage1, stage2, stage3)):
            stages[i, g] = functools.partial(fn, g)
    stages["drain"] = links.drain
    return stages


def back_kernel(
    sizes, n, fsdp, plans, deal_ref, lengths_ref, q_ref, kv_in, do_ref, delta_ref, lse_ref,
    x_ref, n1_ref, gr_ref, gains_ref, gain_two_ref, cos_ref, sin_ref, qkv_ref, out_grad_ref, ff_grad, down_grad,
    tg_ref, gain_out, attn_out, ff_out, down_out,
    start_ref, spill_ref, chunk_ref, dqt_ref, dq_ref, dkv_ref, kv_sum, kv_got0, kv_got1, kv_got2, gp_ref, gn_ref, turned_ref, attn_grad,
    ff_a, down_a, attn_0, ff_0, down_0, attn_1, ff_1, down_1, attn_2, ff_2, down_2, attn_3, ff_3, down_3, attn_4, ff_4, down_4,
    gain_sum, gain_got, gain_z, send, recv, kv_send, kv_recv, local, ahead_sem,
):
    heads, kvh, block = sizes
    share = heads // kvh
    me = lax.axis_index("ctx")
    width = x_ref.shape[1]
    rows = x_ref.shape[0]
    greet("z", fsdp)
    sources = {ATTN: attn_grad, FF: ff_grad, DOWN: down_grad}
    held = {FF: ff_a, DOWN: down_a}
    got = {
        ATTN: (attn_0, attn_1, attn_2, attn_3, attn_4),
        FF: (ff_0, ff_1, ff_2, ff_3, ff_4),
        DOWN: (down_0, down_1, down_2, down_3, down_4),
    }
    outs = {ATTN: attn_out, FF: ff_out, DOWN: down_out}
    run = both_cores(
        lambda core: grad_stages(
            core, fsdp, plans[0], sources, held, got, outs, (gain_sum, gain_got, gain_z, gain_out), send, recv, local
        )
    )
    run_kv = both_cores(
        lambda core: kv_grad_stages(core, plans[1], dkv_ref, kv_sum, kv_got0, kv_got1, kv_got2, kv_send, kv_recv)
    )
    start_ref[...] = first_keys(n, deal_ref, lengths_ref, block, start_ref.shape[1])
    order = [d for d in range(1, fsdp)] + [0]
    chunks = [(k, d) for k in (FF, DOWN) for d in order]
    steps = []
    for i in range(len(chunks) + 7):
        names = []
        if i + 1 < len(chunks):
            names.append(("begin",) + chunks[i + 1])
        if i < len(chunks):
            names.append(("stage1",) + chunks[i])
        if 1 <= i <= len(chunks):
            names.append(("stage2",) + chunks[i - 1])
        if 2 <= i <= len(chunks) + 1:
            names.append(("stage3",) + chunks[i - 2])
        for last, k in ((len(order) + 1, FF), (len(chunks) + 1, DOWN)):
            for extra, what in enumerate(("close", "close2", "close3", "close4")):
                if i == last + 1 + extra:
                    names.append((what, k))
        steps.append(names)
    run(("begin",) + chunks[0])
    width_tiles = -(-(heads + 2 * kvh) // 2)
    ahead = [
        pltpu.make_async_copy(out_grad_ref.at[0], spill_ref, ahead_sem.at[0]),
        pltpu.make_async_copy(
            out_grad_ref.at[pl.ds(1, attn_grad.shape[0] - width_tiles)],
            attn_grad.at[pl.ds(width_tiles, attn_grad.shape[0] - width_tiles)], ahead_sem.at[1],
        ),
    ]
    def weight_rows(i):
        size = chunk_ref.shape[1]
        return pltpu.make_async_copy(qkv_ref.at[i, pl.ds(0, size)], chunk_ref.at[i % 2], ahead_sem.at[2 + i % 2])

    for copy in ahead + [weight_rows(0), weight_rows(1)]:
        copy.start()
    total = kvh * n
    pace = 9
    kv_due = sorted((8 * (i + 1) + (0, 3, 15, 27)[stage], stage, i) for i in range(kvh) for stage in range(4))

    @pl.loop(0, total)
    def _(step):
        g, j = step // n, step % n
        for i, names in enumerate(steps):
            if i * pace < total:
                pl.when(step == i * pace)(functools.partial(run, *names))
        for due, stage, i in kv_due:
            if due < total:
                pl.when(step == due)(functools.partial(run_kv, (stage, i)))
        own, other = attend_back_step(
            n, me, g, j, deal_ref, start_ref, q_ref, kv_in, do_ref, lse_ref, delta_ref, dqt_ref, dkv_ref
        )
        pl.when(j == 0)(own)
        pl.when(j > 0)(other)

        @pl.when(j == n - 1)
        def _():
            dq_ref[g] = jnp.concatenate([(dqt_ref[b] * 0.125).T[:, :HD] for b in range(2)], axis=1)

    cos, sin = cos_ref[...], -sin_ref[...]

    def head(index):
        if index < heads:
            return jnp.concatenate(
                [
                    dq_ref[index // share, (index % share) * block : (index % share + 1) * block, b * HD : (b + 1) * HD]
                    for b in range(2)
                ],
                axis=0,
            )
        g = index - heads
        low = 0 if g < kvh else HD
        return jnp.concatenate([kv_sum[g % kvh, b, :, low : low + HD] for b in range(2)], axis=0)

    count = heads + 2 * kvh
    tiles = -(-count // 2)
    turned_ref[...] = n1_ref[...].T

    def some_tiles(low, high):
        for t in range(low, high):
            right = head(2 * t + 1) if 2 * t + 1 < count else jnp.zeros((rows, HD), F32)
            pair = jnp.concatenate([head(2 * t), right], axis=1)
            if 2 * t < heads + kvh:
                pair = rope_tile(pair, cos, sin)
            gp_ref[:, t * LANES : (t + 1) * LANES] = pair.astype(BF16)
        for t in range(low, high, 2):
            some = min(2, high - t)
            part = nn(turned_ref[...], gp_ref[:, t * LANES : (t + some) * LANES]).astype(BF16)
            for i in range(some):
                tile = part[:, i * LANES : (i + 1) * LANES]
                attn_grad[t + i] = tile + spill_ref[...] if t + i == tiles - 1 else tile

    rest = [names for i, names in enumerate(steps) if i * pace >= total]
    late = [(stage, i) for due, stage, i in kv_due if due >= total]
    run_kv(late[0])
    some_tiles(0, heads // 2)
    for copy in ahead:
        copy.wait()
    run_kv(*[key for key in late[1:] if key[0] < 2 or key[1] < kvh - 1])
    run(*rest[0])
    run_kv(*[key for key in late[1:] if key[0] >= 2 and key[1] == kvh - 1])
    some_tiles(heads // 2, tiles)
    run(("begin", ATTN, order[0]), ("begin", ATTN, order[1]), ("stage1", ATTN, order[0]), *rest[1])
    shard = width // fsdp
    pieces = []
    for i in range(fsdp):
        weight_rows(i).wait()
        rows_in = jnp.concatenate([chunk_ref[i % 2, t * shard : (t + 1) * shard, :] for t in range(tiles)], axis=1)
        pieces.append(nt(gp_ref[...], rows_in))
        if i + 2 < fsdp:
            weight_rows(i + 2).start()
    gn_ref[...] = jnp.concatenate(pieces, axis=1)
    x = x_ref[...].astype(F32)
    inverse = rms_inverse(x)
    scaled = x * inverse
    grad_normed = gn_ref[...]
    weighted = grad_normed * gain_row(gains_ref, 0, fsdp, width // fsdp)
    gain_one = jnp.sum(grad_normed * scaled, axis=0, keepdims=True)
    gain_two = gain_two_ref[0:1, :]
    tail = gain_sum.shape[3] - shard
    for i in range(fsdp):
        both = jnp.concatenate(
            [gain_one[:, i * shard : (i + 1) * shard], gain_two[:, i * shard : (i + 1) * shard]], axis=0
        )
        both = jnp.concatenate([both, jnp.zeros((2, tail), F32)], axis=1)
        gain_sum[0, i] = jnp.concatenate([both, jnp.zeros((6, gain_sum.shape[3]), F32)], axis=0)
    run(("gain", 0))
    tg_ref[...] = (
        gr_ref[...] + inverse * (weighted - scaled * jnp.mean(weighted * scaled, axis=1, keepdims=True))
    ).astype(BF16)
    chunk2 = [(ATTN, d) for d in order]
    for i in range(1, len(chunk2) + 2):
        names = []
        if i + 1 < len(chunk2):
            names.append(("begin",) + chunk2[i + 1])
        if i < len(chunk2):
            names.append(("stage1",) + chunk2[i])
        if i <= len(chunk2):
            names.append(("stage2",) + chunk2[i - 1])
        if i >= 2:
            names.append(("stage3",) + chunk2[i - 2])
        if i <= 3:
            names.append(("gain", i))
        if i + 1 < len(rest):
            names += rest[i + 1]
        run(*names)
    for i, what in enumerate(("close", "close2", "close3", "close4")):
        names = rest[len(chunk2) + 3 + i] if len(chunk2) + 3 + i < len(rest) else []
        run((what, ATTN), *names)
    for names in rest[len(chunk2) + 7 :]:
        run(*names)
    run("gain close", "drain")
    run_kv("drain")


def whole(shape, dtype):
    return jax.ShapeDtypeStruct(shape, dtype)


def params(ident=None):
    extra = {} if ident is None else {"collective_id": ident, "has_side_effects": True}
    return pltpu.CompilerParams(vmem_limit_bytes=VMEM_LIMIT, **extra)


SMEM = pl.BlockSpec(memory_space=pltpu.SMEM)
VMEM = pl.BlockSpec(memory_space=pltpu.VMEM)
ANY = pl.BlockSpec(memory_space=pl.ANY)


def finish_kernel(
    heads, deal_ref, result_ref, tokens_ref, attn_ref, ff_ref, down_ref,
    out_ref, tg_ref, q_ref, kt_ref, vt_ref, o_ref, gate_ref, up_ref, dt_ref,
):
    me = lax.axis_index("ctx")
    flip = deal_ref[2 * me] > deal_ref[2 * me + 1]
    out_ref[...] = ordered(flip, result_ref[...]).T
    tg_ref[...] = ordered(flip, tokens_ref[...]).T
    width, kv_width = q_ref.shape[1], kt_ref.shape[0]
    half = width % LANES
    full = width // LANES

    def tile(t):
        return attn_ref[t].astype(F32)

    for t in range(full):
        q_ref[:, t * LANES : (t + 1) * LANES] = tile(t)
    q_ref[:, full * LANES :] = tile(full)[:, :half]
    kt_ref[0 : LANES - half, :] = tile(full).T[half:, :]
    at = LANES - half
    for t in range(full + 1, (width + kv_width) // LANES):
        kt_ref[at : at + LANES, :] = tile(t).T
        at += LANES
    first = (width + kv_width) // LANES
    spill = (width + 2 * kv_width) // LANES
    for i in range(spill - first):
        vt_ref[i * LANES : (i + 1) * LANES, :] = tile(first + i).T
    vt_ref[(spill - first) * LANES :, :] = tile(spill).T[: kv_width % LANES, :]
    for i in range(full):
        o_ref[:, i * LANES : (i + 1) * LANES] = tile(spill + 1 + i)
    o_ref[:, full * LANES :] = tile(spill)[:, LANES - half :]
    for t in range(ff_ref.shape[1]):
        gate_ref[:, t * LANES : (t + 1) * LANES] = ff_ref[0, t].astype(F32)
        up_ref[:, t * LANES : (t + 1) * LANES] = ff_ref[1, t].astype(F32)
    for t in range(down_ref.shape[0]):
        high = min((t + 1) * LANES, dt_ref.shape[0])
        dt_ref[t * LANES : high, :] = down_ref[t].astype(F32).T[: high - t * LANES, :]


def cube_body(
    tokens, attn_gain, query_weight, key_weight, value_weight, out_weight, mlp_gain, gate_weight,
    up_weight, down_weight, cotangent, cont_lengths, block_deal,
):
    n, fsdp = lax.axis_size("ctx"), lax.axis_size("fsdp")
    me = lax.axis_index("ctx")
    row_count, width = tokens.shape[1:]
    kv_width = key_weight.shape[1]
    shard, hidden = gate_weight.shape
    down_shard = down_weight.shape[0]
    block = row_count // 2
    heads, kvh = width // HD, kv_width // HD
    share = heads // kvh
    stack = share * block
    sizes = (heads, kvh, block)
    half_turns = THETA ** (-2.0 * jnp.arange(HD // 2, dtype=F32) / HD)
    turns = jnp.tile(half_turns, (8, LANES // (HD // 2)))
    pad = -shard % LANES
    gains_in = jnp.pad(jnp.stack([attn_gain, mlp_gain]).astype(F32), ((0, 6), (0, pad)))
    gain_shape = (fsdp,) + gains_in.shape
    attn_tiles = (2 * width + 2 * kv_width) // LANES
    ff_tiles = hidden // LANES
    down_tiles = -(-width // LANES)
    heads_shape = (kvh, 2, stack, LANES)
    row_shape = (kvh, 2, 8, stack)
    kv_shape = (n, 2, kvh, block, LANES)
    dma = pltpu.SemaphoreType.DMA
    mixed = (width + 2 * kv_width) // LANES
    qkv_tiles = -(-(width + 2 * kv_width) // LANES)
    qkv_shape = (fsdp, -(-qkv_tiles * shard // LANES) * LANES, LANES)
    (
        x, cos, sin, normed_one, q, kv_all, lse, gains, w_qkv,
        result, grad_resid, grad_heads, deltas, gain_two, out_grad, ff_grad, down_grad,
    ) = pl.pallas_call(
        functools.partial(front_kernel, sizes, n, fsdp, ({}, {})),
        out_shape=(
            whole((row_count, width), BF16),
            whole((row_count, LANES), F32),
            whole((row_count, LANES), F32),
            whole((row_count, width), BF16),
            whole(heads_shape, BF16),
            whole(kv_shape, BF16),
            whole(row_shape, F32),
            whole(gain_shape, F32),
            whole(qkv_shape, BF16),
            whole((row_count, width), BF16),
            whole((row_count, width), F32),
            whole(heads_shape, BF16),
            whole(row_shape, F32),
            whole((8, width), F32),
            whole((attn_tiles - mixed, width, LANES), BF16),
            whole((2, ff_tiles, width, LANES), BF16),
            whole((down_tiles, hidden, LANES), BF16),
        ),
        in_specs=[SMEM] * 2 + [VMEM] * 11,
        out_specs=(VMEM,) * 5 + (ANY, VMEM, VMEM, ANY) + (VMEM,) * 5 + (ANY,) * 3,
        scratch_shapes=[
            pltpu.VMEM(qkv_shape, BF16),
            pltpu.VMEM((fsdp, down_tiles * shard, LANES), BF16),
            pltpu.VMEM((2, ff_tiles, fsdp * shard, LANES), BF16),
            pltpu.VMEM((down_tiles, fsdp * down_shard, LANES), BF16),
            pltpu.VMEM(kv_shape, BF16),
            pltpu.VMEM(heads_shape, F32),
            pltpu.VMEM(gain_shape, F32),
            pltpu.VMEM((8, stack), jnp.int32),
            pltpu.VMEM((kvh, 2, 8, stack), F32),
            pltpu.VMEM((kvh, 2, LANES, stack), F32),
            pltpu.VMEM((row_count, width), BF16),
            pltpu.VMEM((row_count, width), F32),
            pltpu.VMEM((row_count, width), BF16),
            pltpu.VMEM((row_count, hidden // 4), BF16),
            pltpu.VMEM((row_count, hidden // 4), BF16),
            pltpu.VMEM((row_count, hidden // 4), BF16),
            pltpu.VMEM((width, row_count), BF16),
            pltpu.VMEM((row_count, width), F32),
            pltpu.VMEM((attn_tiles - mixed, width, LANES), BF16),
            pltpu.VMEM((2, ff_tiles // 4, width, LANES), BF16),
            pltpu.VMEM((down_tiles, hidden // 4, LANES), BF16),
            dma((99,)), dma((99,)), dma((14,)), dma((14,)), dma((2,)), dma((3,)),
        ],
        compiler_params=params(0),
        name="front",
    )(
        block_deal, cont_lengths, tokens[0].T, gains_in, turns,
        query_weight, key_weight.T, value_weight.T, out_weight, gate_weight, up_weight, down_weight.T,
        cotangent[0].T,
    )

    attn_rows = -(-shard // 32) * 16
    shapes = ((attn_tiles // 4, attn_rows, LANES), (ff_tiles // 4, shard, LANES), (down_shard, LANES))
    buffers = [pltpu.VMEM((fsdp, 4) + shape, BF16) for shape in shapes[1:]]
    for lead in ((fsdp, 4), (fsdp - 1, 2), (fsdp - 1,), (fsdp - 2,), (4,)):
        buffers += [pltpu.VMEM(lead + shape, BF16) for shape in shapes]
    piece = (2, block, LANES)
    tokens_grad, gain_grads, attn_w, ff_w, down_w = pl.pallas_call(
        functools.partial(back_kernel, sizes, n, fsdp, ({}, {})),
        out_shape=(
            whole((row_count, width), BF16),
            whole(gains_in.shape, F32),
            whole((attn_tiles, shard, LANES), BF16),
            whole((2, ff_tiles, shard, LANES), BF16),
            whole((down_tiles, down_shard, LANES), BF16),
        ),
        in_specs=[SMEM] * 2 + [VMEM] * 12 + [ANY] * 4,
        out_specs=(VMEM, VMEM, ANY, ANY, ANY),
        scratch_shapes=[
            pltpu.VMEM((8, stack), jnp.int32),
            pltpu.VMEM((width, LANES), BF16),
            pltpu.VMEM((2, qkv_tiles * shard, LANES), BF16),
            pltpu.VMEM((2, LANES, stack), F32),
            pltpu.VMEM((kvh, stack, LANES), F32),
            pltpu.VMEM((n, kvh) + piece, BF16),
            pltpu.VMEM((kvh,) + piece, F32),
            pltpu.VMEM((kvh, 4) + piece, BF16),
            pltpu.VMEM((kvh, 2) + piece, BF16),
            pltpu.VMEM((kvh,) + piece, BF16),
            pltpu.VMEM((row_count, qkv_tiles * LANES), BF16),
            pltpu.VMEM((row_count, width), F32),
            pltpu.VMEM((width, row_count), BF16),
            pltpu.VMEM((attn_tiles, width, LANES), BF16),
        ]
        + buffers
        + [
            pltpu.VMEM((4,) + gain_shape, F32),
            pltpu.VMEM((3,) + gain_shape, F32),
            pltpu.VMEM((fsdp - 1,) + gains_in.shape, F32),
            dma((123,)), dma((123,)), dma((7 * kvh,)), dma((7 * kvh,)), dma((51,)), dma((4,)),
        ],
        compiler_params=params(1),
        name="back",
    )(
        block_deal, cont_lengths, q, kv_all, grad_heads, deltas, lse, x, normed_one, grad_resid, gains, gain_two,
        cos, sin, w_qkv, out_grad, ff_grad, down_grad,
    )

    out_t, tg_t, q_w, k_t, v_t, o_w, gate_w, up_w, d_t = pl.pallas_call(
        functools.partial(finish_kernel, heads),
        out_shape=(
            whole((width, row_count), BF16),
            whole((width, row_count), BF16),
            whole((shard, width), F32),
            whole((kv_width, shard), F32),
            whole((kv_width, shard), F32),
            whole((shard, width), F32),
            whole((shard, hidden), F32),
            whole((shard, hidden), F32),
            whole((width, down_shard), F32),
        ),
        in_specs=[SMEM] + [VMEM] * 5,
        out_specs=(VMEM,) * 9,
        compiler_params=params(),
        name="finish",
    )(block_deal, result, tokens_grad, attn_w, ff_w, down_w)
    return (
        out_t.T[None],
        tg_t.T[None],
        gain_grads[0, :shard],
        q_w,
        k_t.T,
        v_t.T,
        o_w,
        gain_grads[1, :shard],
        gate_w,
        up_w,
        d_t.T,
    )


def head_of(tiles, index):
    start = (index % 2) * HD
    return tiles[index // 2][:, start : start + HD]


def project_kernel(sizes, x_ref, gain_ref, w_ref, cos_ref, sin_ref, n1_ref, q_ref, kv_ref):
    heads, kvh, block = sizes
    share = heads // kvh
    x = x_ref[...].astype(F32)
    inverse = lax.rsqrt(jnp.mean(x * x, axis=1, keepdims=True) + EPSILON)
    normed = (x * inverse * gain_ref[...]).astype(BF16)
    n1_ref[...] = normed
    width = (heads + 2 * kvh) * HD
    raw = nn(normed, w_ref[:, :width])
    cos = cos_ref[...]
    sin = sin_ref[...]
    tiles = []
    for j in range((heads + kvh) * HD // LANES):
        tiles.append(rope_tile(raw[:, j * LANES : (j + 1) * LANES], cos, sin).astype(BF16))
    zero = jnp.zeros((block, HD), BF16)
    for h in range(heads):
        piece = head_of(tiles, h) * jnp.asarray(0.125, BF16)
        g, i = h // share, h % share
        for b in range(2):
            q_ref[g, b, i * block : (i + 1) * block, :] = jnp.concatenate(
                [piece[b * block : (b + 1) * block], zero], axis=1
            )
    for g in range(kvh):
        start = (heads + kvh + g) * HD
        value = raw[:, start : start + HD].astype(BF16)
        pair = jnp.concatenate([head_of(tiles, heads + g), value], axis=1)
        for b in range(2):
            kv_ref[b, :, g * LANES : (g + 1) * LANES] = pair[b * block : (b + 1) * block]


def attend_kernel(
    n, me_ref, pick_ref, segq_ref, segk_ref, q_ref, kv_ref, o_ref, lse_ref, s1_ref, p1_ref, s2_ref, p2_ref
):
    me = me_ref[0]
    block = kv_ref.shape[2]
    rows = q_ref.shape[2]
    keys = n * block
    qc = q_ref[0, 1]
    prompt = kv_ref[:, 0].reshape(keys, LANES)
    s1_ref[...] = nt(qc, prompt)
    own = []
    for b in range(2):
        s2_ref[b] = nt(q_ref[0, b], kv_ref[me, b])
    for j in range(1, n):
        at = lax.rem(me + j, n)
        kind = pick_ref[j]
        s2_ref[j + 1] = nt(q_ref[0, kind], kv_ref[at, kind])
    step = 16
    kinds = [pick_ref[j] == 0 for j in range(n)]

    def fold(s):
        return jnp.maximum(
            s[:, :LANES],
            jnp.concatenate(
                [s[:, LANES:], jnp.full((step, 2 * LANES - block), MASKED, F32)], axis=1
            ),
        )

    def chunk(at, carry):
        r = pl.multiple_of(at * step, step)
        rs = pl.ds(r, step)
        in_block = lax.rem(r, block)
        tri = lax.broadcasted_iota(jnp.int32, (step, block), 1) <= (
            in_block + lax.broadcasted_iota(jnp.int32, (step, block), 0)
        )
        segq = segq_ref[rs, :]
        s1 = s1_ref[rs, :]
        top_c = s1[:, :LANES]
        for t in range(1, keys // LANES):
            top_c = jnp.maximum(top_c, s1[:, t * LANES : (t + 1) * LANES])
        dp = jnp.where(tri, s2_ref[0, rs, :], MASKED)
        dc = jnp.where(tri & (segq == segk_ref[0]), s2_ref[1, rs, :], MASKED)
        top_c = jnp.maximum(top_c, fold(dc))
        top_p = fold(dp)
        others = []
        for j in range(1, n):
            s = jnp.where((segq == segk_ref[j]) | kinds[j], s2_ref[j + 1, rs, :], MASKED)
            others.append(s)
            f = fold(s)
            top_p = jnp.maximum(top_p, jnp.where(kinds[j], f, MASKED))
            top_c = jnp.maximum(top_c, jnp.where(kinds[j], MASKED, f))
        m_p = jnp.max(top_p, axis=1, keepdims=True)
        m_c = jnp.max(top_c, axis=1, keepdims=True)
        p1_ref[rs, :] = jnp.exp2((s1 - m_c) * LOG2E).astype(BF16)
        p2_ref[0, rs, :] = jnp.exp2((dp - m_p) * LOG2E).astype(BF16)
        p2_ref[1, rs, :] = jnp.exp2((dc - m_c) * LOG2E).astype(BF16)
        for j in range(1, n):
            m = jnp.where(kinds[j], m_p, m_c)
            p2_ref[j + 1, rs, :] = jnp.exp2((others[j - 1] - m) * LOG2E).astype(BF16)
        lse_ref[0, 0, rs, :] = jnp.broadcast_to(m_p * LOG2E, (step, LANES))
        lse_ref[0, 1, rs, :] = jnp.broadcast_to(m_c * LOG2E, (step, LANES))
        return carry

    lax.fori_loop(0, rows // step, chunk, 0)

    def with_ones(tile):
        return jnp.concatenate([tile, jnp.ones(tile.shape, BF16)], axis=1)

    acc = [nn(p2_ref[b], with_ones(kv_ref[me, b])) for b in range(2)]
    acc[1] = acc[1] + nn(p1_ref[...], with_ones(prompt))
    for j in range(1, n):
        at = lax.rem(me + j, n)
        part = nn(p2_ref[j + 1], with_ones(kv_ref[at, pick_ref[j]]))
        acc[0] = acc[0] + jnp.where(kinds[j], part, 0.0)
        acc[1] = acc[1] + jnp.where(kinds[j], 0.0, part)
    for b in range(2):
        total = acc[b][:, LANES:]
        o_ref[0, b] = acc[b][:, :LANES] / total
        lse_ref[0, b] = lse_ref[0, b] + jnp.log2(total)


def attend_back_kernel(
    n, me_ref, pick_ref, segq_ref, segk_ref, q_ref, kv_ref, do_ref, o_ref, lse_ref, dq_ref, dkv_ref, row_ref, dqt_ref
):
    me = me_ref[0]
    block = kv_ref.shape[2]
    rows = q_ref.shape[2]
    first = (lax.broadcasted_iota(jnp.int32, (8, LANES), 1) == 0).astype(F32)
    ones = jnp.ones((8, LANES), F32)

    def to_row(lhs, matrix):
        return lax.dot_general(
            lhs, matrix, (((1,), (1,)), ((), ())), precision=lax.Precision.HIGHEST,
            preferred_element_type=F32,
        )

    for b in range(2):
        row_ref[b] = to_row(first, lse_ref[0, b])
        row_ref[2 + b] = to_row(ones, do_ref[0, b].astype(F32) * o_ref[0, b])
    lane_rows = lax.rem(lax.broadcasted_iota(jnp.int32, (block, rows), 1), block)
    tri = lax.broadcasted_iota(jnp.int32, (block, rows), 0) <= lane_rows

    def pair(kind, tile, mask):
        q = q_ref[0, kind]
        do = do_ref[0, kind]
        p = jnp.exp2(nt(tile, q) * LOG2E - row_ref[kind, 0:1, :])
        if mask is not None:
            p = jnp.where(mask, p, 0.0)
        ds = (p * (nt(tile, do) - row_ref[2 + kind, 0:1, :])).astype(BF16)
        return nn(ds, q) + nn(p.astype(BF16), do), tn(tile, ds)

    segq = segq_ref[0:1, :]
    same_own = segq == segk_ref[0]
    own0, own1 = kv_ref[me, 0], kv_ref[me, 1]
    d0, q0 = pair(0, own0, tri)
    d1, q1 = pair(1, own1, tri & same_own)
    d2, q2 = pair(1, own0, None)
    dkv_ref[me, 0] = (d0 + d2).astype(dkv_ref.dtype)
    dkv_ref[me, 1] = d1.astype(dkv_ref.dtype)
    dqt_ref[0] = q0
    dqt_ref[1] = q1 + q2

    def other(j, carry):
        at = lax.rem(me + j, n)
        kind = pick_ref[j]
        is_prompt = kind == 0
        full, q_full = pair(1, kv_ref[at, 0], None)
        mask = (segq == segk_ref[j]) | is_prompt
        part, q_part = pair(kind, kv_ref[at, kind], mask)
        dkv_ref[at, 0] = (full + jnp.where(is_prompt, part, 0.0)).astype(dkv_ref.dtype)
        dkv_ref[at, 1] = jnp.where(is_prompt, 0.0, part).astype(dkv_ref.dtype)
        dqt_ref[0] = dqt_ref[0] + jnp.where(is_prompt, q_part, 0.0)
        dqt_ref[1] = dqt_ref[1] + q_full + jnp.where(is_prompt, 0.0, q_part)
        return carry

    lax.fori_loop(1, n, other, 0)
    for b in range(2):
        dq_ref[0, b] = (dqt_ref[b] * 0.125).T


def mid_kernel(sizes, o_ref, x_ref, wo_ref, gain_ref, att_ref, resid_ref, n2_ref):
    heads, kvh, block = sizes
    share = heads // kvh
    for b in range(2):
        columns = []
        for h in range(heads):
            g, i = h // share, h % share
            columns.append(o_ref[g, b, i * block : (i + 1) * block, HD:])
        attended = jnp.concatenate(columns, axis=1).astype(BF16)
        rs = slice(b * block, (b + 1) * block)
        att_ref[rs, :] = attended
        resid = x_ref[rs, :].astype(F32) + nn(attended, wo_ref[...])
        resid_ref[rs, :] = resid
        inverse = lax.rsqrt(jnp.mean(resid * resid, axis=1, keepdims=True) + EPSILON)
        n2_ref[rs, :] = (resid * inverse * gain_ref[...]).astype(BF16)


def branch_kernel(sizes, gb_ref, wo_ref, do_ref):
    heads, kvh, block = sizes
    share = heads // kvh
    grad = nt(gb_ref[...], wo_ref[...]).astype(BF16)
    zero = jnp.zeros((block, HD), BF16)
    for h in range(heads):
        g, i = h // share, h % share
        for b in range(2):
            do_ref[g, b, i * block : (i + 1) * block, :] = jnp.concatenate(
                [zero, grad[b * block : (b + 1) * block, h * HD : (h + 1) * HD]], axis=1
            )


def unrope_kernel(sizes, dq_ref, dkv_ref, cos_ref, sin_ref, out_ref):
    heads, kvh, block = sizes
    share = heads // kvh
    for b in range(2):
        rs = slice(b * block, (b + 1) * block)
        cos, sin = cos_ref[rs, :], -sin_ref[rs, :]
        columns = [
            dq_ref[h // share, b, (h % share) * block : (h % share + 1) * block, :HD]
            for h in range(heads)
        ]
        columns += [dkv_ref[b, :, g * LANES : g * LANES + HD].astype(F32) for g in range(kvh)]
        tiles = []
        for j in range((heads + kvh) // 2):
            pair = jnp.concatenate(columns[2 * j : 2 * j + 2], axis=1)
            tiles.append(rope_tile(pair, cos, sin).astype(BF16))
        values = [dkv_ref[b, :, g * LANES + HD : (g + 1) * LANES].astype(BF16) for g in range(kvh)]
        out_ref[rs, :] = jnp.concatenate(tiles + values, axis=1)


def local_call(kernel, out_shape, name, **extra):
    return pl.pallas_call(
        kernel,
        out_shape=out_shape,
        compiler_params=pltpu.CompilerParams(vmem_limit_bytes=VMEM_LIMIT),
        name=name,
        **extra,
    )


def gather_rows(array, axis):
    return lax.all_gather(array, axis, axis=0, tiled=True)


def norm_back(grad_normed, scaled, inverse, gain):
    weighted = grad_normed * gain
    return inverse * (weighted - scaled * jnp.mean(weighted * scaled, axis=1, keepdims=True))


def general_body(
    tokens, attn_gain, query_weight, key_weight, value_weight, out_weight, mlp_gain, gate_weight,
    up_weight, down_weight, cotangent, cont_lengths, block_deal,
):
    n = lax.axis_size("ctx")
    me = lax.axis_index("ctx")
    row_count, width = tokens.shape[1:]
    kv_width = key_weight.shape[1]
    hidden = gate_weight.shape[1]
    block = row_count // 2
    total_rows = row_count * n
    prompt_size = total_rows // 2
    heads, kvh = width // HD, kv_width // HD
    share = heads // kvh
    stack = share * block
    sizes = (heads, kvh, block)

    deal = block_deal.reshape(n, 2)
    flip = deal[me, 0] > deal[me, 1]

    def ordered(rows):
        halves = rows.reshape(2, block, rows.shape[-1])
        return jnp.where(flip, halves[::-1], halves).reshape(rows.shape)

    x = ordered(tokens[0])
    cot = ordered(cotangent[0])
    naturals = jnp.sort(deal, axis=1)
    natural = naturals[:, :, None] * block + jnp.arange(block, dtype=jnp.int32)
    offset = natural - prompt_size
    lengths = cont_lengths[0]
    ending = jnp.cumsum(lengths)
    segment = jnp.sum((offset[..., None] >= ending).astype(jnp.int32), axis=-1)
    inside = segment[..., None] == jnp.arange(lengths.shape[0], dtype=jnp.int32)
    beginning = jnp.sum(jnp.where(inside, ending - lengths, 0), axis=-1)
    position = jnp.where(offset < 0, natural, prompt_size + offset - beginning)
    own_position = position[me].reshape(row_count)
    frequency = THETA ** (-2.0 * jnp.arange(HD // 2, dtype=F32) / HD)
    angle = own_position.astype(F32)[:, None] * frequency[None, :]
    cos, sin = jnp.cos(angle), jnp.sin(angle)
    cos = jnp.concatenate([cos, cos, cos, cos], axis=1)
    sin = jnp.concatenate([-sin, sin, -sin, sin], axis=1)
    around = (me + jnp.arange(n, dtype=jnp.int32)) % n
    first_natural = naturals[:, 0]
    pick = (first_natural[around] >= first_natural[me]).astype(jnp.int32)
    segk = segment[around, 1]
    segq = jnp.tile(segment[me, 1], share)
    me_arr = me.reshape(1).astype(jnp.int32)

    attn_rows = jnp.concatenate([query_weight, key_weight, value_weight, out_weight], axis=1)
    w_attn = gather_rows(attn_rows, "fsdp")
    qkv_width = width + 2 * kv_width
    w_qkv = w_attn[:, :qkv_width]
    w_out = w_attn[:, qkv_width:]
    gain_one = gather_rows(attn_gain, "fsdp").astype(F32)
    gain_two = gather_rows(mlp_gain, "fsdp").astype(F32)
    w_gate = gather_rows(gate_weight, "fsdp")
    w_up = gather_rows(up_weight, "fsdp")
    w_down = gather_rows(down_weight, "fsdp")

    normed_one, q, kv = local_call(
        functools.partial(project_kernel, sizes),
        (
            whole((row_count, width), BF16),
            whole((kvh, 2, stack, LANES), BF16),
            whole((2, block, kvh * LANES), BF16),
        ),
        "project",
    )(x, gain_one[None], w_attn, cos, sin)
    kv_all = lax.all_gather(kv, "ctx", axis=0)

    smem = pl.BlockSpec(memory_space=pltpu.SMEM)
    per_group = pl.BlockSpec((1, 2, stack, LANES), lambda g: (g, 0, 0, 0))
    kv_spec = pl.BlockSpec((n, 2, block, LANES), lambda g: (0, 0, 0, g))

    def full(array):
        rank = array.ndim
        return pl.BlockSpec(array.shape, lambda g: (0,) * rank)

    segq_col, segk_row = segq[:, None], segk[:, None, :]
    attended_heads, lse = local_call(
        functools.partial(attend_kernel, n),
        (whole((kvh, 2, stack, LANES), F32), whole((kvh, 2, stack, LANES), F32)),
        "attend",
        grid=(kvh,),
        in_specs=[smem, smem, full(segq_col), full(segk_row), per_group, kv_spec],
        out_specs=(per_group, per_group),
        scratch_shapes=[
            pltpu.VMEM((stack, n * block), F32),
            pltpu.VMEM((stack, n * block), BF16),
            pltpu.VMEM((n + 1, stack, block), F32),
            pltpu.VMEM((n + 1, stack, block), BF16),
        ],
    )(me_arr, pick, segq_col, segk_row, q, kv_all)

    attended, resid, normed_two = local_call(
        functools.partial(mid_kernel, sizes),
        (
            whole((row_count, width), BF16),
            whole((row_count, width), F32),
            whole((row_count, width), BF16),
        ),
        "mid",
    )(attended_heads, x, w_out, gain_two[None])

    inverse_two = lax.rsqrt(jnp.mean(resid * resid, axis=1, keepdims=True) + EPSILON)
    scaled_two = resid * inverse_two
    gate = nn(normed_two, w_gate)
    upward = nn(normed_two, w_up)
    sigma = jax.nn.sigmoid(gate)
    activated = gate * sigma
    product = (activated * upward).astype(BF16)
    result = resid + nn(product, w_down)
    grad_prod = nt(cot, w_down)
    grad_gate = (grad_prod * upward * sigma * (1.0 + gate * (1.0 - sigma))).astype(BF16)
    grad_up = (grad_prod * activated).astype(BF16)
    grad_normed_two = nt(grad_gate, w_gate) + nt(grad_up, w_up)
    gain_two_part = jnp.sum(grad_normed_two * scaled_two, axis=0)
    grad_resid = cot.astype(F32) + norm_back(grad_normed_two, scaled_two, inverse_two, gain_two)
    grad_branch = grad_resid.astype(BF16)

    grad_heads = local_call(
        functools.partial(branch_kernel, sizes), whole((kvh, 2, stack, LANES), BF16), "branch"
    )(grad_branch, w_out)

    segq_row, segk_col = segq[None, :], segk[:, :, None]
    grad_query, grad_kv = local_call(
        functools.partial(attend_back_kernel, n),
        (whole((kvh, 2, stack, LANES), F32), whole((n, 2, block, kvh * LANES), F32)),
        "attend_back",
        grid=(kvh,),
        in_specs=[smem, smem, full(segq_row), full(segk_col)]
        + [per_group, kv_spec, per_group, per_group, per_group],
        out_specs=(per_group, kv_spec),
        scratch_shapes=[
            pltpu.VMEM((4, 8, stack), F32),
            pltpu.VMEM((2, LANES, stack), F32),
        ],
    )(me_arr, pick, segq_row, segk_col, q, kv_all, grad_heads, attended_heads, lse)

    kv_sum = lax.psum_scatter(grad_kv, "ctx", scatter_dimension=0, tiled=False)
    grad_projected = local_call(
        functools.partial(unrope_kernel, sizes), whole((row_count, qkv_width), BF16), "unrope"
    )(grad_query, kv_sum, cos, sin)

    x_float = x.astype(F32)
    inverse_one = lax.rsqrt(jnp.mean(x_float * x_float, axis=1, keepdims=True) + EPSILON)
    scaled_one = x_float * inverse_one
    grad_normed_one = nt(grad_projected, w_qkv)
    gain_one_part = jnp.sum(grad_normed_one * scaled_one, axis=0)
    tokens_grad = (
        grad_resid + norm_back(grad_normed_one, scaled_one, inverse_one, gain_one)
    ).astype(BF16)

    def spread(partial):
        rows = lax.psum_scatter(partial.astype(BF16), "fsdp", scatter_dimension=0, tiled=True)
        return lax.psum(rows, "ctx").astype(F32)

    grad_gate_w = spread(tn(normed_two, grad_gate))
    grad_up_w = spread(tn(normed_two, grad_up))
    grad_down_w = spread(tn(product, cot))
    grad_out_w = spread(tn(attended, grad_branch))
    grad_qkv_w = spread(tn(normed_one, grad_projected))
    gains = spread(jnp.stack([gain_one_part, gain_two_part], axis=1))
    return (
        ordered(result.astype(BF16))[None],
        ordered(tokens_grad)[None],
        gains[:, 0],
        grad_qkv_w[:, :width],
        grad_qkv_w[:, width : width + kv_width],
        grad_qkv_w[:, width + kv_width :],
        grad_out_w,
        gains[:, 1],
        grad_gate_w,
        grad_up_w,
        grad_down_w,
    )


def solution(mesh):
    rows, matrix, vector = P("fsdp", "ctx", None), P("fsdp", None), P("fsdp")
    cube = dict(mesh.shape) == {"ctx": 8, "fsdp": 4}
    return jax.shard_map(
        cube_body if cube else general_body,
        mesh=mesh,
        in_specs=(rows, vector, matrix, matrix, matrix, matrix, vector, matrix, matrix, matrix)
        + (rows, matrix, P()),
        out_specs=(rows, rows, vector, matrix, matrix, matrix, matrix, vector, matrix, matrix, matrix),
        check_vma=False,
    )
```

```python
import functools

import jax
import jax.numpy as jnp
import numpy as np
from jax import lax
from jax.experimental import pallas as pl
from jax.experimental.pallas import tpu as pltpu
from jax.sharding import PartitionSpec as P

HD = 64
LANES = 128
EPSILON = 1e-05
THETA = 100000.0
MASKED = -1e30
LOG2E = 1.4426950408889634
VMEM_LIMIT = 63 * 1024 * 1024
F32 = jnp.float32
BF16 = jnp.bfloat16


def nt(left, right):
    return lax.dot_general(left, right, (((1,), (1,)), ((), ())), preferred_element_type=F32)


def nn(left, right):
    return lax.dot_general(left, right, (((1,), (0,)), ((), ())), preferred_element_type=F32)


def tn(left, right):
    return lax.dot_general(left, right, (((0,), (0,)), ((), ())), preferred_element_type=F32)


def rope_tile(tile, cos, sin):
    lane = lax.broadcasted_iota(jnp.int32, tile.shape, 1) % HD
    partner = jnp.where(
        lane < HD // 2,
        pltpu.roll(tile, LANES - HD // 2, 1),
        pltpu.roll(tile, HD // 2, 1),
    )
    return tile * cos + partner * sin


def head_of(tiles, index):
    start = (index % 2) * HD
    return tiles[index // 2][:, start : start + HD]


MESH = pl.DeviceIdType.MESH
ATTN, FF, DOWN = 0, 1, 2
CORE, FIRST, SECOND = -1, -2, -3


class Links:
    def __init__(self, core, fsdp, send, recv, plan):
        self.core = core
        self.fsdp = fsdp
        self.ctx = lax.axis_index("ctx")
        self.z = lax.axis_index("fsdp")
        self.chip = self.ctx // 2
        self.first = 1 if core == 0 else 2
        self.second = 3 - self.first
        self.send_sem, self.recv_sem = send, recv
        self.plan = plan
        self.open = []

    def target(self, hop):
        if hop == CORE:
            return (lax.bitwise_xor(self.ctx, 1), self.z)
        if hop == FIRST:
            return (lax.bitwise_xor(self.ctx, 2 * self.first), self.z)
        if hop == SECOND:
            return (lax.bitwise_xor(self.ctx, 2 * self.second), self.z)
        return (self.ctx, lax.bitwise_xor(self.z, hop))

    def copy(self, key, hop, src, dst):
        slot = self.plan.setdefault(key, len(self.plan))
        return pltpu.make_async_remote_copy(
            src_ref=src,
            dst_ref=dst,
            send_sem=self.send_sem.at[slot],
            recv_sem=self.recv_sem.at[slot],
            device_id=self.target(hop),
            device_id_type=MESH,
        )

    def send(self, key, hop, src, dst):
        copy = self.copy(key, hop, src, dst)
        copy.start()
        self.open.append((key, getattr(src, "ref", src), src.shape))

    def landed(self, key, dst):
        self.copy(key, CORE, dst, dst).wait_recv()

    def drain(self):
        for key, base, shape in self.open:
            at = (0,) * (len(base.shape) - len(shape)) + tuple(pl.ds(0, size) for size in shape)
            self.copy(key, CORE, base.at[at], base.at[at]).wait_send()


def greet(hops, fsdp):
    ctx, z = lax.axis_index("ctx"), lax.axis_index("fsdp")
    barrier = pltpu.get_barrier_semaphore()
    targets = [(lax.bitwise_xor(ctx, h), z) for h in (1, 2, 4)]
    if "z" in hops:
        targets += [(ctx, lax.bitwise_xor(z, d)) for d in range(1, fsdp)]
    for target in targets:
        pl.semaphore_signal(barrier, inc=1, device_id=target, device_id_type=MESH)
    pl.semaphore_wait(barrier, len(targets))


def by_core(program):
    for core in (0, 1):
        pl.when(lax.axis_index("ctx") % 2 == core)(functools.partial(program, core))


def sub(base, size, unit):
    return pl.ds(pl.multiple_of(base, unit), size)


def lanes(ref, tiles, rows=slice(None)):
    return jnp.concatenate([ref[t, rows, :] for t in tiles], axis=1)


def flat_lanes(ref, tiles, shard):
    stacked = [
        jnp.concatenate([ref[zi, t * shard : (t + 1) * shard, :] for zi in range(ref.shape[0])], axis=0)
        for t in tiles
    ]
    return jnp.concatenate(stacked, axis=1)


def pack_tiles(parts):
    matrix = jnp.concatenate(parts, axis=1)
    short = -matrix.shape[1] % LANES
    if short:
        matrix = jnp.concatenate([matrix, jnp.zeros((matrix.shape[0], short), matrix.dtype)], axis=1)
    return [matrix[:, t * LANES : (t + 1) * LANES] for t in range(matrix.shape[1] // LANES)]


class Share:
    def __init__(self, name, core, shard):
        self.name, self.core = name, core
        self.shard = shard
        self.offset, self.rows = 0, shard
        if name == ATTN:
            half = -(-shard // 32) * 16
            self.offset, self.rows = (0, half) if core == 0 else (half, shard - half)

    def at(self, ref, zi, q):
        rows = sub(zi * self.shard + self.offset, self.rows, 16)
        if self.name == ATTN:
            return ref.at[pl.ds(q * (ref.shape[0] // 4), ref.shape[0] // 4), rows]
        if self.name == FF:
            return ref.at[self.core, pl.ds(q * (ref.shape[1] // 4), ref.shape[1] // 4), rows]
        return ref.at[2 * q + self.core, rows]

    def buffer(self, ref):
        return ref.at[:, pl.ds(0, self.rows)] if self.name == ATTN else ref


class Flat:
    def __init__(self, core):
        self.core = core

    def at(self, ref, zi, q):
        size = ref.shape[1] // 8
        return ref.at[zi, sub((2 * q + self.core) * size, size, 16)]


PACKAGES = (ATTN, FF, DOWN)
QKV, OUT = 3, 4
GATHERED = (QKV, OUT, FF, DOWN)
FINISH = 0


def both_cores(make):
    tables = [make(0), make(1)]

    def run(*names):
        for core in (0, 1):
            def program(core=core):
                for name in names:
                    tables[core][name]()

            pl.when(lax.axis_index("ctx") % 2 == core)(program)

    return run


def weight_stages(core, fsdp, plan, refs, send, recv):
    links = Links(core, fsdp, send, recv, plan)
    z, chip = links.z, links.chip
    near, far = lax.bitwise_xor(chip, links.first), lax.bitwise_xor(chip, links.second)
    corner = lax.bitwise_xor(chip, 3)
    shards = {FF: refs[FF].shape[2] // fsdp, DOWN: refs[DOWN].shape[1] // fsdp}

    def shares(core):
        cut = {k: Share(k, core, shards[k]) for k in shards}
        return {**cut, QKV: Flat(core), OUT: Flat(core)}

    mine, twin = shares(core), shares(1 - core)
    stages = {}

    def over_z(k):
        here = mine[k].at(refs[k], z, chip)
        for d in range(1, fsdp):
            links.send((k, "z", d), d, here, here)

    def spread(k):
        for d in range(1, fsdp):
            piece = mine[k].at(refs[k], lax.bitwise_xor(z, d), chip)
            links.landed((k, "z", d), piece)
            links.send((k, FIRST, d), FIRST, piece, piece)
            links.send((k, SECOND, d), SECOND, piece, piece)
            links.send((k, CORE, d, 0), CORE, piece, piece)

    def forward(k):
        for d in range(1, fsdp):
            piece = mine[k].at(refs[k], lax.bitwise_xor(z, d), near)
            links.landed((k, FIRST, d), piece)
            links.send((k, "corner", d), SECOND, piece, piece)
            links.send((k, CORE, d, 1), CORE, piece, piece)

    def pass_some(k, i, what, q):
        for d in range(1, fsdp):
            piece = mine[k].at(refs[k], lax.bitwise_xor(z, d), q)
            links.landed((k, what, d), piece)
            links.send((k, CORE, d, i), CORE, piece, piece)

    def pass_far(k):
        pass_some(k, 2, SECOND, far)

    def pass_corner(k):
        pass_some(k, 3, "corner", corner)

    def finish_some(k, i, q):
        for d in range(1, fsdp):
            links.landed((k, CORE, d, i), twin[k].at(refs[k], lax.bitwise_xor(z, d), q))

    def finish(k):
        for i in range(4):
            stages[FINISH, k, i]()

    for k in GATHERED:
        for i, q in ((0, chip), (1, far), (2, near), (3, corner)):
            stages[FINISH, k, i] = functools.partial(finish_some, k, i, q)
    for k in GATHERED:
        for fn in (over_z, spread, forward, pass_far, pass_corner, finish):
            stages[fn.__name__, k] = functools.partial(fn, k)

    def gains_out():
        for d in range(1, fsdp):
            links.send(("gains", d), d, refs["gains"].at[z], refs["gains"].at[z])

    def gains_in():
        for d in range(1, fsdp):
            links.landed(("gains", d), refs["gains"].at[lax.bitwise_xor(z, d)])

    stages["gains_out"], stages["gains_in"], stages["drain"] = gains_out, gains_in, links.drain
    return stages


def kv_stages(core, plan, kv_all, send, recv):
    links = Links(core, 1, send, recv, plan)
    ctx = links.ctx
    near = lax.bitwise_xor(ctx, 2 * links.first)
    far = lax.bitwise_xor(ctx, 2 * links.second)
    corner = lax.bitwise_xor(ctx, 6)

    def start():
        for b in range(2):
            piece = kv_all.at[ctx, b]
            links.send(("kv first", b), FIRST, piece, piece)
            links.send(("kv second", b), SECOND, piece, piece)
            links.send(("kv core", 0, b), CORE, piece, piece)

    def forward():
        for b in range(2):
            piece = kv_all.at[near, b]
            links.landed(("kv first", b), piece)
            links.send(("kv corner", b), SECOND, piece, piece)
            links.send(("kv core", 1, b), CORE, piece, piece)

    def pass_some(i, what, owner):
        for b in range(2):
            piece = kv_all.at[owner, b]
            links.landed((what, b), piece)
            links.send(("kv core", i, b), CORE, piece, piece)

    def finish(i, owner):
        for b in range(2):
            links.landed(("kv core", i, b), kv_all.at[lax.bitwise_xor(owner, 1), b])

    stages = {"start": start, "forward": forward, "drain": links.drain}
    stages["pass_far"] = functools.partial(pass_some, 2, "kv second", far)
    stages["pass_corner"] = functools.partial(pass_some, 3, "kv corner", corner)
    for i, owner in ((0, ctx), (1, far), (2, near), (3, corner)):
        stages[FINISH, i] = functools.partial(finish, i, owner)
    return stages


def store_projection(sizes, raw_tiles, cos, sin, q_ref, kv_at):
    heads, kvh, block = sizes
    share = heads // kvh
    tiles = [rope_tile(raw_tiles[j], cos, sin).astype(BF16) for j in range((heads + kvh) // 2)]
    tiles += [raw_tiles[j].astype(BF16) for j in range((heads + kvh) // 2, len(raw_tiles))]

    def head(index):
        start = (index % 2) * HD
        return tiles[index // 2][:, start : start + HD]

    zero = jnp.zeros((block, HD), BF16)
    for h in range(heads):
        piece = head(h) * jnp.asarray(0.125, BF16)
        g, i = h // share, h % share
        for b in range(2):
            q_ref[g, b, i * block : (i + 1) * block, :] = jnp.concatenate(
                [piece[b * block : (b + 1) * block], zero], axis=1
            )
    for g in range(kvh):
        pair = jnp.concatenate([head(heads + g), head(heads + kvh + g)], axis=1)
        for b in range(2):
            kv_at(b, g)[...] = pair[b * block : (b + 1) * block]


def rms_inverse(x):
    return lax.rsqrt(jnp.mean(x * x, axis=1, keepdims=True) + EPSILON)


def natural_blocks(deal_ref, c):
    one, two = deal_ref[2 * c], deal_ref[2 * c + 1]
    return jnp.minimum(one, two), jnp.maximum(one, two)


def segment_start(lengths_ref, offset):
    start = jnp.zeros_like(offset)
    ending = 0
    for c in range(lengths_ref.shape[1]):
        ending = ending + lengths_ref[0, c]
        start = jnp.where(offset >= ending, ending, start)
    return start


def ordered(flip, rows):
    half = rows.shape[0] // 2
    return jnp.where(flip, jnp.concatenate([rows[half:], rows[:half]], axis=0), rows)


def first_keys(n, deal_ref, lengths_ref, block, rows):
    _, last = natural_blocks(deal_ref, lax.axis_index("ctx"))
    offset = (last - n) * block + lax.rem(lax.broadcasted_iota(jnp.int32, (8, rows), 1), block)
    return segment_start(lengths_ref, offset)


def attend_masks(n, deal_ref, start_ref, block, rows):
    key = lax.broadcasted_iota(jnp.int32, (block, rows), 0)

    def own(b):
        allowed = key <= lax.rem(lax.broadcasted_iota(jnp.int32, (block, rows), 1), block)
        if b == 0:
            return allowed
        _, last = natural_blocks(deal_ref, lax.axis_index("ctx"))
        return allowed & (key >= start_ref[0:1, :] - (last - n) * block)

    def other(at):
        mine, _ = natural_blocks(deal_ref, lax.axis_index("ctx"))
        first, last = natural_blocks(deal_ref, at)
        kind = jnp.where(first >= mine, 1, 0)
        bound = jnp.where(kind == 0, -1, start_ref[0:1, :] - (last - n) * block)
        return kind, key >= bound

    return own, other


def attend_step(n, me, g, at, deal_ref, start_ref, q_ref, kv_ref, top_ref, acc_ref):
    block = kv_ref.shape[3]
    rows = q_ref.shape[2]
    value_lane = lax.broadcasted_iota(jnp.int32, (block, LANES), 1) >= HD
    own_mask, other_mask = attend_masks(n, deal_ref, start_ref, block, rows)

    def scores(kind, tile, mask):
        s = nt(tile, q_ref[g, kind])
        return s if mask is None else jnp.where(mask, s, MASKED)

    def weigh(s, top, tile):
        p = jnp.exp2((s - top) * LOG2E).astype(BF16)
        return tn(jnp.where(value_lane, tile, jnp.asarray(1, BF16)), p)

    def own():
        own0, own1 = kv_ref[me, 0, g], kv_ref[me, 1, g]
        s0 = scores(0, own0, own_mask(0))
        top0 = jnp.max(s0, axis=0, keepdims=True)
        acc_ref[g, 0] = weigh(s0, top0, own0)
        top_ref[g, 0] = jnp.broadcast_to(top0, top_ref.shape[2:])
        s1 = scores(1, own1, own_mask(1))
        s2 = scores(1, own0, None)
        top1 = jnp.maximum(jnp.max(s1, axis=0, keepdims=True), jnp.max(s2, axis=0, keepdims=True))
        acc_ref[g, 1] = weigh(s1, top1, own1) + weigh(s2, top1, own0)
        top_ref[g, 1] = jnp.broadcast_to(top1, top_ref.shape[2:])

    def other():
        kind, mask = other_mask(at)
        is_prompt = kind == 0
        tile0 = kv_ref[at, 0, g]
        tile1 = jnp.where(is_prompt, tile0, kv_ref[at, 1, g])
        s1 = scores(1, tile0, None)
        s2 = scores(kind, tile1, mask)
        old_p, old_c = top_ref[g, 0, 0:1, :], top_ref[g, 1, 0:1, :]
        high1 = jnp.max(s1, axis=0, keepdims=True)
        high2 = jnp.max(s2, axis=0, keepdims=True)
        top_p = jnp.where(is_prompt, jnp.maximum(old_p, high2), old_p)
        top_c = jnp.maximum(old_c, jnp.where(is_prompt, high1, jnp.maximum(high1, high2)))
        part1 = weigh(s1, top_c, tile0)
        part2 = weigh(s2, jnp.where(is_prompt, top_p, top_c), tile1)
        acc_ref[g, 0] = acc_ref[g, 0] * jnp.exp2((old_p - top_p) * LOG2E) + jnp.where(is_prompt, part2, 0.0)
        acc_ref[g, 1] = (
            acc_ref[g, 1] * jnp.exp2((old_c - top_c) * LOG2E) + part1 + jnp.where(is_prompt, 0.0, part2)
        )
        top_ref[g, 0] = jnp.broadcast_to(top_p, top_ref.shape[2:])
        top_ref[g, 1] = jnp.broadcast_to(top_c, top_ref.shape[2:])

    return own, other


def attend_close(g, top_ref, acc_ref, o_ref, lse_ref):
    for b in range(2):
        acc = acc_ref[g, b]
        total = acc[0:1, :]
        o_ref[g, b] = (acc / total).T
        lse_ref[g, b] = jnp.broadcast_to(top_ref[g, b, 0:1, :] * LOG2E + jnp.log2(total), lse_ref.shape[2:])


def attend_back_step(n, me, g, j, deal_ref, start_ref, q_ref, kv_ref, do_ref, lse_ref, delta_ref, dqt_ref, dkv_ref):
    block = kv_ref.shape[3]
    rows = q_ref.shape[2]
    own_mask, other_mask = attend_masks(n, deal_ref, start_ref, block, rows)

    def pair(kind, tile, mask):
        q = q_ref[g, kind]
        do = do_ref[g, kind]
        p = jnp.exp2(nt(tile, q) * LOG2E - lse_ref[g, kind, 0:1, :])
        if mask is not None:
            p = jnp.where(mask, p, 0.0)
        ds = (p * (nt(tile, do) - delta_ref[g, kind, 0:1, :])).astype(BF16)
        return nn(ds, q) + nn(p.astype(BF16), do), tn(tile, ds)

    def own():
        own0, own1 = kv_ref[me, 0, g], kv_ref[me, 1, g]
        d0, q0 = pair(0, own0, own_mask(0))
        d1, q1 = pair(1, own1, own_mask(1))
        d2, q2 = pair(1, own0, None)
        dkv_ref[me, g, 0] = (d0 + d2).astype(dkv_ref.dtype)
        dkv_ref[me, g, 1] = d1.astype(dkv_ref.dtype)
        dqt_ref[0] = q0
        dqt_ref[1] = q1 + q2

    def other():
        at = lax.rem(me + j, n)
        kind, mask = other_mask(at)
        is_prompt = kind == 0
        full, q_full = pair(1, kv_ref[at, 0, g], None)
        part, q_part = pair(kind, kv_ref[at, kind, g], mask)
        dkv_ref[at, g, 0] = (full + jnp.where(is_prompt, part, 0.0)).astype(dkv_ref.dtype)
        dkv_ref[at, g, 1] = jnp.where(is_prompt, 0.0, part).astype(dkv_ref.dtype)
        dqt_ref[0] = dqt_ref[0] + jnp.where(is_prompt, q_part, 0.0)
        dqt_ref[1] = dqt_ref[1] + q_full + jnp.where(is_prompt, 0.0, q_part)

    return own, other


def row_deltas(g, do_ref, o_ref, row_ref):
    ones = jnp.ones((8, LANES), F32)
    for b in range(2):
        row_ref[b] = lax.dot_general(
            ones, do_ref[g, b].astype(F32) * o_ref[g, b], (((1,), (1,)), ((), ())),
            precision=lax.Precision.HIGHEST, preferred_element_type=F32,
        )


def gain_row(gains_ref, which, fsdp, shard):
    return jnp.concatenate([gains_ref[i, which : which + 1, :shard] for i in range(fsdp)], axis=1)


def project(sizes, fsdp, x_ref, gains_ref, attn_ref, cos_ref, sin_ref, n1_ref, q_ref, kv_at):
    heads, kvh, block = sizes
    x = x_ref[...].astype(F32)
    normed = (x * rms_inverse(x) * gain_row(gains_ref, 0, fsdp, x.shape[1] // fsdp)).astype(BF16)
    n1_ref[...] = normed
    count = -(-(heads + 2 * kvh) * HD // LANES)
    shard = x.shape[1] // fsdp
    raw = []
    for t in range(0, count, 2):
        some = range(t, min(t + 2, count))
        wide = nn(normed, flat_lanes(attn_ref, some, shard))
        raw += [wide[:, i * LANES : (i + 1) * LANES] for i in range(len(some))]
    store_projection(sizes, raw, cos_ref[...], sin_ref[...], q_ref, kv_at)


def front_kernel(
    sizes, n, fsdp, plans, deal_ref, lengths_ref, xt_ref, gain_one_in, gain_two_in, turns_ref,
    wq_ref, wkt_ref, wvt_ref, wo_ref, wg_ref, wu_ref, wdt_ref, cott_ref,
    x_ref, cos_ref, sin_ref, n1_ref, q_ref, kv_out, lse_ref, gains_ref, qkv_out,
    result_ref, gr_ref, do_ref, delta_ref, gain_ref, out_grad, ff_grad, down_grad,
    qkv, wout, ff, down, kv_all, o_ref, gains, start_ref, top_ref, acc_ref, cot_ref,
    resid_ref, n2_ref, product_ref, gg_ref, gu_ref, turned_ref, gn_ref, out_stage, ff_stage, down_stage,
    send, recv, kv_send, kv_recv, local, out_sem,
):
    heads, kvh, block = sizes
    me, z = lax.axis_index("ctx"), lax.axis_index("fsdp")
    shard = wq_ref.shape[0]
    rows = sub(z * shard, shard, 16)
    for ref, parts in ((qkv, [wq_ref[...], wkt_ref[...].T, wvt_ref[...].T]), (wout, [wo_ref[...]])):
        for t, tile in enumerate(pack_tiles(parts)):
            ref[z, t * shard : (t + 1) * shard, :] = tile
    used = -(-(heads + 2 * kvh) * HD // LANES) * shard
    qkv[z, used:, :] = jnp.zeros((qkv.shape[1] - used, LANES), BF16)
    gains[z] = jnp.zeros(gains.shape[1:], F32)
    for i, ref in enumerate((gain_one_in, gain_two_in)):
        gains[z, i : i + 1, 0:shard] = ref[...].astype(F32)
    greet("z", fsdp)
    refs = {QKV: qkv, OUT: wout, FF: ff, DOWN: down, "gains": gains}
    run = both_cores(lambda core: weight_stages(core, fsdp, plans[0], refs, send, recv))
    run_kv = both_cores(lambda core: kv_stages(core, plans[1], kv_all, kv_send, kv_recv))
    run("gains_out", ("over_z", QKV))
    for t in range(ff.shape[1]):
        ff[0, t, rows, :] = wg_ref[:, t * LANES : (t + 1) * LANES]
        ff[1, t, rows, :] = wu_ref[:, t * LANES : (t + 1) * LANES]
    down_shard = wdt_ref.shape[1]
    down_rows = sub(z * down_shard, down_shard, 16)
    for t, tile in enumerate(pack_tiles([wdt_ref[...].T])):
        down[t, down_rows, :] = tile
    first, last = natural_blocks(deal_ref, me)
    flip = deal_ref[2 * me] > deal_ref[2 * me + 1]
    x_ref[...] = ordered(flip, xt_ref[...].T)
    cot_ref[...] = ordered(flip, cott_ref[...].T)
    row = lax.broadcasted_iota(jnp.int32, cos_ref.shape, 0)
    natural = jnp.where(row < block, first * block + row, (last - 1) * block + row)
    offset = natural - n * block
    position = jnp.where(offset < 0, natural, natural - segment_start(lengths_ref, offset))
    angle = position.astype(F32) * turns_ref[0:1, :]
    lane = lax.broadcasted_iota(jnp.int32, cos_ref.shape, 1)
    cos_ref[...] = jnp.cos(angle)
    sine = jnp.sin(angle)
    sin_ref[...] = jnp.where(lax.rem(lane, HD) < HD // 2, -sine, sine)
    start_ref[...] = first_keys(n, deal_ref, lengths_ref, block, start_ref.shape[1])
    run(("spread", QKV), ("over_z", OUT), ("over_z", DOWN), ("over_z", FF), ("forward", QKV))
    run(("pass_far", QKV), ("pass_corner", QKV), ("finish", QKV), "gains_in")
    project(
        sizes, fsdp, x_ref, gains, qkv, cos_ref, sin_ref, n1_ref, q_ref,
        lambda b, g: kv_all.at[me, b, g],
    )
    run_kv("start")
    gains_ref[...] = gains[...]
    outs = [pltpu.make_async_copy(qkv, qkv_out, local.at[0]), pltpu.make_async_copy(kv_all, kv_out, local.at[1])]
    outs[0].start()
    kv_schedule = {
        kvh: ((FINISH, 0),),
        2 * kvh: ("forward", "pass_far"),
        4 * kvh: ((FINISH, 1), (FINISH, 2)),
        6 * kvh: ("pass_corner",),
        7 * kvh: ((FINISH, 3),),
    }
    schedule = {
        3: (("spread", OUT),),
        11: (("spread", DOWN),),
        14: (("forward", OUT),),
        18: (("forward", DOWN),),
        20: (("spread", FF),),
        24: (("pass_far", OUT), ("pass_corner", OUT)),
        28: (("pass_far", DOWN), ("pass_corner", DOWN)),
        32: (("forward", FF),),
        38: (("finish", OUT), ("finish", DOWN)),
    }

    @pl.loop(0, kvh * n)
    def _(step):
        j, g = step // kvh, step % kvh
        turn = jnp.where(j == 3, 4, jnp.where(j == 4, 3, j))
        for at, names in kv_schedule.items():
            pl.when(step == at)(functools.partial(run_kv, *names))
        for at, names in schedule.items():
            pl.when(step == at)(functools.partial(run, *names))
        own, other = attend_step(
            n, me, g, lax.bitwise_xor(me, turn), deal_ref, start_ref, q_ref, kv_all, top_ref, acc_ref
        )
        pl.when(j == 0)(own)
        pl.when(j > 0)(other)
        pl.when(j == n - 1)(lambda: attend_close(g, top_ref, acc_ref, o_ref, lse_ref))

    outs[1].start()
    run(("pass_far", FF))

    def quarter_ready(i):
        pl.when(i == 0)(lambda: run((FINISH, FF, 0)))
        pl.when(i == 1)(lambda: run((FINISH, FF, 1), (FINISH, FF, 2)))
        pl.when(i == 3)(lambda: run(("pass_corner", FF), (FINISH, FF, 3)))
        return lax.bitwise_xor(me // 2, i)

    feed_forward(
        sizes, fsdp, quarter_ready, x_ref, cot_ref, gains, wout, ff, down, o_ref,
        result_ref, gr_ref, do_ref, delta_ref, gain_ref, out_grad, ff_grad, down_grad,
        resid_ref, n2_ref, product_ref, gg_ref, gu_ref, turned_ref, gn_ref, out_stage, ff_stage, down_stage, out_sem,
    )
    run("drain")
    run_kv("drain")
    for copy in outs:
        copy.wait()


def head_columns(sizes, ref, low):
    heads, kvh, block = sizes
    share = heads // kvh
    return jnp.concatenate(
        [
            jnp.concatenate(
                [
                    ref[h // share, b, (h % share) * block : (h % share + 1) * block, low : low + HD]
                    for h in range(heads)
                ],
                axis=1,
            )
            for b in range(2)
        ],
        axis=0,
    )


def feed_forward(
    sizes, fsdp, quarter_ready, x_ref, cot_ref, gains_ref, wout_ref, ff_ref, down_ref, o_ref,
    result_ref, gr_ref, do_ref, delta_ref, gain_ref, out_grad, ff_grad, down_grad,
    resid_ref, n2_ref, product_ref, gg_ref, gu_ref, turned_ref, gn_ref, out_stage, ff_stage, down_stage, sem,
):
    heads, kvh, block = sizes
    share = heads // kvh
    rows, width = x_ref.shape
    shard = width // fsdp
    half = (heads + 2 * kvh) * HD % LANES
    out_tiles = -(-width // LANES)
    down_tiles = down_ref.shape[0]
    gain = gain_row(gains_ref, 1, fsdp, width // fsdp)
    attended = head_columns(sizes, o_ref, HD).astype(BF16)
    pieces = []
    for t in range(0, out_tiles, 2):
        pieces.append(nn(attended, flat_lanes(wout_ref, range(t, min(t + 2, out_tiles)), shard)))
    resid = x_ref[...].astype(F32) + jnp.concatenate(pieces, axis=1)[:, :width]
    resid_ref[...] = resid
    n2_ref[...] = (resid * rms_inverse(resid) * gain).astype(BF16)
    pad = down_tiles * LANES - width
    wide = 2 * LANES
    per = ff_ref.shape[1] // 4
    turned_ref[...] = n2_ref[...].T
    gn_ref[...] = jnp.zeros(gn_ref.shape, F32)
    gr_ref[...] = jnp.zeros(gr_ref.shape, F32)

    def moves(q):
        columns = sub(q * per * LANES, per * LANES, LANES)
        return (
            pltpu.make_async_copy(ff_stage, ff_grad.at[:, pl.ds(q * per, per)], sem.at[0]),
            pltpu.make_async_copy(down_stage, down_grad.at[:, columns], sem.at[1]),
        )

    @pl.loop(0, 4)
    def _(i):
        q = quarter_ready(i)
        cot_wide = jnp.concatenate([cot_ref[...], jnp.zeros((rows, pad), BF16)], axis=1)
        for low in range(0, per, 2):
            size = min(2, per - low)
            first = q * per + low
            at = sub(first * LANES, size * LANES, LANES)
            n2 = n2_ref[...]
            gate = nn(n2, jnp.concatenate([ff_ref[0, first + t] for t in range(size)], axis=1))
            upward = nn(n2, jnp.concatenate([ff_ref[1, first + t] for t in range(size)], axis=1))
            grad = nt(cot_wide, jnp.concatenate([down_ref[t, at, :] for t in range(down_tiles)], axis=1))
            sigma = 1.0 / (1.0 + jnp.exp(-gate))
            activated = gate * sigma
            here = slice(low * LANES, (low + size) * LANES)
            product_ref[:, here] = (activated * upward).astype(BF16)
            gg_ref[:, here] = (grad * upward * (sigma + activated * (1.0 - sigma))).astype(BF16)
            gu_ref[:, here] = (grad * activated).astype(BF16)
        for low in range(0, width, wide):
            size = min(wide, width - low)
            part = 0.0
            for c, grad_ref in enumerate((gg_ref, gu_ref)):
                weights = [ff_ref[c, q * per + t, low : low + size, :] for t in range(per)]
                part = part + nt(grad_ref[...], jnp.concatenate(weights, axis=1))
            gn_ref[:, low : low + size] = gn_ref[:, low : low + size] + part
        columns = sub(q * per * LANES, per * LANES, LANES)
        for t in range(0, down_tiles, 2):
            low, high = t * LANES, min((t + 2) * LANES, width)
            weights = jnp.concatenate([down_ref[t, columns, :], down_ref[t + 1, columns, :]], axis=1)
            part = nn(product_ref[...], weights)
            gr_ref[:, low:high] = gr_ref[:, low:high] + part[:, : high - low]

        @pl.when(i >= 1)
        def _():
            for copy in moves(q):
                copy.wait()

        for low in range(0, per, 2):
            size = min(2, per - low)
            here = slice(low * LANES, (low + size) * LANES)
            for c, grad_ref in enumerate((gg_ref, gu_ref)):
                part = nn(turned_ref[...], grad_ref[:, here]).astype(BF16)
                for t in range(size):
                    ff_stage[c, low + t] = part[:, t * LANES : (t + 1) * LANES]
            part = nn(product_ref[:, here].T, cot_wide).astype(BF16)
            for t in range(down_tiles):
                down_stage[t, here, :] = part[:, t * LANES : (t + 1) * LANES]
        for copy in moves(q):
            copy.start()

    result_ref[...] = (resid_ref[...] + gr_ref[...]).astype(BF16)
    grad_normed = gn_ref[...]
    resid = resid_ref[...]
    inverse = rms_inverse(resid)
    scaled = resid * inverse
    weighted = grad_normed * gain
    gain_ref[0:1, :] = jnp.sum(grad_normed * scaled, axis=0, keepdims=True)
    grad_resid = cot_ref[...].astype(F32) + inverse * (
        weighted - scaled * jnp.mean(weighted * scaled, axis=1, keepdims=True)
    )
    gr_ref[...] = grad_resid
    gb = grad_resid.astype(BF16)
    main = width - (LANES - half)
    lined = jnp.concatenate([jnp.zeros((rows, half), BF16), gb[:, main:], gb[:, :main]], axis=1)
    turned_ref[...] = head_columns(sizes, o_ref, HD).astype(BF16).T
    for t in range(0, out_tiles, 2):
        part = nn(turned_ref[...], lined[:, t * LANES : (t + 2) * LANES]).astype(BF16)
        out_stage[t] = part[:, :LANES]
        out_stage[t + 1] = part[:, LANES:]
    out_copy = pltpu.make_async_copy(out_stage, out_grad, sem.at[2])
    out_copy.start()
    gb_wide = jnp.concatenate([gb, jnp.zeros((rows, out_tiles * LANES - width), BF16)], axis=1)
    grad_att = []
    for zi in range(fsdp):
        weights = [wout_ref[zi, t * shard : (t + 1) * shard, :] for t in range(out_tiles)]
        grad_att.append(nt(gb_wide, jnp.concatenate(weights, axis=1)).astype(BF16))
    grad_att = jnp.concatenate(grad_att, axis=1)
    zero = jnp.zeros((block, HD), BF16)
    for h in range(heads):
        for b in range(2):
            do_ref[h // share, b, (h % share) * block : (h % share + 1) * block, :] = jnp.concatenate(
                [zero, grad_att[b * block : (b + 1) * block, h * HD : (h + 1) * HD]], axis=1
            )
    for g in range(kvh):
        row_deltas(g, do_ref, o_ref, delta_ref.at[g])
    for copy in moves(0):
        copy.wait()
    out_copy.wait()


def add_rows(out, terms, rows):
    def add(views):
        total = views[1][0:rows, :].astype(F32)
        for term in views[2:]:
            total = total + term[0:rows, :].astype(F32)
        views[0][0:rows, :] = total.astype(out.dtype)

    refs = [out] + list(terms)
    if len(out.shape) == 2:
        add(refs)
    else:

        @pl.loop(0, out.shape[0])
        def _(lead):
            add([r.at[lead] for r in refs])


def grad_stages(core, fsdp, plan, sources, held, got, outs, gain_refs, send, recv, local):
    links = Links(core, fsdp, send, recv, plan)
    z, chip = links.z, links.chip
    near, far = lax.bitwise_xor(chip, links.first), lax.bitwise_xor(chip, links.second)
    corner = lax.bitwise_xor(chip, 3)
    shards = {k: sources[k].shape[-2] // fsdp for k in PACKAGES}
    mine = {k: Share(k, core, shards[k]) for k in PACKAGES}
    twin = {k: Share(k, 1 - core, shards[k]) for k in PACKAGES}
    stages = {}

    def slot_of(d):
        return max(d - 1, 0)

    def hold(k, d, q):
        if k in held:
            return held[k].at[d, q]
        return mine[k].at(sources[k], lax.bitwise_xor(z, d), q)

    def load(k, d, q):
        slot = (PACKAGES.index(k) * fsdp + d) * 4 + q
        return pltpu.make_async_copy(
            mine[k].at(sources[k], lax.bitwise_xor(z, d), q), hold(k, d, q), local.at[slot]
        )

    def begin(k, d):
        zi = lax.bitwise_xor(z, d)
        for q in range(4):
            links.send((k, CORE, d, q), CORE, twin[k].at(sources[k], zi, q), twin[k].buffer(got[k][0].at[d, q]))
            if k in held:
                load(k, d, q).start()

    def stage1(k, d):
        share = mine[k]
        for q in range(4):
            links.landed((k, CORE, d, q), share.buffer(got[k][0].at[d, q]))
            if k in held:
                load(k, d, q).wait()
            terms = [hold(k, d, q), got[k][0].at[d, q]]
            if d == 0:
                links.landed((k, "direct", q), share.buffer(got[k][4].at[q]))
                terms.append(got[k][4].at[q])
            add_rows(hold(k, d, q), terms, share.rows)
            if d == 1:
                links.send((k, "direct", q), d, hold(k, d, q), share.buffer(got[k][4].at[q]))
        for i, q in enumerate((near, corner)):
            if d != 1:
                links.send((k, FIRST, d, i), FIRST, hold(k, d, q), share.buffer(got[k][1].at[slot_of(d), i]))

    def stage2(k, d):
        share, slot = mine[k], slot_of(d)
        if d == 1:
            return
        for i in range(2):
            links.landed((k, FIRST, d, i), share.buffer(got[k][1].at[slot, i]))
        add_rows(hold(k, d, far), (hold(k, d, far), got[k][1].at[slot, 1]), share.rows)
        links.send((k, SECOND, d), SECOND, hold(k, d, far), share.buffer(got[k][2].at[slot]))

    def stage3(k, d):
        share, slot = mine[k], slot_of(d)
        if d == 1:
            return
        links.landed((k, SECOND, d), share.buffer(got[k][2].at[slot]))
        add_rows(hold(k, d, chip), (hold(k, d, chip), got[k][1].at[slot, 0], got[k][2].at[slot]), share.rows)
        if d > 0:
            links.send((k, "z", d), d, hold(k, d, chip), share.buffer(got[k][3].at[d - 2]))

    def out_copy(k):
        slot = len(PACKAGES) * fsdp * 4 + PACKAGES.index(k)
        return pltpu.make_async_copy(hold(k, 0, chip), mine[k].at(outs[k], 0, chip), local.at[slot])

    def close(k):
        share = mine[k]
        for d in range(2, fsdp):
            links.landed((k, "z", d), share.buffer(got[k][3].at[d - 2]))
        final = hold(k, 0, chip)
        add_rows(final, [final] + [got[k][3].at[d - 2] for d in range(2, fsdp)], share.rows)
        for hop in (FIRST, SECOND):
            links.send((k, "out", hop), hop, final, share.at(outs[k], 0, chip))
        links.send((k, "out core", 0), CORE, final, share.at(outs[k], 0, chip))
        out_copy(k).start()

    def close2(k):
        share = mine[k]
        links.landed((k, "out", FIRST), share.at(outs[k], 0, near))
        piece = share.at(outs[k], 0, near)
        links.send((k, "out", "corner"), SECOND, piece, piece)
        links.send((k, "out core", 1), CORE, piece, piece)
        piece = share.at(outs[k], 0, far)
        links.landed((k, "out", SECOND), piece)
        links.send((k, "out core", 2), CORE, piece, piece)

    def close3(k):
        piece = mine[k].at(outs[k], 0, corner)
        links.landed((k, "out", "corner"), piece)
        links.send((k, "out core", 3), CORE, piece, piece)

    def close4(k):
        for i, q in ((0, chip), (1, far), (2, near), (3, corner)):
            links.landed((k, "out core", i), twin[k].at(outs[k], 0, q))
        out_copy(k).wait()

    for k in PACKAGES:
        for fn in (begin, stage1, stage2, stage3):
            for d in range(fsdp):
                stages[fn.__name__, k, d] = functools.partial(fn, k, d)
        for fn in (close, close2, close3, close4):
            stages[fn.__name__, k] = functools.partial(fn, k)

    gain_sum, gain_got, gain_z, gain_out = gain_refs

    def gain_step(i):
        if i > 0:
            links.landed(("gain", i - 1), gain_got.at[i - 1])
            gain_sum[i] = gain_sum[i - 1] + gain_got[i - 1]
        if i < 3:
            links.send(("gain", i), (CORE, FIRST, SECOND)[i], gain_sum.at[i], gain_got.at[i])
        else:
            for d in range(1, fsdp):
                links.send(("gain z", d), d, gain_sum.at[3, lax.bitwise_xor(z, d)], gain_z.at[d - 1])

    def gain_close():
        total = gain_sum[3, z]
        for d in range(1, fsdp):
            links.landed(("gain z", d), gain_z.at[d - 1])
            total = total + gain_z[d - 1]
        gain_out[...] = total

    for i in range(4):
        stages["gain", i] = functools.partial(gain_step, i)
    stages["gain close"] = gain_close
    stages["drain"] = links.drain
    return stages


def kv_grad_stages(core, plan, parts, kv_sum, got0, got1, got2, send, recv):
    links = Links(core, 1, send, recv, plan)
    chip = links.chip
    near, far = lax.bitwise_xor(chip, links.first), lax.bitwise_xor(chip, links.second)
    corner = lax.bitwise_xor(chip, 3)
    rows = parts.shape[3]
    stages = {}

    def start(g):
        for q in range(4):
            links.send((0, g, q), CORE, parts.at[2 * q + 1 - core, g], got0.at[g, q])

    def stage1(g):
        for q in range(4):
            links.landed((0, g, q), got0.at[g, q])
            add_rows(got0.at[g, q], (parts.at[2 * q + core, g], got0.at[g, q]), rows)
        for i, q in enumerate((near, corner)):
            links.send((1, g, i), FIRST, got0.at[g, q], got1.at[g, i])

    def stage2(g):
        for i in range(2):
            links.landed((1, g, i), got1.at[g, i])
        add_rows(got0.at[g, far], (got0.at[g, far], got1.at[g, 1]), rows)
        links.send((2, g), SECOND, got0.at[g, far], got2.at[g])

    def stage3(g):
        links.landed((2, g), got2.at[g])
        add_rows(kv_sum.at[g], (got0.at[g, chip], got1.at[g, 0], got2.at[g]), rows)

    for g in range(parts.shape[1]):
        for i, fn in enumerate((start, stage1, stage2, stage3)):
            stages[i, g] = functools.partial(fn, g)
    stages["drain"] = links.drain
    return stages


def back_kernel(
    sizes, n, fsdp, plans, deal_ref, lengths_ref, q_ref, kv_in, do_ref, delta_ref, lse_ref,
    x_ref, n1_ref, gr_ref, gains_ref, gain_two_ref, cos_ref, sin_ref, qkv_ref, out_grad_ref, ff_grad, down_grad,
    tg_ref, gain_out, attn_out, ff_out, down_out,
    start_ref, spill_ref, chunk_ref, dqt_ref, dq_ref, dkv_ref, kv_sum, kv_got0, kv_got1, kv_got2, gp_ref, gn_ref, turned_ref, attn_grad,
    ff_a, down_a, attn_0, ff_0, down_0, attn_1, ff_1, down_1, attn_2, ff_2, down_2, attn_3, ff_3, down_3, attn_4, ff_4, down_4,
    gain_sum, gain_got, gain_z, send, recv, kv_send, kv_recv, local, ahead_sem,
):
    heads, kvh, block = sizes
    share = heads // kvh
    me = lax.axis_index("ctx")
    width = x_ref.shape[1]
    rows = x_ref.shape[0]
    greet("z", fsdp)
    sources = {ATTN: attn_grad, FF: ff_grad, DOWN: down_grad}
    held = {FF: ff_a, DOWN: down_a}
    got = {
        ATTN: (attn_0, attn_1, attn_2, attn_3, attn_4),
        FF: (ff_0, ff_1, ff_2, ff_3, ff_4),
        DOWN: (down_0, down_1, down_2, down_3, down_4),
    }
    outs = {ATTN: attn_out, FF: ff_out, DOWN: down_out}
    run = both_cores(
        lambda core: grad_stages(
            core, fsdp, plans[0], sources, held, got, outs, (gain_sum, gain_got, gain_z, gain_out), send, recv, local
        )
    )
    run_kv = both_cores(
        lambda core: kv_grad_stages(core, plans[1], dkv_ref, kv_sum, kv_got0, kv_got1, kv_got2, kv_send, kv_recv)
    )
    start_ref[...] = first_keys(n, deal_ref, lengths_ref, block, start_ref.shape[1])
    order = [d for d in range(1, fsdp)] + [0]
    chunks = [(k, d) for k in (FF, DOWN) for d in order]
    steps = []
    for i in range(len(chunks) + 7):
        names = []
        if i < len(chunks):
            names.append(("stage1",) + chunks[i])
        if 1 <= i <= len(chunks):
            names.append(("stage2",) + chunks[i - 1])
        if 2 <= i <= len(chunks) + 1:
            names.append(("stage3",) + chunks[i - 2])
        if i + 1 < len(chunks):
            names.insert(1, ("begin",) + chunks[i + 1])
        for last, k in ((len(order) + 1, FF), (len(chunks) + 1, DOWN)):
            for extra, what in enumerate(("close", "close2", "close3", "close4")):
                if i == last + 1 + extra:
                    names.append((what, k))
        steps.append(names)
    run(("begin",) + chunks[0])
    width_tiles = -(-(heads + 2 * kvh) // 2)
    ahead = [
        pltpu.make_async_copy(out_grad_ref.at[0], spill_ref, ahead_sem.at[0]),
        pltpu.make_async_copy(
            out_grad_ref.at[pl.ds(1, attn_grad.shape[0] - width_tiles)],
            attn_grad.at[pl.ds(width_tiles, attn_grad.shape[0] - width_tiles)], ahead_sem.at[1],
        ),
    ]
    def weight_rows(i):
        size = chunk_ref.shape[1]
        return pltpu.make_async_copy(qkv_ref.at[i, pl.ds(0, size)], chunk_ref.at[i % 2], ahead_sem.at[2 + i % 2])

    for copy in ahead + [weight_rows(0), weight_rows(1)]:
        copy.start()
    total = kvh * n
    pace = 9
    kv_due = sorted((8 * (i + 1) + (0, 3, 15, 27)[stage], stage, i) for i in range(kvh) for stage in range(4))

    @pl.loop(0, total)
    def _(step):
        g, j = step // n, step % n
        for i, names in enumerate(steps):
            if i * pace < total:
                pl.when(step == i * pace)(functools.partial(run, *names))
        for due, stage, i in kv_due:
            if due < total:
                pl.when(step == due)(functools.partial(run_kv, (stage, i)))
        own, other = attend_back_step(
            n, me, g, j, deal_ref, start_ref, q_ref, kv_in, do_ref, lse_ref, delta_ref, dqt_ref, dkv_ref
        )
        pl.when(j == 0)(own)
        pl.when(j > 0)(other)

        @pl.when(j == n - 1)
        def _():
            dq_ref[g] = jnp.concatenate([(dqt_ref[b] * 0.125).T[:, :HD] for b in range(2)], axis=1)

    cos, sin = cos_ref[...], -sin_ref[...]

    def head(index):
        if index < heads:
            return jnp.concatenate(
                [
                    dq_ref[index // share, (index % share) * block : (index % share + 1) * block, b * HD : (b + 1) * HD]
                    for b in range(2)
                ],
                axis=0,
            )
        g = index - heads
        low = 0 if g < kvh else HD
        return jnp.concatenate([kv_sum[g % kvh, b, :, low : low + HD] for b in range(2)], axis=0)

    count = heads + 2 * kvh
    tiles = -(-count // 2)
    turned_ref[...] = n1_ref[...].T

    def some_tiles(low, high):
        for t in range(low, high):
            right = head(2 * t + 1) if 2 * t + 1 < count else jnp.zeros((rows, HD), F32)
            pair = jnp.concatenate([head(2 * t), right], axis=1)
            if 2 * t < heads + kvh:
                pair = rope_tile(pair, cos, sin)
            gp_ref[:, t * LANES : (t + 1) * LANES] = pair.astype(BF16)
        for t in range(low, high, 2):
            some = min(2, high - t)
            part = nn(turned_ref[...], gp_ref[:, t * LANES : (t + some) * LANES]).astype(BF16)
            for i in range(some):
                tile = part[:, i * LANES : (i + 1) * LANES]
                attn_grad[t + i] = tile + spill_ref[...] if t + i == tiles - 1 else tile

    rest = [names for i, names in enumerate(steps) if i * pace >= total]
    late = [(stage, i) for due, stage, i in kv_due if due >= total]
    run_kv(late[0])
    some_tiles(0, heads // 2)
    for copy in ahead:
        copy.wait()
    run_kv(*[key for key in late[1:] if key[0] < 2 or key[1] < kvh - 1])
    run(*rest[0])
    run_kv(*[key for key in late[1:] if key[0] >= 2 and key[1] == kvh - 1])
    some_tiles(heads // 2, tiles)
    run(("begin", ATTN, order[0]), ("begin", ATTN, order[1]), ("stage1", ATTN, order[0]), *rest[1])
    shard = width // fsdp
    pieces = []
    for i in range(fsdp):
        weight_rows(i).wait()
        rows_in = jnp.concatenate([chunk_ref[i % 2, t * shard : (t + 1) * shard, :] for t in range(tiles)], axis=1)
        pieces.append(nt(gp_ref[...], rows_in))
        if i + 2 < fsdp:
            weight_rows(i + 2).start()
    gn_ref[...] = jnp.concatenate(pieces, axis=1)
    x = x_ref[...].astype(F32)
    inverse = rms_inverse(x)
    scaled = x * inverse
    grad_normed = gn_ref[...]
    weighted = grad_normed * gain_row(gains_ref, 0, fsdp, width // fsdp)
    gain_one = jnp.sum(grad_normed * scaled, axis=0, keepdims=True)
    gain_two = gain_two_ref[0:1, :]
    tail = gain_sum.shape[3] - shard
    for i in range(fsdp):
        both = jnp.concatenate(
            [gain_one[:, i * shard : (i + 1) * shard], gain_two[:, i * shard : (i + 1) * shard]], axis=0
        )
        both = jnp.concatenate([both, jnp.zeros((2, tail), F32)], axis=1)
        gain_sum[0, i] = jnp.concatenate([both, jnp.zeros((6, gain_sum.shape[3]), F32)], axis=0)
    run(("gain", 0))
    tg_ref[...] = (
        gr_ref[...] + inverse * (weighted - scaled * jnp.mean(weighted * scaled, axis=1, keepdims=True))
    ).astype(BF16)
    chunk2 = [(ATTN, d) for d in order]
    for i in range(1, len(chunk2) + 2):
        names = []
        if i + 1 < len(chunk2):
            names.append(("begin",) + chunk2[i + 1])
        if i < len(chunk2):
            names.append(("stage1",) + chunk2[i])
        if i <= len(chunk2):
            names.append(("stage2",) + chunk2[i - 1])
        if i >= 2:
            names.append(("stage3",) + chunk2[i - 2])
        if i <= 3:
            names.append(("gain", i))
        if i + 1 < len(rest):
            names += rest[i + 1]
        run(*names)
    for i, what in enumerate(("close", "close2", "close3", "close4")):
        names = rest[len(chunk2) + 3 + i] if len(chunk2) + 3 + i < len(rest) else []
        run((what, ATTN), *names)
    for names in rest[len(chunk2) + 7 :]:
        run(*names)
    run("gain close", "drain")
    run_kv("drain")


def whole(shape, dtype):
    return jax.ShapeDtypeStruct(shape, dtype)


def params(ident=None):
    extra = {} if ident is None else {"collective_id": ident, "has_side_effects": True}
    return pltpu.CompilerParams(vmem_limit_bytes=VMEM_LIMIT, **extra)


SMEM = pl.BlockSpec(memory_space=pltpu.SMEM)
VMEM = pl.BlockSpec(memory_space=pltpu.VMEM)
ANY = pl.BlockSpec(memory_space=pl.ANY)


def finish_kernel(
    heads, deal_ref, result_ref, tokens_ref, attn_ref, ff_ref, down_ref,
    out_ref, tg_ref, q_ref, kt_ref, vt_ref, o_ref, gate_ref, up_ref, dt_ref,
):
    me = lax.axis_index("ctx")
    flip = deal_ref[2 * me] > deal_ref[2 * me + 1]
    out_ref[...] = ordered(flip, result_ref[...]).T
    tg_ref[...] = ordered(flip, tokens_ref[...]).T
    width, kv_width = q_ref.shape[1], kt_ref.shape[0]
    half = width % LANES
    full = width // LANES

    def tile(t):
        return attn_ref[t].astype(F32)

    for t in range(full):
        q_ref[:, t * LANES : (t + 1) * LANES] = tile(t)
    q_ref[:, full * LANES :] = tile(full)[:, :half]
    kt_ref[0 : LANES - half, :] = tile(full).T[half:, :]
    at = LANES - half
    for t in range(full + 1, (width + kv_width) // LANES):
        kt_ref[at : at + LANES, :] = tile(t).T
        at += LANES
    first = (width + kv_width) // LANES
    spill = (width + 2 * kv_width) // LANES
    for i in range(spill - first):
        vt_ref[i * LANES : (i + 1) * LANES, :] = tile(first + i).T
    vt_ref[(spill - first) * LANES :, :] = tile(spill).T[: kv_width % LANES, :]
    for i in range(full):
        o_ref[:, i * LANES : (i + 1) * LANES] = tile(spill + 1 + i)
    o_ref[:, full * LANES :] = tile(spill)[:, LANES - half :]
    for t in range(ff_ref.shape[1]):
        gate_ref[:, t * LANES : (t + 1) * LANES] = ff_ref[0, t].astype(F32)
        up_ref[:, t * LANES : (t + 1) * LANES] = ff_ref[1, t].astype(F32)
    for t in range(down_ref.shape[0]):
        high = min((t + 1) * LANES, dt_ref.shape[0])
        dt_ref[t * LANES : high, :] = down_ref[t].astype(F32).T[: high - t * LANES, :]


def cube_body(
    tokens, attn_gain, query_weight, key_weight, value_weight, out_weight, mlp_gain, gate_weight,
    up_weight, down_weight, cotangent, cont_lengths, block_deal,
):
    n, fsdp = lax.axis_size("ctx"), lax.axis_size("fsdp")
    me = lax.axis_index("ctx")
    row_count, width = tokens.shape[1:]
    kv_width = key_weight.shape[1]
    shard, hidden = gate_weight.shape
    down_shard = down_weight.shape[0]
    block = row_count // 2
    heads, kvh = width // HD, kv_width // HD
    share = heads // kvh
    stack = share * block
    sizes = (heads, kvh, block)
    turns = np.tile(THETA ** (-2.0 * np.arange(HD // 2) / HD), (8, LANES // (HD // 2))).astype(np.float32)
    pad = -shard % LANES
    gains_shape = (8, shard + pad)
    gain_shape = (fsdp,) + gains_shape
    attn_tiles = (2 * width + 2 * kv_width) // LANES
    ff_tiles = hidden // LANES
    down_tiles = -(-width // LANES)
    heads_shape = (kvh, 2, stack, LANES)
    row_shape = (kvh, 2, 8, stack)
    kv_shape = (n, 2, kvh, block, LANES)
    dma = pltpu.SemaphoreType.DMA
    mixed = (width + 2 * kv_width) // LANES
    qkv_tiles = -(-(width + 2 * kv_width) // LANES)
    qkv_shape = (fsdp, -(-qkv_tiles * shard // LANES) * LANES, LANES)
    (
        x, cos, sin, normed_one, q, kv_all, lse, gains, w_qkv,
        result, grad_resid, grad_heads, deltas, gain_two, out_grad, ff_grad, down_grad,
    ) = pl.pallas_call(
        functools.partial(front_kernel, sizes, n, fsdp, ({}, {})),
        out_shape=(
            whole((row_count, width), BF16),
            whole((row_count, LANES), F32),
            whole((row_count, LANES), F32),
            whole((row_count, width), BF16),
            whole(heads_shape, BF16),
            whole(kv_shape, BF16),
            whole(row_shape, F32),
            whole(gain_shape, F32),
            whole(qkv_shape, BF16),
            whole((row_count, width), BF16),
            whole((row_count, width), F32),
            whole(heads_shape, BF16),
            whole(row_shape, F32),
            whole((8, width), F32),
            whole((attn_tiles - mixed, width, LANES), BF16),
            whole((2, ff_tiles, width, LANES), BF16),
            whole((down_tiles, hidden, LANES), BF16),
        ),
        in_specs=[SMEM] * 2 + [VMEM] * 12,
        out_specs=(VMEM,) * 5 + (ANY, VMEM, VMEM, ANY) + (VMEM,) * 5 + (ANY,) * 3,
        scratch_shapes=[
            pltpu.VMEM(qkv_shape, BF16),
            pltpu.VMEM((fsdp, down_tiles * shard, LANES), BF16),
            pltpu.VMEM((2, ff_tiles, fsdp * shard, LANES), BF16),
            pltpu.VMEM((down_tiles, fsdp * down_shard, LANES), BF16),
            pltpu.VMEM(kv_shape, BF16),
            pltpu.VMEM(heads_shape, F32),
            pltpu.VMEM(gain_shape, F32),
            pltpu.VMEM((8, stack), jnp.int32),
            pltpu.VMEM((kvh, 2, 8, stack), F32),
            pltpu.VMEM((kvh, 2, LANES, stack), F32),
            pltpu.VMEM((row_count, width), BF16),
            pltpu.VMEM((row_count, width), F32),
            pltpu.VMEM((row_count, width), BF16),
            pltpu.VMEM((row_count, hidden // 4), BF16),
            pltpu.VMEM((row_count, hidden // 4), BF16),
            pltpu.VMEM((row_count, hidden // 4), BF16),
            pltpu.VMEM((width, row_count), BF16),
            pltpu.VMEM((row_count, width), F32),
            pltpu.VMEM((attn_tiles - mixed, width, LANES), BF16),
            pltpu.VMEM((2, ff_tiles // 4, width, LANES), BF16),
            pltpu.VMEM((down_tiles, hidden // 4, LANES), BF16),
            dma((99,)), dma((99,)), dma((14,)), dma((14,)), dma((2,)), dma((3,)),
        ],
        compiler_params=params(0),
        name="front",
    )(
        block_deal, cont_lengths, tokens[0].T, attn_gain[None], mlp_gain[None], turns,
        query_weight, key_weight.T, value_weight.T, out_weight, gate_weight, up_weight, down_weight.T,
        cotangent[0].T,
    )

    attn_rows = -(-shard // 32) * 16
    shapes = ((attn_tiles // 4, attn_rows, LANES), (ff_tiles // 4, shard, LANES), (down_shard, LANES))
    buffers = [pltpu.VMEM((fsdp, 4) + shape, BF16) for shape in shapes[1:]]
    for lead in ((fsdp, 4), (fsdp - 1, 2), (fsdp - 1,), (fsdp - 2,), (4,)):
        buffers += [pltpu.VMEM(lead + shape, BF16) for shape in shapes]
    piece = (2, block, LANES)
    tokens_grad, gain_grads, attn_w, ff_w, down_w = pl.pallas_call(
        functools.partial(back_kernel, sizes, n, fsdp, ({}, {})),
        out_shape=(
            whole((row_count, width), BF16),
            whole(gains_shape, F32),
            whole((attn_tiles, shard, LANES), BF16),
            whole((2, ff_tiles, shard, LANES), BF16),
            whole((down_tiles, down_shard, LANES), BF16),
        ),
        in_specs=[SMEM] * 2 + [VMEM] * 12 + [ANY] * 4,
        out_specs=(VMEM, VMEM, ANY, ANY, ANY),
        scratch_shapes=[
            pltpu.VMEM((8, stack), jnp.int32),
            pltpu.VMEM((width, LANES), BF16),
            pltpu.VMEM((2, qkv_tiles * shard, LANES), BF16),
            pltpu.VMEM((2, LANES, stack), F32),
            pltpu.VMEM((kvh, stack, LANES), F32),
            pltpu.VMEM((n, kvh) + piece, BF16),
            pltpu.VMEM((kvh,) + piece, F32),
            pltpu.VMEM((kvh, 4) + piece, BF16),
            pltpu.VMEM((kvh, 2) + piece, BF16),
            pltpu.VMEM((kvh,) + piece, BF16),
            pltpu.VMEM((row_count, qkv_tiles * LANES), BF16),
            pltpu.VMEM((row_count, width), F32),
            pltpu.VMEM((width, row_count), BF16),
            pltpu.VMEM((attn_tiles, width, LANES), BF16),
        ]
        + buffers
        + [
            pltpu.VMEM((4,) + gain_shape, F32),
            pltpu.VMEM((3,) + gain_shape, F32),
            pltpu.VMEM((fsdp - 1,) + gains_shape, F32),
            dma((123,)), dma((123,)), dma((7 * kvh,)), dma((7 * kvh,)), dma((51,)), dma((4,)),
        ],
        compiler_params=params(1),
        name="back",
    )(
        block_deal, cont_lengths, q, kv_all, grad_heads, deltas, lse, x, normed_one, grad_resid, gains, gain_two,
        cos, sin, w_qkv, out_grad, ff_grad, down_grad,
    )

    out_t, tg_t, q_w, k_t, v_t, o_w, gate_w, up_w, d_t = pl.pallas_call(
        functools.partial(finish_kernel, heads),
        out_shape=(
            whole((width, row_count), BF16),
            whole((width, row_count), BF16),
            whole((shard, width), F32),
            whole((kv_width, shard), F32),
            whole((kv_width, shard), F32),
            whole((shard, width), F32),
            whole((shard, hidden), F32),
            whole((shard, hidden), F32),
            whole((width, down_shard), F32),
        ),
        in_specs=[SMEM] + [VMEM] * 5,
        out_specs=(VMEM,) * 9,
        compiler_params=params(),
        name="finish",
    )(block_deal, result, tokens_grad, attn_w, ff_w, down_w)
    return (
        out_t.T[None],
        tg_t.T[None],
        gain_grads[0, :shard],
        q_w,
        k_t.T,
        v_t.T,
        o_w,
        gain_grads[1, :shard],
        gate_w,
        up_w,
        d_t.T,
    )


def head_of(tiles, index):
    start = (index % 2) * HD
    return tiles[index // 2][:, start : start + HD]


def project_kernel(sizes, x_ref, gain_ref, w_ref, cos_ref, sin_ref, n1_ref, q_ref, kv_ref):
    heads, kvh, block = sizes
    share = heads // kvh
    x = x_ref[...].astype(F32)
    inverse = lax.rsqrt(jnp.mean(x * x, axis=1, keepdims=True) + EPSILON)
    normed = (x * inverse * gain_ref[...]).astype(BF16)
    n1_ref[...] = normed
    width = (heads + 2 * kvh) * HD
    raw = nn(normed, w_ref[:, :width])
    cos = cos_ref[...]
    sin = sin_ref[...]
    tiles = []
    for j in range((heads + kvh) * HD // LANES):
        tiles.append(rope_tile(raw[:, j * LANES : (j + 1) * LANES], cos, sin).astype(BF16))
    zero = jnp.zeros((block, HD), BF16)
    for h in range(heads):
        piece = head_of(tiles, h) * jnp.asarray(0.125, BF16)
        g, i = h // share, h % share
        for b in range(2):
            q_ref[g, b, i * block : (i + 1) * block, :] = jnp.concatenate(
                [piece[b * block : (b + 1) * block], zero], axis=1
            )
    for g in range(kvh):
        start = (heads + kvh + g) * HD
        value = raw[:, start : start + HD].astype(BF16)
        pair = jnp.concatenate([head_of(tiles, heads + g), value], axis=1)
        for b in range(2):
            kv_ref[b, :, g * LANES : (g + 1) * LANES] = pair[b * block : (b + 1) * block]


def attend_kernel(
    n, me_ref, pick_ref, segq_ref, segk_ref, q_ref, kv_ref, o_ref, lse_ref, s1_ref, p1_ref, s2_ref, p2_ref
):
    me = me_ref[0]
    block = kv_ref.shape[2]
    rows = q_ref.shape[2]
    keys = n * block
    qc = q_ref[0, 1]
    prompt = kv_ref[:, 0].reshape(keys, LANES)
    s1_ref[...] = nt(qc, prompt)
    own = []
    for b in range(2):
        s2_ref[b] = nt(q_ref[0, b], kv_ref[me, b])
    for j in range(1, n):
        at = lax.rem(me + j, n)
        kind = pick_ref[j]
        s2_ref[j + 1] = nt(q_ref[0, kind], kv_ref[at, kind])
    step = 16
    kinds = [pick_ref[j] == 0 for j in range(n)]

    def fold(s):
        return jnp.maximum(
            s[:, :LANES],
            jnp.concatenate(
                [s[:, LANES:], jnp.full((step, 2 * LANES - block), MASKED, F32)], axis=1
            ),
        )

    def chunk(at, carry):
        r = pl.multiple_of(at * step, step)
        rs = pl.ds(r, step)
        in_block = lax.rem(r, block)
        tri = lax.broadcasted_iota(jnp.int32, (step, block), 1) <= (
            in_block + lax.broadcasted_iota(jnp.int32, (step, block), 0)
        )
        segq = segq_ref[rs, :]
        s1 = s1_ref[rs, :]
        top_c = s1[:, :LANES]
        for t in range(1, keys // LANES):
            top_c = jnp.maximum(top_c, s1[:, t * LANES : (t + 1) * LANES])
        dp = jnp.where(tri, s2_ref[0, rs, :], MASKED)
        dc = jnp.where(tri & (segq == segk_ref[0]), s2_ref[1, rs, :], MASKED)
        top_c = jnp.maximum(top_c, fold(dc))
        top_p = fold(dp)
        others = []
        for j in range(1, n):
            s = jnp.where((segq == segk_ref[j]) | kinds[j], s2_ref[j + 1, rs, :], MASKED)
            others.append(s)
            f = fold(s)
            top_p = jnp.maximum(top_p, jnp.where(kinds[j], f, MASKED))
            top_c = jnp.maximum(top_c, jnp.where(kinds[j], MASKED, f))
        m_p = jnp.max(top_p, axis=1, keepdims=True)
        m_c = jnp.max(top_c, axis=1, keepdims=True)
        p1_ref[rs, :] = jnp.exp2((s1 - m_c) * LOG2E).astype(BF16)
        p2_ref[0, rs, :] = jnp.exp2((dp - m_p) * LOG2E).astype(BF16)
        p2_ref[1, rs, :] = jnp.exp2((dc - m_c) * LOG2E).astype(BF16)
        for j in range(1, n):
            m = jnp.where(kinds[j], m_p, m_c)
            p2_ref[j + 1, rs, :] = jnp.exp2((others[j - 1] - m) * LOG2E).astype(BF16)
        lse_ref[0, 0, rs, :] = jnp.broadcast_to(m_p * LOG2E, (step, LANES))
        lse_ref[0, 1, rs, :] = jnp.broadcast_to(m_c * LOG2E, (step, LANES))
        return carry

    lax.fori_loop(0, rows // step, chunk, 0)

    def with_ones(tile):
        return jnp.concatenate([tile, jnp.ones(tile.shape, BF16)], axis=1)

    acc = [nn(p2_ref[b], with_ones(kv_ref[me, b])) for b in range(2)]
    acc[1] = acc[1] + nn(p1_ref[...], with_ones(prompt))
    for j in range(1, n):
        at = lax.rem(me + j, n)
        part = nn(p2_ref[j + 1], with_ones(kv_ref[at, pick_ref[j]]))
        acc[0] = acc[0] + jnp.where(kinds[j], part, 0.0)
        acc[1] = acc[1] + jnp.where(kinds[j], 0.0, part)
    for b in range(2):
        total = acc[b][:, LANES:]
        o_ref[0, b] = acc[b][:, :LANES] / total
        lse_ref[0, b] = lse_ref[0, b] + jnp.log2(total)


def attend_back_kernel(
    n, me_ref, pick_ref, segq_ref, segk_ref, q_ref, kv_ref, do_ref, o_ref, lse_ref, dq_ref, dkv_ref, row_ref, dqt_ref
):
    me = me_ref[0]
    block = kv_ref.shape[2]
    rows = q_ref.shape[2]
    first = (lax.broadcasted_iota(jnp.int32, (8, LANES), 1) == 0).astype(F32)
    ones = jnp.ones((8, LANES), F32)

    def to_row(lhs, matrix):
        return lax.dot_general(
            lhs, matrix, (((1,), (1,)), ((), ())), precision=lax.Precision.HIGHEST,
            preferred_element_type=F32,
        )

    for b in range(2):
        row_ref[b] = to_row(first, lse_ref[0, b])
        row_ref[2 + b] = to_row(ones, do_ref[0, b].astype(F32) * o_ref[0, b])
    lane_rows = lax.rem(lax.broadcasted_iota(jnp.int32, (block, rows), 1), block)
    tri = lax.broadcasted_iota(jnp.int32, (block, rows), 0) <= lane_rows

    def pair(kind, tile, mask):
        q = q_ref[0, kind]
        do = do_ref[0, kind]
        p = jnp.exp2(nt(tile, q) * LOG2E - row_ref[kind, 0:1, :])
        if mask is not None:
            p = jnp.where(mask, p, 0.0)
        ds = (p * (nt(tile, do) - row_ref[2 + kind, 0:1, :])).astype(BF16)
        return nn(ds, q) + nn(p.astype(BF16), do), tn(tile, ds)

    segq = segq_ref[0:1, :]
    same_own = segq == segk_ref[0]
    own0, own1 = kv_ref[me, 0], kv_ref[me, 1]
    d0, q0 = pair(0, own0, tri)
    d1, q1 = pair(1, own1, tri & same_own)
    d2, q2 = pair(1, own0, None)
    dkv_ref[me, 0] = (d0 + d2).astype(dkv_ref.dtype)
    dkv_ref[me, 1] = d1.astype(dkv_ref.dtype)
    dqt_ref[0] = q0
    dqt_ref[1] = q1 + q2

    def other(j, carry):
        at = lax.rem(me + j, n)
        kind = pick_ref[j]
        is_prompt = kind == 0
        full, q_full = pair(1, kv_ref[at, 0], None)
        mask = (segq == segk_ref[j]) | is_prompt
        part, q_part = pair(kind, kv_ref[at, kind], mask)
        dkv_ref[at, 0] = (full + jnp.where(is_prompt, part, 0.0)).astype(dkv_ref.dtype)
        dkv_ref[at, 1] = jnp.where(is_prompt, 0.0, part).astype(dkv_ref.dtype)
        dqt_ref[0] = dqt_ref[0] + jnp.where(is_prompt, q_part, 0.0)
        dqt_ref[1] = dqt_ref[1] + q_full + jnp.where(is_prompt, 0.0, q_part)
        return carry

    lax.fori_loop(1, n, other, 0)
    for b in range(2):
        dq_ref[0, b] = (dqt_ref[b] * 0.125).T


def mid_kernel(sizes, o_ref, x_ref, wo_ref, gain_ref, att_ref, resid_ref, n2_ref):
    heads, kvh, block = sizes
    share = heads // kvh
    for b in range(2):
        columns = []
        for h in range(heads):
            g, i = h // share, h % share
            columns.append(o_ref[g, b, i * block : (i + 1) * block, HD:])
        attended = jnp.concatenate(columns, axis=1).astype(BF16)
        rs = slice(b * block, (b + 1) * block)
        att_ref[rs, :] = attended
        resid = x_ref[rs, :].astype(F32) + nn(attended, wo_ref[...])
        resid_ref[rs, :] = resid
        inverse = lax.rsqrt(jnp.mean(resid * resid, axis=1, keepdims=True) + EPSILON)
        n2_ref[rs, :] = (resid * inverse * gain_ref[...]).astype(BF16)


def branch_kernel(sizes, gb_ref, wo_ref, do_ref):
    heads, kvh, block = sizes
    share = heads // kvh
    grad = nt(gb_ref[...], wo_ref[...]).astype(BF16)
    zero = jnp.zeros((block, HD), BF16)
    for h in range(heads):
        g, i = h // share, h % share
        for b in range(2):
            do_ref[g, b, i * block : (i + 1) * block, :] = jnp.concatenate(
                [zero, grad[b * block : (b + 1) * block, h * HD : (h + 1) * HD]], axis=1
            )


def unrope_kernel(sizes, dq_ref, dkv_ref, cos_ref, sin_ref, out_ref):
    heads, kvh, block = sizes
    share = heads // kvh
    for b in range(2):
        rs = slice(b * block, (b + 1) * block)
        cos, sin = cos_ref[rs, :], -sin_ref[rs, :]
        columns = [
            dq_ref[h // share, b, (h % share) * block : (h % share + 1) * block, :HD]
            for h in range(heads)
        ]
        columns += [dkv_ref[b, :, g * LANES : g * LANES + HD].astype(F32) for g in range(kvh)]
        tiles = []
        for j in range((heads + kvh) // 2):
            pair = jnp.concatenate(columns[2 * j : 2 * j + 2], axis=1)
            tiles.append(rope_tile(pair, cos, sin).astype(BF16))
        values = [dkv_ref[b, :, g * LANES + HD : (g + 1) * LANES].astype(BF16) for g in range(kvh)]
        out_ref[rs, :] = jnp.concatenate(tiles + values, axis=1)


def local_call(kernel, out_shape, name, **extra):
    return pl.pallas_call(
        kernel,
        out_shape=out_shape,
        compiler_params=pltpu.CompilerParams(vmem_limit_bytes=VMEM_LIMIT),
        name=name,
        **extra,
    )


def gather_rows(array, axis):
    return lax.all_gather(array, axis, axis=0, tiled=True)


def norm_back(grad_normed, scaled, inverse, gain):
    weighted = grad_normed * gain
    return inverse * (weighted - scaled * jnp.mean(weighted * scaled, axis=1, keepdims=True))


def general_body(
    tokens, attn_gain, query_weight, key_weight, value_weight, out_weight, mlp_gain, gate_weight,
    up_weight, down_weight, cotangent, cont_lengths, block_deal,
):
    n = lax.axis_size("ctx")
    me = lax.axis_index("ctx")
    row_count, width = tokens.shape[1:]
    kv_width = key_weight.shape[1]
    hidden = gate_weight.shape[1]
    block = row_count // 2
    total_rows = row_count * n
    prompt_size = total_rows // 2
    heads, kvh = width // HD, kv_width // HD
    share = heads // kvh
    stack = share * block
    sizes = (heads, kvh, block)

    deal = block_deal.reshape(n, 2)
    flip = deal[me, 0] > deal[me, 1]

    def ordered(rows):
        halves = rows.reshape(2, block, rows.shape[-1])
        return jnp.where(flip, halves[::-1], halves).reshape(rows.shape)

    x = ordered(tokens[0])
    cot = ordered(cotangent[0])
    naturals = jnp.sort(deal, axis=1)
    natural = naturals[:, :, None] * block + jnp.arange(block, dtype=jnp.int32)
    offset = natural - prompt_size
    lengths = cont_lengths[0]
    ending = jnp.cumsum(lengths)
    segment = jnp.sum((offset[..., None] >= ending).astype(jnp.int32), axis=-1)
    inside = segment[..., None] == jnp.arange(lengths.shape[0], dtype=jnp.int32)
    beginning = jnp.sum(jnp.where(inside, ending - lengths, 0), axis=-1)
    position = jnp.where(offset < 0, natural, prompt_size + offset - beginning)
    own_position = position[me].reshape(row_count)
    frequency = THETA ** (-2.0 * jnp.arange(HD // 2, dtype=F32) / HD)
    angle = own_position.astype(F32)[:, None] * frequency[None, :]
    cos, sin = jnp.cos(angle), jnp.sin(angle)
    cos = jnp.concatenate([cos, cos, cos, cos], axis=1)
    sin = jnp.concatenate([-sin, sin, -sin, sin], axis=1)
    around = (me + jnp.arange(n, dtype=jnp.int32)) % n
    first_natural = naturals[:, 0]
    pick = (first_natural[around] >= first_natural[me]).astype(jnp.int32)
    segk = segment[around, 1]
    segq = jnp.tile(segment[me, 1], share)
    me_arr = me.reshape(1).astype(jnp.int32)

    attn_rows = jnp.concatenate([query_weight, key_weight, value_weight, out_weight], axis=1)
    w_attn = gather_rows(attn_rows, "fsdp")
    qkv_width = width + 2 * kv_width
    w_qkv = w_attn[:, :qkv_width]
    w_out = w_attn[:, qkv_width:]
    gain_one = gather_rows(attn_gain, "fsdp").astype(F32)
    gain_two = gather_rows(mlp_gain, "fsdp").astype(F32)
    w_gate = gather_rows(gate_weight, "fsdp")
    w_up = gather_rows(up_weight, "fsdp")
    w_down = gather_rows(down_weight, "fsdp")

    normed_one, q, kv = local_call(
        functools.partial(project_kernel, sizes),
        (
            whole((row_count, width), BF16),
            whole((kvh, 2, stack, LANES), BF16),
            whole((2, block, kvh * LANES), BF16),
        ),
        "project",
    )(x, gain_one[None], w_attn, cos, sin)
    kv_all = lax.all_gather(kv, "ctx", axis=0)

    smem = pl.BlockSpec(memory_space=pltpu.SMEM)
    per_group = pl.BlockSpec((1, 2, stack, LANES), lambda g: (g, 0, 0, 0))
    kv_spec = pl.BlockSpec((n, 2, block, LANES), lambda g: (0, 0, 0, g))

    def full(array):
        rank = array.ndim
        return pl.BlockSpec(array.shape, lambda g: (0,) * rank)

    segq_col, segk_row = segq[:, None], segk[:, None, :]
    attended_heads, lse = local_call(
        functools.partial(attend_kernel, n),
        (whole((kvh, 2, stack, LANES), F32), whole((kvh, 2, stack, LANES), F32)),
        "attend",
        grid=(kvh,),
        in_specs=[smem, smem, full(segq_col), full(segk_row), per_group, kv_spec],
        out_specs=(per_group, per_group),
        scratch_shapes=[
            pltpu.VMEM((stack, n * block), F32),
            pltpu.VMEM((stack, n * block), BF16),
            pltpu.VMEM((n + 1, stack, block), F32),
            pltpu.VMEM((n + 1, stack, block), BF16),
        ],
    )(me_arr, pick, segq_col, segk_row, q, kv_all)

    attended, resid, normed_two = local_call(
        functools.partial(mid_kernel, sizes),
        (
            whole((row_count, width), BF16),
            whole((row_count, width), F32),
            whole((row_count, width), BF16),
        ),
        "mid",
    )(attended_heads, x, w_out, gain_two[None])

    inverse_two = lax.rsqrt(jnp.mean(resid * resid, axis=1, keepdims=True) + EPSILON)
    scaled_two = resid * inverse_two
    gate = nn(normed_two, w_gate)
    upward = nn(normed_two, w_up)
    sigma = jax.nn.sigmoid(gate)
    activated = gate * sigma
    product = (activated * upward).astype(BF16)
    result = resid + nn(product, w_down)
    grad_prod = nt(cot, w_down)
    grad_gate = (grad_prod * upward * sigma * (1.0 + gate * (1.0 - sigma))).astype(BF16)
    grad_up = (grad_prod * activated).astype(BF16)
    grad_normed_two = nt(grad_gate, w_gate) + nt(grad_up, w_up)
    gain_two_part = jnp.sum(grad_normed_two * scaled_two, axis=0)
    grad_resid = cot.astype(F32) + norm_back(grad_normed_two, scaled_two, inverse_two, gain_two)
    grad_branch = grad_resid.astype(BF16)

    grad_heads = local_call(
        functools.partial(branch_kernel, sizes), whole((kvh, 2, stack, LANES), BF16), "branch"
    )(grad_branch, w_out)

    segq_row, segk_col = segq[None, :], segk[:, :, None]
    grad_query, grad_kv = local_call(
        functools.partial(attend_back_kernel, n),
        (whole((kvh, 2, stack, LANES), F32), whole((n, 2, block, kvh * LANES), F32)),
        "attend_back",
        grid=(kvh,),
        in_specs=[smem, smem, full(segq_row), full(segk_col)]
        + [per_group, kv_spec, per_group, per_group, per_group],
        out_specs=(per_group, kv_spec),
        scratch_shapes=[
            pltpu.VMEM((4, 8, stack), F32),
            pltpu.VMEM((2, LANES, stack), F32),
        ],
    )(me_arr, pick, segq_row, segk_col, q, kv_all, grad_heads, attended_heads, lse)

    kv_sum = lax.psum_scatter(grad_kv, "ctx", scatter_dimension=0, tiled=False)
    grad_projected = local_call(
        functools.partial(unrope_kernel, sizes), whole((row_count, qkv_width), BF16), "unrope"
    )(grad_query, kv_sum, cos, sin)

    x_float = x.astype(F32)
    inverse_one = lax.rsqrt(jnp.mean(x_float * x_float, axis=1, keepdims=True) + EPSILON)
    scaled_one = x_float * inverse_one
    grad_normed_one = nt(grad_projected, w_qkv)
    gain_one_part = jnp.sum(grad_normed_one * scaled_one, axis=0)
    tokens_grad = (
        grad_resid + norm_back(grad_normed_one, scaled_one, inverse_one, gain_one)
    ).astype(BF16)

    def spread(partial):
        rows = lax.psum_scatter(partial.astype(BF16), "fsdp", scatter_dimension=0, tiled=True)
        return lax.psum(rows, "ctx").astype(F32)

    grad_gate_w = spread(tn(normed_two, grad_gate))
    grad_up_w = spread(tn(normed_two, grad_up))
    grad_down_w = spread(tn(product, cot))
    grad_out_w = spread(tn(attended, grad_branch))
    grad_qkv_w = spread(tn(normed_one, grad_projected))
    gains = spread(jnp.stack([gain_one_part, gain_two_part], axis=1))
    return (
        ordered(result.astype(BF16))[None],
        ordered(tokens_grad)[None],
        gains[:, 0],
        grad_qkv_w[:, :width],
        grad_qkv_w[:, width : width + kv_width],
        grad_qkv_w[:, width + kv_width :],
        grad_out_w,
        gains[:, 1],
        grad_gate_w,
        grad_up_w,
        grad_down_w,
    )


def solution(mesh):
    rows, matrix, vector = P("fsdp", "ctx", None), P("fsdp", None), P("fsdp")
    cube = dict(mesh.shape) == {"ctx": 8, "fsdp": 4}
    return jax.shard_map(
        cube_body if cube else general_body,
        mesh=mesh,
        in_specs=(rows, vector, matrix, matrix, matrix, matrix, vector, matrix, matrix, matrix)
        + (rows, matrix, P()),
        out_specs=(rows, rows, vector, matrix, matrix, matrix, matrix, vector, matrix, matrix, matrix),
        check_vma=False,
    )
```
